32 devices in a mesh: seq: 8 (over z, x), grp: 4 (over y, core).
Axes of the slice: x: 2, y: 2, z: 4, core: 2. Of those that a mesh axis runs over, the one named last changes fastest.
Arguments:
- tokens: float32 [16384, 768], P(('seq', 'grp')), may hold values from -6 to 6
- coordinates: int32 [16384, 2], P(('seq', 'grp')), may hold values from 0 to 1023
- lengths: int32 [5], replicated, may hold values from 1 to 16128, 16384 in all
- valid: int32 [16384], P(('seq', 'grp')), may hold values 0 or 1
- first_gain: float32 [768], replicated, may hold values from 0.5 to 1.5
- first_shift: float32 [768], replicated, may hold values from -3 to 3
- query_weight: bfloat16 [768, 768], P('seq', 'grp'), may hold values from -0.21875 to 0.21875
- query_bias: float32 [768], replicated, may hold values from -3 to 3
- key_weight: bfloat16 [768, 768], P('seq', 'grp'), may hold values from -0.21875 to 0.21875
- value_weight: bfloat16 [768, 768], P('seq', 'grp'), may hold values from -0.21875 to 0.21875
- value_bias: float32 [768], replicated, may hold values from -3 to 3
- output_weight: bfloat16 [768, 768], P('seq', 'grp'), may hold values from -3.5 to 3.5
- output_bias: float32 [768], replicated, may hold values from -3 to 3
- second_gain: float32 [768], replicated, may hold values from 0.5 to 1.5
- second_shift: float32 [768], replicated, may hold values from -3 to 3
- inner_weight: bfloat16 [768, 3072], P('seq', 'grp'), may hold values from -0.21875 to 0.21875
- inner_bias: float32 [3072], replicated, may hold values from -3 to 3
- outer_weight: bfloat16 [3072, 768], P('seq', 'grp'), may hold values from -0.109375 to 0.109375
- outer_bias: float32 [768], replicated, may hold values from -3 to 3
- cotangent: float32 [16384, 768], P(('seq', 'grp')), may hold values from -6 to 6
Outputs:
- output: float32 [16384, 768], P(('seq', 'grp'))
- token_grad: float32 [16384, 768], P(('seq', 'grp'))
- first_gain_grad: float32 [768], replicated
- first_shift_grad: float32 [768], replicated
- query_weight_grad: float32 [768, 768], P('seq', 'grp')
- query_bias_grad: float32 [768], replicated
- key_weight_grad: float32 [768, 768], P('seq', 'grp')
- value_weight_grad: float32 [768, 768], P('seq', 'grp')
- value_bias_grad: float32 [768], replicated
- output_weight_grad: float32 [768, 768], P('seq', 'grp')
- output_bias_grad: float32 [768], replicated
- second_gain_grad: float32 [768], replicated
- second_shift_grad: float32 [768], replicated
- inner_weight_grad: float32 [768, 3072], P('seq', 'grp')
- inner_bias_grad: float32 [3072], replicated
- outer_weight_grad: float32 [3072, 768], P('seq', 'grp')
- outer_bias_grad: float32 [768], replicated
The draws below stay inside these ranges and needn't reach their ends.
Inputs may be any that keep to these rules, and one draw needn't show every extreme that they name: Every slide has at least one row; the lengths add up to 16384.
All inputs are finite; a program needn't handle non-finite values. No bound on the sum of `valid` on one device may be relied on, other than what follows from the above.
Results may differ from the reference program's by a relative error of at most 0.013.
Values may be sent and summed in bfloat16 or wider, within the bound.
A program may use at most 320 MiB of HBM per device.

```python
import math
import jax
import jax.numpy as jnp
import numpy as np
from jax import lax

HEADS = 16
HD = 48
D = 768
FF = 3072
SUBLEN = 1024
SLIDES = 5
TOK_DEV = 512
TOKENS = 16384


def plant(drawn, stream_key, least, top_value):
    shape = drawn.shape
    spot = [jax.random.randint(jax.random.fold_in(stream_key, axis), (), 0, shape[axis]) for axis in range(len(shape))]
    drawn = drawn.at[tuple(spot)].set(least)
    longest = shape.index(max(shape))
    spot[longest] = (spot[longest] + 1) % shape[longest]
    return drawn.at[tuple(spot)].set(top_value)


def level_of(own_key, dims, cuts, smallest, top_value):
    factor_of, own = 1.0, jax.random.fold_in(own_key, 6)
    for dim, blocks in cuts:
        draws = jnp.exp(jax.random.uniform(jax.random.fold_in(own, dim), (blocks,), jnp.float32, smallest / len(cuts), top_value / len(cuts)))
        factor_of = factor_of * jnp.repeat(draws, dims[dim] // blocks).reshape([-1 if axis == dim else 1 for axis in range(len(dims))])
    return factor_of


def length_profile(number_of, total, bound, skew):
    weights = [(1 << 20) // math.isqrt(standing ** skew) + 1 for standing in range(2, number_of + 1)]
    rest, counts = total - bound - (number_of - 1), [1] * (number_of - 1)
    while rest > 0:
        free = [i for i in range(number_of - 1) if counts[i] < bound]
        whole, budget = sum([weights[i] for i in free]), rest
        for i in free:
            extra = min(bound - counts[i], max(1, budget * weights[i] // whole), rest)
            counts[i] = counts[i] + extra
            rest = rest - extra
    return np.array([bound] + counts)


def ragged(rng, number_of, total, most, skew):
    if number_of == 2:
        one = jax.random.randint(rng, (), max(1, total - most), min(most, total - 1) + 1)
        return jnp.stack([one, total - one])
    sizes = jnp.asarray(length_profile(number_of, total, most, skew), jnp.int32)
    twos = (number_of - 1) // 2
    donor, taker = sizes[1:1 + 2 * twos:2], sizes[2:2 + 2 * twos:2]
    margin = jnp.minimum(donor - 1, most - taker)
    shifted = jax.random.randint(jax.random.fold_in(rng, 1), (twos,), 0, 1 << 20) % (margin + 1)
    sizes = sizes.at[1:1 + 2 * twos:2].set(donor - shifted).at[2:2 + 2 * twos:2].set(taker + shifted)
    return sizes[jax.random.permutation(jax.random.fold_in(rng, 2), number_of)]


def normal_values(rng, extent, spread, reach, shards=(), kind=jnp.bfloat16):
    entries = jax.random.normal(rng, extent, jnp.float32) * spread
    if len(shards) > 0:
        entries = level_of(rng, extent, shards, -0.22, 0.18) * entries
    return jnp.clip(entries, min=-reach, max=reach).astype(kind)


def setup_inputs(seed: int = 0) -> dict:
    key_of = jax.random.split(jax.random.key(seed), 21)
    tokens = normal_values(key_of[0], (TOKENS, D), 1.0, 6.0, ((0, 32),), jnp.float32)
    coordinates = plant(jax.random.randint(key_of[1], (TOKENS, 2), 0, 1024), jax.random.fold_in(key_of[1], 1), 0, 1023).astype(jnp.int32)
    lengths = ragged(key_of[2], SLIDES, TOKENS, min(32 * SUBLEN, TOKENS - 4 * (TOK_DEV // 8)), 1).astype(jnp.int32)
    valid = plant((jax.random.randint(key_of[3], (TOKENS,), 0, 8) < 7).astype(jnp.int32), jax.random.fold_in(key_of[3], 1), 0, 1)
    first_gain = jnp.clip(1.0 + 0.1 * jax.random.normal(key_of[4], (D,), jnp.float32), 0.5, 1.5)
    first_shift = normal_values(key_of[5], (D,), 0.5, 3.0, (), jnp.float32)
    query_weight = normal_values(key_of[6], (D, D), D ** -0.5, 0.21875, ((0, 8), (1, 4)))
    query_bias = normal_values(key_of[7], (D,), 0.5, 3.0, (), jnp.float32)
    key_weight = normal_values(key_of[8], (D, D), D ** -0.5, 0.21875, ((0, 8), (1, 4)))
    value_weight = normal_values(key_of[9], (D, D), D ** -0.5, 0.21875, ((0, 8), (1, 4)))
    value_bias = normal_values(key_of[10], (D,), 0.5, 3.0, (), jnp.float32)
    output_weight = normal_values(key_of[11], (D, D), (max(D // 256, 1)) ** -0.5, 3.5, ((0, 8), (1, 4)))
    output_bias = normal_values(key_of[12], (D,), 0.5, 3.0, (), jnp.float32)
    second_gain = jnp.clip(1.0 + 0.1 * jax.random.normal(key_of[13], (D,), jnp.float32), 0.5, 1.5)
    second_shift = normal_values(key_of[14], (D,), 0.5, 3.0, (), jnp.float32)
    inner_weight = normal_values(key_of[15], (D, FF), D ** -0.5, 0.21875, ((0, 8), (1, 4)))
    inner_bias = normal_values(key_of[16], (FF,), 0.5, 3.0, (), jnp.float32)
    outer_weight = normal_values(key_of[17], (FF, D), FF ** -0.5, 0.109375, ((0, 8), (1, 4)))
    outer_bias = normal_values(key_of[18], (D,), 0.5, 3.0, (), jnp.float32)
    cotangent = normal_values(key_of[19], (TOKENS, D), 1.0, 6.0, ((0, 32),), jnp.float32)
    return {"tokens": tokens, "coordinates": coordinates, "lengths": lengths, "valid": valid, "first_gain": first_gain, "first_shift": first_shift, "query_weight": query_weight, "query_bias": query_bias, "key_weight": key_weight, "value_weight": value_weight, "value_bias": value_bias, "output_weight": output_weight, "output_bias": output_bias, "second_gain": second_gain, "second_shift": second_shift, "inner_weight": inner_weight, "inner_bias": inner_bias, "outer_weight": outer_weight, "outer_bias": outer_bias, "cotangent": cotangent}


ratios = (1, 2, 4, 8, 16)
big_negative = -1e+30
epsilon = 1e-05
highest = lax.Precision.HIGHEST

@jax.custom_vjp
def low(v):
    return lax.optimization_barrier(v.astype(jnp.bfloat16)).astype(jnp.float32)

@jax.custom_vjp
def low_back(v):
    return v

def low_keep(v):
    return (low(v), None)

def low_pass(kept, grad):
    return (grad,)

def back_keep(v):
    return (v, None)

def back_low(kept, grad):
    return (low(grad),)
low.defvjp(low_keep, low_pass)
low_back.defvjp(back_keep, back_low)

def position_table(coordinates, width):
    quarter = width // 4
    frequency = jnp.exp(jnp.arange(quarter, dtype=jnp.float32) * (-math.log(10000.0) / quarter))
    column = coordinates[:, 0:1].astype(jnp.float32) * frequency[None, :]
    across = coordinates[:, 1:2].astype(jnp.float32) * frequency[None, :]
    return jnp.concatenate([jnp.sin(column), jnp.cos(column), jnp.sin(across), jnp.cos(across)], axis=1)

def slide_of(positions, lengths):
    ends = jnp.cumsum(lengths)
    return lax.optimization_barrier(jnp.sum((positions[..., None] >= ends).astype(jnp.int32), axis=-1))

def layer_norm(values, norm_gain, norm_shift):
    average = lax.optimization_barrier(jnp.mean(values, axis=-1, keepdims=True))
    centred = values - average
    variance = lax.optimization_barrier(jnp.mean(centred * centred, axis=-1, keepdims=True))
    return centred * lax.rsqrt(variance + epsilon) * norm_gain + norm_shift

def select_rows(tensor, ratio):
    count = tensor.shape[0] // ratio
    heads = tensor.shape[1]
    feature = tensor.shape[2]
    shaped = tensor.reshape(count, ratio, heads // ratio, ratio, feature)
    picked = jnp.diagonal(shaped, axis1=1, axis2=3)
    return jnp.swapaxes(picked, 2, 3).reshape(count, heads, feature)

def spread_rows(tensor, ratio, filler):
    count = tensor.shape[0]
    heads = tensor.shape[1]
    feature = tensor.shape[2]
    shaped = tensor.reshape(count, 1, heads // ratio, ratio, feature)
    match = jnp.arange(ratio)[:, None] == jnp.arange(ratio)[None, :]
    full = jnp.where(match[None, :, None, :, None], shaped, filler)
    return full.reshape(count * ratio, heads, feature)

def segment_attention(parts):
    query, key, value, keep, slides = parts
    scores = low_back(jnp.einsum('ihx,jhx->hij', query, key, precision=highest) * HD ** (-0.5))
    same = slides.T[:, :, None] == slides.T[:, None, :]
    own = jnp.eye(SUBLEN, dtype=bool)[None]
    allowed = same & ((keep.T[:, None, :] == 1) | own)
    masked = jnp.where(allowed, scores, big_negative)
    total = jax.nn.logsumexp(masked, axis=2)
    prob = jnp.exp(masked - total[:, :, None])
    result = low_back(jnp.einsum('hij,jhx->ihx', low(prob), value, precision=highest))
    return (result, total.T)

def dilated(query, key, value, valid, lengths):
    positions = jnp.arange(TOKENS, dtype=jnp.int32)
    results = []
    totals = []
    for ratio in ratios:
        count = TOKENS // ratio
        segments = count // SUBLEN
        picked = [select_rows(item, ratio) for item in (query, key, value)]
        keep_picked = jnp.tile(valid.reshape(count, ratio), (1, HEADS // ratio))
        place_picked = jnp.tile(positions.reshape(count, ratio), (1, HEADS // ratio))
        slide_picked = slide_of(place_picked, lengths)
        shaped = tuple((item.reshape((segments, SUBLEN) + item.shape[1:]) for item in picked + [keep_picked, slide_picked]))
        result, total = lax.map(jax.checkpoint(segment_attention), shaped)
        results.append(result.reshape(count, HEADS, HD))
        totals.append(total.reshape(count, HEADS))
    spread_totals = jnp.stack([spread_rows(total[:, :, None], ratio, big_negative)[:, :, 0] for total, ratio in zip(totals, ratios)])
    overall = jax.nn.logsumexp(spread_totals, axis=0)
    merged = jnp.zeros((TOKENS, HEADS, HD), jnp.float32)
    for result, total, ratio in zip(results, totals, ratios):
        weight = jnp.exp(total - select_rows(overall[:, :, None], ratio)[:, :, 0])
        merged = merged + spread_rows(result * weight[:, :, None], ratio, 0.0)
    return merged

def reference(tokens, coordinates, lengths, valid, first_gain, first_shift, query_weight, query_bias, key_weight, value_weight, value_bias, output_weight, output_bias, second_gain, second_shift, inner_weight, inner_bias, outer_weight, outer_bias, cotangent):
    table = position_table(coordinates, D)

    def forward(tokens, first_gain, first_shift, query_weight, query_bias, key_weight, value_weight, value_bias, output_weight, output_bias, second_gain, second_shift, inner_weight, inner_bias, outer_weight, outer_bias):
        base = tokens + table
        normed = low(layer_norm(base, first_gain, first_shift))
        query = low_back(low(jnp.dot(normed, query_weight, precision=highest) + query_bias)).reshape(TOKENS, HEADS, HD)
        key = low_back(low(jnp.dot(normed, key_weight, precision=highest))).reshape(TOKENS, HEADS, HD)
        value = low_back(low(jnp.dot(normed, value_weight, precision=highest) + value_bias)).reshape(TOKENS, HEADS, HD)
        merged = dilated(query, key, value, valid, lengths)
        attended = low_back(jnp.dot(low(merged.reshape(TOKENS, D)), output_weight, precision=highest) + output_bias)
        middle = base + attended
        normed_two = low(layer_norm(middle, second_gain, second_shift))
        inner = low_back(jnp.dot(normed_two, inner_weight, precision=highest) + inner_bias)
        activated = low(jax.nn.gelu(inner, approximate=False))
        outer = low_back(jnp.dot(activated, outer_weight, precision=highest) + outer_bias)
        return middle + outer
    output, pullback = jax.vjp(forward, tokens, first_gain, first_shift, query_weight.astype(jnp.float32), query_bias, key_weight.astype(jnp.float32), value_weight.astype(jnp.float32), value_bias, output_weight.astype(jnp.float32), output_bias, second_gain, second_shift, inner_weight.astype(jnp.float32), inner_bias, outer_weight.astype(jnp.float32), outer_bias)
    token_grad, first_gain_grad, first_shift_grad, query_weight_grad, query_bias_grad, key_weight_grad, value_weight_grad, value_bias_grad, output_weight_grad, output_bias_grad, second_gain_grad, second_shift_grad, inner_weight_grad, inner_bias_grad, outer_weight_grad, outer_bias_grad = pullback(cotangent)
    return (output, token_grad, first_gain_grad, first_shift_grad, query_weight_grad, query_bias_grad, key_weight_grad, value_weight_grad, value_bias_grad, output_weight_grad, output_bias_grad, second_gain_grad, second_shift_grad, inner_weight_grad, inner_bias_grad, outer_weight_grad, outer_bias_grad)
```

```python
import functools
import math

import jax
import jax.numpy as jnp
from jax import lax
from jax.experimental import pallas as pl
from jax.experimental.pallas import tpu as pltpu
from jax.sharding import PartitionSpec as P

HEADS = 16

epsilon = 1e-05
NT = (((1,), (1,)), ((), ()))
NN = (((1,), (0,)), ((), ()))
f32 = jnp.float32
bf16 = jnp.bfloat16
BIG = 1e30
HD = 48
GROUP = 8
LANES = 128
BLOCK = 32
MSG = 160
FLAG = 2 * HD
MESH = pl.DeviceIdType.MESH
scale = HD ** (-0.5)
scale2 = scale * math.log2(math.e)
q_at = (0, 4096, 6144, 7168, 7680)
q_all = 7936
k_at = (0, 4096, 6144, 7168, 8192)
k_all = 9216


def reverse4(b):
    return (b & 1) * 8 + (b & 2) * 2 + (b & 4) // 2 + (b & 8) // 8


order = [reverse4(b) for b in range(16)]


def chunk_swap(head):
    return reverse4(head) >> 2


def block_swap(quad):
    return reverse4(4 * quad) & 3


def swap_blocks(rows, quad):
    return jnp.concatenate(
        [rows[BLOCK * (b ^ block_swap(quad)) :][:BLOCK] for b in range(16)], axis=0
    )


def swap_chunks(wide, head):
    return jnp.concatenate(
        [wide[:, LANES * (c ^ chunk_swap(head)) :][:, :LANES] for c in range(4)], axis=1
    )


def matmul(a, b, dims=NN):
    return lax.dot_general(a, b, dims, preferred_element_type=f32)


def spot(grp):
    linear = lax.axis_index("seq") * grp + lax.axis_index("grp")
    member = linear % GROUP
    return linear, member, linear - member


def device(linear, grp):
    return (linear // grp, linear % grp)


def greet(barrier, peers, grp):
    for peer in peers:
        pl.semaphore_signal(barrier, inc=1, device_id=device(peer, grp), device_id_type=MESH)


def plane_barrier(grp, deep):
    linear, member, base = spot(grp)
    barrier = pltpu.get_barrier_semaphore()
    for j in range(GROUP):

        @pl.when(member != j)
        def _():
            greet(barrier, [base + j], grp)

    total = GROUP - 1
    if deep:
        layer = linear // GROUP % 4
        for o in range(1, 4):
            greet(barrier, [linear + GROUP * ((layer + o) % 4 - layer)], grp)
        total += 3
    return barrier, total


def plane_copy(send, recv, send_sem, recv_sem, j, member, base, grp):
    return pltpu.make_async_remote_copy(
        src_ref=send.at[j],
        dst_ref=recv.at[member],
        send_sem=send_sem.at[j],
        recv_sem=recv_sem.at[member],
        device_id=device(base + j, grp),
        device_id_type=MESH,
    )


def plane_arrival(send, recv, send_sem, recv_sem, j, base, grp):
    return pltpu.make_async_remote_copy(
        src_ref=send.at[j],
        dst_ref=recv.at[j],
        send_sem=send_sem.at[j],
        recv_sem=recv_sem.at[j],
        device_id=device(base + j, grp),
        device_id_type=MESH,
    )


def plane_send(send, recv, send_sem, recv_sem, j, member, base, grp):
    @pl.when(member != j)
    def _():
        plane_copy(send, recv, send_sem, recv_sem, j, member, base, grp).start()

    @pl.when(member == j)
    def _():
        pltpu.make_async_copy(send.at[j], recv.at[j], recv_sem.at[j]).start()


def plane_wait(send, recv, send_sem, recv_sem, j, member, base, grp):
    @pl.when(member != j)
    def _():
        plane_arrival(send, recv, send_sem, recv_sem, j, base, grp).wait_recv()

    @pl.when(member == j)
    def _():
        pltpu.make_async_copy(send.at[j], recv.at[j], recv_sem.at[j]).wait()


def plane_drain(send, recv, send_sem, recv_sem, j, member, base, grp):
    @pl.when(member != j)
    def _():
        plane_copy(send, recv, send_sem, recv_sem, j, member, base, grp).wait_send()


def qkv_kernel(
    grp, slides, n_ref, w_ref, b_ref, f_ref, msg, q_ref, kv_ref, kv8, kv16,
    send, send_sem, recv_sem, deep_send, deep_recv,
):
    linear, member, base = spot(grp)
    barrier, total = plane_barrier(grp, True)
    plane = (send, msg, send_sem, recv_sem)
    for quad in range(4):
        part = matmul(n_ref[...], w_ref[quad]) + b_ref[quad]
        wide = swap_blocks(part.astype(bf16), quad).T
        flags = f_ref[...]
        flags = jnp.concatenate(
            [flags[:, BLOCK * (b ^ block_swap(quad)) :][:, :BLOCK] for b in range(16)], axis=1
        ).astype(bf16)
        for inner in range(4):
            head = 4 * quad + inner
            owner, at = head // 2, MSG * (head % 2)
            own = swap_chunks(wide[144 * inner : 144 * inner + 144], head)
            send[owner, at : at + 96] = own[48:]
            send[owner, at + 96 : at + 112] = swap_chunks(flags, head)
            send[owner, at + 112 : at + 160] = own[:48]
        if quad == 0:
            pl.semaphore_wait(barrier, total)
        for owner in (2 * quad, 2 * quad + 1):
            plane_send(*plane, owner, member, base, grp)
    row = lax.broadcasted_iota(jnp.int32, (16, 512), 0)
    layer = linear // GROUP % 4
    half = layer % 2
    for j in range(GROUP):
        plane_wait(*plane, j, member, base, grp)
        for i in range(2):
            block = msg[j, MSG * i : MSG * i + MSG]
            key_part = jnp.concatenate([block[:112], jnp.zeros((16, 512), bf16)], axis=0).T
            flags = block[96:112].astype(f32)
            chosen = jnp.where(
                row == 0, 1.0, jnp.where((row <= slides) & (flags == 0.0), 1.0, 0.0)
            )
            query_part = jnp.concatenate(
                [
                    block[112:160],
                    jnp.zeros((48, 512), bf16),
                    chosen.astype(bf16),
                    jnp.zeros((16, 512), bf16),
                ],
                axis=0,
            ).T
            kv_ref[i, 512 * j : 512 * j + 512] = key_part
            q_ref[i, 512 * j : 512 * j + 512] = query_part
            kv8[half, i, 64 * j : 64 * j + 64] = key_part[:64]
            kv16[layer, i, 32 * j : 32 * j + 32] = key_part[:32]
    copies = []
    for o in range(1, 4):
        other = (layer + o) % 4
        copies.append(
            pltpu.make_async_remote_copy(
                src_ref=kv16.at[layer],
                dst_ref=kv16.at[layer],
                send_sem=deep_send.at[o],
                recv_sem=deep_recv.at[4 - o],
                device_id=device(linear + GROUP * (other - layer), grp),
                device_id_type=MESH,
            )
        )
    copies.append(
        pltpu.make_async_remote_copy(
            src_ref=kv8.at[half],
            dst_ref=kv8.at[half],
            send_sem=deep_send.at[0],
            recv_sem=deep_recv.at[0],
            device_id=device(linear + GROUP - 2 * GROUP * half, grp),
            device_id_type=MESH,
        )
    )
    for copy in copies:
        copy.start()
    for j in range(GROUP):
        plane_drain(*plane, j, member, base, grp)
    for copy in copies:
        copy.wait_send()
    for o in range(1, 4):
        other = (layer + o) % 4
        pltpu.make_async_remote_copy(
            src_ref=kv16.at[layer],
            dst_ref=kv16.at[other],
            send_sem=deep_send.at[o],
            recv_sem=deep_recv.at[o],
            device_id=device(linear + GROUP * (other - layer), grp),
            device_id_type=MESH,
        ).wait_recv()
    pltpu.make_async_remote_copy(
        src_ref=kv8.at[half],
        dst_ref=kv8.at[1 - half],
        send_sem=deep_send.at[0],
        recv_sem=deep_recv.at[0],
        device_id=device(linear + GROUP - 2 * GROUP * half, grp),
        device_id_type=MESH,
    ).wait_recv()


def compact(rows, packed, at):
    for j in range(GROUP):
        for place, size in at:
            packed[place + size * j : place + size * j + size] = rows[512 * j : 512 * j + size]


def gather_keys(kv, kv8, kv16, kvc):
    compact(kv, kvc, ((0, 256), (2048, 128)))
    for i in range(2):
        kvc[3072 + 512 * i : 3584 + 512 * i] = kv8[i]
    for i in range(4):
        kvc[4096 + 256 * i : 4352 + 256 * i] = kv16[i]


def unit_forward(query, key, out):
    lane = lax.broadcasted_iota(jnp.int32, (256, LANES), 1)
    count = len(query)
    scores = [matmul(query[i](), key, NT) for i in range(count)]
    for i in range(count):
        top = jnp.max(scores[i], axis=1, keepdims=True) * scale2
        prob = jnp.exp2(scores[i] * scale2 - top).astype(bf16)
        out[i](jnp.where(lane == FLAG + 8, top, matmul(prob, key)))


def forward_kernel(slides, q_ref, kv_ref, kv8, kv16, om, stat, acc, qc, kvc):
    ones_lane = FLAG + 1 + slides
    q = q_ref.at[0]
    kv = kv_ref.at[0]
    compact(q, qc, ((0, 256), (2048, 128), (3072, 64), (3584, 32)))
    gather_keys(kv, kv8.at[:, 0], kv16.at[:, 0], kvc)

    def unit(source, q_from, keys, k_from, out_from, count):
        def reader(i):
            return lambda: source[pl.ds(q_from + 256 * i, 256)]

        def writer(i):
            def put(value):
                acc[pl.ds(out_from + 256 * i, 256)] = value

            return put

        unit_forward(
            [reader(i) for i in range(count)],
            keys[pl.ds(k_from, 1024)],
            [writer(i) for i in range(count)],
        )

    def first(u, _):
        at = pl.multiple_of(u * 1024, 1024)
        unit(q, at, kv, at, at, 4)
        return 0

    lax.fori_loop(0, 4, first, 0)

    def second(u, _):
        at = pl.multiple_of(u * 1024, 1024)
        unit(qc, at, kvc, at, at + 4096, 4)
        return 0

    lax.fori_loop(0, 3, second, 0)
    unit(qc, 3072, kvc, 3072, 7168, 2)
    unit(qc, 3584, kvc, 4096, 7680, 1)

    def merge(j, _):
        spans = ((256, 512, 1), (128, 256, 2), (64, 128, 3), (32, 64, 4), (0, 32, 5))
        parts = []
        for low, high, uses in reversed(spans):
            size = high - low
            lane = lax.broadcasted_iota(jnp.int32, (size, LANES), 1)
            pieces = [
                acc[pl.ds(q_at[r] + (512 >> r) * j + low, size)] for r in range(uses)
            ]
            tops = [piece[:, FLAG + 8 : FLAG + 9] for piece in pieces]
            query = q[pl.ds(512 * j + low, size)].astype(f32)
            key = kv[pl.ds(512 * j + low, size)].astype(f32)
            dots = jnp.sum(jnp.where(lane < HD, query * key, 0.0), axis=1, keepdims=True)
            own = jnp.where(
                key[:, FLAG : FLAG + 1] == 0.0, -BIG, dots * scale2 + math.log2(uses)
            )
            top = own
            for item in tops:
                top = jnp.maximum(top, item)
            weight = jnp.exp2(own - top)
            total = weight
            mix = weight * key
            for piece, item in zip(pieces, tops):
                weight = jnp.exp2(item - top)
                total = total + weight * piece[:, ones_lane : ones_lane + 1]
                mix = mix + weight * piece
            mix = mix / total
            parts.append(jnp.where(lane == FLAG, top + jnp.log2(total), mix))
        wide = jnp.concatenate(parts, axis=0).T
        om[j] = wide[HD : 2 * HD].astype(bf16)
        stat[0, j] = wide[HD : HD + 56]
        return 0

    lax.fori_loop(0, GROUP, merge, 0)


def join_quads(read):
    pairs = []
    for half in range(2):
        quads = []
        for quad in (2 * half, 2 * half + 1):
            wide = jnp.concatenate(
                [swap_chunks(read(4 * quad + i), 4 * quad + i) for i in range(4)], axis=0
            )
            quads.append(swap_blocks(wide.T, quad))
        pairs.append(jnp.concatenate(quads, axis=1))
    return jnp.concatenate(pairs, axis=1)


def merged_kernel(grp, om, out, recv, send_sem, recv_sem):
    linear, member, base = spot(grp)
    barrier, total = plane_barrier(grp, False)
    pl.semaphore_wait(barrier, total)
    plane = (om, recv, send_sem, recv_sem)
    for j in range(GROUP):
        plane_send(*plane, j, member, base, grp)
    for j in range(GROUP):
        plane_wait(*plane, j, member, base, grp)
    out[...] = join_quads(lambda h: recv[h // 2, HD * (h % 2) : HD * (h % 2) + HD])
    for j in range(GROUP):
        plane_drain(*plane, j, member, base, grp)


def spread_kernel(grp, rows_ref, recv, send, send_sem, recv_sem):
    linear, member, base = spot(grp)
    barrier, total = plane_barrier(grp, False)
    plane = (send, recv, send_sem, recv_sem)
    for quad in range(4):
        wide = swap_blocks(rows_ref[:, 192 * quad : 192 * quad + 192], quad).T
        for inner in range(4):
            head = 4 * quad + inner
            at = HD * (head % 2)
            send[head // 2, at : at + HD] = swap_chunks(wide[HD * inner : HD * inner + HD], head)
        if quad == 0:
            pl.semaphore_wait(barrier, total)
        for owner in (2 * quad, 2 * quad + 1):
            plane_send(*plane, owner, member, base, grp)
    for j in range(GROUP):
        plane_wait(*plane, j, member, base, grp)
    for j in range(GROUP):
        plane_drain(*plane, j, member, base, grp)


def backward_kernel(
    q_ref, kv_ref, kv8, kv16, msg, gm, stat, pre, dkv8, dkv16,
    qc, kvc, dor, kt, ld, dkv, dqt,
):
    q = q_ref.at[0]
    kv = kv_ref.at[0]
    compact(q, qc, ((0, 256), (2048, 128), (3072, 64), (3584, 32)))
    gather_keys(kv, kv8.at[:, 0], kv16.at[:, 0], kvc)
    rows = []
    for j in range(GROUP):
        grad = gm[j]
        delta = jnp.sum(grad.astype(f32) * stat[0, j, :HD], axis=0, keepdims=True)
        both = jnp.concatenate(
            [stat[0, j, HD : HD + 1], delta, jnp.zeros((6, 512), f32)], axis=0
        )
        rows.append(both)
        ld[:, 512 * j : 512 * j + 512] = both
        ld[:, 4096 + 256 * j : 4352 + 256 * j] = both[:, :256]
        ld[:, 6144 + 128 * j : 6272 + 128 * j] = both[:, :128]
        tall = jnp.concatenate(
            [jnp.zeros((HD, 512), bf16), grad, jnp.zeros((32, 512), bf16)], axis=0
        ).T
        for r, at in enumerate(q_at):
            size = 512 >> r
            dor[at + size * j : at + size * j + size] = tall[:size]
        key = msg[j, :HD]
        kt[j // 2, :, 512 * (j % 2) : 512 * (j % 2) + 512] = key
        kt[4 + j // 4, :, 256 * (j % 4) : 256 * (j % 4) + 256] = key[:, :256]
        kt[6, :, 128 * j : 128 * j + 128] = key[:, :128]
    ld[:, 7168:7680] = jnp.concatenate([both[:, :64] for both in rows], axis=1)
    ld[:, 7680:7936] = jnp.concatenate([both[:, :32] for both in rows], axis=1)
    for i in range(2):
        kt[7 + i] = kvc[3072 + 1024 * i : 4096 + 1024 * i].T[:HD]

    def unit(source, q_from, keys, k_from, place, seg, count):
        width = 256 * count
        query = source[pl.ds(q_from, width)]
        grad = dor[pl.ds(place, width)]
        total = ld[0:1, pl.ds(place, width)]
        delta = ld[1:2, pl.ds(place, width)]
        sides = jnp.concatenate([grad, query], axis=0)
        size = 256
        dq = jnp.zeros((HD, width), f32)
        for c in range(1024 // size):
            key = keys[pl.ds(k_from + size * c, size)]
            prob = jnp.exp2(matmul(key, query, NT) * scale2 - total)
            slope = (prob * (matmul(key, grad, NT) - delta)).astype(bf16)
            both = jnp.concatenate([prob.astype(bf16), slope], axis=1)
            dkv[pl.ds(seg * 1024 + size * c, size)] = matmul(both, sides)
            dq = dq + matmul(kt[seg, :, size * c : size * c + size], slope)
        dqt[:, pl.ds(place, width)] = dq

    def first(u, _):
        at = pl.multiple_of(u * 1024, 1024)
        unit(q, at, kv, at, at, u, 4)
        return 0

    lax.fori_loop(0, 4, first, 0)

    def second(u, _):
        at = pl.multiple_of(u * 1024, 1024)
        unit(qc, at, kvc, at, at + 4096, u + 4, 4)
        return 0

    lax.fori_loop(0, 3, second, 0)
    unit(qc, 3072, kvc, 3072, 7168, 7, 2)
    unit(qc, 3584, kvc, 4096, 7680, 8, 1)
    for i in range(2):
        dkv8[i, 0] = dkv[7168 + 512 * i : 7680 + 512 * i].astype(bf16)
    for i in range(4):
        dkv16[i, 0] = dkv[8192 + 256 * i : 8448 + 256 * i].astype(bf16)
    lane = lax.broadcasted_iota(jnp.int32, (1, 512), 1)
    uses = jnp.where(
        lane < 32, 5.0, jnp.where(lane < 64, 4.0, jnp.where(lane < 128, 3.0, jnp.where(lane < 256, 2.0, 1.0)))
    )
    for j in range(GROUP):
        tall = dkv[512 * j : 512 * j + 512]
        tall = jnp.concatenate(
            [
                tall[:128] + dkv[4096 + 256 * j : 4224 + 256 * j] + dkv[6144 + 128 * j : 6272 + 128 * j],
                tall[128:256] + dkv[4224 + 256 * j : 4352 + 256 * j],
                tall[256:],
            ],
            axis=0,
        )
        wide = tall.T
        key = msg[j, :HD].astype(f32)
        value = msg[j, HD : 2 * HD].astype(f32)
        query = msg[j, 112:160].astype(f32)
        grad = gm[j].astype(f32)
        total = ld[0:1, 512 * j : 512 * j + 512]
        delta = ld[1:2, 512 * j : 512 * j + 512]
        dots = jnp.sum(query * key, axis=0, keepdims=True)
        dropped = msg[j, FLAG : FLAG + 1].astype(f32) != 0.0
        prob = jnp.where(
            dropped, uses * jnp.exp2(jnp.where(dropped, dots * scale2 - total, 0.0)), 0.0
        )
        slope = prob * (jnp.sum(grad * value, axis=0, keepdims=True) - delta)
        dq = dqt[:, 512 * j : 512 * j + 512] + slope * key
        second_part = dqt[:, 4096 + 256 * j : 4352 + 256 * j]
        third_part = dqt[:, 6144 + 128 * j : 6272 + 128 * j]
        fourth_part = dqt[:, 7168 + 64 * j : 7232 + 64 * j]
        fifth_part = dqt[:, 7680 + 32 * j : 7712 + 32 * j]
        fifth_part = jnp.concatenate([fifth_part, jnp.zeros((HD, 32), f32)], axis=1)
        fourth_part = jnp.concatenate([fourth_part + fifth_part, jnp.zeros((HD, 64), f32)], axis=1)
        third_part = jnp.concatenate([third_part + fourth_part, jnp.zeros((HD, 128), f32)], axis=1)
        second_part = jnp.concatenate([second_part + third_part, jnp.zeros((HD, 256), f32)], axis=1)
        pre[0, j, :HD] = (wide[:HD] + slope * query) * scale
        pre[0, j, HD : 2 * HD] = wide[HD : 2 * HD] + prob * grad
        pre[0, j, 2 * HD :] = (dq + second_part) * scale


def return_kernel(
    grp, pre, dkv8, dkv16, dq_ref, dk_ref, dv_ref,
    send, recv, got8, got16, send_sem, recv_sem, deep_send, deep_recv,
):
    linear, member, base = spot(grp)
    barrier, total = plane_barrier(grp, True)
    pl.semaphore_wait(barrier, total)
    plane = (send, recv, send_sem, recv_sem)
    layer = linear // GROUP % 4
    half = layer % 2
    copies = []
    for o in range(1, 4):
        other = (layer + o) % 4
        copies.append(
            pltpu.make_async_remote_copy(
                src_ref=dkv16.at[other],
                dst_ref=got16.at[4 - o],
                send_sem=deep_send.at[o],
                recv_sem=deep_recv.at[4 - o],
                device_id=device(linear + GROUP * (other - layer), grp),
                device_id_type=MESH,
            )
        )
    copies.append(
        pltpu.make_async_remote_copy(
            src_ref=dkv8.at[1 - half],
            dst_ref=got8.at[0],
            send_sem=deep_send.at[0],
            recv_sem=deep_recv.at[0],
            device_id=device(linear + GROUP - 2 * GROUP * half, grp),
            device_id_type=MESH,
        )
    )
    for copy in copies:
        copy.start()
    for copy in copies:
        copy.wait()
    row = lax.broadcasted_iota(jnp.int32, (96, 1), 0)
    factor = jnp.where(row < HD, scale, 1.0)
    for j in range(GROUP):
        for i in range(2):
            eight = dkv8[half, i, 64 * j : 64 * j + 64].astype(f32) + got8[
                0, i, 64 * j : 64 * j + 64
            ].astype(f32)
            sixteen = dkv16[layer, i, 32 * j : 32 * j + 32].astype(f32)
            for o in range(1, 4):
                sixteen = sixteen + got16[o, i, 32 * j : 32 * j + 32].astype(f32)
            more = jnp.concatenate(
                [eight[:32] + sixteen, eight[32:], jnp.zeros((64, LANES), f32)], axis=0
            ).T
            at = 144 * i
            first_part = pre[i, j, :96]
            send[j, at : at + 96] = jnp.concatenate(
                [first_part[:, :LANES] + more[:96] * factor, first_part[:, LANES:]], axis=1
            ).astype(bf16)
            send[j, at + 96 : at + 144] = pre[i, j, 96:].astype(bf16)
        plane_send(*plane, j, member, base, grp)
    for j in range(GROUP):
        plane_wait(*plane, j, member, base, grp)
    for n, out in enumerate((dk_ref, dv_ref, dq_ref)):

        def read(h, n=n):
            at = 144 * (h % 2) + HD * n
            return recv[h // 2, at : at + HD]

        out[...] = join_quads(read)
    for j in range(GROUP):
        plane_drain(*plane, j, member, base, grp)


def vmem():
    return pl.BlockSpec(memory_space=pltpu.VMEM)


def sems(n):
    return pltpu.SemaphoreType.DMA((n,))


def params(identity=None):
    if identity is None:
        return pltpu.CompilerParams(vmem_limit_bytes=58 << 20)
    return pltpu.CompilerParams(
        vmem_limit_bytes=58 << 20, collective_id=identity, has_side_effects=True
    )


def shape(dims, dtype):
    return jax.ShapeDtypeStruct(dims, dtype)


def attention_in(grp, slides, normed, weight, bias, flags):
    return pl.pallas_call(
        functools.partial(qkv_kernel, grp, slides),
        name="project_and_share",
        in_specs=[vmem()] * 4,
        out_specs=[vmem()] * 5,
        out_shape=[
            shape((GROUP, 2 * MSG, 512), bf16),
            shape((2, 4096, LANES), bf16),
            shape((2, 4096, LANES), bf16),
            shape((2, 2, 512, LANES), bf16),
            shape((4, 2, 256, LANES), bf16),
        ],
        scratch_shapes=[
            pltpu.VMEM((GROUP, 2 * MSG, 512), bf16),
            sems(GROUP),
            sems(GROUP),
            sems(4),
            sems(4),
        ],
        compiler_params=params(1),
    )(normed, weight, bias, flags)


def attention_forward(slides, q, kv, kv8, kv16):
    return pl.pallas_call(
        functools.partial(forward_kernel, slides),
        name="attention_forward",
        grid=(2,),
        in_specs=[
            pl.BlockSpec((1, 4096, LANES), lambda h: (h, 0, 0)),
            pl.BlockSpec((1, 4096, LANES), lambda h: (h, 0, 0)),
            pl.BlockSpec((2, 1, 512, LANES), lambda h: (0, h, 0, 0)),
            pl.BlockSpec((4, 1, 256, LANES), lambda h: (0, h, 0, 0)),
        ],
        out_specs=[
            pl.BlockSpec((GROUP, HD, 512), lambda h: (0, h, 0)),
            pl.BlockSpec((1, GROUP, 56, 512), lambda h: (h, 0, 0, 0)),
        ],
        out_shape=[shape((GROUP, 2 * HD, 512), bf16), shape((2, GROUP, 56, 512), f32)],
        scratch_shapes=[
            pltpu.VMEM((q_all, LANES), f32),
            pltpu.VMEM((q_all - 4096, LANES), bf16),
            pltpu.VMEM((k_all - 4096, LANES), bf16),
        ],
        compiler_params=params(),
    )(q, kv, kv8, kv16)


def attention_out(grp, om):
    return pl.pallas_call(
        functools.partial(merged_kernel, grp),
        name="share_merged",
        in_specs=[vmem()],
        out_specs=vmem(),
        out_shape=shape((512, 768), bf16),
        scratch_shapes=[pltpu.VMEM((GROUP, 2 * HD, 512), bf16), sems(GROUP), sems(GROUP)],
        compiler_params=params(2),
    )(om)


def gradient_in(grp, grad):
    return pl.pallas_call(
        functools.partial(spread_kernel, grp),
        name="share_gradient",
        in_specs=[vmem()],
        out_specs=vmem(),
        out_shape=shape((GROUP, 2 * HD, 512), bf16),
        scratch_shapes=[pltpu.VMEM((GROUP, 2 * HD, 512), bf16), sems(GROUP), sems(GROUP)],
        compiler_params=params(3),
    )(grad)


def attention_backward(q, kv, kv8, kv16, msg, gm, stat):
    return pl.pallas_call(
        backward_kernel,
        name="attention_backward",
        grid=(2,),
        in_specs=[
            pl.BlockSpec((1, 4096, LANES), lambda h: (h, 0, 0)),
            pl.BlockSpec((1, 4096, LANES), lambda h: (h, 0, 0)),
            pl.BlockSpec((2, 1, 512, LANES), lambda h: (0, h, 0, 0)),
            pl.BlockSpec((4, 1, 256, LANES), lambda h: (0, h, 0, 0)),
            pl.BlockSpec((GROUP, MSG, 512), lambda h: (0, h, 0)),
            pl.BlockSpec((GROUP, HD, 512), lambda h: (0, h, 0)),
            pl.BlockSpec((1, GROUP, 56, 512), lambda h: (h, 0, 0, 0)),
        ],
        out_specs=[
            pl.BlockSpec((1, GROUP, 144, 512), lambda h: (h, 0, 0, 0)),
            pl.BlockSpec((2, 1, 512, LANES), lambda h: (0, h, 0, 0)),
            pl.BlockSpec((4, 1, 256, LANES), lambda h: (0, h, 0, 0)),
        ],
        out_shape=[
            shape((2, GROUP, 144, 512), f32),
            shape((2, 2, 512, LANES), bf16),
            shape((4, 2, 256, LANES), bf16),
        ],
        scratch_shapes=[
            pltpu.VMEM((q_all - 4096, LANES), bf16),
            pltpu.VMEM((k_all - 4096, LANES), bf16),
            pltpu.VMEM((q_all, LANES), bf16),
            pltpu.VMEM((9, HD, 1024), bf16),
            pltpu.VMEM((8, q_all), f32),
            pltpu.VMEM((k_all, LANES), f32),
            pltpu.VMEM((HD, q_all), f32),
        ],
        compiler_params=params(),
    )(q, kv, kv8, kv16, msg, gm, stat)


def gradient_out(grp, pre, dkv8, dkv16):
    return pl.pallas_call(
        functools.partial(return_kernel, grp),
        name="return_gradients",
        in_specs=[vmem()] * 3,
        out_specs=[vmem()] * 3,
        out_shape=[shape((512, 768), bf16)] * 3,
        scratch_shapes=[
            pltpu.VMEM((GROUP, 288, 512), bf16),
            pltpu.VMEM((GROUP, 288, 512), bf16),
            pltpu.VMEM((1, 2, 512, LANES), bf16),
            pltpu.VMEM((4, 2, 256, LANES), bf16),
            sems(GROUP),
            sems(GROUP),
            sems(4),
            sems(4),
        ],
        compiler_params=params(4),
    )(pre, dkv8, dkv16)


def position_table(coordinates, width):
    quarter = width // 4
    frequency = jnp.exp(jnp.arange(quarter, dtype=jnp.float32) * (-math.log(10000.0) / quarter))
    column = coordinates[:, 0:1].astype(jnp.float32) * frequency[None, :]
    across = coordinates[:, 1:2].astype(jnp.float32) * frequency[None, :]
    return jnp.concatenate(
        [jnp.sin(column), jnp.cos(column), jnp.sin(across), jnp.cos(across)], axis=1
    )


def layer_norm(values, norm_gain, norm_shift):
    average = jnp.mean(values, axis=-1, keepdims=True)
    centred = values - average
    variance = jnp.mean(centred * centred, axis=-1, keepdims=True)
    return centred * lax.rsqrt(variance + epsilon) * norm_gain + norm_shift


def gelu_slope(values):
    return (
        0.5 * (1.0 + lax.erf(values * 0.7071067811865476))
        + values * jnp.exp(-0.5 * values * values) * 0.3989422804014327
    )


def product(left, right):
    return jnp.dot(left, right, preferred_element_type=jnp.float32)


def product_left(left, right):
    return jnp.einsum("rd,rf->df", left, right, preferred_element_type=jnp.float32)


def product_right(left, right):
    return jnp.einsum("rf,df->rd", left, right, preferred_element_type=jnp.float32)


def in_order(rows):
    split = rows.reshape((BLOCK, 16) + rows.shape[1:])
    return jnp.stack([split[:, b] for b in order]).reshape(rows.shape)


def back_order(rows):
    split = rows.reshape((16, BLOCK) + rows.shape[1:])
    return jnp.stack([split[b] for b in order], axis=1).reshape(rows.shape)


def body(
    tokens,
    coordinates,
    lengths,
    valid,
    first_gain,
    first_shift,
    query_weight,
    query_bias,
    key_weight,
    value_weight,
    value_bias,
    output_weight,
    output_bias,
    second_gain,
    second_shift,
    inner_weight,
    inner_bias,
    outer_weight,
    outer_bias,
    cotangent,
):
    rows, width = tokens.shape
    grp = lax.axis_size("grp")
    slides = lengths.shape[0]
    linear = lax.axis_index("seq") * grp + lax.axis_index("grp")
    start = linear * rows
    part = [
        lax.all_gather(w, "grp", axis=1, tiled=True)
        for w in (query_weight, key_weight, value_weight, output_weight, inner_weight, outer_weight)
    ]
    full_query, full_key, full_value, full_output, full_inner, full_outer = [
        lax.all_gather(w, "seq", axis=0, tiled=True) for w in part
    ]
    quads = [
        w.reshape(width, 4, 4, HD).transpose(1, 0, 2, 3) for w in (full_query, full_key, full_value)
    ]
    joint_weight = jnp.stack(quads, axis=3).reshape(4, width, 576)
    joint_bias = jnp.stack(
        [b.reshape(4, 4, HD) for b in (query_bias, jnp.zeros_like(query_bias), value_bias)], axis=2
    ).reshape(4, 1, 576)
    base = in_order(tokens + position_table(coordinates, width))
    cotangent = in_order(cotangent)
    places = in_order(start + jnp.arange(rows, dtype=jnp.int32))
    keep = in_order(valid)
    slide = jnp.sum((places[:, None] >= jnp.cumsum(lengths)).astype(jnp.int32), axis=-1)
    apart = slide[None, :] != jnp.arange(slides, dtype=jnp.int32)[:, None]
    flags = jnp.concatenate(
        [
            jnp.where(keep == 1, 0.0, -BIG)[None, :],
            jnp.where(apart, -BIG, 0.0),
            jnp.ones((1, rows), f32),
            jnp.zeros((14 - slides, rows), f32),
        ],
        axis=0,
    )
    normed, first_back = jax.vjp(layer_norm, base, first_gain, first_shift)
    normed_low = normed.astype(bf16)
    msg, q_rows, kv_rows, kv8, kv16 = attention_in(
        grp, slides, normed_low, joint_weight, joint_bias, flags
    )
    own, stat = attention_forward(slides, q_rows, kv_rows, kv8, kv16)
    merged_low = attention_out(grp, own)
    middle = base + product(merged_low, full_output) + output_bias
    normed_two, second_back = jax.vjp(layer_norm, middle, second_gain, second_shift)
    normed_two_low = normed_two.astype(jnp.bfloat16)
    inner = product(normed_two_low, full_inner) + inner_bias
    activated = jax.nn.gelu(inner, approximate=False).astype(jnp.bfloat16)
    output = middle + product(activated, full_outer) + outer_bias
    grad_outer = cotangent.astype(jnp.bfloat16)
    outer_weight_grad = product_left(activated, grad_outer)
    outer_bias_grad = jnp.sum(grad_outer.astype(jnp.float32), axis=0)
    grad_inner = (product_right(grad_outer, full_outer) * gelu_slope(inner)).astype(jnp.bfloat16)
    inner_weight_grad = product_left(normed_two_low, grad_inner)
    inner_bias_grad = jnp.sum(grad_inner.astype(jnp.float32), axis=0)
    grad_middle_part, second_gain_grad, second_shift_grad = second_back(
        product_right(grad_inner, full_inner)
    )
    grad_middle = cotangent + grad_middle_part
    grad_attended = grad_middle.astype(jnp.bfloat16)
    output_weight_grad = product_left(merged_low, grad_attended)
    output_bias_grad = jnp.sum(grad_attended.astype(jnp.float32), axis=0)
    grad_merged = product_right(grad_attended, full_output).astype(bf16)
    shared = gradient_in(grp, grad_merged)
    pre, dkv8, dkv16 = attention_backward(q_rows, kv_rows, kv8, kv16, msg, shared, stat)
    query_low, key_low, value_low = gradient_out(grp, pre, dkv8, dkv16)
    query_weight_grad = product_left(normed_low, query_low)
    key_weight_grad = product_left(normed_low, key_low)
    value_weight_grad = product_left(normed_low, value_low)
    query_bias_grad = jnp.sum(query_low.astype(jnp.float32), axis=0)
    value_bias_grad = jnp.sum(value_low.astype(jnp.float32), axis=0)
    grad_normed = (
        product_right(query_low, full_query)
        + product_right(key_low, full_key)
        + product_right(value_low, full_value)
    )
    grad_base_part, first_gain_grad, first_shift_grad = first_back(grad_normed)
    token_grad = grad_middle + grad_base_part
    sum_query, sum_key, sum_value, sum_output, sum_inner, sum_outer = (
        lax.psum_scatter(query_weight_grad, "grp", scatter_dimension=1, tiled=True),
        lax.psum_scatter(key_weight_grad, "grp", scatter_dimension=1, tiled=True),
        lax.psum_scatter(value_weight_grad, "grp", scatter_dimension=1, tiled=True),
        lax.psum_scatter(output_weight_grad, "grp", scatter_dimension=1, tiled=True),
        lax.psum_scatter(inner_weight_grad, "grp", scatter_dimension=1, tiled=True),
        lax.psum_scatter(outer_weight_grad, "grp", scatter_dimension=1, tiled=True),
    )
    sum_query, sum_key, sum_value, sum_output, sum_inner, sum_outer = (
        lax.psum_scatter(sum_query, "seq", scatter_dimension=0, tiled=True),
        lax.psum_scatter(sum_key, "seq", scatter_dimension=0, tiled=True),
        lax.psum_scatter(sum_value, "seq", scatter_dimension=0, tiled=True),
        lax.psum_scatter(sum_output, "seq", scatter_dimension=0, tiled=True),
        lax.psum_scatter(sum_inner, "seq", scatter_dimension=0, tiled=True),
        lax.psum_scatter(sum_outer, "seq", scatter_dimension=0, tiled=True),
    )
    small = lax.psum(
        (
            first_gain_grad,
            first_shift_grad,
            query_bias_grad,
            value_bias_grad,
            output_bias_grad,
            second_gain_grad,
            second_shift_grad,
            inner_bias_grad,
            outer_bias_grad,
        ),
        ("seq", "grp"),
    )
    return (
        back_order(output),
        back_order(token_grad),
        small[0],
        small[1],
        sum_query,
        small[2],
        sum_key,
        sum_value,
        small[3],
        sum_output,
        small[4],
        small[5],
        small[6],
        sum_inner,
        small[7],
        sum_outer,
        small[8],
    )


def solution(mesh):
    placed = (
        P(("seq", "grp"), None),
        P(("seq", "grp"), None),
        P(),
        P(("seq", "grp")),
        P(),
        P(),
        P("seq", "grp"),
        P(),
        P("seq", "grp"),
        P("seq", "grp"),
        P(),
        P("seq", "grp"),
        P(),
        P(),
        P(),
        P("seq", "grp"),
        P(),
        P("seq", "grp"),
        P(),
        P(("seq", "grp"), None),
    )
    return jax.shard_map(
        body,
        mesh=mesh,
        in_specs=placed,
        out_specs=(
            P(("seq", "grp"), None),
            P(("seq", "grp"), None),
            P(),
            P(),
            P("seq", "grp"),
            P(),
            P("seq", "grp"),
            P("seq", "grp"),
            P(),
            P("seq", "grp"),
            P(),
            P(),
            P(),
            P("seq", "grp"),
            P(),
            P("seq", "grp"),
            P(),
        ),
        check_vma=False,
    )
```

```python
import functools
import math

import jax
import jax.numpy as jnp
from jax import lax
from jax.experimental import pallas as pl
from jax.experimental.pallas import tpu as pltpu
from jax.sharding import PartitionSpec as P

HEADS = 16

epsilon = 1e-05
NT = (((1,), (1,)), ((), ()))
NN = (((1,), (0,)), ((), ()))
f32 = jnp.float32
bf16 = jnp.bfloat16
BIG = 1e30
HD = 48
GROUP = 8
LANES = 128
BLOCK = 32
MSG = 160
FLAG = 2 * HD
MESH = pl.DeviceIdType.MESH
scale = HD ** (-0.5)
scale2 = scale * math.log2(math.e)
q_at = (0, 4096, 6144, 7168, 7680)
q_all = 7936
k_at = (0, 4096, 6144, 7168, 8192)
k_all = 9216


def reverse4(b):
    return (b & 1) * 8 + (b & 2) * 2 + (b & 4) // 2 + (b & 8) // 8


order = [reverse4(b) for b in range(16)]


def chunk_swap(head):
    return reverse4(head) >> 2


def block_swap(quad):
    return reverse4(4 * quad) & 3


def swap_blocks(rows, quad):
    return jnp.concatenate(
        [rows[BLOCK * (b ^ block_swap(quad)) :][:BLOCK] for b in range(16)], axis=0
    )


def swap_chunks(wide, head):
    return jnp.concatenate(
        [wide[:, LANES * (c ^ chunk_swap(head)) :][:, :LANES] for c in range(4)], axis=1
    )


def matmul(a, b, dims=NN):
    return lax.dot_general(a, b, dims, preferred_element_type=f32)


def spot(grp):
    linear = lax.axis_index("seq") * grp + lax.axis_index("grp")
    member = linear % GROUP
    return linear, member, linear - member


def device(linear, grp):
    return (linear // grp, linear % grp)


def greet(barrier, peers, grp):
    for peer in peers:
        pl.semaphore_signal(barrier, inc=1, device_id=device(peer, grp), device_id_type=MESH)


def plane_barrier(grp, deep):
    linear, member, base = spot(grp)
    barrier = pltpu.get_barrier_semaphore()
    for j in range(GROUP):

        @pl.when(member != j)
        def _():
            greet(barrier, [base + j], grp)

    total = GROUP - 1
    if deep:
        layer = linear // GROUP % 4
        for o in range(1, 4):
            greet(barrier, [linear + GROUP * ((layer + o) % 4 - layer)], grp)
        total += 3
    return barrier, total


def plane_copy(send, recv, send_sem, recv_sem, j, member, base, grp):
    return pltpu.make_async_remote_copy(
        src_ref=send.at[j],
        dst_ref=recv.at[member],
        send_sem=send_sem.at[j],
        recv_sem=recv_sem.at[member],
        device_id=device(base + j, grp),
        device_id_type=MESH,
    )


def plane_arrival(send, recv, send_sem, recv_sem, j, base, grp):
    return pltpu.make_async_remote_copy(
        src_ref=send.at[j],
        dst_ref=recv.at[j],
        send_sem=send_sem.at[j],
        recv_sem=recv_sem.at[j],
        device_id=device(base + j, grp),
        device_id_type=MESH,
    )


def plane_send(send, recv, send_sem, recv_sem, j, member, base, grp):
    @pl.when(member != j)
    def _():
        plane_copy(send, recv, send_sem, recv_sem, j, member, base, grp).start()

    @pl.when(member == j)
    def _():
        pltpu.make_async_copy(send.at[j], recv.at[j], recv_sem.at[j]).start()


def plane_wait(send, recv, send_sem, recv_sem, j, member, base, grp):
    @pl.when(member != j)
    def _():
        plane_arrival(send, recv, send_sem, recv_sem, j, base, grp).wait_recv()

    @pl.when(member == j)
    def _():
        pltpu.make_async_copy(send.at[j], recv.at[j], recv_sem.at[j]).wait()


def plane_drain(send, recv, send_sem, recv_sem, j, member, base, grp):
    @pl.when(member != j)
    def _():
        plane_copy(send, recv, send_sem, recv_sem, j, member, base, grp).wait_send()


def qkv_kernel(
    grp, slides, n_ref, w_ref, b_ref, f_ref, msg, q_ref, kv_ref, kv8, kv16,
    send, send_sem, recv_sem, deep_send, deep_recv,
):
    linear, member, base = spot(grp)
    barrier, total = plane_barrier(grp, True)
    plane = (send, msg, send_sem, recv_sem)
    for quad in range(4):
        part = matmul(n_ref[...], pick(w_ref, quad)) + b_ref[quad]
        wide = swap_blocks(part.astype(bf16), quad).T
        flags = f_ref[...]
        flags = jnp.concatenate(
            [flags[:, BLOCK * (b ^ block_swap(quad)) :][:, :BLOCK] for b in range(16)], axis=1
        ).astype(bf16)
        for inner in range(4):
            head = 4 * quad + inner
            owner, at = head // 2, MSG * (head % 2)
            own = swap_chunks(wide[144 * inner : 144 * inner + 144], head)
            send[owner, at : at + 96] = own[48:]
            send[owner, at + 96 : at + 112] = swap_chunks(flags, head)
            send[owner, at + 112 : at + 160] = own[:48]
        if quad == 0:
            pl.semaphore_wait(barrier, total)
        for owner in (2 * quad, 2 * quad + 1):
            plane_send(*plane, owner, member, base, grp)
    row = lax.broadcasted_iota(jnp.int32, (16, 512), 0)
    layer = linear // GROUP % 4
    half = layer % 2
    for j in range(GROUP):
        plane_wait(*plane, j, member, base, grp)
        for i in range(2):
            block = msg[j, MSG * i : MSG * i + MSG]
            key_part = jnp.concatenate([block[:112], jnp.zeros((16, 512), bf16)], axis=0).T
            flags = block[96:112].astype(f32)
            chosen = jnp.where(
                row == 0, 1.0, jnp.where((row <= slides) & (flags == 0.0), 1.0, 0.0)
            )
            query_part = jnp.concatenate(
                [
                    block[112:160],
                    jnp.zeros((48, 512), bf16),
                    chosen.astype(bf16),
                    jnp.zeros((16, 512), bf16),
                ],
                axis=0,
            ).T
            kv_ref[i, 512 * j : 512 * j + 512] = key_part
            q_ref[i, 512 * j : 512 * j + 512] = query_part
            kv8[half, i, 64 * j : 64 * j + 64] = key_part[:64]
            kv16[layer, i, 32 * j : 32 * j + 32] = key_part[:32]
    copies = []
    for o in range(1, 4):
        other = (layer + o) % 4
        copies.append(
            pltpu.make_async_remote_copy(
                src_ref=kv16.at[layer],
                dst_ref=kv16.at[layer],
                send_sem=deep_send.at[o],
                recv_sem=deep_recv.at[4 - o],
                device_id=device(linear + GROUP * (other - layer), grp),
                device_id_type=MESH,
            )
        )
    copies.append(
        pltpu.make_async_remote_copy(
            src_ref=kv8.at[half],
            dst_ref=kv8.at[half],
            send_sem=deep_send.at[0],
            recv_sem=deep_recv.at[0],
            device_id=device(linear + GROUP - 2 * GROUP * half, grp),
            device_id_type=MESH,
        )
    )
    for copy in copies:
        copy.start()
    for j in range(GROUP):
        plane_drain(*plane, j, member, base, grp)
    for copy in copies:
        copy.wait_send()
    for o in range(1, 4):
        other = (layer + o) % 4
        pltpu.make_async_remote_copy(
            src_ref=kv16.at[layer],
            dst_ref=kv16.at[other],
            send_sem=deep_send.at[o],
            recv_sem=deep_recv.at[o],
            device_id=device(linear + GROUP * (other - layer), grp),
            device_id_type=MESH,
        ).wait_recv()
    pltpu.make_async_remote_copy(
        src_ref=kv8.at[half],
        dst_ref=kv8.at[1 - half],
        send_sem=deep_send.at[0],
        recv_sem=deep_recv.at[0],
        device_id=device(linear + GROUP - 2 * GROUP * half, grp),
        device_id_type=MESH,
    ).wait_recv()


def compact(rows, packed, at):
    for j in range(GROUP):
        for place, size in at:
            packed[place + size * j : place + size * j + size] = rows[512 * j : 512 * j + size]


def gather_keys(kv, kv8, kv16, kvc):
    compact(kv, kvc, ((0, 256), (2048, 128)))
    for i in range(2):
        kvc[3072 + 512 * i : 3584 + 512 * i] = kv8[i]
    for i in range(4):
        kvc[4096 + 256 * i : 4352 + 256 * i] = kv16[i]


def unit_forward(query, key, out):
    lane = lax.broadcasted_iota(jnp.int32, (256, LANES), 1)
    count = len(query)
    scores = [matmul(query[i](), key, NT) for i in range(count)]
    for i in range(count):
        top = jnp.max(scores[i], axis=1, keepdims=True) * scale2
        prob = jnp.exp2(scores[i] * scale2 - top).astype(bf16)
        out[i](jnp.where(lane == FLAG + 8, top, matmul(prob, key)))


def forward_kernel(slides, q_ref, kv_ref, kv8, kv16, om, stat, acc, qc, kvc):
    ones_lane = FLAG + 1 + slides
    q = q_ref.at[0]
    kv = kv_ref.at[0]
    compact(q, qc, ((0, 256), (2048, 128), (3072, 64), (3584, 32)))
    gather_keys(kv, kv8.at[:, 0], kv16.at[:, 0], kvc)

    def unit(source, q_from, keys, k_from, out_from, count):
        def reader(i):
            return lambda: source[pl.ds(q_from + 256 * i, 256)]

        def writer(i):
            def put(value):
                acc[pl.ds(out_from + 256 * i, 256)] = value

            return put

        unit_forward(
            [reader(i) for i in range(count)],
            keys[pl.ds(k_from, 1024)],
            [writer(i) for i in range(count)],
        )

    def first(u, _):
        at = pl.multiple_of(u * 1024, 1024)
        unit(q, at, kv, at, at, 4)
        return 0

    lax.fori_loop(0, 4, first, 0)

    def second(u, _):
        at = pl.multiple_of(u * 1024, 1024)
        unit(qc, at, kvc, at, at + 4096, 4)
        return 0

    lax.fori_loop(0, 3, second, 0)
    unit(qc, 3072, kvc, 3072, 7168, 2)
    unit(qc, 3584, kvc, 4096, 7680, 1)

    def merge(j, _):
        spans = ((256, 512, 1), (128, 256, 2), (64, 128, 3), (32, 64, 4), (0, 32, 5))
        parts = []
        for low, high, uses in reversed(spans):
            size = high - low
            lane = lax.broadcasted_iota(jnp.int32, (size, LANES), 1)
            pieces = [
                acc[pl.ds(q_at[r] + (512 >> r) * j + low, size)] for r in range(uses)
            ]
            tops = [piece[:, FLAG + 8 : FLAG + 9] for piece in pieces]
            query = q[pl.ds(512 * j + low, size)].astype(f32)
            key = kv[pl.ds(512 * j + low, size)].astype(f32)
            dots = jnp.sum(jnp.where(lane < HD, query * key, 0.0), axis=1, keepdims=True)
            own = jnp.where(
                key[:, FLAG : FLAG + 1] == 0.0, -BIG, dots * scale2 + math.log2(uses)
            )
            top = own
            for item in tops:
                top = jnp.maximum(top, item)
            weight = jnp.exp2(own - top)
            total = weight
            mix = weight * key
            for piece, item in zip(pieces, tops):
                weight = jnp.exp2(item - top)
                total = total + weight * piece[:, ones_lane : ones_lane + 1]
                mix = mix + weight * piece
            mix = mix / total
            parts.append(jnp.where(lane == FLAG, top + jnp.log2(total), mix))
        wide = jnp.concatenate(parts, axis=0).T
        om[j] = wide[HD : 2 * HD].astype(bf16)
        stat[0, j] = wide[HD : HD + 56]
        return 0

    lax.fori_loop(0, GROUP, merge, 0)


def join_quads(read):
    pairs = []
    for half in range(2):
        quads = []
        for quad in (2 * half, 2 * half + 1):
            wide = jnp.concatenate(
                [swap_chunks(read(4 * quad + i), 4 * quad + i) for i in range(4)], axis=0
            )
            quads.append(swap_blocks(wide.T, quad))
        pairs.append(jnp.concatenate(quads, axis=1))
    return jnp.concatenate(pairs, axis=1)


def merged_kernel(grp, om, out, recv, send_sem, recv_sem):
    linear, member, base = spot(grp)
    barrier, total = plane_barrier(grp, False)
    pl.semaphore_wait(barrier, total)
    plane = (om, recv, send_sem, recv_sem)
    for j in range(GROUP):
        plane_send(*plane, j, member, base, grp)
    for j in range(GROUP):
        plane_wait(*plane, j, member, base, grp)
    out[...] = join_quads(lambda h: recv[h // 2, HD * (h % 2) : HD * (h % 2) + HD])
    for j in range(GROUP):
        plane_drain(*plane, j, member, base, grp)


def spread_kernel(grp, rows_ref, recv, send, send_sem, recv_sem):
    linear, member, base = spot(grp)
    barrier, total = plane_barrier(grp, False)
    plane = (send, recv, send_sem, recv_sem)
    for quad in range(4):
        wide = swap_blocks(rows_ref[:, 192 * quad : 192 * quad + 192], quad).T
        for inner in range(4):
            head = 4 * quad + inner
            at = HD * (head % 2)
            send[head // 2, at : at + HD] = swap_chunks(wide[HD * inner : HD * inner + HD], head)
        if quad == 0:
            pl.semaphore_wait(barrier, total)
        for owner in (2 * quad, 2 * quad + 1):
            plane_send(*plane, owner, member, base, grp)
    for j in range(GROUP):
        plane_wait(*plane, j, member, base, grp)
    for j in range(GROUP):
        plane_drain(*plane, j, member, base, grp)


def backward_kernel(
    q_ref, kv_ref, kv8, kv16, msg, gm, stat, pre, dkv8, dkv16,
    qc, kvc, dor, kt, ld, dkv, dqt,
):
    q = q_ref.at[0]
    kv = kv_ref.at[0]
    compact(q, qc, ((0, 256), (2048, 128), (3072, 64), (3584, 32)))
    gather_keys(kv, kv8.at[:, 0], kv16.at[:, 0], kvc)
    rows = []
    for j in range(GROUP):
        grad = gm[j]
        delta = jnp.sum(grad.astype(f32) * stat[0, j, :HD], axis=0, keepdims=True)
        both = jnp.concatenate(
            [stat[0, j, HD : HD + 1], delta, jnp.zeros((6, 512), f32)], axis=0
        )
        rows.append(both)
        ld[:, 512 * j : 512 * j + 512] = both
        ld[:, 4096 + 256 * j : 4352 + 256 * j] = both[:, :256]
        ld[:, 6144 + 128 * j : 6272 + 128 * j] = both[:, :128]
        tall = jnp.concatenate(
            [jnp.zeros((HD, 512), bf16), grad, jnp.zeros((32, 512), bf16)], axis=0
        ).T
        for r, at in enumerate(q_at):
            size = 512 >> r
            dor[at + size * j : at + size * j + size] = tall[:size]
        key = msg[j, :HD]
        kt[j // 2, :, 512 * (j % 2) : 512 * (j % 2) + 512] = key
        kt[4 + j // 4, :, 256 * (j % 4) : 256 * (j % 4) + 256] = key[:, :256]
        kt[6, :, 128 * j : 128 * j + 128] = key[:, :128]
    ld[:, 7168:7680] = jnp.concatenate([both[:, :64] for both in rows], axis=1)
    ld[:, 7680:7936] = jnp.concatenate([both[:, :32] for both in rows], axis=1)
    for i in range(2):
        kt[7 + i] = kvc[3072 + 1024 * i : 4096 + 1024 * i].T[:HD]

    def unit(source, q_from, keys, k_from, place, seg, count):
        width = 256 * count
        query = source[pl.ds(q_from, width)]
        grad = dor[pl.ds(place, width)]
        total = ld[0:1, pl.ds(place, width)]
        delta = ld[1:2, pl.ds(place, width)]
        sides = jnp.concatenate([grad, query], axis=0)
        size = 256
        dq = jnp.zeros((HD, width), f32)
        for c in range(1024 // size):
            key = keys[pl.ds(k_from + size * c, size)]
            prob = jnp.exp2(matmul(key, query, NT) * scale2 - total)
            slope = (prob * (matmul(key, grad, NT) - delta)).astype(bf16)
            both = jnp.concatenate([prob.astype(bf16), slope], axis=1)
            dkv[pl.ds(seg * 1024 + size * c, size)] = matmul(both, sides)
            dq = dq + matmul(kt[seg, :, size * c : size * c + size], slope)
        dqt[:, pl.ds(place, width)] = dq

    def first(u, _):
        at = pl.multiple_of(u * 1024, 1024)
        unit(q, at, kv, at, at, u, 4)
        return 0

    lax.fori_loop(0, 4, first, 0)

    def second(u, _):
        at = pl.multiple_of(u * 1024, 1024)
        unit(qc, at, kvc, at, at + 4096, u + 4, 4)
        return 0

    lax.fori_loop(0, 3, second, 0)
    unit(qc, 3072, kvc, 3072, 7168, 7, 2)
    unit(qc, 3584, kvc, 4096, 7680, 8, 1)
    for i in range(2):
        dkv8[i, 0] = dkv[7168 + 512 * i : 7680 + 512 * i].astype(bf16)
    for i in range(4):
        dkv16[i, 0] = dkv[8192 + 256 * i : 8448 + 256 * i].astype(bf16)
    lane = lax.broadcasted_iota(jnp.int32, (1, 512), 1)
    uses = jnp.where(
        lane < 32, 5.0, jnp.where(lane < 64, 4.0, jnp.where(lane < 128, 3.0, jnp.where(lane < 256, 2.0, 1.0)))
    )
    for j in range(GROUP):
        tall = dkv[512 * j : 512 * j + 512]
        tall = jnp.concatenate(
            [
                tall[:128] + dkv[4096 + 256 * j : 4224 + 256 * j] + dkv[6144 + 128 * j : 6272 + 128 * j],
                tall[128:256] + dkv[4224 + 256 * j : 4352 + 256 * j],
                tall[256:],
            ],
            axis=0,
        )
        wide = tall.T
        key = msg[j, :HD].astype(f32)
        value = msg[j, HD : 2 * HD].astype(f32)
        query = msg[j, 112:160].astype(f32)
        grad = gm[j].astype(f32)
        total = ld[0:1, 512 * j : 512 * j + 512]
        delta = ld[1:2, 512 * j : 512 * j + 512]
        dots = jnp.sum(query * key, axis=0, keepdims=True)
        dropped = msg[j, FLAG : FLAG + 1].astype(f32) != 0.0
        prob = jnp.where(
            dropped, uses * jnp.exp2(jnp.where(dropped, dots * scale2 - total, 0.0)), 0.0
        )
        slope = prob * (jnp.sum(grad * value, axis=0, keepdims=True) - delta)
        dq = dqt[:, 512 * j : 512 * j + 512] + slope * key
        second_part = dqt[:, 4096 + 256 * j : 4352 + 256 * j]
        third_part = dqt[:, 6144 + 128 * j : 6272 + 128 * j]
        fourth_part = dqt[:, 7168 + 64 * j : 7232 + 64 * j]
        fifth_part = dqt[:, 7680 + 32 * j : 7712 + 32 * j]
        fifth_part = jnp.concatenate([fifth_part, jnp.zeros((HD, 32), f32)], axis=1)
        fourth_part = jnp.concatenate([fourth_part + fifth_part, jnp.zeros((HD, 64), f32)], axis=1)
        third_part = jnp.concatenate([third_part + fourth_part, jnp.zeros((HD, 128), f32)], axis=1)
        second_part = jnp.concatenate([second_part + third_part, jnp.zeros((HD, 256), f32)], axis=1)
        pre[0, j, :HD] = (wide[:HD] + slope * query) * scale
        pre[0, j, HD : 2 * HD] = wide[HD : 2 * HD] + prob * grad
        pre[0, j, 2 * HD :] = (dq + second_part) * scale


def return_kernel(
    grp, pre, dkv8, dkv16, *refs,
):
    outs, sums_ref = refs[:4], refs[4]
    send, recv, got8, got16, send_sem, recv_sem, deep_send, deep_recv = refs[5:]
    linear, member, base = spot(grp)
    barrier, total = plane_barrier(grp, True)
    pl.semaphore_wait(barrier, total)
    plane = (send, recv, send_sem, recv_sem)
    layer = linear // GROUP % 4
    half = layer % 2
    copies = []
    for o in range(1, 4):
        other = (layer + o) % 4
        copies.append(
            pltpu.make_async_remote_copy(
                src_ref=dkv16.at[other],
                dst_ref=got16.at[4 - o],
                send_sem=deep_send.at[o],
                recv_sem=deep_recv.at[4 - o],
                device_id=device(linear + GROUP * (other - layer), grp),
                device_id_type=MESH,
            )
        )
    copies.append(
        pltpu.make_async_remote_copy(
            src_ref=dkv8.at[1 - half],
            dst_ref=got8.at[0],
            send_sem=deep_send.at[0],
            recv_sem=deep_recv.at[0],
            device_id=device(linear + GROUP - 2 * GROUP * half, grp),
            device_id_type=MESH,
        )
    )
    for copy in copies:
        copy.start()
    for copy in copies:
        copy.wait()
    row = lax.broadcasted_iota(jnp.int32, (96, 1), 0)
    factor = jnp.where(row < HD, scale, 1.0)
    for j in range(GROUP):
        for i in range(2):
            eight = dkv8[half, i, 64 * j : 64 * j + 64].astype(f32) + got8[
                0, i, 64 * j : 64 * j + 64
            ].astype(f32)
            sixteen = dkv16[layer, i, 32 * j : 32 * j + 32].astype(f32)
            for o in range(1, 4):
                sixteen = sixteen + got16[o, i, 32 * j : 32 * j + 32].astype(f32)
            more = jnp.concatenate(
                [eight[:32] + sixteen, eight[32:], jnp.zeros((64, LANES), f32)], axis=0
            ).T
            at = 144 * i
            first_part = pre[i, j, :96]
            send[j, at : at + 96] = jnp.concatenate(
                [first_part[:, :LANES] + more[:96] * factor, first_part[:, LANES:]], axis=1
            ).astype(bf16)
            send[j, at + 96 : at + 144] = pre[i, j, 96:].astype(bf16)
        plane_send(*plane, j, member, base, grp)
    for j in range(GROUP):
        plane_wait(*plane, j, member, base, grp)
    for quad, out in enumerate(outs):
        parts = []
        for inner in range(4):
            head = 4 * quad + inner
            block = recv[head // 2, 144 * (head % 2) : 144 * (head % 2) + 144]
            block = jnp.concatenate([block[96:], block[:96]], axis=0)
            parts.append(swap_chunks(block, head))
        rows = swap_blocks(jnp.concatenate(parts, axis=0).T, quad)
        out[...] = rows
        sums = column_sum(rows.astype(f32))
        sums_ref[quad] = sums
    for j in range(GROUP):
        plane_drain(*plane, j, member, base, grp)


def pick(ref, g):
    both = jnp.stack([ref[:, g], ref[:, g + 4]], axis=1)
    return both.reshape(768, ref.shape[3])


def put(ref, g, value):
    value = value.reshape(4, 2, 96, ref.shape[3])
    ref[:, g] = value[:, 0]
    ref[:, g + 4] = value[:, 1]


def vmem():
    return pl.BlockSpec(memory_space=pltpu.VMEM)


def sems(n):
    return pltpu.SemaphoreType.DMA((n,))


def params(identity=None):
    if identity is None:
        return pltpu.CompilerParams(vmem_limit_bytes=58 << 20)
    return pltpu.CompilerParams(
        vmem_limit_bytes=58 << 20, collective_id=identity, has_side_effects=True
    )


def shape(dims, dtype):
    return jax.ShapeDtypeStruct(dims, dtype)


def attention_in(grp, slides, normed, weight, bias, flags):
    return pl.pallas_call(
        functools.partial(qkv_kernel, grp, slides),
        name="project_and_share",
        in_specs=[vmem()] * 4,
        out_specs=[vmem()] * 5,
        out_shape=[
            shape((GROUP, 2 * MSG, 512), bf16),
            shape((2, 4096, LANES), bf16),
            shape((2, 4096, LANES), bf16),
            shape((2, 2, 512, LANES), bf16),
            shape((4, 2, 256, LANES), bf16),
        ],
        scratch_shapes=[
            pltpu.VMEM((GROUP, 2 * MSG, 512), bf16),
            sems(GROUP),
            sems(GROUP),
            sems(4),
            sems(4),
        ],
        compiler_params=params(1),
    )(normed, weight, bias, flags)


def attention_forward(slides, q, kv, kv8, kv16):
    return pl.pallas_call(
        functools.partial(forward_kernel, slides),
        name="attention_forward",
        grid=(2,),
        in_specs=[
            pl.BlockSpec((1, 4096, LANES), lambda h: (h, 0, 0)),
            pl.BlockSpec((1, 4096, LANES), lambda h: (h, 0, 0)),
            pl.BlockSpec((2, 1, 512, LANES), lambda h: (0, h, 0, 0)),
            pl.BlockSpec((4, 1, 256, LANES), lambda h: (0, h, 0, 0)),
        ],
        out_specs=[
            pl.BlockSpec((GROUP, HD, 512), lambda h: (0, h, 0)),
            pl.BlockSpec((1, GROUP, 56, 512), lambda h: (h, 0, 0, 0)),
        ],
        out_shape=[shape((GROUP, 2 * HD, 512), bf16), shape((2, GROUP, 56, 512), f32)],
        scratch_shapes=[
            pltpu.VMEM((q_all, LANES), f32),
            pltpu.VMEM((q_all - 4096, LANES), bf16),
            pltpu.VMEM((k_all - 4096, LANES), bf16),
        ],
        compiler_params=params(),
    )(q, kv, kv8, kv16)


def attention_out(grp, om):
    return pl.pallas_call(
        functools.partial(merged_kernel, grp),
        name="share_merged",
        in_specs=[vmem()],
        out_specs=vmem(),
        out_shape=shape((512, 768), bf16),
        scratch_shapes=[pltpu.VMEM((GROUP, 2 * HD, 512), bf16), sems(GROUP), sems(GROUP)],
        compiler_params=params(2),
    )(om)


def gradient_in(grp, grad):
    return pl.pallas_call(
        functools.partial(spread_kernel, grp),
        name="share_gradient",
        in_specs=[vmem()],
        out_specs=vmem(),
        out_shape=shape((GROUP, 2 * HD, 512), bf16),
        scratch_shapes=[pltpu.VMEM((GROUP, 2 * HD, 512), bf16), sems(GROUP), sems(GROUP)],
        compiler_params=params(3),
    )(grad)


def attention_backward(q, kv, kv8, kv16, msg, gm, stat):
    return pl.pallas_call(
        backward_kernel,
        name="attention_backward",
        grid=(2,),
        in_specs=[
            pl.BlockSpec((1, 4096, LANES), lambda h: (h, 0, 0)),
            pl.BlockSpec((1, 4096, LANES), lambda h: (h, 0, 0)),
            pl.BlockSpec((2, 1, 512, LANES), lambda h: (0, h, 0, 0)),
            pl.BlockSpec((4, 1, 256, LANES), lambda h: (0, h, 0, 0)),
            pl.BlockSpec((GROUP, MSG, 512), lambda h: (0, h, 0)),
            pl.BlockSpec((GROUP, HD, 512), lambda h: (0, h, 0)),
            pl.BlockSpec((1, GROUP, 56, 512), lambda h: (h, 0, 0, 0)),
        ],
        out_specs=[
            pl.BlockSpec((1, GROUP, 144, 512), lambda h: (h, 0, 0, 0)),
            pl.BlockSpec((2, 1, 512, LANES), lambda h: (0, h, 0, 0)),
            pl.BlockSpec((4, 1, 256, LANES), lambda h: (0, h, 0, 0)),
        ],
        out_shape=[
            shape((2, GROUP, 144, 512), f32),
            shape((2, 2, 512, LANES), bf16),
            shape((4, 2, 256, LANES), bf16),
        ],
        scratch_shapes=[
            pltpu.VMEM((q_all - 4096, LANES), bf16),
            pltpu.VMEM((k_all - 4096, LANES), bf16),
            pltpu.VMEM((q_all, LANES), bf16),
            pltpu.VMEM((9, HD, 1024), bf16),
            pltpu.VMEM((8, q_all), f32),
            pltpu.VMEM((k_all, LANES), f32),
            pltpu.VMEM((HD, q_all), f32),
        ],
        compiler_params=params(),
    )(q, kv, kv8, kv16, msg, gm, stat)


def gradient_out(grp, pre, dkv8, dkv16):
    return pl.pallas_call(
        functools.partial(return_kernel, grp),
        name="return_gradients",
        in_specs=[vmem()] * 3,
        out_specs=[vmem()] * 5,
        out_shape=[shape((512, 576), bf16)] * 4 + [shape((4, 1, 576), f32)],
        scratch_shapes=[
            pltpu.VMEM((GROUP, 288, 512), bf16),
            pltpu.VMEM((GROUP, 288, 512), bf16),
            pltpu.VMEM((1, 2, 512, LANES), bf16),
            pltpu.VMEM((4, 2, 256, LANES), bf16),
            sems(GROUP),
            sems(GROUP),
            sems(4),
            sems(4),
        ],
        compiler_params=params(4),
    )(pre, dkv8, dkv16)


def norm_parts(values):
    average = jnp.mean(values, axis=-1, keepdims=True)
    centred = values - average
    variance = jnp.mean(centred * centred, axis=-1, keepdims=True)
    inverse = lax.rsqrt(variance + epsilon)
    return centred * inverse, inverse


def norm_backward(hat, inverse, gain, grad):
    scaled = grad * gain
    first = jnp.mean(scaled, axis=-1, keepdims=True)
    second = jnp.mean(scaled * hat, axis=-1, keepdims=True)
    return (scaled - first - hat * second) * inverse


def column_sum(values):
    return jnp.sum(values, axis=0, keepdims=True)


def dense_kernel(
    merged, base, cot, wo, wi, wt, out_bias, gain, shift, in_bias, last_bias,
    out, grad_middle, grad_merged, wo_grad, wi_grad, wt_grad, small, small_in,
    full, middle, hat, low, low_t, cot_low, cot_t, grad_low,
):
    for g in range(0, 4, 2):
        pair = [pick(wo, g + i) for i in range(2)]
        full[:, 192 * g : 192 * g + 384] = jnp.concatenate(pair, axis=1)
    middle[...] = base[...] + matmul(merged[...], full[...]) + out_bias[...]
    normal, inverse = norm_parts(middle[...])
    hat[...] = normal
    low[...] = (normal * gain[...] + shift[...]).astype(bf16)
    low_t[...] = low[...].T
    cot_low[...] = cot[...].astype(bf16)
    cot_t[...] = cot_low[...].T
    out[...] = middle[...] + last_bias[...]
    small[0:1] = column_sum(cot_low[...].astype(f32))
    grad_middle[...] = jnp.zeros((512, 768), f32)

    def chunk(g, _):
        weight = pick(wi, g)
        inner = matmul(low[...], weight) + in_bias[g]
        phi = 0.5 * (1.0 + lax.erf(inner * 0.7071067811865476))
        active = (inner * phi).astype(bf16)
        slope = phi + inner * jnp.exp(-0.5 * inner * inner) * 0.3989422804014327
        for x in range(2):
            part = wt[g, 4 * x : 4 * x + 4].reshape(768, 384)
            now = active[:, 384 * x : 384 * x + 384]
            out[...] += matmul(now, part, NT)
            wt_grad[g, 4 * x : 4 * x + 4] = (
                matmul(cot_t[...], now).astype(bf16).reshape(4, 192, 384)
            )
            back = matmul(cot_low[...], part)
            grad_low[:, 384 * x : 384 * x + 384] = (
                back * slope[:, 384 * x : 384 * x + 384]
            ).astype(bf16)
        small_in[g] = column_sum(grad_low[...].astype(f32))
        put(wi_grad, g, matmul(low_t[...], grad_low[...]).astype(bf16))
        grad_middle[...] += matmul(grad_low[...], weight, NT)
        return 0

    lax.fori_loop(0, 4, chunk, 0)
    grad = grad_middle[...]
    small[1:2] = column_sum(grad * hat[...])
    small[2:3] = column_sum(grad)
    grad = cot[...] + norm_backward(hat[...], inverse, gain[...], grad)
    grad_middle[...] = grad
    attended = grad.astype(bf16)
    small[3:4] = column_sum(attended.astype(f32))
    small[4:8] = jnp.zeros((4, 768), f32)
    grads = matmul(merged[...].T, attended).astype(bf16)
    for g in range(4):
        put(wo_grad, g, grads[:, 192 * g : 192 * g + 192])
    grad_merged[...] = matmul(attended, full[...], NT).astype(bf16)


def dense(merged, base, cot, wo, wi, wt, out_bias, gain, shift, in_bias, last_bias):
    rows = (512, 768)
    return pl.pallas_call(
        dense_kernel,
        name="dense",
        in_specs=[vmem()] * 11,
        out_specs=[vmem()] * 8,
        out_shape=[
            shape(rows, f32), shape(rows, f32), shape(rows, bf16),
            shape((4, GROUP, 96, 192), bf16), shape((4, GROUP, 96, 768), bf16),
            shape((4, GROUP, 192, 384), bf16), shape((8, 768), f32), shape((4, 1, 768), f32),
        ],
        scratch_shapes=[
            pltpu.VMEM((768, 768), bf16), pltpu.VMEM(rows, f32), pltpu.VMEM(rows, f32),
            pltpu.VMEM(rows, bf16), pltpu.VMEM((768, 512), bf16), pltpu.VMEM(rows, bf16),
            pltpu.VMEM((768, 512), bf16), pltpu.VMEM(rows, bf16),
        ],
        compiler_params=params(),
    )(merged, base, cot, wo, wi, wt, out_bias, gain, shift, in_bias, last_bias)


def final_kernel(
    base, grad_middle, d0, d1, d2, d3, weight, gain, shift, token_grad, grads_out, small,
):
    hat, inverse = norm_parts(base[...])
    low_t = (hat * gain[...] + shift[...]).astype(bf16).T
    grad = jnp.zeros((512, 768), f32)
    small[...] = jnp.zeros((8, 768), f32)
    for quad, part in enumerate((d0, d1, d2, d3)):
        now = part[...]
        put(grads_out, quad, matmul(low_t, now).astype(bf16))
        grad = grad + matmul(now, pick(weight, quad), NT)
    small[0:1] = column_sum(grad * hat)
    small[1:2] = column_sum(grad)
    token_grad[...] = grad_middle[...] + norm_backward(hat, inverse, gain[...], grad)


def final(base, grad_middle, quads, weight, gain, shift):
    rows = (512, 768)
    return pl.pallas_call(
        final_kernel,
        name="input_gradients",
        in_specs=[vmem()] * 9,
        out_specs=[vmem()] * 3,
        out_shape=[shape(rows, f32), shape((4, GROUP, 96, 576), bf16), shape((8, 768), f32)],
        compiler_params=params(),
    )(base, grad_middle, *quads, weight, gain, shift)


def member_of(x, y, c):
    return x * 4 + y * 2 + c


def place():
    seq, col = lax.axis_index("seq"), lax.axis_index("grp")
    return seq // 2, seq % 2, col // 2, col % 2


def at_place(z, x, y, c):
    return (z * 2 + x, y * 2 + c)


def remote(src, dst, send_sem, recv_sem, target):
    return pltpu.make_async_remote_copy(
        src_ref=src, dst_ref=dst, send_sem=send_sem, recv_sem=recv_sem,
        device_id=target, device_id_type=MESH,
    )


def block_barrier(z, x, y, c):
    barrier = pltpu.get_barrier_semaphore()
    near = [at_place((z + o) % 4, x, y, c) for o in (1, 2, 3)]
    near += [at_place(z, 1 - x, y, c), at_place(z, x, 1 - y, c), at_place(z, 1 - x, 1 - y, c)]
    near += [at_place(z, x, y, 1 - c)]
    for target in near:
        pl.semaphore_signal(barrier, inc=1, device_id=target, device_id_type=MESH)
    pl.semaphore_wait(barrier, len(near))


def gather_kernel(count, *refs):
    ins, outs = refs[:count], refs[count : 2 * count]
    loc, zs, zr, ps, pr, qs, qr, cs, cr = refs[2 * count :]
    z, x, y, c = place()
    me = member_of(x, y, c)
    block_barrier(z, x, y, c)
    arrays = range(count)
    local = [pltpu.make_async_copy(ins[k], outs[k].at[z, me], loc.at[k]) for k in arrays]
    for copy in local:
        copy.start()
    started = []
    beside = [(1 - x, y), (x, 1 - y)]

    def go(copy):
        copy.start()
        started.append(copy)

    for o in (1, 2, 3):
        for k in arrays:
            go(remote(ins[k], outs[k].at[z, me], zs.at[o, k], zr.at[4 - o, k],
                      at_place((z + o) % 4, x, y, c)))

    def push(layer, slot, sources):
        for p, (px, py) in enumerate(beside):
            for k in arrays:
                go(remote(sources[k], outs[k].at[layer, me], ps.at[p, slot, k], pr.at[p, slot, k],
                          at_place(z, px, py, c)))

    def relay(layer, slot):
        for p, (px, py) in enumerate(beside):
            m = member_of(px, py, c)
            for k in arrays:
                part = outs[k].at[layer, m]
                remote(part, part, ps.at[p, slot, k], pr.at[p, slot, k],
                       at_place(z, px, py, c)).wait_recv()
        for k in arrays:
            rows = ins[k].shape[0] // 2
            for p, (px, py) in enumerate(beside):
                part = outs[k].at[layer, member_of(px, py, c), p * rows : (p + 1) * rows]
                tx, ty = beside[1 - p]
                go(remote(part, part, qs.at[p, slot, k], qr.at[p, slot, k],
                          at_place(z, tx, ty, c)))

    push(z, 0, ins)
    for copy in local:
        copy.wait()
    for o in (1, 2, 3):
        layer = (z + o) % 4
        for k in arrays:
            part = outs[k].at[layer, me]
            remote(part, part, zs.at[o, k], zr.at[o, k], at_place(layer, x, y, c)).wait_recv()
        push(layer, o, [outs[k].at[layer, me] for k in arrays])
        relay((z + o - 1) % 4, o - 1)
    relay((z + 3) % 4, 3)

    def across(slot, px, py):
        m = member_of(px, py, c)
        for k in arrays:
            part = outs[k].at[:, m]
            go(remote(part, part, cs.at[slot, k], cr.at[slot, k], at_place(z, x, y, 1 - c)))

    across(0, x, y)
    across(1, 1 - x, y)
    across(2, x, 1 - y)
    far = member_of(1 - x, 1 - y, c)
    for slot in range(4):
        layer = (z + slot) % 4
        for k in arrays:
            rows = ins[k].shape[0] // 2
            for p in range(2):
                part = outs[k].at[layer, far, p * rows : (p + 1) * rows]
                remote(part, part, qs.at[p, slot, k], qr.at[p, slot, k],
                       at_place(z, *beside[1 - p], c)).wait_recv()
    across(3, 1 - x, 1 - y)
    for slot, (px, py) in enumerate([(x, y), (1 - x, y), (x, 1 - y), (1 - x, 1 - y)]):
        m = member_of(px, py, 1 - c)
        for k in arrays:
            part = outs[k].at[:, m]
            remote(part, part, cs.at[slot, k], cr.at[slot, k], at_place(z, x, y, 1 - c)).wait_recv()
    for copy in started:
        copy.wait_send()


def gather_weights(parts, identity):
    count = len(parts)
    return pl.pallas_call(
        functools.partial(gather_kernel, count),
        name="gather_weights",
        in_specs=[pl.BlockSpec(memory_space=pl.ANY)] * count,
        out_specs=[pl.BlockSpec(memory_space=pl.ANY)] * count,
        out_shape=[shape((4, GROUP) + part.shape, part.dtype) for part in parts],
        scratch_shapes=[
            sems(count), dsems(4, count), dsems(4, count), dsems(2, 4, count), dsems(2, 4, count),
            dsems(2, 4, count), dsems(2, 4, count), dsems(4, count), dsems(4, count),
        ],
        compiler_params=params(identity),
    )(*parts)


def dsems(*dims):
    return pltpu.SemaphoreType.DMA(dims)


def reduce_kernel(count, *refs):
    ins, small = refs[:count], refs[count]
    outs, total = refs[count + 1 : 2 * count + 1], refs[2 * count + 1]
    rest = refs[2 * count + 2 :]
    own, across, one, two, deep = [rest[i * count : (i + 1) * count] for i in range(5)]
    (sm_c, sm_p, sm_z, loc, cs, cr, xs, xr, ys, yr, zs, zr, sms, smr) = rest[5 * count :]
    z, x, y, c = place()
    block_barrier(z, x, y, c)
    arrays = range(count)
    started = []

    def go(copy):
        copy.start()
        started.append(copy)

    mine, px_, py_, far = (x, y), (1 - x, y), (x, 1 - y), (1 - x, 1 - y)
    other = at_place(z, x, y, 1 - c)
    slot_of = lambda p: p[0] * 2 + p[1]
    sm_c[c] = small[...]
    go(remote(sm_c.at[c], sm_c.at[c], sms.at[0], smr.at[0], other))
    for n, p in enumerate((far, px_, py_, mine)):
        for k in arrays:
            go(remote(ins[k].at[:, member_of(*p, 1 - c)], across[k].at[slot_of(p)],
                      cs.at[n, k], cr.at[n, k], other))
            pltpu.make_async_copy(
                ins[k].at[:, member_of(*p, c)], own[k].at[slot_of(p)], loc.at[n, k]
            ).start()
    remote(sm_c.at[c], sm_c.at[1 - c], sms.at[0], smr.at[0], other).wait_recv()
    flat = x * 2 + y
    sm_p[flat] = sm_c[0] + sm_c[1]
    plane = (px_, py_, far)
    for n, p in enumerate(plane):
        go(remote(sm_p.at[flat], sm_p.at[flat], sms.at[1 + n], smr.at[1 + n], at_place(z, *p, c)))

    def add(target, source):
        rows = target.shape[-2]

        def step(i, _):
            target[i] = (target[i].astype(f32) + source[i].astype(f32)).astype(bf16)
            return 0

        lax.fori_loop(0, 4, step, 0)

    def landed(n, p):
        for k in arrays:
            pltpu.make_async_copy(
                ins[k].at[:, member_of(*p, c)], own[k].at[slot_of(p)], loc.at[n, k]
            ).wait()
            remote(ins[k].at[:, member_of(*p, 1 - c)], across[k].at[slot_of(p)],
                   cs.at[n, k], cr.at[n, k], other).wait_recv()
            add(own[k].at[slot_of(p)], across[k].at[slot_of(p)])

    halves = [ins[k].shape[2] // 2 for k in arrays]
    hx = lambda k: slice(0, halves[k])
    hy = lambda k: slice(halves[k], 2 * halves[k])
    to_x, to_y = at_place(z, *px_, c), at_place(z, *py_, c)

    def x_first(k, p, i, target):
        src = own[k].at[slot_of(p), :, hx(k)]
        return remote(src, target, xs.at[i, k], xr.at[i, k], to_x)

    def y_first(k, p, i, target):
        src = own[k].at[slot_of(p), :, hy(k)]
        return remote(src, target, ys.at[i, k], yr.at[i, k], to_y)

    landed(0, far)
    for k in arrays:
        go(x_first(k, far, 0, one[k].at[0]))
        go(y_first(k, far, 0, one[k].at[1]))
    landed(1, px_)
    for k in arrays:
        go(x_first(k, px_, 1, one[k].at[2]))
    landed(2, py_)
    for k in arrays:
        go(y_first(k, py_, 1, one[k].at[3]))
    landed(3, mine)
    for n, p in enumerate(plane):
        index = slot_of(p)
        remote(sm_p.at[index], sm_p.at[index], sms.at[1 + n], smr.at[1 + n],
               at_place(z, *p, c)).wait_recv()
    sm_z[z] = (sm_p[0] + sm_p[1]) + (sm_p[2] + sm_p[3])
    for o in (1, 2, 3):
        go(remote(sm_z.at[z], sm_z.at[z], sms.at[3 + o], smr.at[7 - o],
                  at_place((z + o) % 4, x, y, c)))
    for k in arrays:
        x_first(k, far, 0, one[k].at[0]).wait_recv()
        add(own[k].at[slot_of(py_), :, hx(k)], one[k].at[0])
        go(remote(own[k].at[slot_of(py_), :, hx(k)], two[k].at[0], ys.at[2, k], yr.at[2, k], to_y))
        y_first(k, far, 0, one[k].at[1]).wait_recv()
        add(own[k].at[slot_of(px_), :, hy(k)], one[k].at[1])
        go(remote(own[k].at[slot_of(px_), :, hy(k)], two[k].at[1], xs.at[2, k], xr.at[2, k], to_x))
    for k in arrays:
        x_first(k, px_, 1, one[k].at[2]).wait_recv()
        add(own[k].at[slot_of(mine), :, hx(k)], one[k].at[2])
        y_first(k, py_, 1, one[k].at[3]).wait_recv()
        add(own[k].at[slot_of(mine), :, hy(k)], one[k].at[3])
    for k in arrays:
        remote(own[k].at[slot_of(py_), :, hx(k)], two[k].at[0], ys.at[2, k], yr.at[2, k], to_y).wait_recv()
        add(own[k].at[slot_of(mine), :, hx(k)], two[k].at[0])
        remote(own[k].at[slot_of(px_), :, hy(k)], two[k].at[1], xs.at[2, k], xr.at[2, k], to_x).wait_recv()
        add(own[k].at[slot_of(mine), :, hy(k)], two[k].at[1])
        for o in (1, 2, 3):
            layer = (z + o) % 4
            go(remote(own[k].at[slot_of(mine), layer], deep[k].at[4 - o], zs.at[o, k],
                      zr.at[4 - o, k], at_place(layer, x, y, c)))
    for o in (1, 2, 3):
        layer = (z + o) % 4
        remote(sm_z.at[layer], sm_z.at[layer], sms.at[3 + o], smr.at[3 + o],
               at_place(layer, x, y, c)).wait_recv()
    total[...] = (sm_z[0] + sm_z[1]) + (sm_z[2] + sm_z[3])
    for k in arrays:
        value = own[k][slot_of(mine), z].astype(f32)
        for o in (1, 2, 3):
            remote(own[k].at[slot_of(mine), z], deep[k].at[o], zs.at[o, k], zr.at[o, k],
                   at_place((z + o) % 4, x, y, c)).wait_recv()
            value = value + deep[k][o].astype(f32)
        outs[k][...] = value
    for copy in started:
        copy.wait_send()


def reduce_gradients(parts, small, identity):
    count = len(parts)
    dims = [part.shape[2:] for part in parts]
    half = [(rows // 2, lanes) for rows, lanes in dims]
    return pl.pallas_call(
        functools.partial(reduce_kernel, count),
        name="reduce_gradients",
        in_specs=[pl.BlockSpec(memory_space=pl.ANY)] * count + [vmem()],
        out_specs=[vmem()] * (count + 1),
        out_shape=[shape(d, f32) for d in dims] + [shape(small.shape, f32)],
        scratch_shapes=[pltpu.VMEM((4, 4) + d, bf16) for d in dims]
        + [pltpu.VMEM((4, 4) + d, bf16) for d in dims]
        + [pltpu.VMEM((4, 4) + d, bf16) for d in half]
        + [pltpu.VMEM((2, 4) + d, bf16) for d in half]
        + [pltpu.VMEM((4,) + d, bf16) for d in dims]
        + [
            pltpu.VMEM((2,) + small.shape, f32),
            pltpu.VMEM((4,) + small.shape, f32),
            pltpu.VMEM((4,) + small.shape, f32),
            dsems(4, count), dsems(4, count), dsems(4, count),
            dsems(3, count), dsems(3, count), dsems(3, count), dsems(3, count),
            dsems(4, count), dsems(4, count), sems(7), sems(7),
        ],
        compiler_params=params(identity),
    )(*parts, small)


def all_weights(parts, seq, grp):
    if (seq, grp) == (8, 4):
        return gather_weights(parts, 5)
    gathered = []
    for n, part in enumerate(parts):
        whole = lax.all_gather(lax.all_gather(part, "grp"), "seq")
        lead = whole.shape[0] // 8
        whole = whole.reshape((8, lead) + whole.shape[1:])
        if n == 3:
            whole = whole.transpose(0, 2, 3, 1, 4)
            whole = whole.reshape(4, GROUP, part.shape[0], lead * part.shape[1])
        else:
            whole = whole.transpose(0, 2, 1, 3, 4)
            whole = whole.reshape(4, GROUP, lead * part.shape[0], part.shape[1])
        gathered.append(whole)
    return gathered


def sum_gradients(parts, small, seq, grp):
    if (seq, grp) == (8, 4):
        return reduce_gradients(parts, small, 6)
    lead = seq // 8
    sums = []
    for n, part in enumerate(parts):
        height, lanes = part.shape[2:]
        whole = part.reshape(8, grp, height, lanes)
        if n == 3:
            whole = whole.reshape(8, grp, height, lead, lanes // lead).transpose(0, 3, 1, 2, 4)
        else:
            whole = whole.reshape(8, grp, lead, height // lead, lanes).transpose(0, 2, 1, 3, 4)
        whole = whole.reshape((seq, grp) + whole.shape[3:]).astype(f32)
        whole = lax.psum_scatter(whole, "seq", scatter_dimension=0)
        sums.append(lax.psum_scatter(whole, "grp", scatter_dimension=0))
    return sums + [lax.psum(small, ("seq", "grp"))]


def position_table(coordinates, width):
    quarter = width // 4
    frequency = jnp.exp(jnp.arange(quarter, dtype=jnp.float32) * (-math.log(10000.0) / quarter))
    column = coordinates[:, 0:1].astype(jnp.float32) * frequency[None, :]
    across = coordinates[:, 1:2].astype(jnp.float32) * frequency[None, :]
    return jnp.concatenate(
        [jnp.sin(column), jnp.cos(column), jnp.sin(across), jnp.cos(across)], axis=1
    )


def layer_norm(values, norm_gain, norm_shift):
    average = jnp.mean(values, axis=-1, keepdims=True)
    centred = values - average
    variance = jnp.mean(centred * centred, axis=-1, keepdims=True)
    return centred * lax.rsqrt(variance + epsilon) * norm_gain + norm_shift


def in_order(rows):
    split = rows.reshape((BLOCK, 16) + rows.shape[1:])
    return jnp.stack([split[:, b] for b in order]).reshape(rows.shape)


def back_order(rows):
    split = rows.reshape((16, BLOCK) + rows.shape[1:])
    return jnp.stack([split[b] for b in order], axis=1).reshape(rows.shape)


def body(
    tokens,
    coordinates,
    lengths,
    valid,
    first_gain,
    first_shift,
    query_weight,
    query_bias,
    key_weight,
    value_weight,
    value_bias,
    output_weight,
    output_bias,
    second_gain,
    second_shift,
    inner_weight,
    inner_bias,
    outer_weight,
    outer_bias,
    cotangent,
):
    rows, width = tokens.shape
    grp = lax.axis_size("grp")
    seq = lax.axis_size("seq")
    slides = lengths.shape[0]
    linear = lax.axis_index("seq") * grp + lax.axis_index("grp")
    start = linear * rows
    shard = query_weight.shape[0]
    heads = [w.reshape(shard, 4, 1, HD) for w in (query_weight, key_weight, value_weight)]
    parts = [
        jnp.concatenate(heads, axis=2).reshape(shard, 576),
        output_weight,
        inner_weight,
        outer_weight.T,
    ]
    joint_weight, wo, wi, wt = all_weights(parts, seq, grp)
    joint_bias = jnp.stack(
        [b.reshape(4, 4, HD) for b in (query_bias, jnp.zeros_like(query_bias), value_bias)], axis=2
    ).reshape(4, 1, 576)
    base = in_order(tokens + position_table(coordinates, width))
    cotangent = in_order(cotangent)
    places = in_order(start + jnp.arange(rows, dtype=jnp.int32))
    keep = in_order(valid)
    slide = jnp.sum((places[:, None] >= jnp.cumsum(lengths)).astype(jnp.int32), axis=-1)
    apart = slide[None, :] != jnp.arange(slides, dtype=jnp.int32)[:, None]
    flags = jnp.concatenate(
        [
            jnp.where(keep == 1, 0.0, -BIG)[None, :],
            jnp.where(apart, -BIG, 0.0),
            jnp.ones((1, rows), f32),
            jnp.zeros((14 - slides, rows), f32),
        ],
        axis=0,
    )
    row = lambda v: v.reshape(1, -1)
    normed_low = layer_norm(base, first_gain, first_shift).astype(bf16)
    msg, q_rows, kv_rows, kv8, kv16 = attention_in(
        grp, slides, normed_low, joint_weight, joint_bias, flags
    )
    own, stat = attention_forward(slides, q_rows, kv_rows, kv8, kv16)
    merged_low = attention_out(grp, own)
    output, grad_middle, grad_merged, wo_grad, wi_grad, wt_grad, small, small_in = dense(
        merged_low, base, cotangent, wo, wi, wt, row(output_bias), row(second_gain),
        row(second_shift), inner_bias.reshape(4, 1, 768), row(outer_bias),
    )
    shared = gradient_in(grp, grad_merged)
    pre, dkv8, dkv16 = attention_backward(q_rows, kv_rows, kv8, kv16, msg, shared, stat)
    *quads, sums = gradient_out(grp, pre, dkv8, dkv16)
    token_grad, joint_grad, first_small = final(
        base, grad_middle, quads, joint_weight, row(first_gain), row(first_shift)
    )
    sums = sums.reshape(4, 4, 3, HD)
    vectors = [
        first_small[0], first_small[1], sums[:, :, 0].reshape(-1), sums[:, :, 2].reshape(-1),
        small[3], small[1], small[2], small_in.reshape(-1), small[0],
    ]
    sizes = [v.shape[0] for v in vectors]
    pack = jnp.concatenate(vectors).reshape(-1, LANES)
    joint_sum, sum_output, sum_inner, sum_outer, pack = sum_gradients(
        [joint_grad, wo_grad, wi_grad, wt_grad], pack, seq, grp
    )
    joint_sum = joint_sum.reshape(shard, 4, 3, HD)
    sum_query, sum_key, sum_value = [joint_sum[:, :, i].reshape(shard, 192) for i in range(3)]
    sum_outer = sum_outer.T
    small = []
    pack = pack.reshape(-1)
    for size in sizes:
        small.append(pack[:size])
        pack = pack[size:]
    return (
        back_order(output),
        back_order(token_grad),
        small[0],
        small[1],
        sum_query,
        small[2],
        sum_key,
        sum_value,
        small[3],
        sum_output,
        small[4],
        small[5],
        small[6],
        sum_inner,
        small[7],
        sum_outer,
        small[8],
    )


def solution(mesh):
    placed = (
        P(("seq", "grp"), None),
        P(("seq", "grp"), None),
        P(),
        P(("seq", "grp")),
        P(),
        P(),
        P("seq", "grp"),
        P(),
        P("seq", "grp"),
        P("seq", "grp"),
        P(),
        P("seq", "grp"),
        P(),
        P(),
        P(),
        P("seq", "grp"),
        P(),
        P("seq", "grp"),
        P(),
        P(("seq", "grp"), None),
    )
    return jax.shard_map(
        body,
        mesh=mesh,
        in_specs=placed,
        out_specs=(
            P(("seq", "grp"), None),
            P(("seq", "grp"), None),
            P(),
            P(),
            P("seq", "grp"),
            P(),
            P("seq", "grp"),
            P("seq", "grp"),
            P(),
            P("seq", "grp"),
            P(),
            P(),
            P(),
            P("seq", "grp"),
            P(),
            P("seq", "grp"),
            P(),
        ),
        check_vma=False,
    )
```

```python
import functools
import math

import jax
import jax.numpy as jnp
from jax import lax
from jax.experimental import pallas as pl
from jax.experimental.pallas import tpu as pltpu
from jax.sharding import PartitionSpec as P

HEADS = 16

epsilon = 1e-05


NT = (((1,), (1,)), ((), ()))
NN = (((1,), (0,)), ((), ()))
f32 = jnp.float32
bf16 = jnp.bfloat16
BIG = 1e30
HD = 48
GROUP = 8
LANES = 128
BLOCK = 32
MSG = 160
FLAG = 2 * HD
MESH = pl.DeviceIdType.MESH
scale = HD ** (-0.5)
scale2 = scale * math.log2(math.e)
q_at = (0, 4096, 6144, 7168, 7680)
q_all = 7936
k_all = 9216


def reverse4(b):
    return (b & 1) * 8 + (b & 2) * 2 + (b & 4) // 2 + (b & 8) // 8


order = [reverse4(b) for b in range(16)]


def chunk_swap(head):
    return reverse4(head) >> 2


def block_swap(quad):
    return reverse4(4 * quad) & 3


def swap_blocks(rows, quad):
    return jnp.concatenate(
        [rows[BLOCK * (b ^ block_swap(quad)) :][:BLOCK] for b in range(16)], axis=0
    )


def swap_chunks(wide, head):
    return jnp.concatenate(
        [wide[:, LANES * (c ^ chunk_swap(head)) :][:, :LANES] for c in range(4)], axis=1
    )


def matmul(a, b, dims=NN):
    return lax.dot_general(a, b, dims, preferred_element_type=f32)


def column_sum(values):
    return jnp.sum(values, axis=0, keepdims=True)


def pick(ref, g):
    both = jnp.stack([ref[:, g], ref[:, g + 4]], axis=1)
    return both.reshape(768, ref.shape[3])


def put(ref, g, value):
    value = value.reshape(4, 2, 96, ref.shape[3])
    ref[:, g] = value[:, 0]
    ref[:, g + 4] = value[:, 1]


def vmem():
    return pl.BlockSpec(memory_space=pltpu.VMEM)


def anywhere():
    return pl.BlockSpec(memory_space=pl.ANY)


def sems(*dims):
    return pltpu.SemaphoreType.DMA(dims)


def params(identity=None):
    if identity is None:
        return pltpu.CompilerParams(vmem_limit_bytes=60 << 20)
    return pltpu.CompilerParams(
        vmem_limit_bytes=60 << 20, collective_id=identity, has_side_effects=True
    )


def shape(dims, dtype):
    return jax.ShapeDtypeStruct(dims, dtype)


def remote(src, dst, send_sem, recv_sem, target):
    return pltpu.make_async_remote_copy(
        src_ref=src, dst_ref=dst, send_sem=send_sem, recv_sem=recv_sem,
        device_id=target, device_id_type=MESH,
    )


class Spot:
    def __init__(self, grp):
        self.grp = grp
        self.linear = lax.axis_index("seq") * grp + lax.axis_index("grp")
        self.member = self.linear % GROUP
        self.base = self.linear - self.member
        self.layer = self.linear // GROUP % 4
        self.half = self.layer % 2

    def device(self, linear):
        return (linear // self.grp, linear % self.grp)

    def beside(self, j):
        return self.device(self.base + j)

    def over(self, layer):
        return self.device(self.linear + GROUP * (layer - self.layer))

    def pair(self):
        return self.device(self.linear + GROUP - 2 * GROUP * self.half)

    def greet(self):
        barrier = pltpu.get_barrier_semaphore()
        for j in range(GROUP):

            @pl.when(self.member != j)
            def _():
                pl.semaphore_signal(barrier, inc=1, device_id=self.beside(j), device_id_type=MESH)

        for o in range(1, 4):
            target = self.over((self.layer + o) % 4)
            pl.semaphore_signal(barrier, inc=1, device_id=target, device_id_type=MESH)
        return lambda: pl.semaphore_wait(barrier, GROUP + 2)


class Exchange:
    def __init__(self, spot, send, recv, send_sem, recv_sem):
        self.spot, self.send_ref, self.recv = spot, send, recv
        self.send_sem, self.recv_sem = send_sem, recv_sem

    def out(self, j):
        s = self.spot
        return remote(self.send_ref.at[j], self.recv.at[s.member], self.send_sem.at[j],
                      self.recv_sem.at[s.member], s.beside(j))

    def inner(self, j):
        return pltpu.make_async_copy(self.send_ref.at[j], self.recv.at[j], self.recv_sem.at[j])

    def choose(self, j, far, near):
        pl.when(self.spot.member != j)(far)
        pl.when(self.spot.member == j)(near)

    def send(self, j):
        self.choose(j, lambda: self.out(j).start(), lambda: self.inner(j).start())

    def wait(self, j):
        def far():
            remote(self.send_ref.at[j], self.recv.at[j], self.send_sem.at[j], self.recv_sem.at[j],
                   self.spot.beside(j)).wait_recv()

        self.choose(j, far, lambda: self.inner(j).wait())

    def drain(self):
        for j in range(GROUP):
            pl.when(self.spot.member != j)(lambda j=j: self.out(j).wait_send())


class Deep:
    def __init__(self, spot, eight, sixteen, send_sem, recv_sem):
        self.copies, self.waits = [], []
        s = spot
        for o in range(1, 4):
            other = (s.layer + o) % 4
            src, there, here = sixteen(o, other)
            self.copies.append(remote(src, there, send_sem.at[o], recv_sem.at[4 - o], s.over(other)))
            self.waits.append(remote(src, here, send_sem.at[o], recv_sem.at[o], s.over(other)))
        src, there, here = eight
        self.copies.append(remote(src, there, send_sem.at[0], recv_sem.at[0], s.pair()))
        self.waits.append(remote(src, here, send_sem.at[0], recv_sem.at[0], s.pair()))

    def start(self):
        for copy in self.copies:
            copy.start()

    def wait(self):
        for copy in self.waits:
            copy.wait_recv()

    def drain(self):
        for copy in self.copies:
            copy.wait_send()


def member_of(x, y, c):
    return x * 4 + y * 2 + c


def place():
    seq, col = lax.axis_index("seq"), lax.axis_index("grp")
    return seq // 2, seq % 2, col // 2, col % 2


def at_place(z, x, y, c):
    return (z * 2 + x, y * 2 + c)


def gather_sems(count):
    return [
        sems(count), sems(4, count), sems(4, count), sems(2, 4, count), sems(2, 4, count),
        sems(2, 4, count), sems(2, 4, count), sems(4, count), sems(4, count),
    ]


class Gather:
    def __init__(self, ins, outs, semaphores):
        self.ins, self.outs = ins, outs
        (self.loc, self.zs, self.zr, self.ps, self.pr,
         self.qs, self.qr, self.cs, self.cr) = semaphores
        self.place = z, x, y, c = place()
        self.me = member_of(x, y, c)
        self.arrays = range(len(ins))
        self.near = [(1 - x, y), (x, 1 - y)]
        self.started = []
        self.done = 0
        self.local = [
            pltpu.make_async_copy(ins[k], outs[k].at[z, self.me], self.loc.at[k])
            for k in self.arrays
        ]
        self.stages = [self.stage1, self.stage2, self.stage3, self.stage4, self.stage5, self.stage6]

    def go(self, copy):
        copy.start()
        self.started.append(copy)

    def start_layers(self):
        z, x, y, c = self.place
        for copy in self.local:
            copy.start()
        for o in (1, 2, 3):
            for k in self.arrays:
                self.go(remote(self.ins[k], self.outs[k].at[z, self.me], self.zs.at[o, k],
                               self.zr.at[4 - o, k], at_place((z + o) % 4, x, y, c)))

    def push(self, layer, slot, sources):
        z, x, y, c = self.place
        for p, (px, py) in enumerate(self.near):
            for k in self.arrays:
                self.go(remote(sources[k], self.outs[k].at[layer, self.me], self.ps.at[p, slot, k],
                               self.pr.at[p, slot, k], at_place(z, px, py, c)))

    def start_plane(self):
        self.push(self.place[0], 0, self.ins)

    def relay(self, slot):
        z, x, y, c = self.place
        layer = (z + slot) % 4
        for p, (px, py) in enumerate(self.near):
            m = member_of(px, py, c)
            for k in self.arrays:
                part = self.outs[k].at[layer, m]
                remote(part, part, self.ps.at[p, slot, k], self.pr.at[p, slot, k],
                       at_place(z, px, py, c)).wait_recv()
        for k in self.arrays:
            rows = self.ins[k].shape[0] // 2
            for p, (px, py) in enumerate(self.near):
                part = self.outs[k].at[layer, member_of(px, py, c), p * rows : (p + 1) * rows]
                self.go(remote(part, part, self.qs.at[p, slot, k], self.qr.at[p, slot, k],
                               at_place(z, *self.near[1 - p], c)))

    def layer_step(self, o):
        z, x, y, c = self.place
        layer = (z + o) % 4
        parts = [self.outs[k].at[layer, self.me] for k in self.arrays]
        for k in self.arrays:
            remote(parts[k], parts[k], self.zs.at[o, k], self.zr.at[o, k],
                   at_place(layer, x, y, c)).wait_recv()
        self.push(layer, o, parts)

    def stage1(self):
        for copy in self.local:
            copy.wait()
        self.layer_step(1)
        self.relay(0)

    def stage2(self):
        self.layer_step(2)
        self.relay(1)

    def stage3(self):
        self.layer_step(3)
        self.relay(2)

    def across(self, slot, px, py):
        z, x, y, c = self.place
        m = member_of(px, py, c)
        for k in self.arrays:
            part = self.outs[k].at[:, m]
            self.go(remote(part, part, self.cs.at[slot, k], self.cr.at[slot, k],
                           at_place(z, x, y, 1 - c)))

    def stage4(self):
        z, x, y, c = self.place
        self.across(0, x, y)
        self.relay(3)
        self.across(1, 1 - x, y)
        self.across(2, x, 1 - y)

    def stage5(self):
        z, x, y, c = self.place
        far = member_of(1 - x, 1 - y, c)
        for slot in range(4):
            layer = (z + slot) % 4
            for k in self.arrays:
                rows = self.ins[k].shape[0] // 2
                for p in range(2):
                    part = self.outs[k].at[layer, far, p * rows : (p + 1) * rows]
                    remote(part, part, self.qs.at[p, slot, k], self.qr.at[p, slot, k],
                           at_place(z, *self.near[1 - p], c)).wait_recv()
        self.across(3, 1 - x, 1 - y)

    def stage6(self):
        z, x, y, c = self.place
        for slot, (px, py) in enumerate([(x, y), (1 - x, y), (x, 1 - y), (1 - x, 1 - y)]):
            m = member_of(px, py, 1 - c)
            for k in self.arrays:
                part = self.outs[k].at[:, m]
                remote(part, part, self.cs.at[slot, k], self.cr.at[slot, k],
                       at_place(z, x, y, 1 - c)).wait_recv()

    def advance(self, upto):
        while self.done < upto:
            self.stages[self.done]()
            self.done += 1

    def finish(self):
        self.advance(6)

    def drain(self):
        for copy in self.started:
            copy.wait_send()


def reduce_scratch(dims):
    half = [(rows // 2, lanes) for rows, lanes in dims]
    count = len(dims)
    return (
        [pltpu.VMEM((4, 4) + d, bf16) for d in dims]
        + [pltpu.VMEM((4, 4) + d, bf16) for d in dims]
        + [pltpu.VMEM((4, 4) + d, bf16) for d in half]
        + [pltpu.VMEM((2, 4) + d, bf16) for d in half]
        + [pltpu.VMEM((4,) + d, bf16) for d in dims]
        + [sems(4, count), sems(4, count), sems(4, count)]
        + [sems(3, count) for _ in range(4)]
        + [sems(4, count), sems(4, count)]
    )


def add_to(target, source):
    def step(i, _):
        target[i] = (target[i].astype(f32) + source[i].astype(f32)).astype(bf16)
        return 0

    lax.fori_loop(0, 4, step, 0)


class Reduce:
    def __init__(self, ins, outs, scratch):
        count = len(ins)
        self.ins, self.outs, self.arrays = ins, outs, range(count)
        self.own, self.across, self.one, self.two, self.deep = [
            scratch[i * count : (i + 1) * count] for i in range(5)
        ]
        (self.loc, self.cs, self.cr, self.xs, self.xr, self.ys, self.yr, self.zs, self.zr) = scratch[
            5 * count :
        ]
        self.place = z, x, y, c = place()
        self.mine, self.px, self.py, self.far = (x, y), (1 - x, y), (x, 1 - y), (1 - x, 1 - y)
        self.other = at_place(z, x, y, 1 - c)
        self.to_x, self.to_y = at_place(z, *self.px, c), at_place(z, *self.py, c)
        self.started = []
        self.done = 0
        self.stages = [self.stage1, self.stage2, self.stage3, self.stage4, self.stage5, self.stage6]

    def slot(self, p):
        return p[0] * 2 + p[1]

    def go(self, copy):
        copy.start()
        self.started.append(copy)

    def theirs(self, n, p, k):
        c = self.place[3]
        return remote(self.ins[k].at[:, member_of(*p, 1 - c)], self.across[k].at[self.slot(p)],
                      self.cs.at[n, k], self.cr.at[n, k], self.other)

    def ours(self, n, p, k):
        c = self.place[3]
        return pltpu.make_async_copy(self.ins[k].at[:, member_of(*p, c)],
                                     self.own[k].at[self.slot(p)], self.loc.at[n, k])

    def start(self):
        for n, p in enumerate((self.far, self.px, self.py, self.mine)):
            for k in self.arrays:
                self.go(self.theirs(n, p, k))
                self.ours(n, p, k).start()

    def landed(self, n, p):
        for k in self.arrays:
            self.ours(n, p, k).wait()
            self.theirs(n, p, k).wait_recv()
            add_to(self.own[k].at[self.slot(p)], self.across[k].at[self.slot(p)])

    def part(self, k, p, along_x):
        rows = self.ins[k].shape[2] // 2
        at = 0 if along_x else rows
        return self.own[k].at[self.slot(p), :, at : at + rows]

    def hop(self, k, p, along_x, i, target):
        source = self.part(k, p, along_x)
        if along_x:
            return remote(source, target, self.xs.at[i, k], self.xr.at[i, k], self.to_x)
        return remote(source, target, self.ys.at[i, k], self.yr.at[i, k], self.to_y)

    def first(self, k, p, along_x):
        i = 0 if p is self.far else 1
        return self.hop(k, p, along_x, i, self.one[k].at[2 * i + (0 if along_x else 1)])

    def second(self, k, along_x):
        if along_x:
            return remote(self.part(k, self.py, True), self.two[k].at[0], self.ys.at[2, k],
                          self.yr.at[2, k], self.to_y)
        return remote(self.part(k, self.px, False), self.two[k].at[1], self.xs.at[2, k],
                      self.xr.at[2, k], self.to_x)

    def stage1(self):
        self.landed(0, self.far)
        for k in self.arrays:
            self.go(self.first(k, self.far, True))
            self.go(self.first(k, self.far, False))

    def stage2(self):
        self.landed(1, self.px)
        for k in self.arrays:
            self.go(self.first(k, self.px, True))
        self.landed(2, self.py)
        for k in self.arrays:
            self.go(self.first(k, self.py, False))

    def stage3(self):
        self.landed(3, self.mine)
        for k in self.arrays:
            for along_x, p in ((True, self.py), (False, self.px)):
                self.first(k, self.far, along_x).wait_recv()
                add_to(self.part(k, p, along_x), self.one[k].at[0 if along_x else 1])
                self.go(self.second(k, along_x))

    def stage4(self):
        for k in self.arrays:
            for along_x, p in ((True, self.px), (False, self.py)):
                self.first(k, p, along_x).wait_recv()
                add_to(self.part(k, self.mine, along_x), self.one[k].at[2 if along_x else 3])

    def last(self, k, o):
        z, x, y, c = self.place
        layer = (z + o) % 4
        return remote(self.own[k].at[self.slot(self.mine), layer], self.deep[k].at[4 - o],
                      self.zs.at[o, k], self.zr.at[4 - o, k], at_place(layer, x, y, c))

    def stage5(self):
        for k in self.arrays:
            for along_x in (True, False):
                self.second(k, along_x).wait_recv()
                add_to(self.part(k, self.mine, along_x), self.two[k].at[0 if along_x else 1])
            for o in (1, 2, 3):
                self.go(self.last(k, o))

    def stage6(self):
        z, x, y, c = self.place
        for k in self.arrays:
            value = self.own[k][self.slot(self.mine), z].astype(f32)
            for o in (1, 2, 3):
                here = self.deep[k].at[o]
                remote(here, here, self.zs.at[o, k], self.zr.at[o, k],
                       at_place((z + o) % 4, x, y, c)).wait_recv()
                value = value + self.deep[k][o].astype(f32)
            self.outs[k][...] = value

    def advance(self, upto):
        while self.done < upto:
            self.stages[self.done]()
            self.done += 1

    def drain(self):
        for copy in self.started:
            copy.wait_send()


class Total:
    def __init__(self, small, out, scratch):
        self.small, self.out = small, out
        self.at_c, self.at_p, self.at_z, self.ss, self.rs = scratch
        self.place = z, x, y, c = place()
        self.plane = ((1 - x, y), (x, 1 - y), (1 - x, 1 - y))
        self.started = []

    def swap(self, buffer, index, n, m, target):
        here = buffer.at[index]
        copy = remote(here, here, self.ss.at[n], self.rs.at[m], target)
        copy.start()
        self.started.append(copy)

    def arrive(self, buffer, index, n, target):
        here = buffer.at[index]
        remote(here, here, self.ss.at[n], self.rs.at[n], target).wait_recv()

    def start(self):
        z, x, y, c = self.place
        self.at_c[c] = self.small[...]
        self.swap(self.at_c, c, 0, 0, at_place(z, x, y, 1 - c))

    def middle(self):
        z, x, y, c = self.place
        self.arrive(self.at_c, 1 - c, 0, at_place(z, x, y, 1 - c))
        self.at_p[x * 2 + y] = self.at_c[0] + self.at_c[1]
        for n, p in enumerate(self.plane):
            self.swap(self.at_p, x * 2 + y, 1 + n, 1 + n, at_place(z, *p, c))

    def late(self):
        z, x, y, c = self.place
        for n, p in enumerate(self.plane):
            self.arrive(self.at_p, p[0] * 2 + p[1], 1 + n, at_place(z, *p, c))
        self.at_z[z] = (self.at_p[0] + self.at_p[1]) + (self.at_p[2] + self.at_p[3])
        for o in (1, 2, 3):
            self.swap(self.at_z, z, 3 + o, 7 - o, at_place((z + o) % 4, x, y, c))

    def finish(self):
        z, x, y, c = self.place
        for o in (1, 2, 3):
            self.arrive(self.at_z, (z + o) % 4, 3 + o, at_place((z + o) % 4, x, y, c))
        self.out[...] = (self.at_z[0] + self.at_z[1]) + (self.at_z[2] + self.at_z[3])
        for copy in self.started:
            copy.wait_send()


def block_barrier():
    z, x, y, c = place()
    barrier = pltpu.get_barrier_semaphore()
    near = [at_place((z + o) % 4, x, y, c) for o in (1, 2, 3)]
    near += [at_place(z, 1 - x, y, c), at_place(z, x, 1 - y, c), at_place(z, 1 - x, 1 - y, c)]
    near += [at_place(z, x, y, 1 - c)]
    for target in near:
        pl.semaphore_signal(barrier, inc=1, device_id=target, device_id_type=MESH)
    pl.semaphore_wait(barrier, len(near))


def total_scratch(dims):
    return [
        pltpu.VMEM((2,) + dims, f32), pltpu.VMEM((4,) + dims, f32), pltpu.VMEM((4,) + dims, f32),
        sems(7), sems(7),
    ]


def reduce_kernel(count, *refs):
    ins, small = refs[:count], refs[count]
    outs, total = refs[count + 1 : 2 * count + 1], refs[2 * count + 1]
    scratch = refs[2 * count + 2 :]
    block_barrier()
    sums = Reduce(ins, outs, scratch[:-5])
    rest = Total(small, total, scratch[-5:])
    rest.start()
    sums.start()
    sums.advance(1)
    rest.middle()
    sums.advance(3)
    rest.late()
    sums.advance(6)
    rest.finish()
    sums.drain()


def reduce_gradients(parts, small, identity):
    count = len(parts)
    dims = [part.shape[2:] for part in parts]
    return pl.pallas_call(
        functools.partial(reduce_kernel, count),
        name="reduce_gradients",
        in_specs=[anywhere()] * count + [vmem()],
        out_specs=[vmem()] * (count + 1),
        out_shape=[shape(d, f32) for d in dims] + [shape(small.shape, f32)],
        scratch_shapes=reduce_scratch(dims) + total_scratch(small.shape),
        compiler_params=params(identity),
    )(*parts, small)


def norm_parts(values):
    average = jnp.mean(values, axis=-1, keepdims=True)
    centred = values - average
    variance = jnp.mean(centred * centred, axis=-1, keepdims=True)
    inverse = lax.rsqrt(variance + epsilon)
    return centred * inverse, inverse


def norm_backward(hat, inverse, gain, grad):
    scaled = grad * gain
    first = jnp.mean(scaled, axis=-1, keepdims=True)
    second = jnp.mean(scaled * hat, axis=-1, keepdims=True)
    return (scaled - first - hat * second) * inverse


def compact(j, rows, packed, places):
    for place, size in places:
        packed[place + size * j : place + size * j + size] = rows[:size]


def widen(pieces):
    total = pieces[-1]
    for piece in reversed(pieces[:-1]):
        blank = jnp.zeros((piece.shape[0], piece.shape[1] - total.shape[1]), f32)
        total = piece + jnp.concatenate([total, blank], axis=1)
    return total


def join_quad(quad, read):
    wide = jnp.concatenate(
        [swap_chunks(read(4 * quad + i), 4 * quad + i) for i in range(4)], axis=0
    )
    return swap_blocks(wide.T, quad)


def join_quads(read):
    pairs = []
    for half in range(2):
        pairs.append(
            jnp.concatenate([join_quad(quad, read) for quad in (2 * half, 2 * half + 1)], axis=1)
        )
    return jnp.concatenate(pairs, axis=1)


def unit_forward(query, key, out):
    lane = lax.broadcasted_iota(jnp.int32, (256, LANES), 1)
    count = len(query)
    scores = [matmul(query[i](), key, NT) for i in range(count)]
    for i in range(count):
        top = jnp.max(scores[i], axis=1, keepdims=True) * scale2
        prob = jnp.exp2(scores[i] * scale2 - top).astype(bf16)
        value = jnp.where(lane == FLAG + 8, top, matmul(prob, key))
        out[i](value.T[HD : HD + 64])


def forward_kernel(grp, slides, gather, *refs):
    refs = list(refs)
    take = lambda n: [refs.pop(0) for _ in range(n)]
    tokens, coordinates, frequency, gain, shift, flags_ref, bias = take(7)
    shards = take(4) if gather else None
    (weight_in,) = (None,) if gather else take(1)
    base, msg, q_ref, kv_ref, kv8, kv16, stat, merged = take(8)
    gathered = take(4) if gather else None
    weight = gathered[0] if gather else weight_in
    send, osend, orecv, acc, qc, kvc, tok_sem, ss, rs, os_, or_, ds, dr = take(13)
    spot = Spot(grp)
    joined = spot.greet()
    loads = [
        pltpu.make_async_copy(
            tokens.at[:, order[b]], base.at[BLOCK * b : BLOCK * b + BLOCK], tok_sem.at[b]
        )
        for b in range(16)
    ]
    for copy in loads:
        copy.start()
    if gather:
        first = Gather(shards[:1], gathered[:1], take(9))
        rest = Gather(shards[1:], gathered[1:], take(9))
        joined()
        first.start_layers()
        first.start_plane()
        rest.start_layers()
    lane = lax.broadcasted_iota(jnp.int32, (512, 384), 1)
    angle = jnp.where(lane < 192, coordinates[:, 0:1], coordinates[:, 1:2]) * frequency[...]
    sine, cosine = jnp.sin(angle), jnp.cos(angle)
    table = jnp.concatenate(
        [
            jnp.concatenate([sine[:, :192], cosine[:, :192]], axis=1),
            jnp.concatenate([sine[:, 192:], cosine[:, 192:]], axis=1),
        ],
        axis=1,
    )
    for copy in loads:
        copy.wait()
    base[...] = base[...] + table
    hat, _ = norm_parts(base[...])
    normed = (hat * gain[...] + shift[...]).astype(bf16)
    if gather:
        first.finish()
    else:
        joined()
    plane = [Exchange(spot, send.at[i], msg.at[i], ss.at[i], rs.at[i]) for i in range(2)]
    for quad in range(4):
        part = matmul(normed, pick(weight, quad)) + bias[quad]
        wide = swap_blocks(part.astype(bf16), quad).T
        flags = flags_ref[...]
        flags = jnp.concatenate(
            [flags[:, BLOCK * (b ^ block_swap(quad)) :][:, :BLOCK] for b in range(16)], axis=1
        ).astype(bf16)
        for inner in (0, 2, 1, 3):
            head = 4 * quad + inner
            owner, i = head // 2, head % 2
            own = swap_chunks(wide[144 * inner : 144 * inner + 144], head)
            send[i, owner, :96] = own[48:]
            send[i, owner, 96:112] = swap_chunks(flags, head)
            send[i, owner, 112:] = own[:48]
            if i == 0:
                plane[0].send(owner)
    for owner in range(GROUP):
        plane[1].send(owner)
    row = lax.broadcasted_iota(jnp.int32, (16, 512), 0)
    deeps = []
    results = [Exchange(spot, osend.at[i], orecv.at[i], os_.at[i], or_.at[i]) for i in range(2)]
    if gather:
        rest.start_plane()
    for i in range(2):
        q, kv = q_ref.at[i], kv_ref.at[i]
        for j in range(GROUP):
            plane[i].wait(j)
            block = msg[i, j]
            key_part = jnp.concatenate([block[:112], jnp.zeros((16, 512), bf16)], axis=0).T
            flags = block[96:112].astype(f32)
            chosen = jnp.where(
                row == 0, 1.0, jnp.where((row <= slides) & (flags == 0.0), 1.0, 0.0)
            )
            query_part = jnp.concatenate(
                [block[112:], jnp.zeros((HD, 512), bf16), chosen.astype(bf16),
                 jnp.zeros((16, 512), bf16)],
                axis=0,
            ).T
            kv[512 * j : 512 * j + 512] = key_part
            q[512 * j : 512 * j + 512] = query_part
            compact(j, query_part, qc, ((0, 256), (2048, 128), (3072, 64), (3584, 32)))
            compact(j, key_part, kvc, ((0, 256), (2048, 128)))
            kv8[spot.half, i, 64 * j : 64 * j + 64] = key_part[:64]
            kv16[spot.layer, i, 32 * j : 32 * j + 32] = key_part[:32]
        own8, own16 = kv8.at[spot.half, i], kv16.at[spot.layer, i]
        deep = Deep(
            spot, (own8, own8, kv8.at[1 - spot.half, i]),
            lambda o, other: (own16, own16, kv16.at[other, i]), ds.at[i], dr.at[i],
        )
        deep.start()
        deeps.append(deep)
        if gather:
            rest.advance(1 + 2 * i)

        def unit(source, q_from, keys, k_from, out_from, count):
            def reader(n):
                return lambda: source[pl.ds(q_from + 256 * n, 256)]

            def writer(n):
                def save(value):
                    acc[:, pl.ds(out_from + 256 * n, 256)] = value

                return save

            unit_forward(
                [reader(n) for n in range(count)], keys[pl.ds(k_from, 1024)],
                [writer(n) for n in range(count)],
            )

        def early(u, _):
            at = pl.multiple_of(u * 1024, 1024)
            unit(q, at, kv, at, at, 4)
            return 0

        lax.fori_loop(0, 4, early, 0)
        if gather:
            rest.advance(2 + 2 * i)

        def late(u, _):
            at = pl.multiple_of(u * 1024, 1024)
            unit(qc, at, kvc, at, pl.multiple_of(at + 4096, 1024), 4)
            return 0

        lax.fori_loop(0, 3, late, 0)
        deep.wait()
        for n in range(2):
            kvc[3072 + 512 * n : 3584 + 512 * n] = kv8[n, i]
        for n in range(4):
            kvc[4096 + 256 * n : 4352 + 256 * n] = kv16[n, i]
        unit(qc, 3072, kvc, 3072, 7168, 2)
        unit(qc, 3584, kvc, 4096, 7680, 1)
        place = lax.broadcasted_iota(jnp.int32, (1, 512), 1)
        uses = jnp.where(place < 32, 5.0, jnp.where(place < 64, 4.0, jnp.where(
            place < 128, 3.0, jnp.where(place < 256, 2.0, 1.0))))
        for j in range(GROUP):
            key = msg[i, j, :HD].astype(f32)
            value = msg[i, j, HD : 2 * HD].astype(f32)
            query = msg[i, j, 112:].astype(f32)
            dropped = msg[i, j, FLAG : FLAG + 1].astype(f32) != 0.0
            own = jnp.where(dropped, column_sum(query * key) * scale2 + jnp.log2(uses), -BIG)
            pieces = [
                acc[:, q_at[r] + (512 >> r) * j : q_at[r] + (512 >> r) * (j + 1)] for r in range(5)
            ]
            top = own
            tops = [piece[HD + 8 : HD + 9] for piece in pieces]
            for item in tops:
                spread = item
                if spread.shape[1] < 512:
                    blank = jnp.full((1, 512 - spread.shape[1]), -BIG, f32)
                    spread = jnp.concatenate([spread, blank], axis=1)
                top = jnp.maximum(top, spread)
            scaled = [
                piece[: HD + 8] * jnp.exp2(item - top[:, : item.shape[1]])
                for piece, item in zip(pieces, tops)
            ]
            mix = widen(scaled)
            weight_own = jnp.exp2(own - top)
            total = mix[HD + 1 + slides : HD + 2 + slides] + weight_own
            result = (mix[:HD] + weight_own * value) / total
            stat[i, j, :HD] = result
            stat[i, j, HD : HD + 8] = jnp.broadcast_to(top + jnp.log2(total), (8, 512))
            osend[i, j] = result.astype(bf16)
            results[i].send(j)
    if gather:
        rest.advance(5)
    for i in range(2):
        for j in range(GROUP):
            results[i].wait(j)
    merged[...] = join_quads(lambda h: orecv[h % 2, h // 2])
    if gather:
        rest.finish()
        first.drain()
        rest.drain()
    for item in plane + deeps + results:
        item.drain()


def attention_forward(grp, slides, gather, inputs, weights):
    out_shape = [
        shape((512, 768), f32),
        shape((2, GROUP, MSG, 512), bf16),
        shape((2, 4096, LANES), bf16),
        shape((2, 4096, LANES), bf16),
        shape((2, 2, 512, LANES), bf16),
        shape((4, 2, 256, LANES), bf16),
        shape((2, GROUP, 56, 512), f32),
        shape((512, 768), bf16),
    ]
    out_specs = [vmem()] * 8
    in_specs = [anywhere()] + [vmem()] * 6
    extra = []
    if gather:
        in_specs += [anywhere()] * 4
        out_shape += [shape((4, GROUP) + w.shape, bf16) for w in weights]
        out_specs += [vmem()] + [anywhere()] * 3
        extra = gather_sems(1) + gather_sems(3)
    else:
        in_specs += [vmem()]
    return pl.pallas_call(
        functools.partial(forward_kernel, grp, slides, gather),
        name="attention_forward",
        in_specs=in_specs,
        out_specs=out_specs,
        out_shape=out_shape,
        scratch_shapes=[
            pltpu.VMEM((2, GROUP, MSG, 512), bf16),
            pltpu.VMEM((2, GROUP, HD, 512), bf16),
            pltpu.VMEM((2, GROUP, HD, 512), bf16),
            pltpu.VMEM((64, q_all), f32),
            pltpu.VMEM((q_all - 4096, LANES), bf16),
            pltpu.VMEM((k_all - 4096, LANES), bf16),
            sems(16),
            sems(2, GROUP), sems(2, GROUP), sems(2, GROUP), sems(2, GROUP), sems(2, 4), sems(2, 4),
        ] + extra,
        compiler_params=params(1),
    )(*inputs, *weights)


def dense_kernel(
    merged, base, cot, wo, wi, wt, out_bias, gain, shift, in_bias, last_bias,
    out, grad_middle, grad_merged, wo_grad, wi_grad, wt_grad, small, small_in,
    full, middle, hat, low, low_t, cot_low, cot_t, grad_low,
):
    for g in range(0, 4, 2):
        pair = [pick(wo, g + i) for i in range(2)]
        full[:, 192 * g : 192 * g + 384] = jnp.concatenate(pair, axis=1)
    middle[...] = base[...] + matmul(merged[...], full[...]) + out_bias[...]
    normal, inverse = norm_parts(middle[...])
    hat[...] = normal
    low[...] = (normal * gain[...] + shift[...]).astype(bf16)
    low_t[...] = low[...].T
    cot_low[...] = cot[...].astype(bf16)
    cot_t[...] = cot_low[...].T
    out[...] = middle[...] + last_bias[...]
    small[0:1] = column_sum(cot_low[...].astype(f32))
    grad_middle[...] = jnp.zeros((512, 768), f32)

    def chunk(g, _):
        weight = pick(wi, g)
        inner = matmul(low[...], weight) + in_bias[g]
        phi = 0.5 * (1.0 + lax.erf(inner * 0.7071067811865476))
        active = (inner * phi).astype(bf16)
        slope = phi + inner * jnp.exp(-0.5 * inner * inner) * 0.3989422804014327
        for x in range(2):
            part = wt[g, 4 * x : 4 * x + 4].reshape(768, 384)
            now = active[:, 384 * x : 384 * x + 384]
            out[...] += matmul(now, part, NT)
            wt_grad[g, 4 * x : 4 * x + 4] = (
                matmul(cot_t[...], now).astype(bf16).reshape(4, 192, 384)
            )
            back = matmul(cot_low[...], part)
            grad_low[:, 384 * x : 384 * x + 384] = (
                back * slope[:, 384 * x : 384 * x + 384]
            ).astype(bf16)
        small_in[g] = column_sum(grad_low[...].astype(f32))
        put(wi_grad, g, matmul(low_t[...], grad_low[...]).astype(bf16))
        grad_middle[...] += matmul(grad_low[...], weight, NT)
        return 0

    lax.fori_loop(0, 4, chunk, 0)
    grad = grad_middle[...]
    small[1:2] = column_sum(grad * hat[...])
    small[2:3] = column_sum(grad)
    grad = cot[...] + norm_backward(hat[...], inverse, gain[...], grad)
    grad_middle[...] = grad
    attended = grad.astype(bf16)
    small[3:4] = column_sum(attended.astype(f32))
    small[4:8] = jnp.zeros((4, 768), f32)
    grads = matmul(merged[...].T, attended).astype(bf16)
    for g in range(4):
        put(wo_grad, g, grads[:, 192 * g : 192 * g + 192])
    grad_merged[...] = matmul(attended, full[...], NT).astype(bf16)


def dense(merged, base, cot, wo, wi, wt, out_bias, gain, shift, in_bias, last_bias):
    rows = (512, 768)
    return pl.pallas_call(
        dense_kernel,
        name="dense",
        in_specs=[vmem()] * 11,
        out_specs=[vmem()] * 8,
        out_shape=[
            shape(rows, f32), shape(rows, f32), shape(rows, bf16),
            shape((4, GROUP, 96, 192), bf16), shape((4, GROUP, 96, 768), bf16),
            shape((4, GROUP, 192, 384), bf16), shape((8, 768), f32), shape((4, 1, 768), f32),
        ],
        scratch_shapes=[
            pltpu.VMEM((768, 768), bf16), pltpu.VMEM(rows, f32), pltpu.VMEM(rows, f32),
            pltpu.VMEM(rows, bf16), pltpu.VMEM((768, 512), bf16), pltpu.VMEM(rows, bf16),
            pltpu.VMEM((768, 512), bf16), pltpu.VMEM(rows, bf16),
        ],
        compiler_params=params(),
    )(merged, base, cot, wo, wi, wt, out_bias, gain, shift, in_bias, last_bias)


def final_kernel(
    base, grad_middle, d0, d1, d2, d3, weight, gain, shift, token_grad, grads_out, small,
):
    hat, inverse = norm_parts(base[...])
    low_t = (hat * gain[...] + shift[...]).astype(bf16).T
    grad = jnp.zeros((512, 768), f32)
    small[...] = jnp.zeros((8, 768), f32)
    for quad, part in enumerate((d0, d1, d2, d3)):
        now = part[...]
        put(grads_out, quad, matmul(low_t, now).astype(bf16))
        grad = grad + matmul(now, pick(weight, quad), NT)
    small[0:1] = column_sum(grad * hat)
    small[1:2] = column_sum(grad)
    token_grad[...] = grad_middle[...] + norm_backward(hat, inverse, gain[...], grad)


def final(base, grad_middle, quads, weight, gain, shift):
    rows = (512, 768)
    return pl.pallas_call(
        final_kernel,
        name="input_gradients",
        in_specs=[vmem()] * 9,
        out_specs=[vmem()] * 3,
        out_shape=[shape(rows, f32), shape((4, GROUP, 96, 576), bf16), shape((8, 768), f32)],
        compiler_params=params(),
    )(base, grad_middle, *quads, weight, gain, shift)


def backward_kernel(grp, reduce, *refs):
    refs = list(refs)
    take = lambda n: [refs.pop(0) for _ in range(n)]
    gm, q_ref, kv_ref, kv8, kv16, msg, stat = take(7)
    parts = take(3) if reduce else None
    outs, sums_ref = take(4), take(1)[0]
    reduced = take(3) if reduce else None
    (gsend, grecv, rsend, rrecv, got8, got16, send8, send16, qc, kvc, dor, kt, ld, dkv, dqt,
     gs, gr, ss, rs, ds, dr) = take(21)
    spot = Spot(grp)
    joined = spot.greet()
    shares = [Exchange(spot, gsend.at[i], grecv.at[i], gs.at[i], gr.at[i]) for i in range(2)]
    backs = [Exchange(spot, rsend.at[i], rrecv.at[i], ss.at[i], rs.at[i]) for i in range(2)]
    sums = Reduce(parts, reduced, refs) if reduce else None
    for quad in range(4):
        wide = swap_blocks(gm[:, 192 * quad : 192 * quad + 192], quad).T
        for inner in (0, 2, 1, 3):
            head = 4 * quad + inner
            i = head % 2
            gsend[i, head // 2] = swap_chunks(wide[HD * inner : HD * inner + HD], head)
            if quad == 0 and inner == 0:
                joined()
            if i == 0:
                shares[0].send(head // 2)
    for j in range(GROUP):
        shares[1].send(j)
    if reduce:
        sums.start()
    row = lax.broadcasted_iota(jnp.int32, (96, 1), 0)
    factor = jnp.where(row < HD, scale, 1.0)
    deeps = []
    for i in range(2):
        q, kv = q_ref.at[i], kv_ref.at[i]
        for n in range(2):
            kvc[3072 + 512 * n : 3584 + 512 * n] = kv8[n, i]
        for n in range(4):
            kvc[4096 + 256 * n : 4352 + 256 * n] = kv16[n, i]
        for n in range(2):
            kt[7 + n] = kvc[3072 + 1024 * n : 4096 + 1024 * n].T[:HD]
        rows = []
        for j in range(GROUP):
            compact(j, q[512 * j : 512 * j + 512], qc, ((0, 256), (2048, 128), (3072, 64), (3584, 32)))
            compact(j, kv[512 * j : 512 * j + 512], kvc, ((0, 256), (2048, 128)))
            key = msg[i, j, :HD]
            kt[j // 2, :, 512 * (j % 2) : 512 * (j % 2) + 512] = key
            kt[4 + j // 4, :, 256 * (j % 4) : 256 * (j % 4) + 256] = key[:, :256]
            kt[6, :, 128 * j : 128 * j + 128] = key[:, :128]
        for j in range(GROUP):
            shares[i].wait(j)
            grad = grecv[i, j]
            delta = column_sum(grad.astype(f32) * stat[i, j, :HD])
            both = jnp.concatenate(
                [stat[i, j, HD : HD + 1], delta, jnp.zeros((6, 512), f32)], axis=0
            )
            rows.append(both)
            ld[:, 512 * j : 512 * j + 512] = both
            ld[:, 4096 + 256 * j : 4352 + 256 * j] = both[:, :256]
            ld[:, 6144 + 128 * j : 6272 + 128 * j] = both[:, :128]
            tall = jnp.concatenate(
                [jnp.zeros((HD, 512), bf16), grad, jnp.zeros((32, 512), bf16)], axis=0
            ).T
            for r, at in enumerate(q_at):
                size = 512 >> r
                dor[at + size * j : at + size * j + size] = tall[:size]
        ld[:, 7168:7680] = jnp.concatenate([both[:, :64] for both in rows], axis=1)
        ld[:, 7680:7936] = jnp.concatenate([both[:, :32] for both in rows], axis=1)

        def unit(source, q_from, keys, k_from, at, seg, count):
            width = 256 * count
            query = source[pl.ds(q_from, width)]
            grad = dor[pl.ds(at, width)]
            total = ld[0:1, pl.ds(at, width)]
            delta = ld[1:2, pl.ds(at, width)]
            sides = jnp.concatenate([grad, query], axis=0)
            size = 256
            dq = jnp.zeros((HD, width), f32)
            for c in range(1024 // size):
                key = keys[pl.ds(k_from + size * c, size)]
                prob = jnp.exp2(matmul(key, query, NT) * scale2 - total)
                slope = (prob * (matmul(key, grad, NT) - delta)).astype(bf16)
                both = jnp.concatenate([prob.astype(bf16), slope], axis=1)
                dkv[pl.ds(seg * 1024 + size * c, size)] = matmul(both, sides)
                dq = dq + matmul(kt[seg, :, size * c : size * c + size], slope)
            dqt[:, pl.ds(at, width)] = dq

        unit(qc, 3072, kvc, 3072, 7168, 7, 2)
        unit(qc, 3584, kvc, 4096, 7680, 8, 1)
        for n in range(2):
            send8[n, i] = dkv[7168 + 512 * n : 7680 + 512 * n].astype(bf16)
        for n in range(4):
            send16[n, i] = dkv[8192 + 256 * n : 8448 + 256 * n].astype(bf16)
        deep = Deep(
            spot, (send8.at[1 - spot.half, i], got8.at[i], got8.at[i]),
            lambda o, other: (send16.at[other, i], got16.at[4 - o, i], got16.at[o, i]),
            ds.at[i], dr.at[i],
        )
        deep.start()
        deeps.append(deep)
        if reduce:
            sums.advance(1 + 2 * i)

        def early(u, _):
            at = pl.multiple_of(u * 1024, 1024)
            unit(q, at, kv, at, at, u, 4)
            return 0

        lax.fori_loop(0, 4, early, 0)
        if reduce:
            sums.advance(2 + 2 * i)

        def late(u, _):
            at = pl.multiple_of(u * 1024, 1024)
            unit(qc, at, kvc, at, pl.multiple_of(at + 4096, 1024), u + 4, 4)
            return 0

        lax.fori_loop(0, 3, late, 0)
        deep.wait()
        spot_lane = lax.broadcasted_iota(jnp.int32, (1, 512), 1)
        uses = jnp.where(spot_lane < 32, 5.0, jnp.where(spot_lane < 64, 4.0, jnp.where(
            spot_lane < 128, 3.0, jnp.where(spot_lane < 256, 2.0, 1.0))))
        for j in range(GROUP):
            tall = dkv[512 * j : 512 * j + 512]
            eight = send8[spot.half, i, 64 * j : 64 * j + 64].astype(f32) + got8[
                i, 64 * j : 64 * j + 64
            ].astype(f32)
            sixteen = send16[spot.layer, i, 32 * j : 32 * j + 32].astype(f32)
            for o in range(1, 4):
                sixteen = sixteen + got16[o, i, 32 * j : 32 * j + 32].astype(f32)
            second = dkv[4096 + 256 * j : 4352 + 256 * j]
            third = dkv[6144 + 128 * j : 6272 + 128 * j]
            fourth = third[:64] + eight
            fourth = jnp.concatenate([fourth[:32] + sixteen, fourth[32:]], axis=0)
            third = jnp.concatenate([fourth, third[64:]], axis=0)
            second = jnp.concatenate([second[:128] + third, second[128:]], axis=0)
            wide = jnp.concatenate([tall[:256] + second, tall[256:]], axis=0).T
            key = msg[i, j, :HD].astype(f32)
            value = msg[i, j, HD : 2 * HD].astype(f32)
            query = msg[i, j, 112:].astype(f32)
            grad = grecv[i, j].astype(f32)
            total = ld[0:1, 512 * j : 512 * j + 512]
            delta = ld[1:2, 512 * j : 512 * j + 512]
            dropped = msg[i, j, FLAG : FLAG + 1].astype(f32) != 0.0
            dots = column_sum(query * key) * scale2 - total
            prob = jnp.where(dropped, uses * jnp.exp2(jnp.where(dropped, dots, 0.0)), 0.0)
            slope = prob * (column_sum(grad * value) - delta)
            dq = widen([dqt[:, at + (512 >> r) * j : at + (512 >> r) * (j + 1)]
                        for r, at in enumerate(q_at)])
            rsend[i, j, :HD] = ((wide[:HD] + slope * query) * scale).astype(bf16)
            rsend[i, j, HD : 2 * HD] = (wide[HD : 2 * HD] + prob * grad).astype(bf16)
            rsend[i, j, 2 * HD :] = ((dq + slope * key) * scale).astype(bf16)
            backs[i].send(j)
    if reduce:
        sums.advance(5)
    for i in range(2):
        for j in range(GROUP):
            backs[i].wait(j)
    for quad, out in enumerate(outs):

        def read(head):
            block = rrecv[head % 2, head // 2]
            return jnp.concatenate([block[2 * HD :], block[: 2 * HD]], axis=0)

        result = join_quad(quad, read)
        out[...] = result
        sums_ref[quad] = column_sum(result.astype(f32))
    if reduce:
        sums.advance(6)
        sums.drain()
    for item in shares + backs + deeps:
        item.drain()


def attention_backward(grp, reduce, inputs, parts):
    out_shape = [shape((512, 576), bf16)] * 4 + [shape((4, 1, 576), f32)]
    extra = []
    if reduce:
        dims = [part.shape[2:] for part in parts]
        out_shape += [shape(d, f32) for d in dims]
        extra = reduce_scratch(dims)
    return pl.pallas_call(
        functools.partial(backward_kernel, grp, reduce),
        name="attention_backward",
        in_specs=[vmem()] * 7 + [anywhere()] * len(parts),
        out_specs=[vmem()] * len(out_shape),
        out_shape=out_shape,
        scratch_shapes=[
            pltpu.VMEM((2, GROUP, HD, 512), bf16),
            pltpu.VMEM((2, GROUP, HD, 512), bf16),
            pltpu.VMEM((2, GROUP, 3 * HD, 512), bf16),
            pltpu.VMEM((2, GROUP, 3 * HD, 512), bf16),
            pltpu.VMEM((2, 512, LANES), bf16),
            pltpu.VMEM((4, 2, 256, LANES), bf16),
            pltpu.VMEM((2, 2, 512, LANES), bf16),
            pltpu.VMEM((4, 2, 256, LANES), bf16),
            pltpu.VMEM((q_all - 4096, LANES), bf16),
            pltpu.VMEM((k_all - 4096, LANES), bf16),
            pltpu.VMEM((q_all, LANES), bf16),
            pltpu.VMEM((9, HD, 1024), bf16),
            pltpu.VMEM((8, q_all), f32),
            pltpu.VMEM((k_all, LANES), f32),
            pltpu.VMEM((HD, q_all), f32),
            sems(2, GROUP), sems(2, GROUP), sems(2, GROUP), sems(2, GROUP), sems(2, 4), sems(2, 4),
        ] + extra,
        compiler_params=params(2),
    )(*inputs, *parts)


def all_weights(parts, seq, grp):
    gathered = []
    for n, part in enumerate(parts):
        whole = lax.all_gather(lax.all_gather(part, "grp"), "seq")
        lead = whole.shape[0] // 8
        whole = whole.reshape((8, lead) + whole.shape[1:])
        if n == 3:
            whole = whole.transpose(0, 2, 3, 1, 4)
            whole = whole.reshape(4, GROUP, part.shape[0], lead * part.shape[1])
        else:
            whole = whole.transpose(0, 2, 1, 3, 4)
            whole = whole.reshape(4, GROUP, lead * part.shape[0], part.shape[1])
        gathered.append(whole)
    return gathered


def sum_gradients(parts, small, seq, grp):
    lead = seq // 8
    sums = []
    for n, part in enumerate(parts):
        height, lanes = part.shape[2:]
        whole = part.reshape(8, grp, height, lanes)
        if n == 3:
            whole = whole.reshape(8, grp, height, lead, lanes // lead).transpose(0, 3, 1, 2, 4)
        else:
            whole = whole.reshape(8, grp, lead, height // lead, lanes).transpose(0, 2, 1, 3, 4)
        whole = whole.reshape((seq, grp) + whole.shape[3:]).astype(f32)
        whole = lax.psum_scatter(whole, "seq", scatter_dimension=0)
        sums.append(lax.psum_scatter(whole, "grp", scatter_dimension=0))
    return sums + [lax.psum(small, ("seq", "grp"))]


def in_order(rows):
    split = rows.reshape((BLOCK, 16) + rows.shape[1:])
    return jnp.stack([split[:, b] for b in order]).reshape(rows.shape)


def back_order(rows):
    split = rows.reshape((16, BLOCK) + rows.shape[1:])
    return jnp.stack([split[b] for b in order], axis=1).reshape(rows.shape)


def body(
    tokens,
    coordinates,
    lengths,
    valid,
    first_gain,
    first_shift,
    query_weight,
    query_bias,
    key_weight,
    value_weight,
    value_bias,
    output_weight,
    output_bias,
    second_gain,
    second_shift,
    inner_weight,
    inner_bias,
    outer_weight,
    outer_bias,
    cotangent,
):
    rows, width = tokens.shape
    grp = lax.axis_size("grp")
    seq = lax.axis_size("seq")
    near = (seq, grp) == (8, 4)
    slides = lengths.shape[0]
    linear = lax.axis_index("seq") * grp + lax.axis_index("grp")
    shard = query_weight.shape[0]
    heads = [w.reshape(shard, 4, 1, HD) for w in (query_weight, key_weight, value_weight)]
    parts = [
        jnp.concatenate(heads, axis=2).reshape(shard, 576),
        output_weight,
        inner_weight,
        outer_weight.T,
    ]
    joint_bias = jnp.stack(
        [b.reshape(4, 4, HD) for b in (query_bias, jnp.zeros_like(query_bias), value_bias)], axis=2
    ).reshape(4, 1, 576)
    cotangent = in_order(cotangent)
    places = in_order(linear * rows + jnp.arange(rows, dtype=jnp.int32))
    keep = in_order(valid)
    slide = jnp.sum((places[:, None] >= jnp.cumsum(lengths)).astype(jnp.int32), axis=-1)
    apart = slide[None, :] != jnp.arange(slides, dtype=jnp.int32)[:, None]
    flags = jnp.concatenate(
        [
            jnp.where(keep == 1, 0.0, -BIG)[None, :],
            jnp.where(apart, -BIG, 0.0),
            jnp.ones((1, rows), f32),
            jnp.zeros((14 - slides, rows), f32),
        ],
        axis=0,
    )
    frequency = jnp.exp(jnp.arange(192, dtype=jnp.float32) * (-math.log(10000.0) / 192))
    row = lambda v: v.reshape(1, -1)
    inputs = [
        tokens.reshape(BLOCK, 16, width), in_order(coordinates).astype(f32),
        row(jnp.concatenate([frequency, frequency])), row(first_gain), row(first_shift), flags,
        joint_bias,
    ]
    if near:
        results = attention_forward(grp, slides, True, inputs, parts)
        joint_weight, wo, wi, wt = results[8:]
    else:
        joint_weight, wo, wi, wt = all_weights(parts, seq, grp)
        results = attention_forward(grp, slides, False, inputs, [joint_weight])
    base, msg, q_rows, kv_rows, kv8, kv16, stat, merged_low = results[:8]
    output, grad_middle, grad_merged, wo_grad, wi_grad, wt_grad, small, small_in = dense(
        merged_low, base, cotangent, wo, wi, wt, row(output_bias), row(second_gain),
        row(second_shift), inner_bias.reshape(4, 1, 768), row(outer_bias),
    )
    saved = [grad_merged, q_rows, kv_rows, kv8, kv16, msg, stat]
    late = [wo_grad, wi_grad, wt_grad]
    results = attention_backward(grp, near, saved, late if near else [])
    quads, sums = results[:4], results[4]
    token_grad, joint_grad, first_small = final(
        base, grad_middle, quads, joint_weight, row(first_gain), row(first_shift)
    )
    sums = sums.reshape(4, 4, 3, HD)
    vectors = [
        first_small[0], first_small[1], sums[:, :, 0].reshape(-1), sums[:, :, 2].reshape(-1),
        small[3], small[1], small[2], small_in.reshape(-1), small[0],
    ]
    sizes = [v.shape[0] for v in vectors]
    pack = jnp.concatenate(vectors).reshape(-1, LANES)
    if near:
        sum_output, sum_inner, sum_outer = results[5:]
        joint_sum, pack = reduce_gradients([joint_grad], pack, 3)
    else:
        joint_sum, sum_output, sum_inner, sum_outer, pack = sum_gradients(
            [joint_grad] + late, pack, seq, grp
        )
    joint_sum = joint_sum.reshape(shard, 4, 3, HD)
    sum_query, sum_key, sum_value = [joint_sum[:, :, i].reshape(shard, 192) for i in range(3)]
    sum_outer = sum_outer.T
    small = []
    pack = pack.reshape(-1)
    for size in sizes:
        small.append(pack[:size])
        pack = pack[size:]
    return (
        back_order(output),
        back_order(token_grad),
        small[0],
        small[1],
        sum_query,
        small[2],
        sum_key,
        sum_value,
        small[3],
        sum_output,
        small[4],
        small[5],
        small[6],
        sum_inner,
        small[7],
        sum_outer,
        small[8],
    )


def solution(mesh):
    placed = (
        P(("seq", "grp"), None),
        P(("seq", "grp"), None),
        P(),
        P(("seq", "grp")),
        P(),
        P(),
        P("seq", "grp"),
        P(),
        P("seq", "grp"),
        P("seq", "grp"),
        P(),
        P("seq", "grp"),
        P(),
        P(),
        P(),
        P("seq", "grp"),
        P(),
        P("seq", "grp"),
        P(),
        P(("seq", "grp"), None),
    )
    return jax.shard_map(
        body,
        mesh=mesh,
        in_specs=placed,
        out_specs=(
            P(("seq", "grp"), None),
            P(("seq", "grp"), None),
            P(),
            P(),
            P("seq", "grp"),
            P(),
            P("seq", "grp"),
            P("seq", "grp"),
            P(),
            P("seq", "grp"),
            P(),
            P(),
            P(),
            P("seq", "grp"),
            P(),
            P("seq", "grp"),
            P(),
        ),
        check_vma=False,
    )
```

```python
import functools
import math

import jax
import jax.numpy as jnp
from jax import lax
from jax.experimental import pallas as pl
from jax.experimental.pallas import tpu as pltpu
from jax.sharding import PartitionSpec as P

epsilon = 1e-05


NT = (((1,), (1,)), ((), ()))
NN = (((1,), (0,)), ((), ()))
f32 = jnp.float32
bf16 = jnp.bfloat16
BIG = 1e30
HD = 48
GROUP = 8
LANES = 128
BLOCK = 32
MSG = 160
FLAG = 2 * HD
MESH = pl.DeviceIdType.MESH
scale = HD ** (-0.5)
scale2 = scale * math.log2(math.e)
q_at = (0, 4096, 6144, 7168, 7680)
q_all = 7936
k_all = 9216


def reverse4(b):
    return (b & 1) * 8 + (b & 2) * 2 + (b & 4) // 2 + (b & 8) // 8


order = [reverse4(b) for b in range(16)]


def chunk_swap(head):
    return reverse4(head) >> 2


def block_swap(quad):
    return reverse4(4 * quad) & 3


def swap_blocks(rows, quad):
    return jnp.concatenate(
        [rows[BLOCK * (b ^ block_swap(quad)) :][:BLOCK] for b in range(16)], axis=0
    )


def swap_chunks(wide, head):
    return jnp.concatenate(
        [wide[:, LANES * (c ^ chunk_swap(head)) :][:, :LANES] for c in range(4)], axis=1
    )


def matmul(a, b, dims=NN):
    return lax.dot_general(a, b, dims, preferred_element_type=f32)


def column_sum(values):
    return jnp.sum(values, axis=0, keepdims=True)


def pick(ref, g):
    both = jnp.stack([ref[:, g], ref[:, g + 4]], axis=1)
    return both.reshape(768, ref.shape[3])


def put(ref, g, value):
    value = value.reshape(4, 2, 96, ref.shape[3])
    ref[:, g] = value[:, 0]
    ref[:, g + 4] = value[:, 1]


def vmem():
    return pl.BlockSpec(memory_space=pltpu.VMEM)


def anywhere():
    return pl.BlockSpec(memory_space=pl.ANY)


def sems(*dims):
    return pltpu.SemaphoreType.DMA(dims)


def params(identity=None):
    if identity is None:
        return pltpu.CompilerParams(vmem_limit_bytes=60 << 20)
    return pltpu.CompilerParams(
        vmem_limit_bytes=60 << 20, collective_id=identity, has_side_effects=True
    )


def shape(dims, dtype):
    return jax.ShapeDtypeStruct(dims, dtype)


def remote(src, dst, send_sem, recv_sem, target):
    return pltpu.make_async_remote_copy(
        src_ref=src, dst_ref=dst, send_sem=send_sem, recv_sem=recv_sem,
        device_id=target, device_id_type=MESH,
    )


class Spot:
    def __init__(self, grp):
        self.grp = grp
        self.linear = lax.axis_index("seq") * grp + lax.axis_index("grp")
        self.member = self.linear % GROUP
        self.base = self.linear - self.member
        self.layer = self.linear // GROUP % 4
        self.half = self.layer % 2

    def device(self, linear):
        return (linear // self.grp, linear % self.grp)

    def beside(self, j):
        return self.device(self.base + j)

    def over(self, layer):
        return self.device(self.linear + GROUP * (layer - self.layer))

    def pair(self):
        return self.device(self.linear + GROUP - 2 * GROUP * self.half)

    def greet(self):
        barrier = pltpu.get_barrier_semaphore()
        for j in range(GROUP):

            @pl.when(self.member != j)
            def _():
                pl.semaphore_signal(barrier, inc=1, device_id=self.beside(j), device_id_type=MESH)

        for o in range(1, 4):
            target = self.over((self.layer + o) % 4)
            pl.semaphore_signal(barrier, inc=1, device_id=target, device_id_type=MESH)
        return lambda: pl.semaphore_wait(barrier, GROUP + 2)


class Exchange:
    def __init__(self, spot, send, recv, send_sem, recv_sem):
        self.spot, self.send_ref, self.recv = spot, send, recv
        self.send_sem, self.recv_sem = send_sem, recv_sem

    def out(self, j):
        s = self.spot
        return remote(self.send_ref.at[j], self.recv.at[s.member], self.send_sem.at[j],
                      self.recv_sem.at[s.member], s.beside(j))

    def inner(self, j):
        return pltpu.make_async_copy(self.send_ref.at[j], self.recv.at[j], self.recv_sem.at[j])

    def choose(self, j, far, near):
        pl.when(self.spot.member != j)(far)
        pl.when(self.spot.member == j)(near)

    def send(self, j):
        self.choose(j, lambda: self.out(j).start(), lambda: self.inner(j).start())

    def wait(self, j):
        def far():
            remote(self.send_ref.at[j], self.recv.at[j], self.send_sem.at[j], self.recv_sem.at[j],
                   self.spot.beside(j)).wait_recv()

        self.choose(j, far, lambda: self.inner(j).wait())

    def drain(self):
        for j in range(GROUP):
            pl.when(self.spot.member != j)(lambda j=j: self.out(j).wait_send())


class Deep:
    def __init__(self, spot, eight, sixteen, send_sem, recv_sem):
        self.copies, self.waits = [], []
        s = spot
        for o in range(1, 4):
            other = (s.layer + o) % 4
            src, there, here = sixteen(o, other)
            self.copies.append(remote(src, there, send_sem.at[o], recv_sem.at[4 - o], s.over(other)))
            self.waits.append(remote(src, here, send_sem.at[o], recv_sem.at[o], s.over(other)))
        src, there, here = eight
        self.copies.append(remote(src, there, send_sem.at[0], recv_sem.at[0], s.pair()))
        self.waits.append(remote(src, here, send_sem.at[0], recv_sem.at[0], s.pair()))

    def start(self):
        for copy in self.copies:
            copy.start()

    def wait(self):
        for copy in self.waits:
            copy.wait_recv()

    def drain(self):
        for copy in self.copies:
            copy.wait_send()


def member_of(x, y, c):
    return x * 4 + y * 2 + c


def place():
    seq, col = lax.axis_index("seq"), lax.axis_index("grp")
    return seq // 2, seq % 2, col // 2, col % 2


def at_place(z, x, y, c):
    return (z * 2 + x, y * 2 + c)


def gather_sems(count):
    return [
        sems(count), sems(4, count), sems(4, count), sems(2, 4, count), sems(2, 4, count),
        sems(2, 4, count), sems(2, 4, count), sems(4, count), sems(4, count),
    ]


class Gather:
    def __init__(self, ins, outs, semaphores):
        self.ins, self.outs = ins, outs
        (self.loc, self.zs, self.zr, self.ps, self.pr,
         self.qs, self.qr, self.cs, self.cr) = semaphores
        self.place = z, x, y, c = place()
        self.me = member_of(x, y, c)
        self.arrays = range(len(ins))
        self.near = [(1 - x, y), (x, 1 - y)]
        self.started = []
        self.done = 0
        self.local = [
            pltpu.make_async_copy(ins[k], outs[k].at[z, self.me], self.loc.at[k])
            for k in self.arrays
        ]
        self.stages = [self.stage1, self.stage2, self.stage3, self.stage4, self.stage5, self.stage6]

    def go(self, copy):
        copy.start()
        self.started.append(copy)

    def start_layers(self):
        z, x, y, c = self.place
        for copy in self.local:
            copy.start()
        for o in (1, 2, 3):
            for k in self.arrays:
                self.go(remote(self.ins[k], self.outs[k].at[z, self.me], self.zs.at[o, k],
                               self.zr.at[4 - o, k], at_place((z + o) % 4, x, y, c)))

    def push(self, layer, slot, sources):
        z, x, y, c = self.place
        for p, (px, py) in enumerate(self.near):
            for k in self.arrays:
                self.go(remote(sources[k], self.outs[k].at[layer, self.me], self.ps.at[p, slot, k],
                               self.pr.at[p, slot, k], at_place(z, px, py, c)))

    def start_plane(self):
        self.push(self.place[0], 0, self.ins)

    def relay(self, slot):
        z, x, y, c = self.place
        layer = (z + slot) % 4
        for p, (px, py) in enumerate(self.near):
            m = member_of(px, py, c)
            for k in self.arrays:
                part = self.outs[k].at[layer, m]
                remote(part, part, self.ps.at[p, slot, k], self.pr.at[p, slot, k],
                       at_place(z, px, py, c)).wait_recv()
        for k in self.arrays:
            rows = self.ins[k].shape[0] // 2
            for p, (px, py) in enumerate(self.near):
                part = self.outs[k].at[layer, member_of(px, py, c), p * rows : (p + 1) * rows]
                self.go(remote(part, part, self.qs.at[p, slot, k], self.qr.at[p, slot, k],
                               at_place(z, *self.near[1 - p], c)))

    def layer_step(self, o):
        z, x, y, c = self.place
        layer = (z + o) % 4
        parts = [self.outs[k].at[layer, self.me] for k in self.arrays]
        for k in self.arrays:
            remote(parts[k], parts[k], self.zs.at[o, k], self.zr.at[o, k],
                   at_place(layer, x, y, c)).wait_recv()
        self.push(layer, o, parts)

    def stage1(self):
        for copy in self.local:
            copy.wait()
        self.layer_step(1)
        self.relay(0)

    def stage2(self):
        self.layer_step(2)
        self.relay(1)

    def stage3(self):
        self.layer_step(3)
        self.relay(2)

    def across(self, slot, px, py):
        z, x, y, c = self.place
        m = member_of(px, py, c)
        for k in self.arrays:
            part = self.outs[k].at[:, m]
            self.go(remote(part, part, self.cs.at[slot, k], self.cr.at[slot, k],
                           at_place(z, x, y, 1 - c)))

    def stage4(self):
        z, x, y, c = self.place
        self.across(0, x, y)
        self.relay(3)
        self.across(1, 1 - x, y)
        self.across(2, x, 1 - y)

    def stage5(self):
        z, x, y, c = self.place
        far = member_of(1 - x, 1 - y, c)
        for slot in range(4):
            layer = (z + slot) % 4
            for k in self.arrays:
                rows = self.ins[k].shape[0] // 2
                for p in range(2):
                    part = self.outs[k].at[layer, far, p * rows : (p + 1) * rows]
                    remote(part, part, self.qs.at[p, slot, k], self.qr.at[p, slot, k],
                           at_place(z, *self.near[1 - p], c)).wait_recv()
        self.across(3, 1 - x, 1 - y)

    def stage6(self):
        z, x, y, c = self.place
        for slot, (px, py) in enumerate([(x, y), (1 - x, y), (x, 1 - y), (1 - x, 1 - y)]):
            m = member_of(px, py, 1 - c)
            for k in self.arrays:
                part = self.outs[k].at[:, m]
                remote(part, part, self.cs.at[slot, k], self.cr.at[slot, k],
                       at_place(z, x, y, 1 - c)).wait_recv()

    def advance(self, upto):
        while self.done < upto:
            self.stages[self.done]()
            self.done += 1

    def finish(self):
        self.advance(6)

    def drain(self):
        for copy in self.started:
            copy.wait_send()


def gather_wide_sems():
    return [sems(1), sems(2), sems(2), sems(2), sems(2), sems(4, 4), sems(4, 4), sems(4, 4), sems(4, 4)]


class GatherWide:
    def __init__(self, source, out, semaphores):
        self.source, self.out = source, out
        (self.loc, self.ps, self.pr, self.qs, self.qr, self.zs, self.zr, self.cs, self.cr) = semaphores
        self.place = z, x, y, c = place()
        self.near = [(1 - x, y), (x, 1 - y)]
        self.spots = [(x, y), (1 - x, y), (x, 1 - y), (1 - x, 1 - y)]
        self.started = []
        self.done = 0
        self.stages = [self.stage1, self.stage2, self.stage3, self.stage4, self.stage5]

    def go(self, copy):
        copy.start()
        self.started.append(copy)

    def block(self, layer, p, c):
        return self.out.at[layer, member_of(*p, c)]

    def start(self):
        z, x, y, c = self.place
        self.local = pltpu.make_async_copy(self.source, self.block(z, (x, y), c), self.loc.at[0])
        self.local.start()
        for n, p in enumerate(self.near):
            self.go(remote(self.source, self.block(z, (x, y), c), self.ps.at[n], self.pr.at[n],
                           at_place(z, *p, c)))

    def up(self, slot):
        z, x, y, c = self.place
        part = self.block(z, self.spots[slot], c)
        for o in (1, 2, 3):
            self.go(remote(part, part, self.zs.at[o, slot], self.zr.at[4 - o, slot],
                           at_place((z + o) % 4, x, y, c)))

    def swap(self, o, slot):
        z, x, y, c = self.place
        part = self.block((z + o) % 4, self.spots[slot], c)
        self.go(remote(part, part, self.cs.at[o, slot], self.cr.at[o, slot],
                       at_place(z, x, y, 1 - c)))

    def stage1(self):
        z, x, y, c = self.place
        self.local.wait()
        self.up(0)
        self.swap(0, 0)
        rows = self.source.shape[0] // 2
        for n, p in enumerate(self.near):
            part = self.block(z, p, c)
            remote(part, part, self.ps.at[n], self.pr.at[n], at_place(z, *p, c)).wait_recv()
            part = self.out.at[z, member_of(*p, c), n * rows : (n + 1) * rows]
            self.go(remote(part, part, self.qs.at[n], self.qr.at[n],
                           at_place(z, *self.near[1 - n], c)))
            self.up(1 + n)
            self.swap(0, 1 + n)

    def stage2(self):
        z, x, y, c = self.place
        rows = self.source.shape[0] // 2
        for n in range(2):
            part = self.out.at[z, member_of(*self.spots[3], c), n * rows : (n + 1) * rows]
            remote(part, part, self.qs.at[n], self.qr.at[n],
                   at_place(z, *self.near[1 - n], c)).wait_recv()
        self.up(3)
        self.swap(0, 3)

    def arrive(self, slots):
        z, x, y, c = self.place
        for slot in slots:
            for o in (1, 2, 3):
                layer = (z + o) % 4
                part = self.block(layer, self.spots[slot], c)
                remote(part, part, self.zs.at[o, slot], self.zr.at[o, slot],
                       at_place(layer, x, y, c)).wait_recv()
                self.swap(o, slot)

    def stage3(self):
        self.arrive((0, 1))

    def stage4(self):
        self.arrive((2, 3))

    def stage5(self):
        z, x, y, c = self.place
        for o in range(4):
            for slot in range(4):
                part = self.block((z + o) % 4, self.spots[slot], 1 - c)
                remote(part, part, self.cs.at[o, slot], self.cr.at[o, slot],
                       at_place(z, x, y, 1 - c)).wait_recv()

    def advance(self, upto):
        while self.done < upto:
            self.stages[self.done]()
            self.done += 1

    def drain(self):
        for copy in self.started:
            copy.wait_send()


def reduce_scratch(dims):
    half = [(rows // 2, lanes) for rows, lanes in dims]
    count = len(dims)
    return (
        [pltpu.VMEM((4,) + d, bf16) for d in dims]
        + [pltpu.VMEM((4, 4) + d, bf16) for d in dims]
        + [pltpu.VMEM((4, 4) + d, bf16) for d in half]
        + [pltpu.VMEM((2, 4) + d, bf16) for d in half]
        + [pltpu.VMEM((4,) + d, bf16) for d in dims]
        + [sems(4, count), sems(4, count), sems(4, count)]
        + [sems(3, count) for _ in range(4)]
        + [sems(4, count), sems(4, count)]
    )


def add_to(target, source):
    def step(i, _):
        target[i] = (target[i].astype(f32) + source[i].astype(f32)).astype(bf16)
        return 0

    lax.fori_loop(0, 4, step, 0)


class Reduce:
    def __init__(self, ins, outs, scratch):
        count = len(ins)
        self.ins, self.outs, self.arrays = ins, outs, range(count)
        self.stage, self.across, self.one, self.two, self.deep = [
            scratch[i * count : (i + 1) * count] for i in range(5)
        ]
        (self.loc, self.cs, self.cr, self.xs, self.xr, self.ys, self.yr, self.zs, self.zr) = scratch[
            5 * count :
        ]
        self.place = z, x, y, c = place()
        self.mine, self.px, self.py, self.far = (x, y), (1 - x, y), (x, 1 - y), (1 - x, 1 - y)
        self.other = at_place(z, x, y, 1 - c)
        self.to_x, self.to_y = at_place(z, *self.px, c), at_place(z, *self.py, c)
        self.started = []
        self.done = 0
        self.stages = [self.stage1, self.stage2, self.stage3, self.stage4, self.stage5, self.stage6]

    def slot(self, p):
        return p[0] * 2 + p[1]

    def held(self, k, p):
        if self.stage[k] is None:
            return self.ins[k].at[:, member_of(*p, self.place[3])]
        return self.across[k].at[self.slot(p)]

    def go(self, copy):
        copy.start()
        self.started.append(copy)

    def theirs(self, n, p, k):
        c = self.place[3]
        return remote(self.ins[k].at[:, member_of(*p, 1 - c)], self.across[k].at[self.slot(p)],
                      self.cs.at[n, k], self.cr.at[n, k], self.other)

    def ours(self, n, p, k):
        c = self.place[3]
        return pltpu.make_async_copy(self.ins[k].at[:, member_of(*p, c)],
                                     self.stage[k], self.loc.at[n, k])

    def start(self):
        for n, p in enumerate((self.far, self.px, self.py, self.mine)):
            for k in self.arrays:
                self.go(self.theirs(n, p, k))
                if n == 0 and self.stage[k] is not None:
                    self.ours(n, p, k).start()

    def landed(self, n, p):
        for k in self.arrays:
            self.theirs(n, p, k).wait_recv()
            if self.stage[k] is None:
                add_to(self.held(k, p), self.across[k].at[self.slot(p)])
                continue
            self.ours(n, p, k).wait()
            add_to(self.held(k, p), self.stage[k])
            if n < 3:
                self.ours(n + 1, (self.far, self.px, self.py, self.mine)[n + 1], k).start()

    def part(self, k, p, along_x):
        rows = self.ins[k].shape[2] // 2
        at = 0 if along_x else rows
        return self.held(k, p).at[:, at : at + rows]

    def hop(self, k, p, along_x, i, target):
        source = self.part(k, p, along_x)
        if along_x:
            return remote(source, target, self.xs.at[i, k], self.xr.at[i, k], self.to_x)
        return remote(source, target, self.ys.at[i, k], self.yr.at[i, k], self.to_y)

    def first(self, k, p, along_x):
        i = 0 if p is self.far else 1
        return self.hop(k, p, along_x, i, self.one[k].at[2 * i + (0 if along_x else 1)])

    def second(self, k, along_x):
        if along_x:
            return remote(self.part(k, self.py, True), self.two[k].at[0], self.ys.at[2, k],
                          self.yr.at[2, k], self.to_y)
        return remote(self.part(k, self.px, False), self.two[k].at[1], self.xs.at[2, k],
                      self.xr.at[2, k], self.to_x)

    def stage1(self):
        self.landed(0, self.far)
        for k in self.arrays:
            self.go(self.first(k, self.far, True))
            self.go(self.first(k, self.far, False))

    def stage2(self):
        self.landed(1, self.px)
        for k in self.arrays:
            self.go(self.first(k, self.px, True))
        self.landed(2, self.py)
        for k in self.arrays:
            self.go(self.first(k, self.py, False))

    def stage3(self):
        self.landed(3, self.mine)
        for k in self.arrays:
            for along_x, p in ((True, self.py), (False, self.px)):
                self.first(k, self.far, along_x).wait_recv()
                add_to(self.part(k, p, along_x), self.one[k].at[0 if along_x else 1])
                self.go(self.second(k, along_x))

    def stage4(self):
        for k in self.arrays:
            for along_x, p in ((True, self.px), (False, self.py)):
                self.first(k, p, along_x).wait_recv()
                add_to(self.part(k, self.mine, along_x), self.one[k].at[2 if along_x else 3])

    def last(self, k, o):
        z, x, y, c = self.place
        layer = (z + o) % 4
        return remote(self.held(k, self.mine).at[layer], self.deep[k].at[4 - o],
                      self.zs.at[o, k], self.zr.at[4 - o, k], at_place(layer, x, y, c))

    def stage5(self):
        for k in self.arrays:
            for along_x in (True, False):
                self.second(k, along_x).wait_recv()
                add_to(self.part(k, self.mine, along_x), self.two[k].at[0 if along_x else 1])
            for o in (1, 2, 3):
                self.go(self.last(k, o))

    def stage6(self):
        z, x, y, c = self.place
        for k in self.arrays:
            value = self.held(k, self.mine)[z].astype(f32)
            for o in (1, 2, 3):
                here = self.deep[k].at[o]
                remote(here, here, self.zs.at[o, k], self.zr.at[o, k],
                       at_place((z + o) % 4, x, y, c)).wait_recv()
                value = value + self.deep[k][o].astype(f32)
            self.outs[k][...] = value

    def advance(self, upto):
        while self.done < upto:
            self.stages[self.done]()
            self.done += 1

    def drain(self):
        for copy in self.started:
            copy.wait_send()


class Total:
    def __init__(self, small, out, scratch):
        self.small, self.out = small, out
        self.at_c, self.at_p, self.at_z, self.ss, self.rs = scratch
        self.place = z, x, y, c = place()
        self.plane = ((1 - x, y), (x, 1 - y), (1 - x, 1 - y))
        self.started = []

    def swap(self, buffer, index, n, m, target):
        here = buffer.at[index]
        copy = remote(here, here, self.ss.at[n], self.rs.at[m], target)
        copy.start()
        self.started.append(copy)

    def arrive(self, buffer, index, n, target):
        here = buffer.at[index]
        remote(here, here, self.ss.at[n], self.rs.at[n], target).wait_recv()

    def start(self):
        z, x, y, c = self.place
        self.at_c[c] = self.small[...]
        self.swap(self.at_c, c, 0, 0, at_place(z, x, y, 1 - c))

    def middle(self):
        z, x, y, c = self.place
        self.arrive(self.at_c, 1 - c, 0, at_place(z, x, y, 1 - c))
        self.at_p[x * 2 + y] = self.at_c[0] + self.at_c[1]
        for n, p in enumerate(self.plane):
            self.swap(self.at_p, x * 2 + y, 1 + n, 1 + n, at_place(z, *p, c))

    def late(self):
        z, x, y, c = self.place
        for n, p in enumerate(self.plane):
            self.arrive(self.at_p, p[0] * 2 + p[1], 1 + n, at_place(z, *p, c))
        self.at_z[z] = (self.at_p[0] + self.at_p[1]) + (self.at_p[2] + self.at_p[3])
        for o in (1, 2, 3):
            self.swap(self.at_z, z, 3 + o, 7 - o, at_place((z + o) % 4, x, y, c))

    def finish(self):
        z, x, y, c = self.place
        for o in (1, 2, 3):
            self.arrive(self.at_z, (z + o) % 4, 3 + o, at_place((z + o) % 4, x, y, c))
        self.out[...] = (self.at_z[0] + self.at_z[1]) + (self.at_z[2] + self.at_z[3])
        for copy in self.started:
            copy.wait_send()


def total_scratch(dims):
    return [
        pltpu.VMEM((2,) + dims, f32), pltpu.VMEM((4,) + dims, f32), pltpu.VMEM((4,) + dims, f32),
        sems(7), sems(7),
    ]


def reduce_wide_scratch(dims):
    rows, lanes = dims
    return [
        pltpu.VMEM((4,) + dims, bf16), pltpu.VMEM((4, 4) + dims, bf16),
        pltpu.VMEM((4, 4) + dims, bf16), pltpu.VMEM((4, rows // 2, lanes), bf16),
        pltpu.VMEM((2, rows // 2, lanes), bf16),
        sems(4), sems(4), sems(4), sems(4, 4), sems(4, 4), sems(4), sems(4), sems(2), sems(2),
    ]


class ReduceWide:
    def __init__(self, source, out, scratch):
        self.source, self.out = source, out
        (self.stage, self.own, self.deep, self.one, self.two, self.loc, self.cs, self.cr, self.zs,
         self.zr, self.ps, self.pr, self.qs, self.qr) = scratch
        self.place = z, x, y, c = place()
        self.spots = [(x, y), (1 - x, y), (x, 1 - y), (1 - x, 1 - y)]
        self.other = at_place(z, x, y, 1 - c)
        self.to_x, self.to_y = at_place(z, 1 - x, y, c), at_place(z, x, 1 - y, c)
        self.rows = source.shape[2] // 2
        self.started = []
        self.done = 0
        self.stages = [self.stage1, self.stage2, self.stage3, self.stage4, self.stage5, self.stage6]

    def go(self, copy):
        copy.start()
        self.started.append(copy)

    def theirs(self, n):
        c = self.place[3]
        return remote(self.source.at[:, member_of(*self.spots[n], 1 - c)], self.own.at[n],
                      self.cs.at[n], self.cr.at[n], self.other)

    def ours(self, n):
        c = self.place[3]
        return pltpu.make_async_copy(self.source.at[:, member_of(*self.spots[n], c)],
                                     self.stage, self.loc.at[n])

    def start(self):
        for n in range(4):
            self.go(self.theirs(n))
        self.ours(0).start()

    def landed(self, n):
        z, x, y, c = self.place
        self.ours(n).wait()
        self.theirs(n).wait_recv()
        add_to(self.own.at[n], self.stage)
        if n < 3:
            self.ours(n + 1).start()
        for o in (1, 2, 3):
            layer = (z + o) % 4
            self.go(remote(self.own.at[n, layer], self.deep.at[n, 4 - o], self.zs.at[o, n],
                           self.zr.at[4 - o, n], at_place(layer, x, y, c)))

    def stage1(self):
        self.landed(0)
        self.landed(1)

    def stage2(self):
        self.landed(2)
        self.landed(3)

    def gathered(self, n):
        z, x, y, c = self.place
        total = self.own[n, z].astype(f32)
        for o in (1, 2, 3):
            here = self.deep.at[n, o]
            remote(here, here, self.zs.at[o, n], self.zr.at[o, n],
                   at_place((z + o) % 4, x, y, c)).wait_recv()
            total = total + self.deep[n, o].astype(f32)
        self.own[n, z] = total.astype(bf16)

    def part(self, n, along_x):
        at = 0 if along_x else self.rows
        return self.own.at[n, self.place[0], at : at + self.rows]

    def first(self, i):
        n, along_x = ((3, True), (3, False), (1, True), (2, False))[i]
        return remote(self.part(n, along_x), self.one.at[i], self.ps.at[i], self.pr.at[i],
                      self.to_x if along_x else self.to_y)

    def second(self, along_x):
        if along_x:
            return remote(self.part(2, True), self.two.at[0], self.qs.at[0], self.qr.at[0], self.to_y)
        return remote(self.part(1, False), self.two.at[1], self.qs.at[1], self.qr.at[1], self.to_x)

    def add(self, n, along_x, source):
        at = 0 if along_x else self.rows
        z = self.place[0]
        rows = slice(at, at + self.rows)
        self.own[n, z, rows] = (
            self.own[n, z, rows].astype(f32) + source[...].astype(f32)
        ).astype(bf16)

    def stage3(self):
        for n in (0, 1, 2, 3):
            self.gathered(n)
        for i in range(4):
            self.go(self.first(i))

    def stage4(self):
        for i, (n, along_x) in enumerate(((2, True), (1, False))):
            self.first(i).wait_recv()
            self.add(n, along_x, self.one.at[i])
            self.go(self.second(along_x))

    def stage5(self):
        for i, along_x in ((2, True), (3, False)):
            self.first(i).wait_recv()
            self.add(0, along_x, self.one.at[i])

    def stage6(self):
        z = self.place[0]
        for i, along_x in ((0, True), (1, False)):
            self.second(along_x).wait_recv()
            at = 0 if along_x else self.rows
            rows = slice(at, at + self.rows)
            self.out[rows] = self.own[0, z, rows].astype(f32) + self.two[i].astype(f32)

    def advance(self, upto):
        while self.done < upto:
            self.stages[self.done]()
            self.done += 1

    def drain(self):
        for copy in self.started:
            copy.wait_send()


def norm_parts(values):
    average = jnp.mean(values, axis=-1, keepdims=True)
    centred = values - average
    variance = jnp.mean(centred * centred, axis=-1, keepdims=True)
    inverse = lax.rsqrt(variance + epsilon)
    return centred * inverse, inverse


def norm_backward(hat, inverse, gain, grad):
    scaled = grad * gain
    first = jnp.mean(scaled, axis=-1, keepdims=True)
    second = jnp.mean(scaled * hat, axis=-1, keepdims=True)
    return (scaled - first - hat * second) * inverse


def compact(j, rows, packed, places):
    for place, size in places:
        packed[place + size * j : place + size * j + size] = rows[:size]


def widen(pieces):
    total = pieces[-1]
    for piece in reversed(pieces[:-1]):
        blank = jnp.zeros((piece.shape[0], piece.shape[1] - total.shape[1]), f32)
        total = piece + jnp.concatenate([total, blank], axis=1)
    return total


def join_quad(quad, read):
    wide = jnp.concatenate(
        [swap_chunks(read(4 * quad + i), 4 * quad + i) for i in range(4)], axis=0
    )
    return swap_blocks(wide.T, quad)


def join_quads(read):
    pairs = []
    for half in range(2):
        pairs.append(
            jnp.concatenate([join_quad(quad, read) for quad in (2 * half, 2 * half + 1)], axis=1)
        )
    return jnp.concatenate(pairs, axis=1)


def unit_forward(query, key, out):
    lane = lax.broadcasted_iota(jnp.int32, (256, LANES), 1)
    count = len(query)
    scores = [matmul(query[i](), key, NT) for i in range(count)]
    for i in range(count):
        top = jnp.max(scores[i], axis=1, keepdims=True) * scale2
        prob = jnp.exp2(scores[i] * scale2 - top).astype(bf16)
        value = jnp.where(lane == FLAG + 8, top, matmul(prob, key))
        out[i](value.T[HD : HD + 64])


def forward_kernel(grp, slides, gather, *refs):
    refs = list(refs)
    take = lambda n: [refs.pop(0) for _ in range(n)]
    tokens, cot_in, local, ends, frequency, vectors, bias = take(7)
    shards = take(4) if gather else take(0)
    given = take(0) if gather else take(4)
    base, msg, q_ref, kv_ref, kv8, kv16, stat = take(7)
    out, grad_middle, grad_merged, small = take(4)
    late_grads = take(3)
    gathered = take(1) if gather else take(0)
    send, osend, orecv, acc, qc, kvc, tok_sem, ss, rs, os_, or_, ds, dr = take(13)
    wo, wi, wt = take(3)
    dense_scratch = take(9)
    save_sem = take(1)[0]
    weight = gathered[0] if gather else given[0]
    cot = dense_scratch[0]
    spot = Spot(grp)
    joined = spot.greet()
    loads = []
    for n, (source, target) in enumerate(((tokens, base), (cot_in, cot))):
        for b in range(16):
            at = BLOCK * b
            loads.append(
                pltpu.make_async_copy(source.at[:, order[b]], target.at[at : at + BLOCK], tok_sem.at[n, b])
            )
    for copy in loads:
        copy.start()
    if gather:
        first = Gather(shards[:1], gathered[:1], take(9))
        rest = Gather([shards[1], shards[3]], [wo, wt], take(9))
        wide_part = GatherWide(shards[2], wi, take(9))
        joined()
        first.start_layers()
        first.start_plane()
        wide_part.start()
        rest.start_layers()
    else:
        loads_late = [
            pltpu.make_async_copy(source, target, save_sem.at[n])
            for n, (source, target) in enumerate(zip(given[1:], (wo, wi, wt)))
        ]
        for copy in loads_late:
            copy.start()
    place_lane = lax.broadcasted_iota(jnp.int32, (1, 512), 1)
    b = place_lane // BLOCK
    b = (b % 2) * 8 + (b // 2 % 2) * 4 + (b // 4 % 2) * 2 + b // 8
    position = spot.linear * 512 + place_lane % BLOCK * 16 + b
    begin = jnp.zeros((1, 512), jnp.int32)
    lines = [jnp.where(local[0:1] == 1.0, 0.0, -BIG)]
    before = 0
    for n in range(slides):
        after = before + ends[n]
        inside = (position >= before) & (position < after)
        lines.append(jnp.where(inside, 0.0, -BIG))
        before = after
    lines += [jnp.ones((1, 512), f32), jnp.zeros((14 - slides, 512), f32)]
    flags_all = jnp.concatenate(lines, axis=0)
    coordinates = local[...].T
    gain, shift = vectors[0:1], vectors[1:2]
    lane = lax.broadcasted_iota(jnp.int32, (512, 384), 1)
    angle = jnp.where(lane < 192, coordinates[:, 1:2], coordinates[:, 2:3]) * frequency[...]
    sine, cosine = jnp.sin(angle), jnp.cos(angle)
    table = jnp.concatenate(
        [
            jnp.concatenate([sine[:, :192], cosine[:, :192]], axis=1),
            jnp.concatenate([sine[:, 192:], cosine[:, 192:]], axis=1),
        ],
        axis=1,
    )
    for copy in loads[:16]:
        copy.wait()
    base[...] = base[...] + table
    hat, _ = norm_parts(base[...])
    normed = (hat * gain + shift).astype(bf16)
    if gather:
        first.advance(4)
        wide_part.advance(1)
        first.finish()
        wide_part.advance(2)
    else:
        joined()
    plane = [Exchange(spot, send.at[i], msg.at[i], ss.at[i], rs.at[i]) for i in range(2)]
    for quad in range(4):
        part = matmul(normed, pick(weight, quad)) + bias[quad]
        wide = swap_blocks(part.astype(bf16), quad).T
        flags = flags_all
        flags = jnp.concatenate(
            [flags[:, BLOCK * (b ^ block_swap(quad)) :][:, :BLOCK] for b in range(16)], axis=1
        ).astype(bf16)
        for inner in (0, 2, 1, 3):
            head = 4 * quad + inner
            owner, i = head // 2, head % 2
            own = swap_chunks(wide[144 * inner : 144 * inner + 144], head)
            send[i, owner, :96] = own[48:]
            send[i, owner, 96:112] = swap_chunks(flags, head)
            send[i, owner, 112:] = own[:48]
            if i == 0:
                plane[0].send(owner)
    for owner in range(GROUP):
        plane[1].send(owner)
    row = lax.broadcasted_iota(jnp.int32, (16, 512), 0)
    deeps = []
    results = [Exchange(spot, osend.at[i], orecv.at[i], os_.at[i], or_.at[i]) for i in range(2)]
    if gather:
        rest.start_plane()
    for i in range(2):
        q, kv = q_ref.at[i], kv_ref.at[i]
        for j in range(GROUP):
            plane[i].wait(j)
            block = msg[i, j]
            key_part = jnp.concatenate([block[:112], jnp.zeros((16, 512), bf16)], axis=0).T
            flags = block[96:112].astype(f32)
            chosen = jnp.where(
                row == 0, 1.0, jnp.where((row <= slides) & (flags == 0.0), 1.0, 0.0)
            )
            query_part = jnp.concatenate(
                [block[112:], jnp.zeros((HD, 512), bf16), chosen.astype(bf16),
                 jnp.zeros((16, 512), bf16)],
                axis=0,
            ).T
            kv[512 * j : 512 * j + 512] = key_part
            q[512 * j : 512 * j + 512] = query_part
            compact(j, query_part, qc, ((0, 256), (2048, 128), (3072, 64), (3584, 32)))
            compact(j, key_part, kvc, ((0, 256), (2048, 128)))
            kv8[spot.half, i, 64 * j : 64 * j + 64] = key_part[:64]
            kv16[spot.layer, i, 32 * j : 32 * j + 32] = key_part[:32]
        own8, own16 = kv8.at[spot.half, i], kv16.at[spot.layer, i]
        deep = Deep(
            spot, (own8, own8, kv8.at[1 - spot.half, i]),
            lambda o, other: (own16, own16, kv16.at[other, i]), ds.at[i], dr.at[i],
        )
        deep.start()
        deeps.append(deep)
        if gather:
            rest.advance(1 + 2 * i)

        def unit(source, q_from, keys, k_from, out_from, count):
            def reader(n):
                return lambda: source[pl.ds(q_from + 256 * n, 256)]

            def writer(n):
                def save(value):
                    acc[:, pl.ds(out_from + 256 * n, 256)] = value

                return save

            unit_forward(
                [reader(n) for n in range(count)], keys[pl.ds(k_from, 1024)],
                [writer(n) for n in range(count)],
            )

        def early(u, _):
            at = pl.multiple_of(u * 1024, 1024)
            unit(q, at, kv, at, at, 4)
            return 0

        lax.fori_loop(0, 4, early, 0)
        if gather:
            rest.advance(2 + 2 * i)

        def late(u, _):
            at = pl.multiple_of(u * 1024, 1024)
            unit(qc, at, kvc, at, pl.multiple_of(at + 4096, 1024), 4)
            return 0

        lax.fori_loop(0, 3, late, 0)
        deep.wait()
        for n in range(2):
            kvc[3072 + 512 * n : 3584 + 512 * n] = kv8[n, i]
        for n in range(4):
            kvc[4096 + 256 * n : 4352 + 256 * n] = kv16[n, i]
        unit(qc, 3072, kvc, 3072, 7168, 2)
        unit(qc, 3584, kvc, 4096, 7680, 1)
        place = lax.broadcasted_iota(jnp.int32, (1, 512), 1)
        uses = jnp.where(place < 32, 5.0, jnp.where(place < 64, 4.0, jnp.where(
            place < 128, 3.0, jnp.where(place < 256, 2.0, 1.0))))
        for j in range(GROUP):
            key = msg[i, j, :HD].astype(f32)
            value = msg[i, j, HD : 2 * HD].astype(f32)
            query = msg[i, j, 112:].astype(f32)
            dropped = msg[i, j, FLAG : FLAG + 1].astype(f32) != 0.0
            own = jnp.where(dropped, column_sum(query * key) * scale2 + jnp.log2(uses), -BIG)
            pieces = [
                acc[:, q_at[r] + (512 >> r) * j : q_at[r] + (512 >> r) * (j + 1)] for r in range(5)
            ]
            top = own
            tops = [piece[HD + 8 : HD + 9] for piece in pieces]
            for item in tops:
                spread = item
                if spread.shape[1] < 512:
                    blank = jnp.full((1, 512 - spread.shape[1]), -BIG, f32)
                    spread = jnp.concatenate([spread, blank], axis=1)
                top = jnp.maximum(top, spread)
            scaled = [
                piece[: HD + 8] * jnp.exp2(item - top[:, : item.shape[1]])
                for piece, item in zip(pieces, tops)
            ]
            mix = widen(scaled)
            weight_own = jnp.exp2(own - top)
            total = mix[HD + 1 + slides : HD + 2 + slides] + weight_own
            result = (mix[:HD] + weight_own * value) / total
            stat[i, j, :HD] = result
            stat[i, j, HD : HD + 8] = jnp.broadcast_to(top + jnp.log2(total), (8, 512))
            osend[i, j] = result.astype(bf16)
            results[i].send(j)
    if gather:
        wide_part.advance(4)
        rest.advance(5)
    for i in range(2):
        for j in range(GROUP):
            results[i].wait(j)
    if gather:
        rest.finish()
        wide_part.advance(5)
        rest.drain()
        wide_part.drain()
        first.drain()
    else:
        for copy in loads_late:
            copy.wait()
    for copy in loads[16:]:
        copy.wait()
    merged = dense_scratch[1]
    merged[...] = join_quads(lambda h: orecv[h % 2, h // 2])
    dense_part(
        merged, base, cot, wo, wi, wt, vectors, out, grad_middle, grad_merged, small,
        late_grads, save_sem, *dense_scratch[2:],
    )
    for item in plane + deeps + results:
        item.drain()


def dense_part(
    merged, base, cot, wo, wi, wt, vectors, out, grad_middle, grad_merged, small,
    late_grads, save_sem, middle, hat, low, low_t, cot_low, cot_t, grad_low,
):
    out_bias, gain, shift, last_bias = [vectors[n : n + 1] for n in range(2, 6)]
    pairs = []
    for g in range(0, 4, 2):
        pair = [pick(wo, g + i) for i in range(2)]
        pairs.append(jnp.concatenate(pair, axis=1))
    full = jnp.concatenate(pairs, axis=1)
    middle[...] = base[...] + matmul(merged[...], full) + out_bias
    normal, inverse = norm_parts(middle[...])
    hat[...] = normal
    low[...] = (normal * gain + shift).astype(bf16)
    low_t[...] = low[...].T
    cot_low[...] = cot[...].astype(bf16)
    cot_t[...] = cot_low[...].T
    out[...] = middle[...] + last_bias
    small[0:1] = column_sum(cot_low[...].astype(f32))
    grad_middle[...] = jnp.zeros((512, 768), f32)

    def chunk(g, _):
        weight = pick(wi, g)
        inner = matmul(low[...], weight) + vectors[pl.ds(6 + g, 1)]
        phi = 0.5 * (1.0 + lax.erf(inner * 0.7071067811865476))
        active = (inner * phi).astype(bf16)
        slope = phi + inner * jnp.exp(-0.5 * inner * inner) * 0.3989422804014327
        for x in range(2):
            part = wt[g, 4 * x : 4 * x + 4].reshape(768, 384)
            now = active[:, 384 * x : 384 * x + 384]
            out[...] += matmul(now, part, NT)
            back = matmul(cot_low[...], part)
            wt[g, 4 * x : 4 * x + 4] = (
                matmul(cot_t[...], now).astype(bf16).reshape(4, 192, 384)
            )
            grad_low[:, 384 * x : 384 * x + 384] = (
                back * slope[:, 384 * x : 384 * x + 384]
            ).astype(bf16)
        small[pl.ds(4 + g, 1)] = column_sum(grad_low[...].astype(f32))
        grad_middle[...] += matmul(grad_low[...], weight, NT)
        put(wi, g, matmul(low_t[...], grad_low[...]).astype(bf16))
        return 0

    lax.fori_loop(0, 4, chunk, 0)
    saves = [
        pltpu.make_async_copy(source, target, save_sem.at[n])
        for n, (source, target) in enumerate(zip((wo, wi, wt), late_grads))
    ]
    saves[1].start()
    saves[2].start()
    grad = grad_middle[...]
    small[1:2] = column_sum(grad * hat[...])
    small[2:3] = column_sum(grad)
    grad = cot[...] + norm_backward(hat[...], inverse, gain, grad)
    grad_middle[...] = grad
    attended = grad.astype(bf16)
    small[3:4] = column_sum(attended.astype(f32))
    grad_merged[...] = matmul(attended, full, NT).astype(bf16)
    grads = matmul(merged[...].T, attended).astype(bf16)
    for g in range(4):
        put(wo, g, grads[:, 192 * g : 192 * g + 192])
    saves[0].start()
    for copy in saves:
        copy.wait()


def attention_forward(grp, slides, gather, inputs, weights):
    out_shape = [
        shape((512, 768), f32),
        shape((2, GROUP, MSG, 512), bf16),
        shape((2, 4096, LANES), bf16),
        shape((2, 4096, LANES), bf16),
        shape((2, 2, 512, LANES), bf16),
        shape((4, 2, 256, LANES), bf16),
        shape((2, GROUP, 56, 512), f32),
        shape((512, 768), f32),
        shape((512, 768), f32),
        shape((512, 768), bf16),
        shape((8, 768), f32),
    ]
    blocks = [(4, GROUP, 96, 192), (4, GROUP, 96, 768), (4, GROUP, 192, 384)]
    out_specs = [vmem()] * len(out_shape) + [anywhere()] * 3
    out_shape += [shape(dims, bf16) for dims in blocks]
    in_specs = [anywhere()] * 2 + [vmem(), pl.BlockSpec(memory_space=pltpu.SMEM)] + [vmem()] * 3
    extra = []
    if gather:
        in_specs += [anywhere()] * 4
        out_shape += [shape((4, GROUP, 96, 576), bf16)]
        out_specs += [vmem()]
        extra = gather_sems(1) + gather_sems(2) + gather_wide_sems()
    else:
        in_specs += [vmem()] + [anywhere()] * 3
    rows = (512, 768)
    return pl.pallas_call(
        functools.partial(forward_kernel, grp, slides, gather),
        name="forward_and_feed",
        in_specs=in_specs,
        out_specs=out_specs,
        out_shape=out_shape,
        scratch_shapes=[
            pltpu.VMEM((2, GROUP, MSG, 512), bf16),
            pltpu.VMEM((2, GROUP, HD, 512), bf16),
            pltpu.VMEM((2, GROUP, HD, 512), bf16),
            pltpu.VMEM((64, q_all), f32),
            pltpu.VMEM((q_all - 4096, LANES), bf16),
            pltpu.VMEM((k_all - 4096, LANES), bf16),
            sems(2, 16),
            sems(2, GROUP), sems(2, GROUP), sems(2, GROUP), sems(2, GROUP), sems(2, 4), sems(2, 4),
        ]
        + [pltpu.VMEM(dims, bf16) for dims in blocks]
        + [
            pltpu.VMEM(rows, f32), pltpu.VMEM(rows, bf16), pltpu.VMEM(rows, f32),
            pltpu.VMEM(rows, f32), pltpu.VMEM(rows, bf16), pltpu.VMEM((768, 512), bf16),
            pltpu.VMEM(rows, bf16), pltpu.VMEM((768, 512), bf16), pltpu.VMEM(rows, bf16),
            sems(3),
        ]
        + extra,
        compiler_params=params(1),
    )(*inputs, *weights)


def backward_kernel(grp, reduce, *refs):
    refs = list(refs)
    take = lambda n: [refs.pop(0) for _ in range(n)]
    gm, vectors, small = take(3)
    saved = take(6)
    base_in, middle_in, weight_in = take(3)
    parts = take(3) if reduce else take(0)
    token_grad, joint_out, pack = take(3)
    reduced = take(3) if reduce else take(0)
    (gsend, grecv, rsend, rrecv, got8, got16, send8, send16, rows_ref,
     gs, gr, ss, rs, ds, dr, load_sem) = take(16)
    local = take(13)
    (grads,) = take(1)
    spot = Spot(grp)
    joined = spot.greet()
    shares = [Exchange(spot, gsend.at[i], grecv.at[i], gs.at[i], gr.at[i]) for i in range(2)]
    backs = [Exchange(spot, rsend.at[i], rrecv.at[i], ss.at[i], rs.at[i]) for i in range(2)]
    deeps = []
    if reduce:
        two = [parts[0], parts[2]], [reduced[0], reduced[2]]
        dims = [part.shape[2:] for part in two[0]]
        sums = Reduce(*two, take(len(reduce_scratch(dims))))
        wide_sum = ReduceWide(parts[1], reduced[1], take(14))
        last_scratch = take(len(reduce_scratch([(96, 576)])) - 1)
        total_sum = take(5)
    else:
        sums = wide_sum = None

    attend_backward(
        spot, joined, gm, saved, shares, backs, deeps, sums, wide_sum, gsend, grecv, rsend,
        got8, got16, send8, send16, ds, dr, load_sem, *local,
    )
    rows_f32 = local[11]
    late_loads = [pltpu.make_async_copy(weight_in, grads, load_sem.at[0])]
    for n, source in enumerate((base_in, middle_in)):
        for chunk in range(6):
            at = 3072 * n + 512 * chunk
            late_loads.append(
                pltpu.make_async_copy(
                    source.at[:, LANES * chunk : LANES * chunk + LANES],
                    rows_f32.at[at : at + 512],
                    load_sem.at[1 + 6 * n + chunk],
                )
            )
    for copy in late_loads:
        copy.start()

    def loaded(n):
        at = 3072 * n
        return jnp.concatenate(
            [rows_f32[at + 512 * chunk : at + 512 * chunk + 512] for chunk in range(6)], axis=1
        )

    if reduce:
        sums.advance(5)
        wide_sum.advance(5)
    for copy in late_loads:
        copy.wait()
    gain, shift = vectors[0:1], vectors[1:2]
    hat, inverse = norm_parts(loaded(0))
    low_t = (hat * gain + shift).astype(bf16).T
    for i in range(2):
        for j in range(GROUP):
            backs[i].wait(j)
    lines = [[], []]
    grad = jnp.zeros((512, 768), f32)
    for quad in range(4):

        def read(head):
            block = rrecv[head % 2, head // 2]
            return jnp.concatenate([block[2 * HD :], block[: 2 * HD]], axis=0)

        now = join_quad(quad, read)
        grad = grad + matmul(now, pick(grads, quad), NT)
        put(grads, quad, matmul(low_t, now).astype(bf16))
        total = column_sum(now.astype(f32))
        for inner in range(4):
            lines[0].append(total[:, 144 * inner : 144 * inner + HD])
            lines[1].append(total[:, 144 * inner + 96 : 144 * inner + 144])
    if reduce:
        joint = Reduce([grads], [joint_out], [None] + list(last_scratch))
        joint.start()
    rows_ref[0:1] = column_sum(grad * hat)
    rows_ref[1:2] = column_sum(grad)
    rows_ref[2:3] = jnp.concatenate(lines[0], axis=1)
    rows_ref[3:4] = jnp.concatenate(lines[1], axis=1)
    rows_ref[4:5] = small[3:4]
    rows_ref[5:6] = small[1:2]
    rows_ref[6:7] = small[2:3]
    rows_ref[7:8] = small[0:1]
    rows_ref[8:12] = small[4:8]
    rows_ref[12:16] = jnp.zeros((4, 768), f32)
    token_grad[...] = loaded(1) + norm_backward(hat, inverse, gain, grad)
    if reduce:
        rest = Total(rows_ref, pack, total_sum)
        rest.start()
        joint.advance(1)
        rest.middle()
        joint.advance(3)
        rest.late()
        joint.advance(5)
        sums.advance(6)
        wide_sum.advance(6)
        joint.advance(6)
        rest.finish()
        joint.drain()
    else:
        pack[...] = rows_ref[...]
        save = pltpu.make_async_copy(grads, joint_out, load_sem.at[3])
        save.start()
        save.wait()
    if reduce:
        sums.drain()
        wide_sum.drain()
    for item in shares + backs + deeps:
        item.drain()


def attend_backward(
    spot, joined, gm, saved, shares, backs, deeps, sums, wide_sum, gsend, grecv, rsend, got8, got16,
    send8, send16, ds, dr, load_sem, q_ref, kv_ref, kv8, kv16, msg, stat,
    qc, kvc, dor, kt, ld, dkv, dqt,
):
    reduce = sums is not None
    loads = [
        pltpu.make_async_copy(source, target, load_sem.at[n])
        for n, (source, target) in enumerate(zip(saved, (q_ref, kv_ref, kv8, kv16, msg, stat)))
    ]
    for copy in loads:
        copy.start()
    for quad in range(4):
        wide = swap_blocks(gm[:, 192 * quad : 192 * quad + 192], quad).T
        for inner in (0, 2, 1, 3):
            head = 4 * quad + inner
            i = head % 2
            gsend[i, head // 2] = swap_chunks(wide[HD * inner : HD * inner + HD], head)
            if quad == 0 and inner == 0:
                joined()
            if i == 0:
                shares[0].send(head // 2)
    for j in range(GROUP):
        shares[1].send(j)
    if reduce:
        wide_sum.start()
        sums.start()
    for copy in loads:
        copy.wait()
    for i in range(2):
        q, kv = q_ref.at[i], kv_ref.at[i]
        for n in range(2):
            kvc[3072 + 512 * n : 3584 + 512 * n] = kv8[n, i]
        for n in range(4):
            kvc[4096 + 256 * n : 4352 + 256 * n] = kv16[n, i]
        for n in range(2):
            kt[7 + n] = kvc[3072 + 1024 * n : 4096 + 1024 * n].T[:HD]
        rows = []
        for j in range(GROUP):
            compact(j, q[512 * j : 512 * j + 512], qc, ((0, 256), (2048, 128), (3072, 64), (3584, 32)))
            compact(j, kv[512 * j : 512 * j + 512], kvc, ((0, 256), (2048, 128)))
            key = msg[i, j, :HD]
            kt[j // 2, :, 512 * (j % 2) : 512 * (j % 2) + 512] = key
            kt[4 + j // 4, :, 256 * (j % 4) : 256 * (j % 4) + 256] = key[:, :256]
            kt[6, :, 128 * j : 128 * j + 128] = key[:, :128]
        for j in range(GROUP):
            shares[i].wait(j)
            grad = grecv[i, j]
            delta = column_sum(grad.astype(f32) * stat[i, j, :HD])
            both = jnp.concatenate(
                [stat[i, j, HD : HD + 1], delta, jnp.zeros((6, 512), f32)], axis=0
            )
            rows.append(both)
            ld[:, 512 * j : 512 * j + 512] = both
            ld[:, 4096 + 256 * j : 4352 + 256 * j] = both[:, :256]
            ld[:, 6144 + 128 * j : 6272 + 128 * j] = both[:, :128]
            tall = jnp.concatenate(
                [jnp.zeros((HD, 512), bf16), grad, jnp.zeros((32, 512), bf16)], axis=0
            ).T
            for r, at in enumerate(q_at):
                size = 512 >> r
                dor[at + size * j : at + size * j + size] = tall[:size]
        ld[:, 7168:7680] = jnp.concatenate([both[:, :64] for both in rows], axis=1)
        ld[:, 7680:7936] = jnp.concatenate([both[:, :32] for both in rows], axis=1)

        def unit(source, q_from, keys, k_from, at, seg, count):
            width = 256 * count
            query = source[pl.ds(q_from, width)]
            grad = dor[pl.ds(at, width)]
            total = ld[0:1, pl.ds(at, width)]
            delta = ld[1:2, pl.ds(at, width)]
            sides = jnp.concatenate([grad, query], axis=0)
            size = 256
            dq = jnp.zeros((HD, width), f32)
            for c in range(1024 // size):
                key = keys[pl.ds(k_from + size * c, size)]
                prob = jnp.exp2(matmul(key, query, NT) * scale2 - total)
                slope = (prob * (matmul(key, grad, NT) - delta)).astype(bf16)
                both = jnp.concatenate([prob.astype(bf16), slope], axis=1)
                dkv[pl.ds(seg * 1024 + size * c, size)] = matmul(both, sides)
                dq = dq + matmul(kt[seg, :, size * c : size * c + size], slope)
            dqt[:, pl.ds(at, width)] = dq

        unit(qc, 3072, kvc, 3072, 7168, 7, 2)
        unit(qc, 3584, kvc, 4096, 7680, 8, 1)
        for n in range(2):
            send8[n, i] = dkv[7168 + 512 * n : 7680 + 512 * n].astype(bf16)
        for n in range(4):
            send16[n, i] = dkv[8192 + 256 * n : 8448 + 256 * n].astype(bf16)
        deep = Deep(
            spot, (send8.at[1 - spot.half, i], got8.at[i], got8.at[i]),
            lambda o, other: (send16.at[other, i], got16.at[4 - o, i], got16.at[o, i]),
            ds.at[i], dr.at[i],
        )
        deep.start()
        deeps.append(deep)
        if reduce:
            wide_sum.advance(2 + i)
            sums.advance(1 + 2 * i)

        def early(u, _):
            at = pl.multiple_of(u * 1024, 1024)
            unit(q, at, kv, at, at, u, 4)
            return 0

        lax.fori_loop(0, 4, early, 0)
        if reduce:
            sums.advance(2 + 2 * i)
            wide_sum.advance(2 + 2 * i)

        def late(u, _):
            at = pl.multiple_of(u * 1024, 1024)
            unit(qc, at, kvc, at, pl.multiple_of(at + 4096, 1024), u + 4, 4)
            return 0

        lax.fori_loop(0, 3, late, 0)
        deep.wait()
        spot_lane = lax.broadcasted_iota(jnp.int32, (1, 512), 1)
        uses = jnp.where(spot_lane < 32, 5.0, jnp.where(spot_lane < 64, 4.0, jnp.where(
            spot_lane < 128, 3.0, jnp.where(spot_lane < 256, 2.0, 1.0))))
        for j in range(GROUP):
            tall = dkv[512 * j : 512 * j + 512]
            eight = send8[spot.half, i, 64 * j : 64 * j + 64].astype(f32) + got8[
                i, 64 * j : 64 * j + 64
            ].astype(f32)
            sixteen = send16[spot.layer, i, 32 * j : 32 * j + 32].astype(f32)
            for o in range(1, 4):
                sixteen = sixteen + got16[o, i, 32 * j : 32 * j + 32].astype(f32)
            second = dkv[4096 + 256 * j : 4352 + 256 * j]
            third = dkv[6144 + 128 * j : 6272 + 128 * j]
            fourth = third[:64] + eight
            fourth = jnp.concatenate([fourth[:32] + sixteen, fourth[32:]], axis=0)
            third = jnp.concatenate([fourth, third[64:]], axis=0)
            second = jnp.concatenate([second[:128] + third, second[128:]], axis=0)
            wide = jnp.concatenate([tall[:256] + second, tall[256:]], axis=0).T
            key = msg[i, j, :HD].astype(f32)
            value = msg[i, j, HD : 2 * HD].astype(f32)
            query = msg[i, j, 112:].astype(f32)
            grad = grecv[i, j].astype(f32)
            total = ld[0:1, 512 * j : 512 * j + 512]
            delta = ld[1:2, 512 * j : 512 * j + 512]
            dropped = msg[i, j, FLAG : FLAG + 1].astype(f32) != 0.0
            dots = column_sum(query * key) * scale2 - total
            prob = jnp.where(dropped, uses * jnp.exp2(jnp.where(dropped, dots, 0.0)), 0.0)
            slope = prob * (column_sum(grad * value) - delta)
            dq = widen([dqt[:, at + (512 >> r) * j : at + (512 >> r) * (j + 1)]
                        for r, at in enumerate(q_at)])
            rsend[i, j, :HD] = ((wide[:HD] + slope * query) * scale).astype(bf16)
            rsend[i, j, HD : 2 * HD] = (wide[HD : 2 * HD] + prob * grad).astype(bf16)
            rsend[i, j, 2 * HD :] = ((dq + slope * key) * scale).astype(bf16)
            backs[i].send(j)


def attention_backward(grp, reduce, inputs, parts):
    out_shape = [
        shape((512, 768), f32),
        shape((96, 576), f32) if reduce else shape((4, GROUP, 96, 576), bf16),
        shape((16, 768), f32),
    ]
    out_specs = [vmem(), vmem() if reduce else anywhere(), vmem()]
    extra = []
    if reduce:
        dims = [part.shape[2:] for part in parts]
        out_shape += [shape(d, f32) for d in dims]
        out_specs += [vmem()] * 3
        extra = (
            reduce_scratch([dims[0], dims[2]]) + reduce_wide_scratch(dims[1])
            + reduce_scratch([(96, 576)])[1:] + total_scratch((16, 768))
        )
    return pl.pallas_call(
        functools.partial(backward_kernel, grp, reduce),
        name="attention_backward",
        in_specs=[vmem()] * 3 + [anywhere()] * (9 + len(parts)),
        out_specs=out_specs,
        out_shape=out_shape,
        scratch_shapes=[
            pltpu.VMEM((2, GROUP, HD, 512), bf16),
            pltpu.VMEM((2, GROUP, HD, 512), bf16),
            pltpu.VMEM((2, GROUP, 3 * HD, 512), bf16),
            pltpu.VMEM((2, GROUP, 3 * HD, 512), bf16),
            pltpu.VMEM((2, 512, LANES), bf16),
            pltpu.VMEM((4, 2, 256, LANES), bf16),
            pltpu.VMEM((2, 2, 512, LANES), bf16),
            pltpu.VMEM((4, 2, 256, LANES), bf16),
            pltpu.VMEM((16, 768), f32),
            sems(2, GROUP), sems(2, GROUP), sems(2, GROUP), sems(2, GROUP), sems(2, 4), sems(2, 4),
            sems(13),
            pltpu.VMEM((2, 4096, LANES), bf16), pltpu.VMEM((2, 4096, LANES), bf16),
            pltpu.VMEM((2, 2, 512, LANES), bf16), pltpu.VMEM((4, 2, 256, LANES), bf16),
            pltpu.VMEM((2, GROUP, MSG, 512), bf16), pltpu.VMEM((2, GROUP, 56, 512), f32),
            pltpu.VMEM((q_all - 4096, LANES), bf16), pltpu.VMEM((k_all - 4096, LANES), bf16),
            pltpu.VMEM((q_all, LANES), bf16), pltpu.VMEM((9, HD, 1024), bf16),
            pltpu.VMEM((8, q_all), f32), pltpu.VMEM((k_all, LANES), f32),
            pltpu.VMEM((HD, q_all), f32),
            pltpu.VMEM((4, GROUP, 96, 576), bf16),
        ] + extra,
        compiler_params=params(2),
    )(*inputs, *parts)


def finish_kernel(out_in, token_in, joint, b_in, c_in, d_in, pack, *refs):
    out, token, query, key, value, b_out, c_out, d_out = refs[:8]
    vectors, done = refs[8:17], refs[17]
    copies = []
    for n, (source, target) in enumerate(((out_in, out), (token_in, token))):
        for b in range(16):
            at = BLOCK * b
            copies.append(
                pltpu.make_async_copy(source.at[at : at + BLOCK], target.at[:, order[b]], done.at[n, b])
            )
    for copy in copies:
        copy.start()
    for n, target in enumerate((query, key, value)):
        target[...] = jnp.concatenate(
            [joint[:, 144 * i + HD * n : 144 * i + HD * n + HD] for i in range(4)], axis=1
        )
    b_out[...] = b_in[...]
    c_out[...] = c_in[...]
    d_out[...] = d_in[...].T
    for n in (0, 1, 2, 3, 4, 5, 6):
        vectors[n][...] = pack[n]
    vectors[7][...] = jnp.concatenate([pack[8 + n] for n in range(4)], axis=0)
    vectors[8][...] = pack[7]
    for copy in copies:
        copy.wait()


def finish(out, token_grad, joint, b_sum, c_sum, d_sum, pack):
    shard, hidden = b_sum.shape[0], d_sum.shape[1]
    rows = (BLOCK, 16, 768)
    sizes = [768] * 7 + [3072, 768]
    return pl.pallas_call(
        finish_kernel,
        name="finish",
        in_specs=[anywhere()] * 2 + [vmem()] * 5,
        out_specs=[anywhere()] * 2 + [vmem()] * 15,
        out_shape=[shape(rows, f32)] * 2
        + [shape((shard, 192), f32)] * 4
        + [shape((shard, 768), f32), shape((hidden, 192), f32)]
        + [shape((size,), f32) for size in sizes],
        scratch_shapes=[sems(2, 16)],
        compiler_params=params(),
    )(out, token_grad, joint, b_sum, c_sum, d_sum, pack)


def all_weights(parts, seq, grp):
    gathered = []
    for n, part in enumerate(parts):
        whole = lax.all_gather(lax.all_gather(part, "grp"), "seq")
        lead = whole.shape[0] // 8
        whole = whole.reshape((8, lead) + whole.shape[1:])
        if n == 3:
            whole = whole.transpose(0, 2, 3, 1, 4)
            whole = whole.reshape(4, GROUP, part.shape[0], lead * part.shape[1])
        else:
            whole = whole.transpose(0, 2, 1, 3, 4)
            whole = whole.reshape(4, GROUP, lead * part.shape[0], part.shape[1])
        gathered.append(whole)
    return gathered


def sum_gradients(parts, small, seq, grp):
    lead = seq // 8
    sums = []
    for n, part in enumerate(parts):
        height, lanes = part.shape[2:]
        whole = part.reshape(8, grp, height, lanes)
        if n == 3:
            whole = whole.reshape(8, grp, height, lead, lanes // lead).transpose(0, 3, 1, 2, 4)
        else:
            whole = whole.reshape(8, grp, lead, height // lead, lanes).transpose(0, 2, 1, 3, 4)
        whole = whole.reshape((seq, grp) + whole.shape[3:]).astype(f32)
        whole = lax.psum_scatter(whole, "seq", scatter_dimension=0)
        sums.append(lax.psum_scatter(whole, "grp", scatter_dimension=0))
    return sums + [lax.psum(small, ("seq", "grp"))]


def body(
    tokens,
    coordinates,
    lengths,
    valid,
    first_gain,
    first_shift,
    query_weight,
    query_bias,
    key_weight,
    value_weight,
    value_bias,
    output_weight,
    output_bias,
    second_gain,
    second_shift,
    inner_weight,
    inner_bias,
    outer_weight,
    outer_bias,
    cotangent,
):
    rows, width = tokens.shape
    grp = lax.axis_size("grp")
    seq = lax.axis_size("seq")
    near = (seq, grp) == (8, 4)
    slides = lengths.shape[0]
    shard = query_weight.shape[0]
    heads = [w.reshape(shard, 4, 1, HD) for w in (query_weight, key_weight, value_weight)]
    parts = [
        jnp.concatenate(heads, axis=2).reshape(shard, 576),
        output_weight,
        inner_weight,
        outer_weight.T,
    ]
    joint_bias = jnp.stack(
        [b.reshape(4, 4, HD) for b in (query_bias, jnp.zeros_like(query_bias), value_bias)], axis=2
    ).reshape(4, 1, 576)
    local = jnp.concatenate([valid[:, None], coordinates], axis=1).astype(f32)
    local = local.reshape(BLOCK, 2, 2, 2, 2, 3).transpose(5, 4, 3, 2, 1, 0).reshape(3, rows)
    local = jnp.concatenate([local, jnp.zeros((5, rows), f32)], axis=0)
    frequency = jnp.exp(jnp.arange(192, dtype=jnp.float32) * (-math.log(10000.0) / 192))
    vectors = [
        first_gain, first_shift, output_bias, second_gain, second_shift, outer_bias, inner_bias,
        jnp.zeros((6 * width,), f32),
    ]
    vectors = jnp.concatenate(vectors).reshape(16, width)
    inputs = [
        tokens.reshape(BLOCK, 16, width), cotangent.reshape(BLOCK, 16, width), local, lengths,
        jnp.concatenate([frequency, frequency]).reshape(1, 384), vectors, joint_bias,
    ]
    weights = parts if near else all_weights(parts, seq, grp)
    results = attention_forward(grp, slides, near, inputs, weights)
    base, msg, q_rows, kv_rows, kv8, kv16, stat, out, grad_middle, grad_merged, small = results[:11]
    late = results[11:14]
    joint_weight = results[14] if near else weights[0]
    saved = [
        grad_merged, vectors, small, q_rows, kv_rows, kv8, kv16, msg, stat, base, grad_middle,
        joint_weight,
    ]
    results = attention_backward(grp, near, saved, late if near else [])
    token_grad, joint_sum, pack = results[:3]
    if near:
        sums = results[3:]
    else:
        joint_sum, *sums, pack = sum_gradients([joint_sum] + list(late), pack, seq, grp)
    results = finish(out, token_grad, joint_sum, *sums, pack)
    output, token_grad = [item.reshape(rows, width) for item in results[:2]]
    sum_query, sum_key, sum_value, sum_output, sum_inner, sum_outer = results[2:8]
    small = results[8:]
    return (
        output,
        token_grad,
        small[0],
        small[1],
        sum_query,
        small[2],
        sum_key,
        sum_value,
        small[3],
        sum_output,
        small[4],
        small[5],
        small[6],
        sum_inner,
        small[7],
        sum_outer,
        small[8],
    )


def solution(mesh):
    placed = (
        P(("seq", "grp"), None),
        P(("seq", "grp"), None),
        P(),
        P(("seq", "grp")),
        P(),
        P(),
        P("seq", "grp"),
        P(),
        P("seq", "grp"),
        P("seq", "grp"),
        P(),
        P("seq", "grp"),
        P(),
        P(),
        P(),
        P("seq", "grp"),
        P(),
        P("seq", "grp"),
        P(),
        P(("seq", "grp"), None),
    )
    return jax.shard_map(
        body,
        mesh=mesh,
        in_specs=placed,
        out_specs=(
            P(("seq", "grp"), None),
            P(("seq", "grp"), None),
            P(),
            P(),
            P("seq", "grp"),
            P(),
            P("seq", "grp"),
            P("seq", "grp"),
            P(),
            P("seq", "grp"),
            P(),
            P(),
            P(),
            P("seq", "grp"),
            P(),
            P("seq", "grp"),
            P(),
        ),
        check_vma=False,
    )
```

```python
import functools
import math

import jax
import jax.numpy as jnp
import numpy as np
from jax import lax
from jax.experimental import pallas as pl
from jax.experimental.pallas import tpu as pltpu
from jax.sharding import PartitionSpec as P

epsilon = 1e-05


NT = (((1,), (1,)), ((), ()))
NN = (((1,), (0,)), ((), ()))
f32 = jnp.float32
bf16 = jnp.bfloat16
BIG = 1e30
HD = 48
GROUP = 8
LANES = 128
BLOCK = 32
MSG = 160
FLAG = 2 * HD
MESH = pl.DeviceIdType.MESH
scale = HD ** (-0.5)
scale2 = scale * math.log2(math.e)
q_at = (0, 4096, 6144, 7168, 7680)
q_all = 7936
k_all = 9216


def reverse4(b):
    return (b & 1) * 8 + (b & 2) * 2 + (b & 4) // 2 + (b & 8) // 8


order = [reverse4(b) for b in range(16)]


def chunk_swap(head):
    return reverse4(head) >> 2


def block_swap(quad):
    return reverse4(4 * quad) & 3


def swap_blocks(rows, quad):
    return jnp.concatenate(
        [rows[BLOCK * (b ^ block_swap(quad)) :][:BLOCK] for b in range(16)], axis=0
    )


def swap_chunks(wide, head):
    return jnp.concatenate(
        [wide[:, LANES * (c ^ chunk_swap(head)) :][:, :LANES] for c in range(4)], axis=1
    )


def matmul(a, b, dims=NN):
    return lax.dot_general(a, b, dims, preferred_element_type=f32)


def column_sum(values):
    return jnp.sum(values, axis=0, keepdims=True)


def pick(ref, g):
    both = jnp.stack([ref[:, g], ref[:, g + 4]], axis=1)
    return both.reshape(768, ref.shape[3])


def put(ref, g, value):
    value = value.reshape(4, 2, 96, ref.shape[3])
    ref[:, g] = value[:, 0]
    ref[:, g + 4] = value[:, 1]


def vmem():
    return pl.BlockSpec(memory_space=pltpu.VMEM)


def anywhere():
    return pl.BlockSpec(memory_space=pl.ANY)


def sems(*dims):
    return pltpu.SemaphoreType.DMA(dims)


def params(identity=None):
    if identity is None:
        return pltpu.CompilerParams(vmem_limit_bytes=60 << 20)
    return pltpu.CompilerParams(
        vmem_limit_bytes=60 << 20, collective_id=identity, has_side_effects=True
    )


def shape(dims, dtype):
    return jax.ShapeDtypeStruct(dims, dtype)


def remote(src, dst, send_sem, recv_sem, target):
    return pltpu.make_async_remote_copy(
        src_ref=src, dst_ref=dst, send_sem=send_sem, recv_sem=recv_sem,
        device_id=target, device_id_type=MESH,
    )


class Spot:
    def __init__(self, grp):
        self.grp = grp
        self.linear = lax.axis_index("seq") * grp + lax.axis_index("grp")
        self.member = self.linear % GROUP
        self.base = self.linear - self.member
        self.layer = self.linear // GROUP % 4
        self.half = self.layer % 2

    def device(self, linear):
        return (linear // self.grp, linear % self.grp)

    def beside(self, j):
        return self.device(self.base + j)

    def over(self, layer):
        return self.device(self.linear + GROUP * (layer - self.layer))

    def pair(self):
        return self.device(self.linear + GROUP - 2 * GROUP * self.half)

    def greet(self):
        barrier = pltpu.get_barrier_semaphore()
        for j in range(GROUP):

            @pl.when(self.member != j)
            def _():
                pl.semaphore_signal(barrier, inc=1, device_id=self.beside(j), device_id_type=MESH)

        for o in range(1, 4):
            target = self.over((self.layer + o) % 4)
            pl.semaphore_signal(barrier, inc=1, device_id=target, device_id_type=MESH)
        return lambda: pl.semaphore_wait(barrier, GROUP + 2)


class Exchange:
    def __init__(self, spot, send, recv, send_sem, recv_sem):
        self.spot, self.send_ref, self.recv = spot, send, recv
        self.send_sem, self.recv_sem = send_sem, recv_sem

    def out(self, j):
        s = self.spot
        return remote(self.send_ref.at[j], self.recv.at[s.member], self.send_sem.at[j],
                      self.recv_sem.at[s.member], s.beside(j))

    def inner(self, j):
        return pltpu.make_async_copy(self.send_ref.at[j], self.recv.at[j], self.recv_sem.at[j])

    def choose(self, j, far, near):
        pl.when(self.spot.member != j)(far)
        pl.when(self.spot.member == j)(near)

    def send(self, j):
        self.choose(j, lambda: self.out(j).start(), lambda: self.inner(j).start())

    def wait(self, j):
        def far():
            remote(self.send_ref.at[j], self.recv.at[j], self.send_sem.at[j], self.recv_sem.at[j],
                   self.spot.beside(j)).wait_recv()

        self.choose(j, far, lambda: self.inner(j).wait())

    def drain(self):
        for j in range(GROUP):
            pl.when(self.spot.member != j)(lambda j=j: self.out(j).wait_send())


class Deep:
    def __init__(self, spot, eight, sixteen, send_sem, recv_sem):
        self.copies, self.waits = [], []
        s = spot
        for o in range(1, 4):
            other = (s.layer + o) % 4
            src, there, here = sixteen(o, other)
            self.copies.append(remote(src, there, send_sem.at[o], recv_sem.at[4 - o], s.over(other)))
            self.waits.append(remote(src, here, send_sem.at[o], recv_sem.at[o], s.over(other)))
        src, there, here = eight
        self.copies.append(remote(src, there, send_sem.at[0], recv_sem.at[0], s.pair()))
        self.waits.append(remote(src, here, send_sem.at[0], recv_sem.at[0], s.pair()))

    def start(self):
        for copy in self.copies:
            copy.start()

    def wait(self):
        for copy in self.waits:
            copy.wait_recv()

    def drain(self):
        for copy in self.copies:
            copy.wait_send()


def member_of(x, y, c):
    return x * 4 + y * 2 + c


def place():
    seq, col = lax.axis_index("seq"), lax.axis_index("grp")
    return seq // 2, seq % 2, col // 2, col % 2


def at_place(z, x, y, c):
    return (z * 2 + x, y * 2 + c)


def gather_sems(count):
    return [
        sems(count), sems(4, count), sems(4, count), sems(2, 4, count), sems(2, 4, count),
        sems(2, 4, count), sems(2, 4, count), sems(4, count), sems(4, count),
    ]


class Gather:
    def __init__(self, ins, outs, semaphores):
        self.ins, self.outs = ins, outs
        (self.loc, self.zs, self.zr, self.ps, self.pr,
         self.qs, self.qr, self.cs, self.cr) = semaphores
        self.place = z, x, y, c = place()
        self.me = member_of(x, y, c)
        self.arrays = range(len(ins))
        self.near = [(1 - x, y), (x, 1 - y)]
        self.started = []
        self.done = 0
        self.local = [
            pltpu.make_async_copy(ins[k], outs[k].at[z, self.me], self.loc.at[k])
            for k in self.arrays
        ]
        self.stages = [self.stage1, self.stage2, self.stage3, self.stage4, self.stage5, self.stage6]

    def go(self, copy):
        copy.start()
        self.started.append(copy)

    def start_layers(self):
        z, x, y, c = self.place
        for copy in self.local:
            copy.start()
        for o in (1, 2, 3):
            for k in self.arrays:
                self.go(remote(self.ins[k], self.outs[k].at[z, self.me], self.zs.at[o, k],
                               self.zr.at[4 - o, k], at_place((z + o) % 4, x, y, c)))

    def push(self, layer, slot, sources):
        z, x, y, c = self.place
        for p, (px, py) in enumerate(self.near):
            for k in self.arrays:
                self.go(remote(sources[k], self.outs[k].at[layer, self.me], self.ps.at[p, slot, k],
                               self.pr.at[p, slot, k], at_place(z, px, py, c)))

    def start_plane(self):
        self.push(self.place[0], 0, self.ins)

    def relay(self, slot):
        z, x, y, c = self.place
        layer = (z + slot) % 4
        for p, (px, py) in enumerate(self.near):
            m = member_of(px, py, c)
            for k in self.arrays:
                part = self.outs[k].at[layer, m]
                remote(part, part, self.ps.at[p, slot, k], self.pr.at[p, slot, k],
                       at_place(z, px, py, c)).wait_recv()
        for k in self.arrays:
            rows = self.ins[k].shape[0] // 2
            for p, (px, py) in enumerate(self.near):
                part = self.outs[k].at[layer, member_of(px, py, c), p * rows : (p + 1) * rows]
                self.go(remote(part, part, self.qs.at[p, slot, k], self.qr.at[p, slot, k],
                               at_place(z, *self.near[1 - p], c)))

    def layer_step(self, o):
        z, x, y, c = self.place
        layer = (z + o) % 4
        parts = [self.outs[k].at[layer, self.me] for k in self.arrays]
        for k in self.arrays:
            remote(parts[k], parts[k], self.zs.at[o, k], self.zr.at[o, k],
                   at_place(layer, x, y, c)).wait_recv()
        self.push(layer, o, parts)

    def stage1(self):
        for copy in self.local:
            copy.wait()
        self.layer_step(1)
        self.relay(0)

    def stage2(self):
        self.layer_step(2)
        self.relay(1)

    def stage3(self):
        self.layer_step(3)
        self.relay(2)

    def across(self, slot, px, py):
        z, x, y, c = self.place
        m = member_of(px, py, c)
        for k in self.arrays:
            part = self.outs[k].at[:, m]
            self.go(remote(part, part, self.cs.at[slot, k], self.cr.at[slot, k],
                           at_place(z, x, y, 1 - c)))

    def stage4(self):
        z, x, y, c = self.place
        self.across(0, x, y)
        self.relay(3)
        self.across(1, 1 - x, y)
        self.across(2, x, 1 - y)

    def stage5(self):
        z, x, y, c = self.place
        far = member_of(1 - x, 1 - y, c)
        for slot in range(4):
            layer = (z + slot) % 4
            for k in self.arrays:
                rows = self.ins[k].shape[0] // 2
                for p in range(2):
                    part = self.outs[k].at[layer, far, p * rows : (p + 1) * rows]
                    remote(part, part, self.qs.at[p, slot, k], self.qr.at[p, slot, k],
                           at_place(z, *self.near[1 - p], c)).wait_recv()
        self.across(3, 1 - x, 1 - y)

    def stage6(self):
        z, x, y, c = self.place
        for slot, (px, py) in enumerate([(x, y), (1 - x, y), (x, 1 - y), (1 - x, 1 - y)]):
            m = member_of(px, py, 1 - c)
            for k in self.arrays:
                part = self.outs[k].at[:, m]
                remote(part, part, self.cs.at[slot, k], self.cr.at[slot, k],
                       at_place(z, x, y, 1 - c)).wait_recv()

    def advance(self, upto):
        while self.done < upto:
            self.stages[self.done]()
            self.done += 1

    def finish(self):
        self.advance(6)

    def drain(self):
        for copy in self.started:
            copy.wait_send()


def gather_wide_sems():
    return [sems(1), sems(2), sems(2), sems(2), sems(2), sems(4, 4), sems(4, 4), sems(4, 4), sems(4, 4)]


class GatherWide:
    def __init__(self, source, out, semaphores):
        self.source, self.out = source, out
        (self.loc, self.ps, self.pr, self.qs, self.qr, self.zs, self.zr, self.cs, self.cr) = semaphores
        self.place = z, x, y, c = place()
        self.near = [(1 - x, y), (x, 1 - y)]
        self.spots = [(x, y), (1 - x, y), (x, 1 - y), (1 - x, 1 - y)]
        self.started = []
        self.done = 0
        self.stages = [self.stage1, self.stage2, self.stage3, self.stage4, self.stage5]

    def go(self, copy):
        copy.start()
        self.started.append(copy)

    def block(self, layer, p, c):
        return self.out.at[layer, member_of(*p, c)]

    def start(self):
        z, x, y, c = self.place
        self.local = pltpu.make_async_copy(self.source, self.block(z, (x, y), c), self.loc.at[0])
        self.local.start()
        for n, p in enumerate(self.near):
            self.go(remote(self.source, self.block(z, (x, y), c), self.ps.at[n], self.pr.at[n],
                           at_place(z, *p, c)))

    def up(self, slot):
        z, x, y, c = self.place
        part = self.block(z, self.spots[slot], c)
        for o in (1, 2, 3):
            self.go(remote(part, part, self.zs.at[o, slot], self.zr.at[4 - o, slot],
                           at_place((z + o) % 4, x, y, c)))

    def swap(self, o, slot):
        z, x, y, c = self.place
        part = self.block((z + o) % 4, self.spots[slot], c)
        self.go(remote(part, part, self.cs.at[o, slot], self.cr.at[o, slot],
                       at_place(z, x, y, 1 - c)))

    def stage1(self):
        z, x, y, c = self.place
        self.local.wait()
        self.up(0)
        self.swap(0, 0)
        rows = self.source.shape[0] // 2
        for n, p in enumerate(self.near):
            part = self.block(z, p, c)
            remote(part, part, self.ps.at[n], self.pr.at[n], at_place(z, *p, c)).wait_recv()
            part = self.out.at[z, member_of(*p, c), n * rows : (n + 1) * rows]
            self.go(remote(part, part, self.qs.at[n], self.qr.at[n],
                           at_place(z, *self.near[1 - n], c)))
            self.up(1 + n)
            self.swap(0, 1 + n)

    def stage2(self):
        z, x, y, c = self.place
        rows = self.source.shape[0] // 2
        for n in range(2):
            part = self.out.at[z, member_of(*self.spots[3], c), n * rows : (n + 1) * rows]
            remote(part, part, self.qs.at[n], self.qr.at[n],
                   at_place(z, *self.near[1 - n], c)).wait_recv()
        self.up(3)
        self.swap(0, 3)

    def arrive(self, slots):
        z, x, y, c = self.place
        for slot in slots:
            for o in (1, 2, 3):
                layer = (z + o) % 4
                part = self.block(layer, self.spots[slot], c)
                remote(part, part, self.zs.at[o, slot], self.zr.at[o, slot],
                       at_place(layer, x, y, c)).wait_recv()
                self.swap(o, slot)

    def stage3(self):
        self.arrive((0, 1))

    def stage4(self):
        self.arrive((2, 3))

    def stage5(self):
        z, x, y, c = self.place
        for o in range(4):
            for slot in range(4):
                part = self.block((z + o) % 4, self.spots[slot], 1 - c)
                remote(part, part, self.cs.at[o, slot], self.cr.at[o, slot],
                       at_place(z, x, y, 1 - c)).wait_recv()

    def advance(self, upto):
        while self.done < upto:
            self.stages[self.done]()
            self.done += 1

    def drain(self):
        for copy in self.started:
            copy.wait_send()


def reduce_scratch(dims):
    half = [(rows // 2, lanes) for rows, lanes in dims]
    count = len(dims)
    return (
        [pltpu.VMEM((4,) + d, bf16) for d in dims]
        + [pltpu.VMEM((4, 4) + d, bf16) for d in dims]
        + [pltpu.VMEM((4, 4) + d, bf16) for d in half]
        + [pltpu.VMEM((2, 4) + d, bf16) for d in half]
        + [pltpu.VMEM((4,) + d, bf16) for d in dims]
        + [sems(4, count), sems(4, count), sems(4, count)]
        + [sems(3, count) for _ in range(4)]
        + [sems(4, count), sems(4, count)]
    )


def add_to(target, source):
    def step(i, _):
        target[i] = (target[i].astype(f32) + source[i].astype(f32)).astype(bf16)
        return 0

    lax.fori_loop(0, 4, step, 0)


class Reduce:
    def __init__(self, ins, outs, scratch):
        count = len(ins)
        self.ins, self.outs, self.arrays = ins, outs, range(count)
        self.stage, self.across, self.one, self.two, self.deep = [
            scratch[i * count : (i + 1) * count] for i in range(5)
        ]
        (self.loc, self.cs, self.cr, self.xs, self.xr, self.ys, self.yr, self.zs, self.zr) = scratch[
            5 * count :
        ]
        self.place = z, x, y, c = place()
        self.mine, self.px, self.py, self.far = (x, y), (1 - x, y), (x, 1 - y), (1 - x, 1 - y)
        self.other = at_place(z, x, y, 1 - c)
        self.to_x, self.to_y = at_place(z, *self.px, c), at_place(z, *self.py, c)
        self.started = []
        self.done = 0
        self.stages = [self.stage1, self.stage2, self.stage3, self.stage4, self.stage5, self.stage6]

    def slot(self, p):
        return p[0] * 2 + p[1]

    def held(self, k, p):
        if self.stage[k] is None:
            return self.ins[k].at[:, member_of(*p, self.place[3])]
        return self.across[k].at[self.slot(p)]

    def go(self, copy):
        copy.start()
        self.started.append(copy)

    def theirs(self, n, p, k):
        c = self.place[3]
        return remote(self.ins[k].at[:, member_of(*p, 1 - c)], self.across[k].at[self.slot(p)],
                      self.cs.at[n, k], self.cr.at[n, k], self.other)

    def ours(self, n, p, k):
        c = self.place[3]
        return pltpu.make_async_copy(self.ins[k].at[:, member_of(*p, c)],
                                     self.stage[k], self.loc.at[n, k])

    def start(self):
        for n, p in enumerate((self.far, self.px, self.py, self.mine)):
            for k in self.arrays:
                self.go(self.theirs(n, p, k))
                if n == 0 and self.stage[k] is not None:
                    self.ours(n, p, k).start()

    def landed(self, n, p):
        for k in self.arrays:
            self.theirs(n, p, k).wait_recv()
            if self.stage[k] is None:
                add_to(self.held(k, p), self.across[k].at[self.slot(p)])
                continue
            self.ours(n, p, k).wait()
            add_to(self.held(k, p), self.stage[k])
            if n < 3:
                self.ours(n + 1, (self.far, self.px, self.py, self.mine)[n + 1], k).start()

    def part(self, k, p, along_x):
        rows = self.ins[k].shape[2] // 2
        at = 0 if along_x else rows
        return self.held(k, p).at[:, at : at + rows]

    def hop(self, k, p, along_x, i, target):
        source = self.part(k, p, along_x)
        if along_x:
            return remote(source, target, self.xs.at[i, k], self.xr.at[i, k], self.to_x)
        return remote(source, target, self.ys.at[i, k], self.yr.at[i, k], self.to_y)

    def first(self, k, p, along_x):
        i = 0 if p is self.far else 1
        return self.hop(k, p, along_x, i, self.one[k].at[2 * i + (0 if along_x else 1)])

    def second(self, k, along_x):
        if along_x:
            return remote(self.part(k, self.py, True), self.two[k].at[0], self.ys.at[2, k],
                          self.yr.at[2, k], self.to_y)
        return remote(self.part(k, self.px, False), self.two[k].at[1], self.xs.at[2, k],
                      self.xr.at[2, k], self.to_x)

    def stage1(self):
        self.landed(0, self.far)
        for k in self.arrays:
            self.go(self.first(k, self.far, True))
            self.go(self.first(k, self.far, False))

    def stage2(self):
        self.landed(1, self.px)
        for k in self.arrays:
            self.go(self.first(k, self.px, True))
        self.landed(2, self.py)
        for k in self.arrays:
            self.go(self.first(k, self.py, False))

    def stage3(self):
        self.landed(3, self.mine)
        for k in self.arrays:
            for along_x, p in ((True, self.py), (False, self.px)):
                self.first(k, self.far, along_x).wait_recv()
                add_to(self.part(k, p, along_x), self.one[k].at[0 if along_x else 1])
                self.go(self.second(k, along_x))

    def stage4(self):
        for k in self.arrays:
            for along_x, p in ((True, self.px), (False, self.py)):
                self.first(k, p, along_x).wait_recv()
                add_to(self.part(k, self.mine, along_x), self.one[k].at[2 if along_x else 3])

    def last(self, k, o):
        z, x, y, c = self.place
        layer = (z + o) % 4
        return remote(self.held(k, self.mine).at[layer], self.deep[k].at[4 - o],
                      self.zs.at[o, k], self.zr.at[4 - o, k], at_place(layer, x, y, c))

    def stage5(self):
        for k in self.arrays:
            for along_x in (True, False):
                self.second(k, along_x).wait_recv()
                add_to(self.part(k, self.mine, along_x), self.two[k].at[0 if along_x else 1])
            for o in (1, 2, 3):
                self.go(self.last(k, o))

    def stage6(self):
        z, x, y, c = self.place
        for k in self.arrays:
            value = self.held(k, self.mine)[z].astype(f32)
            for o in (1, 2, 3):
                here = self.deep[k].at[o]
                remote(here, here, self.zs.at[o, k], self.zr.at[o, k],
                       at_place((z + o) % 4, x, y, c)).wait_recv()
                value = value + self.deep[k][o].astype(f32)
            self.outs[k][...] = value

    def advance(self, upto):
        while self.done < upto:
            self.stages[self.done]()
            self.done += 1

    def drain(self):
        for copy in self.started:
            copy.wait_send()


class Total:
    def __init__(self, small, out, scratch):
        self.small, self.out = small, out
        self.at_c, self.at_p, self.at_z, self.ss, self.rs = scratch
        self.place = z, x, y, c = place()
        self.plane = ((1 - x, y), (x, 1 - y), (1 - x, 1 - y))
        self.started = []

    def swap(self, buffer, index, n, m, target):
        here = buffer.at[index]
        copy = remote(here, here, self.ss.at[n], self.rs.at[m], target)
        copy.start()
        self.started.append(copy)

    def arrive(self, buffer, index, n, target):
        here = buffer.at[index]
        remote(here, here, self.ss.at[n], self.rs.at[n], target).wait_recv()

    def start(self):
        z, x, y, c = self.place
        self.at_c[c] = self.small[...]
        self.swap(self.at_c, c, 0, 0, at_place(z, x, y, 1 - c))

    def middle(self):
        z, x, y, c = self.place
        self.arrive(self.at_c, 1 - c, 0, at_place(z, x, y, 1 - c))
        self.at_p[x * 2 + y] = self.at_c[0] + self.at_c[1]
        for n, p in enumerate(self.plane):
            self.swap(self.at_p, x * 2 + y, 1 + n, 1 + n, at_place(z, *p, c))

    def late(self):
        z, x, y, c = self.place
        for n, p in enumerate(self.plane):
            self.arrive(self.at_p, p[0] * 2 + p[1], 1 + n, at_place(z, *p, c))
        self.at_z[z] = (self.at_p[0] + self.at_p[1]) + (self.at_p[2] + self.at_p[3])
        for o in (1, 2, 3):
            self.swap(self.at_z, z, 3 + o, 7 - o, at_place((z + o) % 4, x, y, c))

    def finish(self):
        z, x, y, c = self.place
        for o in (1, 2, 3):
            self.arrive(self.at_z, (z + o) % 4, 3 + o, at_place((z + o) % 4, x, y, c))
        self.out[...] = (self.at_z[0] + self.at_z[1]) + (self.at_z[2] + self.at_z[3])
        for copy in self.started:
            copy.wait_send()


def total_scratch(dims):
    return [
        pltpu.VMEM((2,) + dims, f32), pltpu.VMEM((4,) + dims, f32), pltpu.VMEM((4,) + dims, f32),
        sems(7), sems(7),
    ]


def reduce_wide_scratch(dims):
    rows, lanes = dims
    return [
        pltpu.VMEM((4,) + dims, bf16), pltpu.VMEM((4, 4) + dims, bf16),
        pltpu.VMEM((4, 4) + dims, bf16), pltpu.VMEM((4, rows // 2, lanes), bf16),
        pltpu.VMEM((2, rows // 2, lanes), bf16),
        sems(4), sems(4), sems(4), sems(4, 4), sems(4, 4), sems(4), sems(4), sems(2), sems(2),
    ]


class ReduceWide:
    def __init__(self, source, out, scratch):
        self.source, self.out = source, out
        (self.stage, self.own, self.deep, self.one, self.two, self.loc, self.cs, self.cr, self.zs,
         self.zr, self.ps, self.pr, self.qs, self.qr) = scratch
        self.place = z, x, y, c = place()
        self.spots = [(x, y), (1 - x, y), (x, 1 - y), (1 - x, 1 - y)]
        self.other = at_place(z, x, y, 1 - c)
        self.to_x, self.to_y = at_place(z, 1 - x, y, c), at_place(z, x, 1 - y, c)
        self.rows = source.shape[2] // 2
        self.started = []
        self.done = 0
        self.stages = [self.stage1, self.stage2, self.stage3, self.stage4, self.stage5, self.stage6]

    def go(self, copy):
        copy.start()
        self.started.append(copy)

    def theirs(self, n):
        c = self.place[3]
        return remote(self.source.at[:, member_of(*self.spots[n], 1 - c)], self.own.at[n],
                      self.cs.at[n], self.cr.at[n], self.other)

    def ours(self, n):
        c = self.place[3]
        return pltpu.make_async_copy(self.source.at[:, member_of(*self.spots[n], c)],
                                     self.stage, self.loc.at[n])

    def start(self):
        for n in range(4):
            self.go(self.theirs(n))
        self.ours(0).start()

    def landed(self, n):
        z, x, y, c = self.place
        self.ours(n).wait()
        self.theirs(n).wait_recv()
        add_to(self.own.at[n], self.stage)
        if n < 3:
            self.ours(n + 1).start()
        for o in (1, 2, 3):
            layer = (z + o) % 4
            self.go(remote(self.own.at[n, layer], self.deep.at[n, 4 - o], self.zs.at[o, n],
                           self.zr.at[4 - o, n], at_place(layer, x, y, c)))

    def stage1(self):
        self.landed(0)
        self.landed(1)

    def stage2(self):
        self.landed(2)
        self.landed(3)

    def gathered(self, n):
        z, x, y, c = self.place
        total = self.own[n, z].astype(f32)
        for o in (1, 2, 3):
            here = self.deep.at[n, o]
            remote(here, here, self.zs.at[o, n], self.zr.at[o, n],
                   at_place((z + o) % 4, x, y, c)).wait_recv()
            total = total + self.deep[n, o].astype(f32)
        self.own[n, z] = total.astype(bf16)

    def part(self, n, along_x):
        at = 0 if along_x else self.rows
        return self.own.at[n, self.place[0], at : at + self.rows]

    def first(self, i):
        n, along_x = ((3, True), (3, False), (1, True), (2, False))[i]
        return remote(self.part(n, along_x), self.one.at[i], self.ps.at[i], self.pr.at[i],
                      self.to_x if along_x else self.to_y)

    def second(self, along_x):
        if along_x:
            return remote(self.part(2, True), self.two.at[0], self.qs.at[0], self.qr.at[0], self.to_y)
        return remote(self.part(1, False), self.two.at[1], self.qs.at[1], self.qr.at[1], self.to_x)

    def add(self, n, along_x, source):
        at = 0 if along_x else self.rows
        z = self.place[0]
        rows = slice(at, at + self.rows)
        self.own[n, z, rows] = (
            self.own[n, z, rows].astype(f32) + source[...].astype(f32)
        ).astype(bf16)

    def stage3(self):
        for n in (0, 1, 2, 3):
            self.gathered(n)
        for i in range(4):
            self.go(self.first(i))

    def stage4(self):
        for i, (n, along_x) in enumerate(((2, True), (1, False))):
            self.first(i).wait_recv()
            self.add(n, along_x, self.one.at[i])
            self.go(self.second(along_x))

    def stage5(self):
        for i, along_x in ((2, True), (3, False)):
            self.first(i).wait_recv()
            self.add(0, along_x, self.one.at[i])

    def stage6(self):
        z = self.place[0]
        for i, along_x in ((0, True), (1, False)):
            self.second(along_x).wait_recv()
            at = 0 if along_x else self.rows
            rows = slice(at, at + self.rows)
            self.out[rows] = self.own[0, z, rows].astype(f32) + self.two[i].astype(f32)

    def advance(self, upto):
        while self.done < upto:
            self.stages[self.done]()
            self.done += 1

    def drain(self):
        for copy in self.started:
            copy.wait_send()


def norm_parts(values):
    average = jnp.mean(values, axis=-1, keepdims=True)
    centred = values - average
    variance = jnp.mean(centred * centred, axis=-1, keepdims=True)
    inverse = lax.rsqrt(variance + epsilon)
    return centred * inverse, inverse


def norm_backward(hat, inverse, gain, grad):
    scaled = grad * gain
    first = jnp.mean(scaled, axis=-1, keepdims=True)
    second = jnp.mean(scaled * hat, axis=-1, keepdims=True)
    return (scaled - first - hat * second) * inverse


def compact(j, rows, packed, places):
    for place, size in places:
        packed[place + size * j : place + size * j + size] = rows[:size]


def widen(pieces):
    total = pieces[-1]
    for piece in reversed(pieces[:-1]):
        blank = jnp.zeros((piece.shape[0], piece.shape[1] - total.shape[1]), f32)
        total = piece + jnp.concatenate([total, blank], axis=1)
    return total


def join_quad(quad, read):
    wide = jnp.concatenate(
        [swap_chunks(read(4 * quad + i), 4 * quad + i) for i in range(4)], axis=0
    )
    return swap_blocks(wide.T, quad)


def join_quads(read):
    pairs = []
    for half in range(2):
        pairs.append(
            jnp.concatenate([join_quad(quad, read) for quad in (2 * half, 2 * half + 1)], axis=1)
        )
    return jnp.concatenate(pairs, axis=1)


def unit_forward(query, key, out):
    lane = lax.broadcasted_iota(jnp.int32, (256, LANES), 1)
    count = len(query)
    scores = [matmul(query[i](), key, NT) for i in range(count)]
    for i in range(count):
        top = jnp.max(scores[i], axis=1, keepdims=True) * scale2
        prob = jnp.exp2(scores[i] * scale2 - top).astype(bf16)
        value = jnp.where(lane == FLAG + 8, top, matmul(prob, key))
        out[i](value.T[HD : HD + 64])


def forward_kernel(grp, slides, gather, *refs):
    refs = list(refs)
    take = lambda n: [refs.pop(0) for _ in range(n)]
    tokens, cot_in, valid, coordinates, ends, frequency = take(6)
    vectors, in_bias = take(6), take(1)[0]
    query_bias, value_bias = take(2)
    shards = take(6) if gather else take(0)
    given = take(0) if gather else take(4)
    base, msg, q_ref, kv_ref, kv8, kv16, stat = take(7)
    out, grad_middle, grad_merged, small = take(4)
    late_grads = take(3)
    gathered = take(1) if gather else take(0)
    send, osend, orecv, acc, qc, kvc, tok_sem, ss, rs, os_, or_, ds, dr = take(13)
    wo, wi, wt = take(3)
    dense_scratch = take(9)
    raw, save_sem = take(2)
    weight = gathered[0] if gather else given[0]
    cot = dense_scratch[0]
    spot = Spot(grp)
    joined = spot.greet()

    def load(source):
        copies = []
        for c in range(6):
            part = source.at[:, LANES * c : LANES * c + LANES]
            copies.append(pltpu.make_async_copy(part, raw.at[c], tok_sem.at[c]))
            copies[-1].start()
        return copies

    def ordered(copies, target):
        for copy in copies:
            copy.wait()
        for b in range(16):
            rows = [raw[c, pl.ds(order[b], BLOCK, stride=16), :] for c in range(6)]
            target[BLOCK * b : BLOCK * b + BLOCK] = jnp.concatenate(rows, axis=1)

    loads = load(tokens)
    vectors = [item[...].reshape(1, 768) for item in vectors]
    if gather:
        joint_shard, turned = take(2)
        pieces = []
        for inner in range(4):
            pieces += [item[:, HD * inner : HD * inner + HD] for item in shards[:3]]
        joint_shard[...] = jnp.concatenate(pieces, axis=1)
        turned[...] = shards[5][...].T
        first = Gather([joint_shard], gathered[:1], take(9))
        rest = Gather([shards[3], turned], [wo, wt], take(9))
        wide_part = GatherWide(shards[4], wi, take(9))
        joined()
        first.start_layers()
        first.start_plane()
        wide_part.start()
        rest.start_layers()
    else:
        loads_late = [
            pltpu.make_async_copy(source, target, save_sem.at[n])
            for n, (source, target) in enumerate(zip(given[1:], (wo, wi, wt)))
        ]
        for copy in loads_late:
            copy.start()
    place_lane = lax.broadcasted_iota(jnp.int32, (1, 512), 1)
    b = place_lane // BLOCK
    b = (b % 2) * 8 + (b // 2 % 2) * 4 + (b // 4 % 2) * 2 + b // 8
    position = spot.linear * 512 + place_lane % BLOCK * 16 + b
    keep = valid[...].astype(f32).T
    keep = jnp.concatenate([keep[b : b + 1] for b in order], axis=1)
    turned_places = coordinates[...].astype(f32).T
    columns = jnp.concatenate([turned_places[2 * b : 2 * b + 1] for b in order], axis=1)
    heights = jnp.concatenate([turned_places[2 * b + 1 : 2 * b + 2] for b in order], axis=1)
    spots = jnp.concatenate([columns, heights, jnp.zeros((6, 512), f32)], axis=0).T
    lines = [jnp.where(keep == 1.0, 0.0, -BIG)]
    before = 0
    for n in range(slides):
        after = before + ends[n]
        inside = (position >= before) & (position < after)
        lines.append(jnp.where(inside, 0.0, -BIG))
        before = after
    lines += [jnp.ones((1, 512), f32), jnp.zeros((14 - slides, 512), f32)]
    flags_all = jnp.concatenate(lines, axis=0)
    gain, shift = vectors[:2]
    lane = lax.broadcasted_iota(jnp.int32, (512, 384), 1)
    angle = jnp.where(lane < 192, spots[:, 0:1], spots[:, 1:2]) * frequency[...]
    sine, cosine = jnp.sin(angle), jnp.cos(angle)
    table = jnp.concatenate(
        [
            jnp.concatenate([sine[:, :192], cosine[:, :192]], axis=1),
            jnp.concatenate([sine[:, 192:], cosine[:, 192:]], axis=1),
        ],
        axis=1,
    )
    ordered(loads, base)
    base[...] = base[...] + table
    loads = load(cot_in)
    hat, _ = norm_parts(base[...])
    normed = (hat * gain + shift).astype(bf16)
    if gather:
        first.advance(4)
        wide_part.advance(1)
        first.finish()
        wide_part.advance(2)
    else:
        joined()
    qb, vb = query_bias[...].reshape(1, 768), value_bias[...].reshape(1, 768)
    plane = [Exchange(spot, send.at[i], msg.at[i], ss.at[i], rs.at[i]) for i in range(2)]
    for quad in range(4):
        pieces = []
        for inner in range(4):
            at = HD * (4 * quad + inner)
            pieces += [qb[:, at : at + HD], jnp.zeros((1, HD), f32), vb[:, at : at + HD]]
        part = matmul(normed, pick(weight, quad)) + jnp.concatenate(pieces, axis=1)
        wide = swap_blocks(part.astype(bf16), quad).T
        flags = flags_all
        flags = jnp.concatenate(
            [flags[:, BLOCK * (b ^ block_swap(quad)) :][:, :BLOCK] for b in range(16)], axis=1
        ).astype(bf16)
        for inner in (0, 2, 1, 3):
            head = 4 * quad + inner
            owner, i = head // 2, head % 2
            own = swap_chunks(wide[144 * inner : 144 * inner + 144], head)
            send[i, owner, :96] = own[48:]
            send[i, owner, 96:112] = swap_chunks(flags, head)
            send[i, owner, 112:] = own[:48]
            if i == 0:
                plane[0].send(owner)
    for owner in range(GROUP):
        plane[1].send(owner)
    row = lax.broadcasted_iota(jnp.int32, (16, 512), 0)
    deeps = []
    results = [Exchange(spot, osend.at[i], orecv.at[i], os_.at[i], or_.at[i]) for i in range(2)]
    if gather:
        rest.start_plane()
    for i in range(2):
        q, kv = q_ref.at[i], kv_ref.at[i]
        for j in range(GROUP):
            plane[i].wait(j)
            block = msg[i, j]
            key_part = jnp.concatenate([block[:112], jnp.zeros((16, 512), bf16)], axis=0).T
            flags = block[96:112].astype(f32)
            chosen = jnp.where(
                row == 0, 1.0, jnp.where((row <= slides) & (flags == 0.0), 1.0, 0.0)
            )
            query_part = jnp.concatenate(
                [block[112:], jnp.zeros((HD, 512), bf16), chosen.astype(bf16),
                 jnp.zeros((16, 512), bf16)],
                axis=0,
            ).T
            kv[512 * j : 512 * j + 512] = key_part
            q[512 * j : 512 * j + 512] = query_part
            compact(j, query_part, qc, ((0, 256), (2048, 128), (3072, 64), (3584, 32)))
            compact(j, key_part, kvc, ((0, 256), (2048, 128)))
            kv8[spot.half, i, 64 * j : 64 * j + 64] = key_part[:64]
            kv16[spot.layer, i, 32 * j : 32 * j + 32] = key_part[:32]
        own8, own16 = kv8.at[spot.half, i], kv16.at[spot.layer, i]
        deep = Deep(
            spot, (own8, own8, kv8.at[1 - spot.half, i]),
            lambda o, other: (own16, own16, kv16.at[other, i]), ds.at[i], dr.at[i],
        )
        deep.start()
        deeps.append(deep)
        if gather:
            rest.advance(1 + 2 * i)

        def unit(source, q_from, keys, k_from, out_from, count):
            def reader(n):
                return lambda: source[pl.ds(q_from + 256 * n, 256)]

            def writer(n):
                def save(value):
                    acc[:, pl.ds(out_from + 256 * n, 256)] = value

                return save

            unit_forward(
                [reader(n) for n in range(count)], keys[pl.ds(k_from, 1024)],
                [writer(n) for n in range(count)],
            )

        def early(u, _):
            at = pl.multiple_of(u * 1024, 1024)
            unit(q, at, kv, at, at, 4)
            return 0

        lax.fori_loop(0, 4, early, 0)
        if gather:
            rest.advance(2 + 2 * i)

        def late(u, _):
            at = pl.multiple_of(u * 1024, 1024)
            unit(qc, at, kvc, at, pl.multiple_of(at + 4096, 1024), 4)
            return 0

        lax.fori_loop(0, 3, late, 0)
        deep.wait()
        for n in range(2):
            kvc[3072 + 512 * n : 3584 + 512 * n] = kv8[n, i]
        for n in range(4):
            kvc[4096 + 256 * n : 4352 + 256 * n] = kv16[n, i]
        unit(qc, 3072, kvc, 3072, 7168, 2)
        unit(qc, 3584, kvc, 4096, 7680, 1)
        place = lax.broadcasted_iota(jnp.int32, (1, 512), 1)
        uses = jnp.where(place < 32, 5.0, jnp.where(place < 64, 4.0, jnp.where(
            place < 128, 3.0, jnp.where(place < 256, 2.0, 1.0))))
        for j in range(GROUP):
            key = msg[i, j, :HD].astype(f32)
            value = msg[i, j, HD : 2 * HD].astype(f32)
            query = msg[i, j, 112:].astype(f32)
            dropped = msg[i, j, FLAG : FLAG + 1].astype(f32) != 0.0
            own = jnp.where(dropped, column_sum(query * key) * scale2 + jnp.log2(uses), -BIG)
            pieces = [
                acc[:, q_at[r] + (512 >> r) * j : q_at[r] + (512 >> r) * (j + 1)] for r in range(5)
            ]
            top = own
            tops = [piece[HD + 8 : HD + 9] for piece in pieces]
            for item in tops:
                spread = item
                if spread.shape[1] < 512:
                    blank = jnp.full((1, 512 - spread.shape[1]), -BIG, f32)
                    spread = jnp.concatenate([spread, blank], axis=1)
                top = jnp.maximum(top, spread)
            scaled = [
                piece[: HD + 8] * jnp.exp2(item - top[:, : item.shape[1]])
                for piece, item in zip(pieces, tops)
            ]
            mix = widen(scaled)
            weight_own = jnp.exp2(own - top)
            total = mix[HD + 1 + slides : HD + 2 + slides] + weight_own
            result = (mix[:HD] + weight_own * value) / total
            stat[i, j, :HD] = result
            stat[i, j, HD : HD + 8] = jnp.broadcast_to(top + jnp.log2(total), (8, 512))
            osend[i, j] = result.astype(bf16)
            results[i].send(j)
    if gather:
        wide_part.advance(4)
        rest.advance(5)
    for i in range(2):
        for j in range(GROUP):
            results[i].wait(j)
    if gather:
        rest.finish()
        wide_part.advance(5)
        rest.drain()
        wide_part.drain()
        first.drain()
    else:
        for copy in loads_late:
            copy.wait()
    ordered(loads, cot)
    merged = dense_scratch[1]
    merged[...] = join_quads(lambda h: orecv[h % 2, h // 2])
    dense_part(
        merged, base, cot, wo, wi, wt, vectors, in_bias, out, grad_middle, grad_merged, small,
        late_grads, save_sem, *dense_scratch[2:],
    )
    for item in plane + deeps + results:
        item.drain()


def dense_part(
    merged, base, cot, wo, wi, wt, vectors, in_bias, out, grad_middle, grad_merged, small,
    late_grads, save_sem, middle, hat, low, low_t, cot_low, cot_t, grad_low,
):
    out_bias, gain, shift, last_bias = vectors[2:]
    pairs = []
    for g in range(0, 4, 2):
        pair = [pick(wo, g + i) for i in range(2)]
        pairs.append(jnp.concatenate(pair, axis=1))
    full = jnp.concatenate(pairs, axis=1)
    middle[...] = base[...] + matmul(merged[...], full) + out_bias
    normal, inverse = norm_parts(middle[...])
    hat[...] = normal
    low[...] = (normal * gain + shift).astype(bf16)
    low_t[...] = low[...].T
    cot_low[...] = cot[...].astype(bf16)
    cot_t[...] = cot_low[...].T
    out[...] = middle[...] + last_bias
    small[0:1] = column_sum(cot_low[...].astype(f32))
    grad_middle[...] = jnp.zeros((512, 768), f32)

    def chunk(g, _):
        weight = pick(wi, g)
        inner = matmul(low[...], weight) + in_bias[pl.ds(pl.multiple_of(768 * g, 768), 768)].reshape(1, 768)
        phi = 0.5 * (1.0 + lax.erf(inner * 0.7071067811865476))
        active = (inner * phi).astype(bf16)
        slope = phi + inner * jnp.exp(-0.5 * inner * inner) * 0.3989422804014327
        for x in range(2):
            part = wt[g, 4 * x : 4 * x + 4].reshape(768, 384)
            now = active[:, 384 * x : 384 * x + 384]
            out[...] += matmul(now, part, NT)
            back = matmul(cot_low[...], part)
            wt[g, 4 * x : 4 * x + 4] = (
                matmul(cot_t[...], now).astype(bf16).reshape(4, 192, 384)
            )
            grad_low[:, 384 * x : 384 * x + 384] = (
                back * slope[:, 384 * x : 384 * x + 384]
            ).astype(bf16)
        small[pl.ds(4 + g, 1)] = column_sum(grad_low[...].astype(f32))
        grad_middle[...] += matmul(grad_low[...], weight, NT)
        put(wi, g, matmul(low_t[...], grad_low[...]).astype(bf16))
        return 0

    lax.fori_loop(0, 4, chunk, 0)
    saves = [
        pltpu.make_async_copy(source, target, save_sem.at[n])
        for n, (source, target) in enumerate(zip((wo, wi, wt), late_grads))
    ]
    saves[1].start()
    saves[2].start()
    grad = grad_middle[...]
    small[1:2] = column_sum(grad * hat[...])
    small[2:3] = column_sum(grad)
    grad = cot[...] + norm_backward(hat[...], inverse, gain, grad)
    grad_middle[...] = grad
    attended = grad.astype(bf16)
    small[3:4] = column_sum(attended.astype(f32))
    grad_merged[...] = matmul(attended, full, NT).astype(bf16)
    grads = matmul(merged[...].T, attended).astype(bf16)
    for g in range(4):
        put(wo, g, grads[:, 192 * g : 192 * g + 192])
    saves[0].start()
    for copy in saves:
        copy.wait()


def attention_forward(grp, slides, gather, inputs, weights):
    out_shape = [
        shape((512, 768), f32),
        shape((2, GROUP, MSG, 512), bf16),
        shape((2, 4096, LANES), bf16),
        shape((2, 4096, LANES), bf16),
        shape((2, 2, 512, LANES), bf16),
        shape((4, 2, 256, LANES), bf16),
        shape((2, GROUP, 56, 512), f32),
        shape((512, 768), f32),
        shape((512, 768), f32),
        shape((512, 768), bf16),
        shape((8, 768), f32),
    ]
    blocks = [(4, GROUP, 96, 192), (4, GROUP, 96, 768), (4, GROUP, 192, 384)]
    out_specs = [vmem()] * len(out_shape) + [anywhere()] * 3
    out_shape += [shape(dims, bf16) for dims in blocks]
    in_specs = [anywhere()] * 2 + [vmem()] * 2 + [pl.BlockSpec(memory_space=pltpu.SMEM)]
    in_specs += [vmem()] * 10
    extra = []
    if gather:
        in_specs += [vmem()] * 3 + [anywhere()] * 2 + [vmem()]
        out_shape += [shape((4, GROUP, 96, 576), bf16)]
        out_specs += [vmem()]
        extra = [pltpu.VMEM((96, 576), bf16), pltpu.VMEM((192, 384), bf16)]
        extra += gather_sems(1) + gather_sems(2) + gather_wide_sems()
    else:
        in_specs += [vmem()] + [anywhere()] * 3
    rows = (512, 768)
    return pl.pallas_call(
        functools.partial(forward_kernel, grp, slides, gather),
        name="forward_and_feed",
        in_specs=in_specs,
        out_specs=out_specs,
        out_shape=out_shape,
        scratch_shapes=[
            pltpu.VMEM((2, GROUP, MSG, 512), bf16),
            pltpu.VMEM((2, GROUP, HD, 512), bf16),
            pltpu.VMEM((2, GROUP, HD, 512), bf16),
            pltpu.VMEM((64, q_all), f32),
            pltpu.VMEM((q_all - 4096, LANES), bf16),
            pltpu.VMEM((k_all - 4096, LANES), bf16),
            sems(6),
            sems(2, GROUP), sems(2, GROUP), sems(2, GROUP), sems(2, GROUP), sems(2, 4), sems(2, 4),
        ]
        + [pltpu.VMEM(dims, bf16) for dims in blocks]
        + [
            pltpu.VMEM(rows, f32), pltpu.VMEM(rows, bf16), pltpu.VMEM(rows, f32),
            pltpu.VMEM(rows, f32), pltpu.VMEM(rows, bf16), pltpu.VMEM((768, 512), bf16),
            pltpu.VMEM(rows, bf16), pltpu.VMEM((768, 512), bf16), pltpu.VMEM(rows, bf16),
            pltpu.VMEM((6, 512, LANES), f32), sems(3),
        ]
        + extra,
        compiler_params=params(1),
    )(*inputs, *weights)


def backward_kernel(grp, reduce, *refs):
    refs = list(refs)
    take = lambda n: [refs.pop(0) for _ in range(n)]
    gm, gain_ref, shift_ref, small = take(4)
    saved = take(6)
    base_in, middle_in, weight_in = take(3)
    parts = take(3) if reduce else take(0)
    token_grad, joint_out, pack = take(3)
    reduced = take(3) if reduce else take(0)
    (gsend, grecv, rsend, rrecv, got8, got16, send8, send16, rows_ref,
     gs, gr, ss, rs, ds, dr, load_sem) = take(16)
    local = take(13)
    (grads,) = take(1)
    spot = Spot(grp)
    joined = spot.greet()
    shares = [Exchange(spot, gsend.at[i], grecv.at[i], gs.at[i], gr.at[i]) for i in range(2)]
    backs = [Exchange(spot, rsend.at[i], rrecv.at[i], ss.at[i], rs.at[i]) for i in range(2)]
    deeps = []
    if reduce:
        two = [parts[0], parts[2]], [reduced[0], reduced[2]]
        dims = [part.shape[2:] for part in two[0]]
        sums = Reduce(*two, take(len(reduce_scratch(dims))))
        wide_sum = ReduceWide(parts[1], reduced[1], take(14))
        last_scratch = take(len(reduce_scratch([(96, 576)])) - 1)
        total_sum = take(5)
    else:
        sums = wide_sum = None

    attend_backward(
        spot, joined, gm, saved, shares, backs, deeps, sums, wide_sum, gsend, grecv, rsend,
        got8, got16, send8, send16, ds, dr, load_sem, *local,
    )
    rows_f32 = local[11]
    late_loads = [pltpu.make_async_copy(weight_in, grads, load_sem.at[0])]
    for n, source in enumerate((base_in, middle_in)):
        for chunk in range(6):
            at = 3072 * n + 512 * chunk
            late_loads.append(
                pltpu.make_async_copy(
                    source.at[:, LANES * chunk : LANES * chunk + LANES],
                    rows_f32.at[at : at + 512],
                    load_sem.at[1 + 6 * n + chunk],
                )
            )
    for copy in late_loads:
        copy.start()

    def loaded(n):
        at = 3072 * n
        return jnp.concatenate(
            [rows_f32[at + 512 * chunk : at + 512 * chunk + 512] for chunk in range(6)], axis=1
        )

    if reduce:
        sums.advance(5)
        wide_sum.advance(5)
    for copy in late_loads:
        copy.wait()
    gain, shift = gain_ref[...].reshape(1, 768), shift_ref[...].reshape(1, 768)
    hat, inverse = norm_parts(loaded(0))
    low_t = (hat * gain + shift).astype(bf16).T
    for i in range(2):
        for j in range(GROUP):
            backs[i].wait(j)
    lines = [[], []]
    grad = jnp.zeros((512, 768), f32)
    for quad in range(4):

        def read(head):
            block = rrecv[head % 2, head // 2]
            return jnp.concatenate([block[2 * HD :], block[: 2 * HD]], axis=0)

        now = join_quad(quad, read)
        grad = grad + matmul(now, pick(grads, quad), NT)
        put(grads, quad, matmul(low_t, now).astype(bf16))
        total = column_sum(now.astype(f32))
        for inner in range(4):
            lines[0].append(total[:, 144 * inner : 144 * inner + HD])
            lines[1].append(total[:, 144 * inner + 96 : 144 * inner + 144])
    if reduce:
        joint = Reduce([grads], [joint_out], [None] + list(last_scratch))
        joint.start()
    rows_ref[0:1] = column_sum(grad * hat)
    rows_ref[1:2] = column_sum(grad)
    rows_ref[2:3] = jnp.concatenate(lines[0], axis=1)
    rows_ref[3:4] = jnp.concatenate(lines[1], axis=1)
    rows_ref[4:5] = small[3:4]
    rows_ref[5:6] = small[1:2]
    rows_ref[6:7] = small[2:3]
    rows_ref[7:8] = small[0:1]
    rows_ref[8:12] = small[4:8]
    rows_ref[12:16] = jnp.zeros((4, 768), f32)
    token_grad[...] = loaded(1) + norm_backward(hat, inverse, gain, grad)
    if reduce:
        rest = Total(rows_ref, pack, total_sum)
        rest.start()
        joint.advance(1)
        rest.middle()
        joint.advance(3)
        rest.late()
        joint.advance(5)
        sums.advance(6)
        wide_sum.advance(6)
        joint.advance(6)
        rest.finish()
        joint.drain()
    else:
        pack[...] = rows_ref[...]
        save = pltpu.make_async_copy(grads, joint_out, load_sem.at[3])
        save.start()
        save.wait()
    if reduce:
        sums.drain()
        wide_sum.drain()
    for item in shares + backs + deeps:
        item.drain()


def attend_backward(
    spot, joined, gm, saved, shares, backs, deeps, sums, wide_sum, gsend, grecv, rsend, got8, got16,
    send8, send16, ds, dr, load_sem, q_ref, kv_ref, kv8, kv16, msg, stat,
    qc, kvc, dor, kt, ld, dkv, dqt,
):
    reduce = sums is not None
    loads = [
        pltpu.make_async_copy(source, target, load_sem.at[n])
        for n, (source, target) in enumerate(zip(saved, (q_ref, kv_ref, kv8, kv16, msg, stat)))
    ]
    for copy in loads:
        copy.start()
    for quad in range(4):
        wide = swap_blocks(gm[:, 192 * quad : 192 * quad + 192], quad).T
        for inner in (0, 2, 1, 3):
            head = 4 * quad + inner
            i = head % 2
            gsend[i, head // 2] = swap_chunks(wide[HD * inner : HD * inner + HD], head)
            if quad == 0 and inner == 0:
                joined()
            if i == 0:
                shares[0].send(head // 2)
    for j in range(GROUP):
        shares[1].send(j)
    if reduce:
        wide_sum.start()
        sums.start()
    for copy in loads:
        copy.wait()
    for i in range(2):
        q, kv = q_ref.at[i], kv_ref.at[i]
        for n in range(2):
            kvc[3072 + 512 * n : 3584 + 512 * n] = kv8[n, i]
        for n in range(4):
            kvc[4096 + 256 * n : 4352 + 256 * n] = kv16[n, i]
        for n in range(2):
            kt[7 + n] = kvc[3072 + 1024 * n : 4096 + 1024 * n].T[:HD]
        rows = []
        for j in range(GROUP):
            compact(j, q[512 * j : 512 * j + 512], qc, ((0, 256), (2048, 128), (3072, 64), (3584, 32)))
            compact(j, kv[512 * j : 512 * j + 512], kvc, ((0, 256), (2048, 128)))
            key = msg[i, j, :HD]
            kt[j // 2, :, 512 * (j % 2) : 512 * (j % 2) + 512] = key
            kt[4 + j // 4, :, 256 * (j % 4) : 256 * (j % 4) + 256] = key[:, :256]
            kt[6, :, 128 * j : 128 * j + 128] = key[:, :128]
        for j in range(GROUP):
            shares[i].wait(j)
            grad = grecv[i, j]
            delta = column_sum(grad.astype(f32) * stat[i, j, :HD])
            both = jnp.concatenate(
                [stat[i, j, HD : HD + 1], delta, jnp.zeros((6, 512), f32)], axis=0
            )
            rows.append(both)
            ld[:, 512 * j : 512 * j + 512] = both
            ld[:, 4096 + 256 * j : 4352 + 256 * j] = both[:, :256]
            ld[:, 6144 + 128 * j : 6272 + 128 * j] = both[:, :128]
            tall = jnp.concatenate(
                [jnp.zeros((HD, 512), bf16), grad, jnp.zeros((32, 512), bf16)], axis=0
            ).T
            for r, at in enumerate(q_at):
                size = 512 >> r
                dor[at + size * j : at + size * j + size] = tall[:size]
        ld[:, 7168:7680] = jnp.concatenate([both[:, :64] for both in rows], axis=1)
        ld[:, 7680:7936] = jnp.concatenate([both[:, :32] for both in rows], axis=1)

        def unit(source, q_from, keys, k_from, at, seg, count):
            width = 256 * count
            query = source[pl.ds(q_from, width)]
            grad = dor[pl.ds(at, width)]
            total = ld[0:1, pl.ds(at, width)]
            delta = ld[1:2, pl.ds(at, width)]
            sides = jnp.concatenate([grad, query], axis=0)
            size = 256
            dq = jnp.zeros((HD, width), f32)
            for c in range(1024 // size):
                key = keys[pl.ds(k_from + size * c, size)]
                prob = jnp.exp2(matmul(key, query, NT) * scale2 - total)
                slope = (prob * (matmul(key, grad, NT) - delta)).astype(bf16)
                both = jnp.concatenate([prob.astype(bf16), slope], axis=1)
                dkv[pl.ds(seg * 1024 + size * c, size)] = matmul(both, sides)
                dq = dq + matmul(kt[seg, :, size * c : size * c + size], slope)
            dqt[:, pl.ds(at, width)] = dq

        unit(qc, 3072, kvc, 3072, 7168, 7, 2)
        unit(qc, 3584, kvc, 4096, 7680, 8, 1)
        for n in range(2):
            send8[n, i] = dkv[7168 + 512 * n : 7680 + 512 * n].astype(bf16)
        for n in range(4):
            send16[n, i] = dkv[8192 + 256 * n : 8448 + 256 * n].astype(bf16)
        deep = Deep(
            spot, (send8.at[1 - spot.half, i], got8.at[i], got8.at[i]),
            lambda o, other: (send16.at[other, i], got16.at[4 - o, i], got16.at[o, i]),
            ds.at[i], dr.at[i],
        )
        deep.start()
        deeps.append(deep)
        if reduce:
            wide_sum.advance(2 + i)
            sums.advance(1 + 2 * i)

        def early(u, _):
            at = pl.multiple_of(u * 1024, 1024)
            unit(q, at, kv, at, at, u, 4)
            return 0

        lax.fori_loop(0, 4, early, 0)
        if reduce:
            sums.advance(2 + 2 * i)
            wide_sum.advance(2 + 2 * i)

        def late(u, _):
            at = pl.multiple_of(u * 1024, 1024)
            unit(qc, at, kvc, at, pl.multiple_of(at + 4096, 1024), u + 4, 4)
            return 0

        lax.fori_loop(0, 3, late, 0)
        deep.wait()
        spot_lane = lax.broadcasted_iota(jnp.int32, (1, 512), 1)
        uses = jnp.where(spot_lane < 32, 5.0, jnp.where(spot_lane < 64, 4.0, jnp.where(
            spot_lane < 128, 3.0, jnp.where(spot_lane < 256, 2.0, 1.0))))
        for j in range(GROUP):
            tall = dkv[512 * j : 512 * j + 512]
            eight = send8[spot.half, i, 64 * j : 64 * j + 64].astype(f32) + got8[
                i, 64 * j : 64 * j + 64
            ].astype(f32)
            sixteen = send16[spot.layer, i, 32 * j : 32 * j + 32].astype(f32)
            for o in range(1, 4):
                sixteen = sixteen + got16[o, i, 32 * j : 32 * j + 32].astype(f32)
            second = dkv[4096 + 256 * j : 4352 + 256 * j]
            third = dkv[6144 + 128 * j : 6272 + 128 * j]
            fourth = third[:64] + eight
            fourth = jnp.concatenate([fourth[:32] + sixteen, fourth[32:]], axis=0)
            third = jnp.concatenate([fourth, third[64:]], axis=0)
            second = jnp.concatenate([second[:128] + third, second[128:]], axis=0)
            wide = jnp.concatenate([tall[:256] + second, tall[256:]], axis=0).T
            key = msg[i, j, :HD].astype(f32)
            value = msg[i, j, HD : 2 * HD].astype(f32)
            query = msg[i, j, 112:].astype(f32)
            grad = grecv[i, j].astype(f32)
            total = ld[0:1, 512 * j : 512 * j + 512]
            delta = ld[1:2, 512 * j : 512 * j + 512]
            dropped = msg[i, j, FLAG : FLAG + 1].astype(f32) != 0.0
            dots = column_sum(query * key) * scale2 - total
            prob = jnp.where(dropped, uses * jnp.exp2(jnp.where(dropped, dots, 0.0)), 0.0)
            slope = prob * (column_sum(grad * value) - delta)
            dq = widen([dqt[:, at + (512 >> r) * j : at + (512 >> r) * (j + 1)]
                        for r, at in enumerate(q_at)])
            rsend[i, j, :HD] = ((wide[:HD] + slope * query) * scale).astype(bf16)
            rsend[i, j, HD : 2 * HD] = (wide[HD : 2 * HD] + prob * grad).astype(bf16)
            rsend[i, j, 2 * HD :] = ((dq + slope * key) * scale).astype(bf16)
            backs[i].send(j)


def attention_backward(grp, reduce, inputs, parts):
    out_shape = [
        shape((512, 768), f32),
        shape((96, 576), f32) if reduce else shape((4, GROUP, 96, 576), bf16),
        shape((16, 768), f32),
    ]
    out_specs = [vmem(), vmem() if reduce else anywhere(), vmem()]
    extra = []
    if reduce:
        dims = [part.shape[2:] for part in parts]
        out_shape += [shape(d, f32) for d in dims]
        out_specs += [vmem()] * 3
        extra = (
            reduce_scratch([dims[0], dims[2]]) + reduce_wide_scratch(dims[1])
            + reduce_scratch([(96, 576)])[1:] + total_scratch((16, 768))
        )
    return pl.pallas_call(
        functools.partial(backward_kernel, grp, reduce),
        name="attention_backward",
        in_specs=[vmem()] * 4 + [anywhere()] * (9 + len(parts)),
        out_specs=out_specs,
        out_shape=out_shape,
        scratch_shapes=[
            pltpu.VMEM((2, GROUP, HD, 512), bf16),
            pltpu.VMEM((2, GROUP, HD, 512), bf16),
            pltpu.VMEM((2, GROUP, 3 * HD, 512), bf16),
            pltpu.VMEM((2, GROUP, 3 * HD, 512), bf16),
            pltpu.VMEM((2, 512, LANES), bf16),
            pltpu.VMEM((4, 2, 256, LANES), bf16),
            pltpu.VMEM((2, 2, 512, LANES), bf16),
            pltpu.VMEM((4, 2, 256, LANES), bf16),
            pltpu.VMEM((16, 768), f32),
            sems(2, GROUP), sems(2, GROUP), sems(2, GROUP), sems(2, GROUP), sems(2, 4), sems(2, 4),
            sems(13),
            pltpu.VMEM((2, 4096, LANES), bf16), pltpu.VMEM((2, 4096, LANES), bf16),
            pltpu.VMEM((2, 2, 512, LANES), bf16), pltpu.VMEM((4, 2, 256, LANES), bf16),
            pltpu.VMEM((2, GROUP, MSG, 512), bf16), pltpu.VMEM((2, GROUP, 56, 512), f32),
            pltpu.VMEM((q_all - 4096, LANES), bf16), pltpu.VMEM((k_all - 4096, LANES), bf16),
            pltpu.VMEM((q_all, LANES), bf16), pltpu.VMEM((9, HD, 1024), bf16),
            pltpu.VMEM((8, q_all), f32), pltpu.VMEM((k_all, LANES), f32),
            pltpu.VMEM((HD, q_all), f32),
            pltpu.VMEM((4, GROUP, 96, 576), bf16),
        ] + extra,
        compiler_params=params(2),
    )(*inputs, *parts)


def finish_kernel(out_in, token_in, joint, b_in, c_in, d_in, pack, *refs):
    out, token, query, key, value, b_out, c_out, d_out = refs[:8]
    vectors = refs[8:]
    for source, target in ((out_in, out), (token_in, token)):
        for b in range(16):
            target[pl.ds(order[b], BLOCK, stride=16), :] = source[BLOCK * b : BLOCK * b + BLOCK]

    @pl.when(pl.program_id(0) == 0)
    def _():
        for n, target in enumerate((query, key, value)):
            target[...] = jnp.concatenate(
                [joint[:, 144 * i + HD * n : 144 * i + HD * n + HD] for i in range(4)], axis=1
            )
        b_out[...] = b_in[...]
        c_out[...] = c_in[...]
        d_out[...] = d_in[...].T
        for n in (0, 1, 2, 3, 4, 5, 6):
            vectors[n][...] = pack[n]
        vectors[7][...] = jnp.concatenate([pack[8 + n] for n in range(4)], axis=0)
        vectors[8][...] = pack[7]


def finish(out, token_grad, joint, b_sum, c_sum, d_sum, pack):
    shard, hidden = b_sum.shape[0], d_sum.shape[1]
    sizes = [768] * 7 + [3072, 768]
    wide = pl.BlockSpec((512, LANES), lambda n: (0, n))
    whole = lambda *dims: pl.BlockSpec(dims, lambda n: (0,) * len(dims))
    small = [(shard, 192)] * 4 + [(shard, 768), (hidden, 192)] + [(size,) for size in sizes]
    return pl.pallas_call(
        finish_kernel,
        name="finish",
        grid=(6,),
        in_specs=[wide] * 2 + [whole(*item.shape) for item in (joint, b_sum, c_sum, d_sum, pack)],
        out_specs=[wide] * 2 + [whole(*dims) for dims in small],
        out_shape=[shape((512, 768), f32)] * 2 + [shape(dims, f32) for dims in small],
        compiler_params=params(),
    )(out, token_grad, joint, b_sum, c_sum, d_sum, pack)


def all_weights(parts, seq, grp):
    gathered = []
    for n, part in enumerate(parts):
        whole = lax.all_gather(lax.all_gather(part, "grp"), "seq")
        lead = whole.shape[0] // 8
        whole = whole.reshape((8, lead) + whole.shape[1:])
        if n == 3:
            whole = whole.transpose(0, 2, 3, 1, 4)
            whole = whole.reshape(4, GROUP, part.shape[0], lead * part.shape[1])
        else:
            whole = whole.transpose(0, 2, 1, 3, 4)
            whole = whole.reshape(4, GROUP, lead * part.shape[0], part.shape[1])
        gathered.append(whole)
    return gathered


def sum_gradients(parts, small, seq, grp):
    lead = seq // 8
    sums = []
    for n, part in enumerate(parts):
        height, lanes = part.shape[2:]
        whole = part.reshape(8, grp, height, lanes)
        if n == 3:
            whole = whole.reshape(8, grp, height, lead, lanes // lead).transpose(0, 3, 1, 2, 4)
        else:
            whole = whole.reshape(8, grp, lead, height // lead, lanes).transpose(0, 2, 1, 3, 4)
        whole = whole.reshape((seq, grp) + whole.shape[3:]).astype(f32)
        whole = lax.psum_scatter(whole, "seq", scatter_dimension=0)
        sums.append(lax.psum_scatter(whole, "grp", scatter_dimension=0))
    return sums + [lax.psum(small, ("seq", "grp"))]


def body(
    tokens,
    coordinates,
    lengths,
    valid,
    first_gain,
    first_shift,
    query_weight,
    query_bias,
    key_weight,
    value_weight,
    value_bias,
    output_weight,
    output_bias,
    second_gain,
    second_shift,
    inner_weight,
    inner_bias,
    outer_weight,
    outer_bias,
    cotangent,
):
    rows, width = tokens.shape
    grp = lax.axis_size("grp")
    seq = lax.axis_size("seq")
    near = (seq, grp) == (8, 4)
    slides = lengths.shape[0]
    shard = query_weight.shape[0]
    frequency = np.exp(np.arange(192) * (-math.log(10000.0) / 192)).astype(np.float32)
    inputs = [
        tokens, cotangent, valid.reshape(BLOCK, 16), coordinates.reshape(BLOCK, 32), lengths,
        np.concatenate([frequency, frequency]).reshape(1, 384),
        first_gain, first_shift, output_bias, second_gain, second_shift, outer_bias, inner_bias,
        query_bias, value_bias,
    ]
    if near:
        weights = [
            query_weight, key_weight, value_weight, output_weight, inner_weight, outer_weight,
        ]
    else:
        heads = [w.reshape(shard, 4, 1, HD) for w in (query_weight, key_weight, value_weight)]
        parts = [
            jnp.concatenate(heads, axis=2).reshape(shard, 576),
            output_weight,
            inner_weight,
            outer_weight.T,
        ]
        weights = all_weights(parts, seq, grp)
    results = attention_forward(grp, slides, near, inputs, weights)
    base, msg, q_rows, kv_rows, kv8, kv16, stat, out, grad_middle, grad_merged, small = results[:11]
    late = results[11:14]
    joint_weight = results[14] if near else weights[0]
    saved = [
        grad_merged, first_gain, first_shift, small, q_rows, kv_rows, kv8, kv16, msg, stat, base, grad_middle,
        joint_weight,
    ]
    results = attention_backward(grp, near, saved, late if near else [])
    token_grad, joint_sum, pack = results[:3]
    if near:
        sums = results[3:]
    else:
        joint_sum, *sums, pack = sum_gradients([joint_sum] + list(late), pack, seq, grp)
    results = finish(out, token_grad, joint_sum, *sums, pack)
    output, token_grad = results[:2]
    sum_query, sum_key, sum_value, sum_output, sum_inner, sum_outer = results[2:8]
    small = results[8:]
    return (
        output,
        token_grad,
        small[0],
        small[1],
        sum_query,
        small[2],
        sum_key,
        sum_value,
        small[3],
        sum_output,
        small[4],
        small[5],
        small[6],
        sum_inner,
        small[7],
        sum_outer,
        small[8],
    )


def solution(mesh):
    placed = (
        P(("seq", "grp"), None),
        P(("seq", "grp"), None),
        P(),
        P(("seq", "grp")),
        P(),
        P(),
        P("seq", "grp"),
        P(),
        P("seq", "grp"),
        P("seq", "grp"),
        P(),
        P("seq", "grp"),
        P(),
        P(),
        P(),
        P("seq", "grp"),
        P(),
        P("seq", "grp"),
        P(),
        P(("seq", "grp"), None),
    )
    return jax.shard_map(
        body,
        mesh=mesh,
        in_specs=placed,
        out_specs=(
            P(("seq", "grp"), None),
            P(("seq", "grp"), None),
            P(),
            P(),
            P("seq", "grp"),
            P(),
            P("seq", "grp"),
            P("seq", "grp"),
            P(),
            P("seq", "grp"),
            P(),
            P(),
            P(),
            P("seq", "grp"),
            P(),
            P("seq", "grp"),
            P(),
        ),
        check_vma=False,
    )
```

```python
import functools
import math

import jax
import jax.numpy as jnp
import numpy as np
from jax import lax
from jax.experimental import pallas as pl
from jax.experimental.pallas import tpu as pltpu
from jax.sharding import PartitionSpec as P

epsilon = 1e-05


NT = (((1,), (1,)), ((), ()))
NN = (((1,), (0,)), ((), ()))
f32 = jnp.float32
bf16 = jnp.bfloat16
BIG = 1e30
HD = 48
GROUP = 8
LANES = 128
BLOCK = 32
MSG = 160
FLAG = 2 * HD
MESH = pl.DeviceIdType.MESH
scale = HD ** (-0.5)
scale2 = scale * math.log2(math.e)
q_at = (0, 4096, 6144, 7168, 7680)
q_all = 7936
k_all = 9216


def reverse4(b):
    return (b & 1) * 8 + (b & 2) * 2 + (b & 4) // 2 + (b & 8) // 8


order = [reverse4(b) for b in range(16)]


def chunk_swap(head):
    return reverse4(head) >> 2


def block_swap(quad):
    return reverse4(4 * quad) & 3


def swap_blocks(rows, quad):
    return jnp.concatenate(
        [rows[BLOCK * (b ^ block_swap(quad)) :][:BLOCK] for b in range(16)], axis=0
    )


def swap_chunks(wide, head):
    return jnp.concatenate(
        [wide[:, LANES * (c ^ chunk_swap(head)) :][:, :LANES] for c in range(4)], axis=1
    )


def matmul(a, b, dims=NN):
    return lax.dot_general(a, b, dims, preferred_element_type=f32)


def column_sum(values):
    return jnp.sum(values, axis=0, keepdims=True)


def pick(ref, g):
    both = jnp.stack([ref[:, g], ref[:, g + 4]], axis=1)
    return both.reshape(768, ref.shape[3])


def put(ref, g, value):
    value = value.reshape(4, 2, 96, ref.shape[3])
    ref[:, g] = value[:, 0]
    ref[:, g + 4] = value[:, 1]


def vmem():
    return pl.BlockSpec(memory_space=pltpu.VMEM)


def anywhere():
    return pl.BlockSpec(memory_space=pl.ANY)


def sems(*dims):
    return pltpu.SemaphoreType.DMA(dims)


def params(identity=None):
    if identity is None:
        return pltpu.CompilerParams(vmem_limit_bytes=60 << 20)
    return pltpu.CompilerParams(
        vmem_limit_bytes=60 << 20, collective_id=identity, has_side_effects=True
    )


def shape(dims, dtype):
    return jax.ShapeDtypeStruct(dims, dtype)


def remote(src, dst, send_sem, recv_sem, target):
    return pltpu.make_async_remote_copy(
        src_ref=src, dst_ref=dst, send_sem=send_sem, recv_sem=recv_sem,
        device_id=target, device_id_type=MESH,
    )


class Spot:
    def __init__(self, grp):
        self.grp = grp
        self.linear = lax.axis_index("seq") * grp + lax.axis_index("grp")
        self.member = self.linear % GROUP
        self.base = self.linear - self.member
        self.layer = self.linear // GROUP % 4
        self.half = self.layer % 2

    def device(self, linear):
        return (linear // self.grp, linear % self.grp)

    def beside(self, j):
        return self.device(self.base + j)

    def over(self, layer):
        return self.device(self.linear + GROUP * (layer - self.layer))

    def pair(self):
        return self.device(self.linear + GROUP - 2 * GROUP * self.half)

    def greet(self):
        barrier = pltpu.get_barrier_semaphore()
        for j in range(GROUP):

            @pl.when(self.member != j)
            def _():
                pl.semaphore_signal(barrier, inc=1, device_id=self.beside(j), device_id_type=MESH)

        for o in range(1, 4):
            target = self.over((self.layer + o) % 4)
            pl.semaphore_signal(barrier, inc=1, device_id=target, device_id_type=MESH)
        return lambda: pl.semaphore_wait(barrier, GROUP + 2)


class Exchange:
    def __init__(self, spot, send, recv, send_sem, recv_sem):
        self.spot, self.send_ref, self.recv = spot, send, recv
        self.send_sem, self.recv_sem = send_sem, recv_sem

    def out(self, j):
        s = self.spot
        return remote(self.send_ref.at[j], self.recv.at[s.member], self.send_sem.at[j],
                      self.recv_sem.at[s.member], s.beside(j))

    def inner(self, j):
        return pltpu.make_async_copy(self.send_ref.at[j], self.recv.at[j], self.recv_sem.at[j])

    def choose(self, j, far, near):
        pl.when(self.spot.member != j)(far)
        pl.when(self.spot.member == j)(near)

    def send(self, j):
        self.choose(j, lambda: self.out(j).start(), lambda: self.inner(j).start())

    def wait(self, j):
        def far():
            remote(self.send_ref.at[j], self.recv.at[j], self.send_sem.at[j], self.recv_sem.at[j],
                   self.spot.beside(j)).wait_recv()

        self.choose(j, far, lambda: self.inner(j).wait())

    def drain(self):
        for j in range(GROUP):
            pl.when(self.spot.member != j)(lambda j=j: self.out(j).wait_send())


class Deep:
    def __init__(self, spot, eight, sixteen, send_sem, recv_sem):
        self.copies, self.waits = [], []
        s = spot
        for o in range(1, 4):
            other = (s.layer + o) % 4
            src, there, here = sixteen(o, other)
            self.copies.append(remote(src, there, send_sem.at[o], recv_sem.at[4 - o], s.over(other)))
            self.waits.append(remote(src, here, send_sem.at[o], recv_sem.at[o], s.over(other)))
        src, there, here = eight
        self.copies.append(remote(src, there, send_sem.at[0], recv_sem.at[0], s.pair()))
        self.waits.append(remote(src, here, send_sem.at[0], recv_sem.at[0], s.pair()))

    def start(self):
        for copy in self.copies:
            copy.start()

    def wait(self):
        for copy in self.waits:
            copy.wait_recv()

    def drain(self):
        for copy in self.copies:
            copy.wait_send()


def member_of(x, y, c):
    return x * 4 + y * 2 + c


def place():
    seq, col = lax.axis_index("seq"), lax.axis_index("grp")
    return seq // 2, seq % 2, col // 2, col % 2


def at_place(z, x, y, c):
    return (z * 2 + x, y * 2 + c)


def gather_sems(count):
    return [
        sems(count), sems(4, count), sems(4, count), sems(2, 4, count), sems(2, 4, count),
        sems(2, 4, count), sems(2, 4, count), sems(4, count), sems(4, count),
    ]


class Gather:
    def __init__(self, ins, outs, semaphores):
        self.ins, self.outs = ins, outs
        (self.loc, self.zs, self.zr, self.ps, self.pr,
         self.qs, self.qr, self.cs, self.cr) = semaphores
        self.place = z, x, y, c = place()
        self.me = member_of(x, y, c)
        self.arrays = range(len(ins))
        self.near = [(1 - x, y), (x, 1 - y)]
        self.started = []
        self.done = 0
        self.local = [
            pltpu.make_async_copy(ins[k], outs[k].at[z, self.me], self.loc.at[k])
            for k in self.arrays
        ]
        self.stages = [self.stage1, self.stage2, self.stage3, self.stage4, self.stage5]

    def go(self, copy):
        copy.start()
        self.started.append(copy)

    def start_layers(self):
        z, x, y, c = self.place
        for copy in self.local:
            copy.start()
        for o in (1, 2, 3):
            for k in self.arrays:
                self.go(remote(self.ins[k], self.outs[k].at[z, self.me], self.zs.at[o, k],
                               self.zr.at[4 - o, k], at_place((z + o) % 4, x, y, c)))

    def push(self, layer, slot, sources):
        z, x, y, c = self.place
        for p, (px, py) in enumerate(self.near):
            for k in self.arrays:
                self.go(remote(sources[k], self.outs[k].at[layer, self.me], self.ps.at[p, slot, k],
                               self.pr.at[p, slot, k], at_place(z, px, py, c)))

    def relay(self, slot):
        z, x, y, c = self.place
        layer = (z + slot) % 4
        for p, (px, py) in enumerate(self.near):
            m = member_of(px, py, c)
            for k in self.arrays:
                part = self.outs[k].at[layer, m]
                remote(part, part, self.ps.at[p, slot, k], self.pr.at[p, slot, k],
                       at_place(z, px, py, c)).wait_recv()
        for k in self.arrays:
            rows = self.ins[k].shape[0] // 2
            for p, (px, py) in enumerate(self.near):
                part = self.outs[k].at[layer, member_of(px, py, c), p * rows : (p + 1) * rows]
                self.go(remote(part, part, self.qs.at[p, slot, k], self.qr.at[p, slot, k],
                               at_place(z, *self.near[1 - p], c)))

    def push_own(self):
        self.push(self.place[0], 0, self.ins)

    def stage1(self):
        z, x, y, c = self.place
        for copy in self.local:
            copy.wait()
        for o in (1, 2, 3):
            layer = (z + o) % 4
            parts = [self.outs[k].at[layer, self.me] for k in self.arrays]
            for k in self.arrays:
                remote(parts[k], parts[k], self.zs.at[o, k], self.zr.at[o, k],
                       at_place(layer, x, y, c)).wait_recv()
            self.push(layer, o, parts)

    def stage2(self):
        self.relay(0)
        self.relay(1)

    def stage3(self):
        z, x, y, c = self.place
        self.relay(2)
        self.across(0, x, y)
        self.relay(3)
        self.across(1, 1 - x, y)
        self.across(2, x, 1 - y)

    def across(self, slot, px, py):
        z, x, y, c = self.place
        m = member_of(px, py, c)
        for k in self.arrays:
            part = self.outs[k].at[:, m]
            self.go(remote(part, part, self.cs.at[slot, k], self.cr.at[slot, k],
                           at_place(z, x, y, 1 - c)))

    def stage4(self):
        z, x, y, c = self.place
        far = member_of(1 - x, 1 - y, c)
        for slot in range(4):
            layer = (z + slot) % 4
            for k in self.arrays:
                rows = self.ins[k].shape[0] // 2
                for p in range(2):
                    part = self.outs[k].at[layer, far, p * rows : (p + 1) * rows]
                    remote(part, part, self.qs.at[p, slot, k], self.qr.at[p, slot, k],
                           at_place(z, *self.near[1 - p], c)).wait_recv()
        self.across(3, 1 - x, 1 - y)

    def stage5(self):
        z, x, y, c = self.place
        for slot, (px, py) in enumerate([(x, y), (1 - x, y), (x, 1 - y), (1 - x, 1 - y)]):
            m = member_of(px, py, 1 - c)
            for k in self.arrays:
                part = self.outs[k].at[:, m]
                remote(part, part, self.cs.at[slot, k], self.cr.at[slot, k],
                       at_place(z, x, y, 1 - c)).wait_recv()

    def advance(self, upto):
        while self.done < upto:
            self.stages[self.done]()
            self.done += 1

    def finish(self):
        self.advance(5)

    def drain(self):
        for copy in self.started:
            copy.wait_send()


def gather_wide_sems():
    return [sems(1), sems(2), sems(2), sems(2), sems(2), sems(4, 4), sems(4, 4), sems(4, 4), sems(4, 4)]


class GatherWide:
    def __init__(self, source, out, semaphores):
        self.source, self.out = source, out
        (self.loc, self.ps, self.pr, self.qs, self.qr, self.zs, self.zr, self.cs, self.cr) = semaphores
        self.place = z, x, y, c = place()
        self.near = [(1 - x, y), (x, 1 - y)]
        self.spots = [(x, y), (1 - x, y), (x, 1 - y), (1 - x, 1 - y)]
        self.started = []
        self.done = 0
        self.stages = [self.stage1, self.stage2, self.stage3, self.stage4, self.stage5]

    def go(self, copy):
        copy.start()
        self.started.append(copy)

    def block(self, layer, p, c):
        return self.out.at[layer, member_of(*p, c)]

    def start(self):
        z, x, y, c = self.place
        self.local = pltpu.make_async_copy(self.source, self.block(z, (x, y), c), self.loc.at[0])
        self.local.start()
        for n, p in enumerate(self.near):
            self.go(remote(self.source, self.block(z, (x, y), c), self.ps.at[n], self.pr.at[n],
                           at_place(z, *p, c)))

    def up(self, slot):
        z, x, y, c = self.place
        part = self.block(z, self.spots[slot], c)
        for o in (1, 2, 3):
            self.go(remote(part, part, self.zs.at[o, slot], self.zr.at[4 - o, slot],
                           at_place((z + o) % 4, x, y, c)))

    def swap(self, o, slot):
        z, x, y, c = self.place
        part = self.block((z + o) % 4, self.spots[slot], c)
        self.go(remote(part, part, self.cs.at[o, slot], self.cr.at[o, slot],
                       at_place(z, x, y, 1 - c)))

    def stage1(self):
        z, x, y, c = self.place
        self.local.wait()
        self.up(0)
        self.swap(0, 0)
        rows = self.source.shape[0] // 2
        for n, p in enumerate(self.near):
            part = self.block(z, p, c)
            remote(part, part, self.ps.at[n], self.pr.at[n], at_place(z, *p, c)).wait_recv()
            part = self.out.at[z, member_of(*p, c), n * rows : (n + 1) * rows]
            self.go(remote(part, part, self.qs.at[n], self.qr.at[n],
                           at_place(z, *self.near[1 - n], c)))
            self.up(1 + n)
            self.swap(0, 1 + n)

    def stage2(self):
        z, x, y, c = self.place
        rows = self.source.shape[0] // 2
        for n in range(2):
            part = self.out.at[z, member_of(*self.spots[3], c), n * rows : (n + 1) * rows]
            remote(part, part, self.qs.at[n], self.qr.at[n],
                   at_place(z, *self.near[1 - n], c)).wait_recv()
        self.up(3)
        self.swap(0, 3)

    def arrive(self, slots):
        z, x, y, c = self.place
        for slot in slots:
            for o in (1, 2, 3):
                layer = (z + o) % 4
                part = self.block(layer, self.spots[slot], c)
                remote(part, part, self.zs.at[o, slot], self.zr.at[o, slot],
                       at_place(layer, x, y, c)).wait_recv()
                self.swap(o, slot)

    def stage3(self):
        self.arrive((0, 1))

    def stage4(self):
        self.arrive((2, 3))

    def stage5(self):
        z, x, y, c = self.place
        for o in range(4):
            for slot in range(4):
                part = self.block((z + o) % 4, self.spots[slot], 1 - c)
                remote(part, part, self.cs.at[o, slot], self.cr.at[o, slot],
                       at_place(z, x, y, 1 - c)).wait_recv()

    def advance(self, upto):
        while self.done < upto:
            self.stages[self.done]()
            self.done += 1

    def drain(self):
        for copy in self.started:
            copy.wait_send()


def reduce_scratch(dims):
    half = [(rows // 2, lanes) for rows, lanes in dims]
    count = len(dims)
    return (
        [pltpu.VMEM((4,) + d, bf16) for d in dims]
        + [pltpu.VMEM((4, 4) + d, bf16) for d in dims]
        + [pltpu.VMEM((4, 4) + d, bf16) for d in half]
        + [pltpu.VMEM((2, 4) + d, bf16) for d in half]
        + [pltpu.VMEM((4,) + d, bf16) for d in dims]
        + [sems(4, count), sems(4, count), sems(4, count)]
        + [sems(3, count) for _ in range(4)]
        + [sems(4, count), sems(4, count)]
    )


def add_to(target, source):
    def step(i, _):
        target[i] = (target[i].astype(f32) + source[i].astype(f32)).astype(bf16)
        return 0

    lax.fori_loop(0, 4, step, 0)


class Reduce:
    def __init__(self, ins, outs, scratch):
        count = len(ins)
        self.ins, self.outs, self.arrays = ins, outs, range(count)
        self.stage, self.across, self.one, self.two, self.deep = [
            scratch[i * count : (i + 1) * count] for i in range(5)
        ]
        (self.loc, self.cs, self.cr, self.xs, self.xr, self.ys, self.yr, self.zs, self.zr) = scratch[
            5 * count :
        ]
        self.place = z, x, y, c = place()
        self.mine, self.px, self.py, self.far = (x, y), (1 - x, y), (x, 1 - y), (1 - x, 1 - y)
        self.other = at_place(z, x, y, 1 - c)
        self.to_x, self.to_y = at_place(z, *self.px, c), at_place(z, *self.py, c)
        self.started = []
        self.done = 0
        self.stages = [self.stage1, self.stage2, self.stage3, self.stage4, self.stage5, self.stage6]

    def slot(self, p):
        return p[0] * 2 + p[1]

    def held(self, k, p):
        if self.stage[k] is None:
            return self.ins[k].at[:, member_of(*p, self.place[3])]
        return self.across[k].at[self.slot(p)]

    def go(self, copy):
        copy.start()
        self.started.append(copy)

    def theirs(self, n, p, k):
        c = self.place[3]
        return remote(self.ins[k].at[:, member_of(*p, 1 - c)], self.across[k].at[self.slot(p)],
                      self.cs.at[n, k], self.cr.at[n, k], self.other)

    def ours(self, n, p, k):
        c = self.place[3]
        return pltpu.make_async_copy(self.ins[k].at[:, member_of(*p, c)],
                                     self.stage[k], self.loc.at[n, k])

    def start(self):
        for n, p in enumerate((self.far, self.px, self.py, self.mine)):
            for k in self.arrays:
                self.go(self.theirs(n, p, k))
                if n == 0 and self.stage[k] is not None:
                    self.ours(n, p, k).start()

    def landed(self, n, p):
        for k in self.arrays:
            self.theirs(n, p, k).wait_recv()
            if self.stage[k] is None:
                add_to(self.held(k, p), self.across[k].at[self.slot(p)])
                continue
            self.ours(n, p, k).wait()
            add_to(self.held(k, p), self.stage[k])
            if n < 3:
                self.ours(n + 1, (self.far, self.px, self.py, self.mine)[n + 1], k).start()

    def part(self, k, p, along_x):
        rows = self.ins[k].shape[2] // 2
        at = 0 if along_x else rows
        return self.held(k, p).at[:, at : at + rows]

    def hop(self, k, p, along_x, i, target):
        source = self.part(k, p, along_x)
        if along_x:
            return remote(source, target, self.xs.at[i, k], self.xr.at[i, k], self.to_x)
        return remote(source, target, self.ys.at[i, k], self.yr.at[i, k], self.to_y)

    def first(self, k, p, along_x):
        i = 0 if p is self.far else 1
        return self.hop(k, p, along_x, i, self.one[k].at[2 * i + (0 if along_x else 1)])

    def second(self, k, along_x):
        if along_x:
            return remote(self.part(k, self.py, True), self.two[k].at[0], self.ys.at[2, k],
                          self.yr.at[2, k], self.to_y)
        return remote(self.part(k, self.px, False), self.two[k].at[1], self.xs.at[2, k],
                      self.xr.at[2, k], self.to_x)

    def stage1(self):
        self.landed(0, self.far)
        for k in self.arrays:
            self.go(self.first(k, self.far, True))
            self.go(self.first(k, self.far, False))

    def stage2(self):
        self.landed(1, self.px)
        for k in self.arrays:
            self.go(self.first(k, self.px, True))
        self.landed(2, self.py)
        for k in self.arrays:
            self.go(self.first(k, self.py, False))

    def stage3(self):
        self.landed(3, self.mine)
        for k in self.arrays:
            for along_x, p in ((True, self.py), (False, self.px)):
                self.first(k, self.far, along_x).wait_recv()
                add_to(self.part(k, p, along_x), self.one[k].at[0 if along_x else 1])
                self.go(self.second(k, along_x))

    def stage4(self):
        for k in self.arrays:
            for along_x, p in ((True, self.px), (False, self.py)):
                self.first(k, p, along_x).wait_recv()
                add_to(self.part(k, self.mine, along_x), self.one[k].at[2 if along_x else 3])

    def last(self, k, o):
        z, x, y, c = self.place
        layer = (z + o) % 4
        return remote(self.held(k, self.mine).at[layer], self.deep[k].at[4 - o],
                      self.zs.at[o, k], self.zr.at[4 - o, k], at_place(layer, x, y, c))

    def stage5(self):
        for k in self.arrays:
            for along_x in (True, False):
                self.second(k, along_x).wait_recv()
                add_to(self.part(k, self.mine, along_x), self.two[k].at[0 if along_x else 1])
            for o in (1, 2, 3):
                self.go(self.last(k, o))

    def stage6(self):
        z, x, y, c = self.place
        for k in self.arrays:
            value = self.held(k, self.mine)[z].astype(f32)
            for o in (1, 2, 3):
                here = self.deep[k].at[o]
                remote(here, here, self.zs.at[o, k], self.zr.at[o, k],
                       at_place((z + o) % 4, x, y, c)).wait_recv()
                value = value + self.deep[k][o].astype(f32)
            self.outs[k][...] = value

    def advance(self, upto):
        while self.done < upto:
            self.stages[self.done]()
            self.done += 1

    def drain(self):
        for copy in self.started:
            copy.wait_send()


class Total:
    def __init__(self, small, out, scratch):
        self.small, self.out = small, out
        self.at_c, self.at_p, self.at_z, self.ss, self.rs = scratch
        self.place = z, x, y, c = place()
        self.plane = ((1 - x, y), (x, 1 - y), (1 - x, 1 - y))
        self.started = []

    def swap(self, buffer, index, n, m, target):
        here = buffer.at[index]
        copy = remote(here, here, self.ss.at[n], self.rs.at[m], target)
        copy.start()
        self.started.append(copy)

    def arrive(self, buffer, index, n, target):
        here = buffer.at[index]
        remote(here, here, self.ss.at[n], self.rs.at[n], target).wait_recv()

    def start(self):
        z, x, y, c = self.place
        self.at_c[c] = self.small[...]
        self.swap(self.at_c, c, 0, 0, at_place(z, x, y, 1 - c))

    def middle(self):
        z, x, y, c = self.place
        self.arrive(self.at_c, 1 - c, 0, at_place(z, x, y, 1 - c))
        self.at_p[x * 2 + y] = self.at_c[0] + self.at_c[1]
        for n, p in enumerate(self.plane):
            self.swap(self.at_p, x * 2 + y, 1 + n, 1 + n, at_place(z, *p, c))

    def late(self):
        z, x, y, c = self.place
        for n, p in enumerate(self.plane):
            self.arrive(self.at_p, p[0] * 2 + p[1], 1 + n, at_place(z, *p, c))
        self.at_z[z] = (self.at_p[0] + self.at_p[1]) + (self.at_p[2] + self.at_p[3])
        for o in (1, 2, 3):
            self.swap(self.at_z, z, 3 + o, 7 - o, at_place((z + o) % 4, x, y, c))

    def finish(self):
        z, x, y, c = self.place
        for o in (1, 2, 3):
            self.arrive(self.at_z, (z + o) % 4, 3 + o, at_place((z + o) % 4, x, y, c))
        self.out[...] = (self.at_z[0] + self.at_z[1]) + (self.at_z[2] + self.at_z[3])
        for copy in self.started:
            copy.wait_send()


def total_scratch(dims):
    return [
        pltpu.VMEM((2,) + dims, f32), pltpu.VMEM((4,) + dims, f32), pltpu.VMEM((4,) + dims, f32),
        sems(7), sems(7),
    ]


def reduce_wide_scratch(dims):
    rows, lanes = dims
    return [
        pltpu.VMEM((4,) + dims, bf16), pltpu.VMEM((4, 4) + dims, bf16),
        pltpu.VMEM((4, 4) + dims, bf16), pltpu.VMEM((4, rows // 2, lanes), bf16),
        pltpu.VMEM((2, rows // 2, lanes), bf16),
        sems(4), sems(4), sems(4), sems(4, 4), sems(4, 4), sems(4), sems(4), sems(2), sems(2),
    ]


class ReduceWide:
    def __init__(self, source, out, scratch):
        self.source, self.out = source, out
        (self.stage, self.own, self.deep, self.one, self.two, self.loc, self.cs, self.cr, self.zs,
         self.zr, self.ps, self.pr, self.qs, self.qr) = scratch
        self.place = z, x, y, c = place()
        self.spots = [(x, y), (1 - x, y), (x, 1 - y), (1 - x, 1 - y)]
        self.other = at_place(z, x, y, 1 - c)
        self.to_x, self.to_y = at_place(z, 1 - x, y, c), at_place(z, x, 1 - y, c)
        self.rows = source.shape[2] // 2
        self.started = []
        self.done = 0
        self.stages = [self.stage1, self.stage2, self.stage3, self.stage4, self.stage5, self.stage6]

    def go(self, copy):
        copy.start()
        self.started.append(copy)

    def theirs(self, n):
        c = self.place[3]
        return remote(self.source.at[:, member_of(*self.spots[n], 1 - c)], self.own.at[n],
                      self.cs.at[n], self.cr.at[n], self.other)

    def ours(self, n):
        c = self.place[3]
        return pltpu.make_async_copy(self.source.at[:, member_of(*self.spots[n], c)],
                                     self.stage, self.loc.at[n])

    def start(self):
        for n in range(4):
            self.go(self.theirs(n))
        self.ours(0).start()

    def landed(self, n):
        z, x, y, c = self.place
        self.ours(n).wait()
        self.theirs(n).wait_recv()
        add_to(self.own.at[n], self.stage)
        if n < 3:
            self.ours(n + 1).start()
        for o in (1, 2, 3):
            layer = (z + o) % 4
            self.go(remote(self.own.at[n, layer], self.deep.at[n, 4 - o], self.zs.at[o, n],
                           self.zr.at[4 - o, n], at_place(layer, x, y, c)))

    def stage1(self):
        self.landed(0)
        self.landed(1)

    def stage2(self):
        self.landed(2)
        self.landed(3)

    def gathered(self, n):
        z, x, y, c = self.place
        total = self.own[n, z].astype(f32)
        for o in (1, 2, 3):
            here = self.deep.at[n, o]
            remote(here, here, self.zs.at[o, n], self.zr.at[o, n],
                   at_place((z + o) % 4, x, y, c)).wait_recv()
            total = total + self.deep[n, o].astype(f32)
        self.own[n, z] = total.astype(bf16)

    def part(self, n, along_x):
        at = 0 if along_x else self.rows
        return self.own.at[n, self.place[0], at : at + self.rows]

    def first(self, i):
        n, along_x = ((3, True), (3, False), (1, True), (2, False))[i]
        return remote(self.part(n, along_x), self.one.at[i], self.ps.at[i], self.pr.at[i],
                      self.to_x if along_x else self.to_y)

    def second(self, along_x):
        if along_x:
            return remote(self.part(2, True), self.two.at[0], self.qs.at[0], self.qr.at[0], self.to_y)
        return remote(self.part(1, False), self.two.at[1], self.qs.at[1], self.qr.at[1], self.to_x)

    def add(self, n, along_x, source):
        at = 0 if along_x else self.rows
        z = self.place[0]
        rows = slice(at, at + self.rows)
        self.own[n, z, rows] = (
            self.own[n, z, rows].astype(f32) + source[...].astype(f32)
        ).astype(bf16)

    def stage3(self):
        for n in (0, 1, 2, 3):
            self.gathered(n)
        for i in range(4):
            self.go(self.first(i))

    def stage4(self):
        for i, (n, along_x) in enumerate(((2, True), (1, False))):
            self.first(i).wait_recv()
            self.add(n, along_x, self.one.at[i])
            self.go(self.second(along_x))

    def stage5(self):
        for i, along_x in ((2, True), (3, False)):
            self.first(i).wait_recv()
            self.add(0, along_x, self.one.at[i])

    def stage6(self):
        z = self.place[0]
        for i, along_x in ((0, True), (1, False)):
            self.second(along_x).wait_recv()
            at = 0 if along_x else self.rows
            rows = slice(at, at + self.rows)
            self.out[rows] = self.own[0, z, rows].astype(f32) + self.two[i].astype(f32)

    def advance(self, upto):
        while self.done < upto:
            self.stages[self.done]()
            self.done += 1

    def drain(self):
        for copy in self.started:
            copy.wait_send()


def norm_parts(values):
    average = jnp.mean(values, axis=-1, keepdims=True)
    centred = values - average
    variance = jnp.mean(centred * centred, axis=-1, keepdims=True)
    inverse = lax.rsqrt(variance + epsilon)
    return centred * inverse, inverse


def norm_backward(hat, inverse, gain, grad):
    scaled = grad * gain
    first = jnp.mean(scaled, axis=-1, keepdims=True)
    second = jnp.mean(scaled * hat, axis=-1, keepdims=True)
    return (scaled - first - hat * second) * inverse


def compact(j, rows, packed, places):
    for place, size in places:
        packed[place + size * j : place + size * j + size] = rows[:size]


def widen(pieces):
    total = pieces[-1]
    for piece in reversed(pieces[:-1]):
        blank = jnp.zeros((piece.shape[0], piece.shape[1] - total.shape[1]), f32)
        total = piece + jnp.concatenate([total, blank], axis=1)
    return total


def join_quad(quad, read):
    wide = jnp.concatenate(
        [swap_chunks(read(4 * quad + i), 4 * quad + i) for i in range(4)], axis=0
    )
    return swap_blocks(wide.T, quad)


def join_quads(read):
    pairs = []
    for half in range(2):
        pairs.append(
            jnp.concatenate([join_quad(quad, read) for quad in (2 * half, 2 * half + 1)], axis=1)
        )
    return jnp.concatenate(pairs, axis=1)


def unit_forward(query, key, out):
    lane = lax.broadcasted_iota(jnp.int32, (256, LANES), 1)
    count = len(query)
    scores = [matmul(query[i](), key, NT) for i in range(count)]
    for i in range(count):
        top = jnp.max(scores[i], axis=1, keepdims=True) * scale2
        prob = jnp.exp2(scores[i] * scale2 - top).astype(bf16)
        value = jnp.where(lane == FLAG + 8, top, matmul(prob, key))
        out[i](value.T[HD : HD + 64])


def forward_kernel(grp, slides, gather, *refs):
    refs = list(refs)
    take = lambda n: [refs.pop(0) for _ in range(n)]
    tokens, cot_in, valid, coordinates, ends, frequency = take(6)
    vectors, in_bias = take(6), take(1)[0]
    query_bias, value_bias = take(2)
    shards = take(6) if gather else take(0)
    given = take(0) if gather else take(4)
    base, msg, q_ref, kv_ref, kv8, kv16, stat = take(7)
    out, grad_middle, grad_merged, small = take(4)
    late_grads = take(3)
    gathered = take(1) if gather else take(0)
    send, osend, orecv, acc, qc, kvc, tok_sem, ss, rs, os_, or_, ds, dr = take(13)
    wo, wi, wt = take(3)
    dense_scratch = take(10)
    raw, lines_ref, save_sem = take(3)
    weight = gathered[0] if gather else given[0]
    cot = dense_scratch[0]
    spot = Spot(grp)
    joined = spot.greet()

    def load(source):
        copies = []
        for c in range(6):
            part = source.at[:, LANES * c : LANES * c + LANES]
            copies.append(pltpu.make_async_copy(part, raw.at[c], tok_sem.at[c]))
            copies[-1].start()
        return copies

    def ordered(copies, target):
        for copy in copies:
            copy.wait()
        for b in range(16):
            rows = [raw[c, pl.ds(order[b], BLOCK, stride=16), :] for c in range(6)]
            target[BLOCK * b : BLOCK * b + BLOCK] = jnp.concatenate(rows, axis=1)

    loads = load(tokens)
    vectors = [item[...].reshape(1, 768) for item in vectors]
    if gather:
        (joint_shard,) = take(1)
        pieces = []
        for inner in range(4):
            pieces += [item[:, HD * inner : HD * inner + HD] for item in shards[:3]]
        joint_shard[...] = jnp.concatenate(pieces, axis=1)
        first = Gather([joint_shard], gathered[:1], take(9))
        rest = Gather([shards[3], shards[4].at[:64]], [wo, wi.at[:, :, :64]], take(9))
        last = Gather([shards[5]], [wt], take(9))
        wide_part = GatherWide(shards[4].at[64:], wi.at[:, :, 64:], take(9))
        joined()
        first.start_layers()
        first.push_own()
        wide_part.start()
        rest.push_own()
    else:
        loads_late = [
            pltpu.make_async_copy(source, target, save_sem.at[n])
            for n, (source, target) in enumerate(zip(given[1:], (wo, wi, wt)))
        ]
        for copy in loads_late:
            copy.start()
    place_lane = lax.broadcasted_iota(jnp.int32, (1, 512), 1)
    b = place_lane // BLOCK
    b = (b % 2) * 8 + (b // 2 % 2) * 4 + (b // 4 % 2) * 2 + b // 8
    position = spot.linear * 512 + place_lane % BLOCK * 16 + b
    along = jnp.concatenate(
        [coordinates[...], valid[...].reshape(1, 512), jnp.zeros((LANES - 3, 512), jnp.int32)], axis=0
    )
    lines_ref[...] = along.astype(f32).T
    spots = jnp.concatenate(
        [lines_ref[pl.ds(order[b], BLOCK, stride=16), :] for b in range(16)], axis=0
    )
    keep = spots.T[2:3]
    lines = [jnp.where(keep == 1.0, 0.0, -BIG)]
    before = 0
    for n in range(slides):
        after = before + ends[n]
        inside = (position >= before) & (position < after)
        lines.append(jnp.where(inside, 0.0, -BIG))
        before = after
    lines += [jnp.ones((1, 512), f32), jnp.zeros((14 - slides, 512), f32)]
    flags_all = jnp.concatenate(lines, axis=0)
    gain, shift = vectors[:2]
    lane = lax.broadcasted_iota(jnp.int32, (512, 384), 1)
    angle = jnp.where(lane < 192, spots[:, 0:1], spots[:, 1:2]) * frequency[...]
    sine, cosine = jnp.sin(angle), jnp.cos(angle)
    table = jnp.concatenate(
        [
            jnp.concatenate([sine[:, :192], cosine[:, :192]], axis=1),
            jnp.concatenate([sine[:, 192:], cosine[:, 192:]], axis=1),
        ],
        axis=1,
    )
    ordered(loads, base)
    base[...] = base[...] + table
    loads = load(cot_in)
    hat, _ = norm_parts(base[...])
    normed = (hat * gain + shift).astype(bf16)
    if gather:
        first.advance(1)
        rest.start_layers()
        last.start_layers()
        first.advance(3)
        wide_part.advance(1)
        first.finish()
        wide_part.advance(2)
    else:
        joined()
    qb, vb = query_bias[...].reshape(1, 768), value_bias[...].reshape(1, 768)
    plane = [Exchange(spot, send.at[i], msg.at[i], ss.at[i], rs.at[i]) for i in range(2)]
    for quad in range(4):
        pieces = []
        for inner in range(4):
            at = HD * (4 * quad + inner)
            pieces += [qb[:, at : at + HD], jnp.zeros((1, HD), f32), vb[:, at : at + HD]]
        part = matmul(normed, pick(weight, quad)) + jnp.concatenate(pieces, axis=1)
        wide = swap_blocks(part.astype(bf16), quad).T
        flags = flags_all
        flags = jnp.concatenate(
            [flags[:, BLOCK * (b ^ block_swap(quad)) :][:, :BLOCK] for b in range(16)], axis=1
        ).astype(bf16)
        for inner in (0, 2, 1, 3):
            head = 4 * quad + inner
            owner, i = head // 2, head % 2
            own = swap_chunks(wide[144 * inner : 144 * inner + 144], head)
            send[i, owner, :96] = own[48:]
            send[i, owner, 96:112] = swap_chunks(flags, head)
            send[i, owner, 112:] = own[:48]
            if i == 0:
                plane[0].send(owner)
    for owner in range(GROUP):
        plane[1].send(owner)
    row = lax.broadcasted_iota(jnp.int32, (16, 512), 0)
    deeps = []
    results = [Exchange(spot, osend.at[i], orecv.at[i], os_.at[i], or_.at[i]) for i in range(2)]
    if gather:
        rest.advance(1)
        last.push_own()
        last.advance(1)
    for i in range(2):
        q, kv = q_ref.at[i], kv_ref.at[i]
        for j in range(GROUP):
            plane[i].wait(j)
            block = msg[i, j]
            key_part = jnp.concatenate([block[:112], jnp.zeros((16, 512), bf16)], axis=0).T
            flags = block[96:112].astype(f32)
            chosen = jnp.where(
                row == 0, 1.0, jnp.where((row <= slides) & (flags == 0.0), 1.0, 0.0)
            )
            query_part = jnp.concatenate(
                [block[112:], jnp.zeros((HD, 512), bf16), chosen.astype(bf16),
                 jnp.zeros((16, 512), bf16)],
                axis=0,
            ).T
            kv[512 * j : 512 * j + 512] = key_part
            q[512 * j : 512 * j + 512] = query_part
            compact(j, query_part, qc, ((0, 256), (2048, 128), (3072, 64), (3584, 32)))
            compact(j, key_part, kvc, ((0, 256), (2048, 128)))
            kv8[spot.half, i, 64 * j : 64 * j + 64] = key_part[:64]
            kv16[spot.layer, i, 32 * j : 32 * j + 32] = key_part[:32]
        own8, own16 = kv8.at[spot.half, i], kv16.at[spot.layer, i]
        deep = Deep(
            spot, (own8, own8, kv8.at[1 - spot.half, i]),
            lambda o, other: (own16, own16, kv16.at[other, i]), ds.at[i], dr.at[i],
        )
        deep.start()
        deeps.append(deep)

        def unit(source, q_from, keys, k_from, out_from, count):
            def reader(n):
                return lambda: source[pl.ds(q_from + 256 * n, 256)]

            def writer(n):
                def save(value):
                    acc[:, pl.ds(out_from + 256 * n, 256)] = value

                return save

            unit_forward(
                [reader(n) for n in range(count)], keys[pl.ds(k_from, 1024)],
                [writer(n) for n in range(count)],
            )

        def early(u, _):
            at = pl.multiple_of(u * 1024, 1024)
            unit(q, at, kv, at, at, 4)
            return 0

        lax.fori_loop(0, 4, early, 0)
        if gather:
            rest.advance(1 + 2 * i)

        def late(u, _):
            at = pl.multiple_of(u * 1024, 1024)
            unit(qc, at, kvc, at, pl.multiple_of(at + 4096, 1024), 4)
            return 0

        lax.fori_loop(0, 3, late, 0)
        deep.wait()
        for n in range(2):
            kvc[3072 + 512 * n : 3584 + 512 * n] = kv8[n, i]
        for n in range(4):
            kvc[4096 + 256 * n : 4352 + 256 * n] = kv16[n, i]
        unit(qc, 3072, kvc, 3072, 7168, 2)
        unit(qc, 3584, kvc, 4096, 7680, 1)
        place = lax.broadcasted_iota(jnp.int32, (1, 512), 1)
        uses = jnp.where(place < 32, 5.0, jnp.where(place < 64, 4.0, jnp.where(
            place < 128, 3.0, jnp.where(place < 256, 2.0, 1.0))))
        for j in range(GROUP):
            key = msg[i, j, :HD].astype(f32)
            value = msg[i, j, HD : 2 * HD].astype(f32)
            query = msg[i, j, 112:].astype(f32)
            dropped = msg[i, j, FLAG : FLAG + 1].astype(f32) != 0.0
            own = jnp.where(dropped, column_sum(query * key) * scale2 + jnp.log2(uses), -BIG)
            pieces = [
                acc[:, q_at[r] + (512 >> r) * j : q_at[r] + (512 >> r) * (j + 1)] for r in range(5)
            ]
            top = own
            tops = [piece[HD + 8 : HD + 9] for piece in pieces]
            for item in tops:
                spread = item
                if spread.shape[1] < 512:
                    blank = jnp.full((1, 512 - spread.shape[1]), -BIG, f32)
                    spread = jnp.concatenate([spread, blank], axis=1)
                top = jnp.maximum(top, spread)
            scaled = [
                piece[: HD + 8] * jnp.exp2(item - top[:, : item.shape[1]])
                for piece, item in zip(pieces, tops)
            ]
            mix = widen(scaled)
            weight_own = jnp.exp2(own - top)
            total = mix[HD + 1 + slides : HD + 2 + slides] + weight_own
            result = (mix[:HD] + weight_own * value) / total
            stat[i, j, :HD] = result
            stat[i, j, HD : HD + 8] = jnp.broadcast_to(top + jnp.log2(total), (8, 512))
            osend[i, j] = result.astype(bf16)
            results[i].send(j)
        if gather:
            rest.advance(2 + 2 * i)
    if gather:
        wide_part.advance(4)
        last.advance(2)
    for i in range(2):
        for j in range(GROUP):
            results[i].wait(j)
    ordered(loads, cot)
    merged = dense_scratch[1]

    def ready(step):
        if not gather:
            for copy in loads_late if step == 0 else ():
                copy.wait()
        elif step == 0:
            rest.finish()
            last.advance(3)
        elif step == 1:
            wide_part.advance(5)
        else:
            last.finish()
            for item in (first, rest, wide_part, last):
                item.drain()

    merged[...] = join_quads(lambda h: orecv[h % 2, h // 2])
    dense_part(
        merged, base, cot, wo, wi, wt, vectors, in_bias, out, grad_middle, grad_merged, small,
        late_grads, save_sem, ready, *dense_scratch[2:],
    )
    for item in plane + deeps + results:
        item.drain()


def dense_part(
    merged, base, cot, wo, wi, wt, vectors, in_bias, out, grad_middle, grad_merged, small,
    late_grads, save_sem, ready, hat, low, low_t, cot_low, cot_t, grad_low, acts, slopes,
):
    out_bias, gain, shift, last_bias = vectors[2:]
    ready(0)
    pairs = []
    for g in range(0, 4, 2):
        pair = [pick(wo, g + i) for i in range(2)]
        pairs.append(jnp.concatenate(pair, axis=1))
    full = jnp.concatenate(pairs, axis=1)
    middle = base[...] + matmul(merged[...], full) + out_bias
    out[...] = middle + last_bias
    normal, inverse = norm_parts(middle)
    hat[...] = normal
    low[...] = (normal * gain + shift).astype(bf16)
    low_t[...] = low[...].T
    cot_low[...] = cot[...].astype(bf16)
    cot_t[...] = cot_low[...].T
    small[0:1] = column_sum(cot_low[...].astype(f32))
    grad_middle[...] = jnp.zeros((512, 768), f32)

    ready(1)

    def early(g, _):
        inner = matmul(low[...], pick(wi, g)) + in_bias[
            pl.ds(pl.multiple_of(768 * g, 768), 768)
        ].reshape(1, 768)
        phi = 0.5 * (1.0 + lax.erf(inner * 0.7071067811865476))
        acts[g] = (inner * phi).astype(bf16)
        slopes[g] = (phi + inner * jnp.exp(-0.5 * inner * inner) * 0.3989422804014327).astype(bf16)
        return 0

    lax.fori_loop(0, 4, early, 0)
    ready(2)

    def late(g, _):
        for x in range(2):
            lanes = slice(384 * x, 384 * x + 384)
            part = wt[g, 4 * x : 4 * x + 4].reshape(768, 384)
            now = acts[g, :, lanes]
            out[...] += matmul(now, part, NT)
            back = matmul(cot_low[...], part)
            wt[g, 4 * x : 4 * x + 4] = (
                matmul(cot_t[...], now).astype(bf16).reshape(4, 192, 384)
            )
            grad_low[:, lanes] = (back * slopes[g, :, lanes].astype(f32)).astype(bf16)
        small[pl.ds(4 + g, 1)] = column_sum(grad_low[...].astype(f32))
        grad_middle[...] += matmul(grad_low[...], pick(wi, g), NT)
        put(wi, g, matmul(low_t[...], grad_low[...]).astype(bf16))
        return 0

    lax.fori_loop(0, 4, late, 0)
    saves = [
        pltpu.make_async_copy(source, target, save_sem.at[n])
        for n, (source, target) in enumerate(zip((wo, wi, wt), late_grads))
    ]
    saves[1].start()
    saves[2].start()
    grad = grad_middle[...]
    small[1:2] = column_sum(grad * hat[...])
    small[2:3] = column_sum(grad)
    grad = cot[...] + norm_backward(hat[...], inverse, gain, grad)
    grad_middle[...] = grad
    attended = grad.astype(bf16)
    small[3:4] = column_sum(attended.astype(f32))
    grad_merged[...] = matmul(attended, full, NT).astype(bf16)
    grads = matmul(merged[...].T, attended).astype(bf16)
    for g in range(4):
        put(wo, g, grads[:, 192 * g : 192 * g + 192])
    saves[0].start()
    for copy in saves:
        copy.wait()


def attention_forward(grp, slides, gather, inputs, weights):
    out_shape = [
        shape((512, 768), f32),
        shape((2, GROUP, MSG, 512), bf16),
        shape((2, 4096, LANES), bf16),
        shape((2, 4096, LANES), bf16),
        shape((2, 2, 512, LANES), bf16),
        shape((4, 2, 256, LANES), bf16),
        shape((2, GROUP, 56, 512), f32),
        shape((512, 768), f32),
        shape((512, 768), f32),
        shape((512, 768), bf16),
        shape((8, 768), f32),
    ]
    blocks = [(4, GROUP, 96, 192), (4, GROUP, 96, 768), (4, GROUP, 192, 384)]
    out_specs = [vmem()] * len(out_shape) + [anywhere()] * 3
    out_shape += [shape(dims, bf16) for dims in blocks]
    in_specs = [anywhere()] * 2 + [vmem()] * 2 + [pl.BlockSpec(memory_space=pltpu.SMEM)]
    in_specs += [vmem()] * 10
    extra = []
    if gather:
        in_specs += [vmem()] * 3 + [anywhere()] * 3
        out_shape += [shape((4, GROUP, 96, 576), bf16)]
        out_specs += [vmem()]
        extra = [pltpu.VMEM((96, 576), bf16)]
        extra += gather_sems(1) + gather_sems(2) + gather_sems(1) + gather_wide_sems()
    else:
        in_specs += [vmem()] + [anywhere()] * 3
    rows = (512, 768)
    return pl.pallas_call(
        functools.partial(forward_kernel, grp, slides, gather),
        name="forward_and_feed",
        in_specs=in_specs,
        out_specs=out_specs,
        out_shape=out_shape,
        scratch_shapes=[
            pltpu.VMEM((2, GROUP, MSG, 512), bf16),
            pltpu.VMEM((2, GROUP, HD, 512), bf16),
            pltpu.VMEM((2, GROUP, HD, 512), bf16),
            pltpu.VMEM((64, q_all), f32),
            pltpu.VMEM((q_all - 4096, LANES), bf16),
            pltpu.VMEM((k_all - 4096, LANES), bf16),
            sems(6),
            sems(2, GROUP), sems(2, GROUP), sems(2, GROUP), sems(2, GROUP), sems(2, 4), sems(2, 4),
        ]
        + [pltpu.VMEM(dims, bf16) for dims in blocks]
        + [
            pltpu.VMEM(rows, f32), pltpu.VMEM(rows, bf16), pltpu.VMEM(rows, f32),
            pltpu.VMEM(rows, bf16), pltpu.VMEM((768, 512), bf16),
            pltpu.VMEM(rows, bf16), pltpu.VMEM((768, 512), bf16), pltpu.VMEM(rows, bf16),
            pltpu.VMEM((4,) + rows, bf16), pltpu.VMEM((4,) + rows, bf16),
            pltpu.VMEM((6, 512, LANES), f32), pltpu.VMEM((512, LANES), f32), sems(3),
        ]
        + extra,
        compiler_params=params(1),
    )(*inputs, *weights)


def backward_kernel(grp, reduce, *refs):
    refs = list(refs)
    take = lambda n: [refs.pop(0) for _ in range(n)]
    gm, gain_ref, shift_ref, small = take(4)
    saved = take(6)
    base_in, middle_in, weight_in = take(3)
    parts = take(3) if reduce else take(0)
    token_grad, joint_out, pack = take(3)
    reduced = take(3) if reduce else take(0)
    (gsend, grecv, rsend, rrecv, got8, got16, send8, send16, rows_ref,
     gs, gr, ss, rs, ds, dr, load_sem) = take(16)
    local = take(13)
    (grads,) = take(1)
    spot = Spot(grp)
    joined = spot.greet()
    shares = [Exchange(spot, gsend.at[i], grecv.at[i], gs.at[i], gr.at[i]) for i in range(2)]
    backs = [Exchange(spot, rsend.at[i], rrecv.at[i], ss.at[i], rs.at[i]) for i in range(2)]
    deeps = []
    if reduce:
        ins = [parts[0], parts[1].at[:, :, :64], parts[2]]
        outs = [reduced[0], reduced[1].at[:64], reduced[2]]
        sums = Reduce(ins, outs, take(len(reduce_scratch([(0, 0)] * 3))))
        wide_sum = ReduceWide(parts[1].at[:, :, 64:], reduced[1].at[64:], take(14))
        last_scratch = [take(len(reduce_scratch([(32, 576)])) - 1) for _ in range(3)]
        total_sum = take(5)
    else:
        sums = wide_sum = None

    attend_backward(
        spot, joined, gm, saved, shares, backs, deeps, sums, wide_sum, gsend, grecv, rsend,
        got8, got16, send8, send16, ds, dr, load_sem, *local,
    )
    rows_f32 = local[11]
    late_loads = [pltpu.make_async_copy(weight_in, grads, load_sem.at[0])]
    for n, source in enumerate((base_in, middle_in)):
        for chunk in range(6):
            at = 3072 * n + 512 * chunk
            late_loads.append(
                pltpu.make_async_copy(
                    source.at[:, LANES * chunk : LANES * chunk + LANES],
                    rows_f32.at[at : at + 512],
                    load_sem.at[1 + 6 * n + chunk],
                )
            )
    for copy in late_loads:
        copy.start()

    def loaded(n):
        at = 3072 * n
        return jnp.concatenate(
            [rows_f32[at + 512 * chunk : at + 512 * chunk + 512] for chunk in range(6)], axis=1
        )

    for copy in late_loads:
        copy.wait()
    gain, shift = gain_ref[...].reshape(1, 768), shift_ref[...].reshape(1, 768)
    hat, inverse = norm_parts(loaded(0))
    low_t = (hat * gain + shift).astype(bf16).T
    for i in range(2):
        for j in range(GROUP):
            backs[i].wait(j)
    if reduce:
        wide_sum.advance(4)
    lines = [[], []]
    grad = jnp.zeros((512, 768), f32)
    for quad in range(4):

        def read(head):
            block = rrecv[head % 2, head // 2]
            return jnp.concatenate([block[2 * HD :], block[: 2 * HD]], axis=0)

        now = join_quad(quad, read)
        grad = grad + matmul(now, pick(grads, quad), NT)
        put(grads, quad, matmul(low_t, now).astype(bf16))
        total = column_sum(now.astype(f32))
        for inner in range(4):
            lines[0].append(total[:, 144 * inner : 144 * inner + HD])
            lines[1].append(total[:, 144 * inner + 96 : 144 * inner + 144])
    if reduce:
        joint = []
        for n in range(3):
            rows = slice(32 * n, 32 * n + 32)
            joint.append(
                Reduce([grads.at[:, :, rows]], [joint_out.at[rows]], [None] + last_scratch[n])
            )
            joint[n].start()
        wide_sum.advance(5)

    def flow(step):
        for n, item in enumerate(joint):
            item.advance(min(max(step - n, 0), 6))

    rows_ref[0:1] = column_sum(grad * hat)
    rows_ref[1:2] = column_sum(grad)
    rows_ref[2:3] = jnp.concatenate(lines[0], axis=1)
    rows_ref[3:4] = jnp.concatenate(lines[1], axis=1)
    rows_ref[4:5] = small[3:4]
    rows_ref[5:6] = small[1:2]
    rows_ref[6:7] = small[2:3]
    rows_ref[7:8] = small[0:1]
    rows_ref[8:12] = small[4:8]
    rows_ref[12:16] = jnp.zeros((4, 768), f32)
    token_grad[...] = loaded(1) + norm_backward(hat, inverse, gain, grad)
    if reduce:
        rest = Total(rows_ref, pack, total_sum)
        rest.start()
        flow(1)
        flow(2)
        rest.middle()
        flow(3)
        flow(4)
        rest.late()
        for step in range(5, 8):
            flow(step)
        sums.advance(6)
        wide_sum.advance(6)
        flow(8)
        rest.finish()
        for item in joint:
            item.drain()
    else:
        pack[...] = rows_ref[...]
        save = pltpu.make_async_copy(grads, joint_out, load_sem.at[3])
        save.start()
        save.wait()
    if reduce:
        sums.drain()
        wide_sum.drain()
    for item in shares + backs + deeps:
        item.drain()


def attend_backward(
    spot, joined, gm, saved, shares, backs, deeps, sums, wide_sum, gsend, grecv, rsend, got8, got16,
    send8, send16, ds, dr, load_sem, q_ref, kv_ref, kv8, kv16, msg, stat,
    qc, kvc, dor, kt, ld, dkv, dqt,
):
    reduce = sums is not None
    loads = [
        pltpu.make_async_copy(source, target, load_sem.at[n])
        for n, (source, target) in enumerate(zip(saved, (q_ref, kv_ref, kv8, kv16, msg, stat)))
    ]
    for copy in loads:
        copy.start()
    for quad in range(4):
        wide = swap_blocks(gm[:, 192 * quad : 192 * quad + 192], quad).T
        for inner in (0, 2, 1, 3):
            head = 4 * quad + inner
            i = head % 2
            gsend[i, head // 2] = swap_chunks(wide[HD * inner : HD * inner + HD], head)
            if quad == 0 and inner == 0:
                joined()
            if i == 0:
                shares[0].send(head // 2)
    for j in range(GROUP):
        shares[1].send(j)
    if reduce:
        wide_sum.start()
        sums.start()
    for copy in loads:
        copy.wait()
    for i in range(2):
        q, kv = q_ref.at[i], kv_ref.at[i]
        for n in range(2):
            kvc[3072 + 512 * n : 3584 + 512 * n] = kv8[n, i]
        for n in range(4):
            kvc[4096 + 256 * n : 4352 + 256 * n] = kv16[n, i]
        for n in range(2):
            kt[7 + n] = kvc[3072 + 1024 * n : 4096 + 1024 * n].T[:HD]
        rows = []
        for j in range(GROUP):
            compact(j, q[512 * j : 512 * j + 512], qc, ((0, 256), (2048, 128), (3072, 64), (3584, 32)))
            compact(j, kv[512 * j : 512 * j + 512], kvc, ((0, 256), (2048, 128)))
            key = msg[i, j, :HD]
            kt[j // 2, :, 512 * (j % 2) : 512 * (j % 2) + 512] = key
            kt[4 + j // 4, :, 256 * (j % 4) : 256 * (j % 4) + 256] = key[:, :256]
            kt[6, :, 128 * j : 128 * j + 128] = key[:, :128]
        for j in range(GROUP):
            shares[i].wait(j)
            grad = grecv[i, j]
            delta = column_sum(grad.astype(f32) * stat[i, j, :HD])
            both = jnp.concatenate(
                [stat[i, j, HD : HD + 1], delta, jnp.zeros((6, 512), f32)], axis=0
            )
            rows.append(both)
            ld[:, 512 * j : 512 * j + 512] = both
            ld[:, 4096 + 256 * j : 4352 + 256 * j] = both[:, :256]
            ld[:, 6144 + 128 * j : 6272 + 128 * j] = both[:, :128]
            tall = jnp.concatenate(
                [jnp.zeros((HD, 512), bf16), grad, jnp.zeros((32, 512), bf16)], axis=0
            ).T
            for r, at in enumerate(q_at):
                size = 512 >> r
                dor[at + size * j : at + size * j + size] = tall[:size]
        ld[:, 7168:7680] = jnp.concatenate([both[:, :64] for both in rows], axis=1)
        ld[:, 7680:7936] = jnp.concatenate([both[:, :32] for both in rows], axis=1)

        def unit(source, q_from, keys, k_from, at, seg, count):
            width = 256 * count
            query = source[pl.ds(q_from, width)]
            grad = dor[pl.ds(at, width)]
            total = ld[0:1, pl.ds(at, width)]
            delta = ld[1:2, pl.ds(at, width)]
            sides = jnp.concatenate([grad, query], axis=0)
            size = 256
            dq = jnp.zeros((HD, width), f32)
            for c in range(1024 // size):
                key = keys[pl.ds(k_from + size * c, size)]
                prob = jnp.exp2(matmul(key, query, NT) * scale2 - total)
                slope = (prob * (matmul(key, grad, NT) - delta)).astype(bf16)
                both = jnp.concatenate([prob.astype(bf16), slope], axis=1)
                dkv[pl.ds(seg * 1024 + size * c, size)] = matmul(both, sides)
                dq = dq + matmul(kt[seg, :, size * c : size * c + size], slope)
            dqt[:, pl.ds(at, width)] = dq

        unit(qc, 3072, kvc, 3072, 7168, 7, 2)
        unit(qc, 3584, kvc, 4096, 7680, 8, 1)
        for n in range(2):
            send8[n, i] = dkv[7168 + 512 * n : 7680 + 512 * n].astype(bf16)
        for n in range(4):
            send16[n, i] = dkv[8192 + 256 * n : 8448 + 256 * n].astype(bf16)
        deep = Deep(
            spot, (send8.at[1 - spot.half, i], got8.at[i], got8.at[i]),
            lambda o, other: (send16.at[other, i], got16.at[4 - o, i], got16.at[o, i]),
            ds.at[i], dr.at[i],
        )
        deep.start()
        deeps.append(deep)
        if reduce:
            if i == 0:
                sums.advance(1)
                wide_sum.advance(1)

        def late(u, _):
            at = pl.multiple_of(u * 1024, 1024)
            unit(qc, at, kvc, at, pl.multiple_of(at + 4096, 1024), u + 4, 4)
            return 0

        lax.fori_loop(0, 3, late, 0)
        if reduce:
            sums.advance(2 + 2 * i)
            wide_sum.advance(2)
        deep.wait()
        spot_lane = lax.broadcasted_iota(jnp.int32, (1, 512), 1)
        uses = jnp.where(spot_lane < 32, 5.0, jnp.where(spot_lane < 64, 4.0, jnp.where(
            spot_lane < 128, 3.0, jnp.where(spot_lane < 256, 2.0, 1.0))))
        for j in range(GROUP):
            if j % 2 == 0:
                unit(q, 512 * j, kv, 512 * j, 512 * j, j // 2, 4)
            tall = dkv[512 * j : 512 * j + 512]
            eight = send8[spot.half, i, 64 * j : 64 * j + 64].astype(f32) + got8[
                i, 64 * j : 64 * j + 64
            ].astype(f32)
            sixteen = send16[spot.layer, i, 32 * j : 32 * j + 32].astype(f32)
            for o in range(1, 4):
                sixteen = sixteen + got16[o, i, 32 * j : 32 * j + 32].astype(f32)
            second = dkv[4096 + 256 * j : 4352 + 256 * j]
            third = dkv[6144 + 128 * j : 6272 + 128 * j]
            fourth = third[:64] + eight
            fourth = jnp.concatenate([fourth[:32] + sixteen, fourth[32:]], axis=0)
            third = jnp.concatenate([fourth, third[64:]], axis=0)
            second = jnp.concatenate([second[:128] + third, second[128:]], axis=0)
            wide = jnp.concatenate([tall[:256] + second, tall[256:]], axis=0).T
            key = msg[i, j, :HD].astype(f32)
            value = msg[i, j, HD : 2 * HD].astype(f32)
            query = msg[i, j, 112:].astype(f32)
            grad = grecv[i, j].astype(f32)
            total = ld[0:1, 512 * j : 512 * j + 512]
            delta = ld[1:2, 512 * j : 512 * j + 512]
            dropped = msg[i, j, FLAG : FLAG + 1].astype(f32) != 0.0
            dots = column_sum(query * key) * scale2 - total
            prob = jnp.where(dropped, uses * jnp.exp2(jnp.where(dropped, dots, 0.0)), 0.0)
            slope = prob * (column_sum(grad * value) - delta)
            dq = widen([dqt[:, at + (512 >> r) * j : at + (512 >> r) * (j + 1)]
                        for r, at in enumerate(q_at)])
            rsend[i, j, :HD] = ((wide[:HD] + slope * query) * scale).astype(bf16)
            rsend[i, j, HD : 2 * HD] = (wide[HD : 2 * HD] + prob * grad).astype(bf16)
            rsend[i, j, 2 * HD :] = ((dq + slope * key) * scale).astype(bf16)
            backs[i].send(j)
        if reduce:
            sums.advance(3 + 2 * i)
            wide_sum.advance(2 + i)


def attention_backward(grp, reduce, inputs, parts):
    out_shape = [
        shape((512, 768), f32),
        shape((96, 576), f32) if reduce else shape((4, GROUP, 96, 576), bf16),
        shape((16, 768), f32),
    ]
    out_specs = [vmem(), vmem() if reduce else anywhere(), vmem()]
    extra = []
    if reduce:
        dims = [part.shape[2:] for part in parts]
        out_shape += [shape(d, f32) for d in dims]
        out_specs += [vmem()] * 3
        extra = (
            reduce_scratch([dims[0], (64, 768), dims[2]]) + reduce_wide_scratch((32, 768))
            + 3 * reduce_scratch([(32, 576)])[1:] + total_scratch((16, 768))
        )
    return pl.pallas_call(
        functools.partial(backward_kernel, grp, reduce),
        name="attention_backward",
        in_specs=[vmem()] * 4 + [anywhere()] * (9 + len(parts)),
        out_specs=out_specs,
        out_shape=out_shape,
        scratch_shapes=[
            pltpu.VMEM((2, GROUP, HD, 512), bf16),
            pltpu.VMEM((2, GROUP, HD, 512), bf16),
            pltpu.VMEM((2, GROUP, 3 * HD, 512), bf16),
            pltpu.VMEM((2, GROUP, 3 * HD, 512), bf16),
            pltpu.VMEM((2, 512, LANES), bf16),
            pltpu.VMEM((4, 2, 256, LANES), bf16),
            pltpu.VMEM((2, 2, 512, LANES), bf16),
            pltpu.VMEM((4, 2, 256, LANES), bf16),
            pltpu.VMEM((16, 768), f32),
            sems(2, GROUP), sems(2, GROUP), sems(2, GROUP), sems(2, GROUP), sems(2, 4), sems(2, 4),
            sems(13),
            pltpu.VMEM((2, 4096, LANES), bf16), pltpu.VMEM((2, 4096, LANES), bf16),
            pltpu.VMEM((2, 2, 512, LANES), bf16), pltpu.VMEM((4, 2, 256, LANES), bf16),
            pltpu.VMEM((2, GROUP, MSG, 512), bf16), pltpu.VMEM((2, GROUP, 56, 512), f32),
            pltpu.VMEM((q_all - 4096, LANES), bf16), pltpu.VMEM((k_all - 4096, LANES), bf16),
            pltpu.VMEM((q_all, LANES), bf16), pltpu.VMEM((9, HD, 1024), bf16),
            pltpu.VMEM((8, q_all), f32), pltpu.VMEM((k_all, LANES), f32),
            pltpu.VMEM((HD, q_all), f32),
            pltpu.VMEM((4, GROUP, 96, 576), bf16),
        ] + extra,
        compiler_params=params(2),
    )(*inputs, *parts)


def finish_kernel(out_in, token_in, joint, b_in, c_in, d_in, pack, *refs):
    out, token, query, key, value, b_out, c_out, d_out = refs[:8]
    vectors = refs[8:]
    for source, target in ((out_in, out), (token_in, token)):
        for b in range(16):
            target[pl.ds(order[b], BLOCK, stride=16), :] = source[BLOCK * b : BLOCK * b + BLOCK]

    @pl.when(pl.program_id(0) == 0)
    def _():
        for n, target in enumerate((query, key, value)):
            target[...] = jnp.concatenate(
                [joint[:, 144 * i + HD * n : 144 * i + HD * n + HD] for i in range(4)], axis=1
            )
        b_out[...] = b_in[...]
        c_out[...] = c_in[...]
        d_out[...] = d_in[...]
        for n in (0, 1, 2, 3, 4, 5, 6):
            vectors[n][...] = pack[n]
        vectors[7][...] = jnp.concatenate([pack[8 + n] for n in range(4)], axis=0)
        vectors[8][...] = pack[7]


def finish(out, token_grad, joint, b_sum, c_sum, d_sum, pack):
    shard, hidden = b_sum.shape[0], d_sum.shape[1]
    sizes = [768] * 7 + [3072, 768]
    wide = pl.BlockSpec((512, LANES), lambda n: (0, n))
    whole = lambda *dims: pl.BlockSpec(dims, lambda n: (0,) * len(dims))
    small = [(shard, 192)] * 4 + [(shard, 768), (192, hidden)] + [(size,) for size in sizes]
    return pl.pallas_call(
        finish_kernel,
        name="finish",
        grid=(6,),
        in_specs=[wide] * 2 + [whole(*item.shape) for item in (joint, b_sum, c_sum, d_sum, pack)],
        out_specs=[wide] * 2 + [whole(*dims) for dims in small],
        out_shape=[shape((512, 768), f32)] * 2 + [shape(dims, f32) for dims in small],
        compiler_params=params(),
    )(out, token_grad, joint, b_sum, c_sum, d_sum, pack)


def all_weights(parts, seq, grp):
    gathered = []
    for n, part in enumerate(parts):
        whole = lax.all_gather(lax.all_gather(part, "grp"), "seq")
        lead = whole.shape[0] // 8
        whole = whole.reshape((8, lead) + whole.shape[1:])
        if n == 3:
            whole = whole.transpose(0, 2, 3, 1, 4)
            whole = whole.reshape(4, GROUP, part.shape[0], lead * part.shape[1])
        else:
            whole = whole.transpose(0, 2, 1, 3, 4)
            whole = whole.reshape(4, GROUP, lead * part.shape[0], part.shape[1])
        gathered.append(whole)
    return gathered


def sum_gradients(parts, small, seq, grp):
    lead = seq // 8
    sums = []
    for n, part in enumerate(parts):
        height, lanes = part.shape[2:]
        whole = part.reshape(8, grp, height, lanes)
        if n == 3:
            whole = whole.reshape(8, grp, height, lead, lanes // lead).transpose(0, 3, 1, 2, 4)
        else:
            whole = whole.reshape(8, grp, lead, height // lead, lanes).transpose(0, 2, 1, 3, 4)
        whole = whole.reshape((seq, grp) + whole.shape[3:]).astype(f32)
        whole = lax.psum_scatter(whole, "seq", scatter_dimension=0)
        sums.append(lax.psum_scatter(whole, "grp", scatter_dimension=0))
    return sums + [lax.psum(small, ("seq", "grp"))]


def body(
    tokens,
    coordinates,
    lengths,
    valid,
    first_gain,
    first_shift,
    query_weight,
    query_bias,
    key_weight,
    value_weight,
    value_bias,
    output_weight,
    output_bias,
    second_gain,
    second_shift,
    inner_weight,
    inner_bias,
    outer_weight,
    outer_bias,
    cotangent,
):
    rows, width = tokens.shape
    grp = lax.axis_size("grp")
    seq = lax.axis_size("seq")
    near = (seq, grp) == (8, 4)
    slides = lengths.shape[0]
    shard = query_weight.shape[0]
    frequency = np.exp(np.arange(192) * (-math.log(10000.0) / 192)).astype(np.float32)
    inputs = [
        tokens, cotangent, valid, coordinates.T, lengths,
        np.concatenate([frequency, frequency]).reshape(1, 384),
        first_gain, first_shift, output_bias, second_gain, second_shift, outer_bias, inner_bias,
        query_bias, value_bias,
    ]
    if near:
        weights = [
            query_weight, key_weight, value_weight, output_weight, inner_weight, outer_weight.T,
        ]
    else:
        heads = [w.reshape(shard, 4, 1, HD) for w in (query_weight, key_weight, value_weight)]
        parts = [
            jnp.concatenate(heads, axis=2).reshape(shard, 576),
            output_weight,
            inner_weight,
            outer_weight.T,
        ]
        weights = all_weights(parts, seq, grp)
    results = attention_forward(grp, slides, near, inputs, weights)
    base, msg, q_rows, kv_rows, kv8, kv16, stat, out, grad_middle, grad_merged, small = results[:11]
    late = results[11:14]
    joint_weight = results[14] if near else weights[0]
    saved = [
        grad_merged, first_gain, first_shift, small, q_rows, kv_rows, kv8, kv16, msg, stat, base, grad_middle,
        joint_weight,
    ]
    results = attention_backward(grp, near, saved, late if near else [])
    token_grad, joint_sum, pack = results[:3]
    if near:
        sums = results[3:]
    else:
        joint_sum, *sums, pack = sum_gradients([joint_sum] + list(late), pack, seq, grp)
    results = finish(out, token_grad, joint_sum, *sums, pack)
    output, token_grad = results[:2]
    sum_query, sum_key, sum_value, sum_output, sum_inner, sum_outer = results[2:8]
    sum_outer = sum_outer.T
    small = results[8:]
    return (
        output,
        token_grad,
        small[0],
        small[1],
        sum_query,
        small[2],
        sum_key,
        sum_value,
        small[3],
        sum_output,
        small[4],
        small[5],
        small[6],
        sum_inner,
        small[7],
        sum_outer,
        small[8],
    )


def solution(mesh):
    placed = (
        P(("seq", "grp"), None),
        P(("seq", "grp"), None),
        P(),
        P(("seq", "grp")),
        P(),
        P(),
        P("seq", "grp"),
        P(),
        P("seq", "grp"),
        P("seq", "grp"),
        P(),
        P("seq", "grp"),
        P(),
        P(),
        P(),
        P("seq", "grp"),
        P(),
        P("seq", "grp"),
        P(),
        P(("seq", "grp"), None),
    )
    return jax.shard_map(
        body,
        mesh=mesh,
        in_specs=placed,
        out_specs=(
            P(("seq", "grp"), None),
            P(("seq", "grp"), None),
            P(),
            P(),
            P("seq", "grp"),
            P(),
            P("seq", "grp"),
            P("seq", "grp"),
            P(),
            P("seq", "grp"),
            P(),
            P(),
            P(),
            P("seq", "grp"),
            P(),
            P("seq", "grp"),
            P(),
        ),
        check_vma=False,
    )
```

```python
import functools
import math

import jax
import jax.numpy as jnp
import numpy as np
from jax import lax
from jax.experimental import pallas as pl
from jax.experimental.pallas import tpu as pltpu
from jax.sharding import PartitionSpec as P

epsilon = 1e-05


NT = (((1,), (1,)), ((), ()))
NN = (((1,), (0,)), ((), ()))
f32 = jnp.float32
bf16 = jnp.bfloat16
BIG = 1e30
HD = 48
GROUP = 8
LANES = 128
BLOCK = 32
MSG = 160
FLAG = 2 * HD
MESH = pl.DeviceIdType.MESH
scale = HD ** (-0.5)
scale2 = scale * math.log2(math.e)
q_at = (0, 4096, 6144, 7168, 7680)
q_all = 7936
k_all = 9216


def reverse4(b):
    return (b & 1) * 8 + (b & 2) * 2 + (b & 4) // 2 + (b & 8) // 8


order = [reverse4(b) for b in range(16)]


def chunk_swap(head):
    return reverse4(head) >> 2


def block_swap(quad):
    return reverse4(4 * quad) & 3


def swap_blocks(rows, quad):
    return jnp.concatenate(
        [rows[BLOCK * (b ^ block_swap(quad)) :][:BLOCK] for b in range(16)], axis=0
    )


def swap_chunks(wide, head):
    return jnp.concatenate(
        [wide[:, LANES * (c ^ chunk_swap(head)) :][:, :LANES] for c in range(4)], axis=1
    )


def matmul(a, b, dims=NN):
    return lax.dot_general(a, b, dims, preferred_element_type=f32)


def column_sum(values):
    return jnp.sum(values, axis=0, keepdims=True)


def pick(ref, g):
    both = jnp.stack([ref[:, g], ref[:, g + 4]], axis=1)
    return both.reshape(768, ref.shape[3])


def put(ref, g, value):
    value = value.reshape(4, 2, 96, ref.shape[3])
    ref[:, g] = value[:, 0]
    ref[:, g + 4] = value[:, 1]


def vmem():
    return pl.BlockSpec(memory_space=pltpu.VMEM)


def anywhere():
    return pl.BlockSpec(memory_space=pl.ANY)


def sems(*dims):
    return pltpu.SemaphoreType.DMA(dims)


def params(identity=None):
    if identity is None:
        return pltpu.CompilerParams(vmem_limit_bytes=60 << 20)
    return pltpu.CompilerParams(
        vmem_limit_bytes=60 << 20, collective_id=identity, has_side_effects=True
    )


def shape(dims, dtype):
    return jax.ShapeDtypeStruct(dims, dtype)


def remote(src, dst, send_sem, recv_sem, target):
    return pltpu.make_async_remote_copy(
        src_ref=src, dst_ref=dst, send_sem=send_sem, recv_sem=recv_sem,
        device_id=target, device_id_type=MESH,
    )


class Spot:
    def __init__(self, grp):
        self.grp = grp
        self.linear = lax.axis_index("seq") * grp + lax.axis_index("grp")
        self.member = self.linear % GROUP
        self.base = self.linear - self.member
        self.layer = self.linear // GROUP % 4
        self.half = self.layer % 2

    def device(self, linear):
        return (linear // self.grp, linear % self.grp)

    def beside(self, j):
        return self.device(self.base + j)

    def over(self, layer):
        return self.device(self.linear + GROUP * (layer - self.layer))

    def pair(self):
        return self.device(self.linear + GROUP - 2 * GROUP * self.half)

    def greet(self):
        barrier = pltpu.get_barrier_semaphore()
        for j in range(GROUP):

            @pl.when(self.member != j)
            def _():
                pl.semaphore_signal(barrier, inc=1, device_id=self.beside(j), device_id_type=MESH)

        for o in range(1, 4):
            target = self.over((self.layer + o) % 4)
            pl.semaphore_signal(barrier, inc=1, device_id=target, device_id_type=MESH)
        return lambda: pl.semaphore_wait(barrier, GROUP + 2)


class Exchange:
    def __init__(self, spot, send, recv, send_sem, recv_sem):
        self.spot, self.send_ref, self.recv = spot, send, recv
        self.send_sem, self.recv_sem = send_sem, recv_sem

    def out(self, j):
        s = self.spot
        return remote(self.send_ref.at[j], self.recv.at[s.member], self.send_sem.at[j],
                      self.recv_sem.at[s.member], s.beside(j))

    def inner(self, j):
        return pltpu.make_async_copy(self.send_ref.at[j], self.recv.at[j], self.recv_sem.at[j])

    def choose(self, j, far, near):
        pl.when(self.spot.member != j)(far)
        pl.when(self.spot.member == j)(near)

    def send(self, j):
        self.choose(j, lambda: self.out(j).start(), lambda: self.inner(j).start())

    def wait(self, j):
        def far():
            remote(self.send_ref.at[j], self.recv.at[j], self.send_sem.at[j], self.recv_sem.at[j],
                   self.spot.beside(j)).wait_recv()

        self.choose(j, far, lambda: self.inner(j).wait())

    def drain(self):
        for j in range(GROUP):
            pl.when(self.spot.member != j)(lambda j=j: self.out(j).wait_send())


class Deep:
    def __init__(self, spot, eight, sixteen, send_sem, recv_sem):
        self.copies, self.waits = [], []
        s = spot
        for o in range(1, 4):
            other = (s.layer + o) % 4
            src, there, here = sixteen(o, other)
            self.copies.append(remote(src, there, send_sem.at[o], recv_sem.at[4 - o], s.over(other)))
            self.waits.append(remote(src, here, send_sem.at[o], recv_sem.at[o], s.over(other)))
        src, there, here = eight
        self.copies.append(remote(src, there, send_sem.at[0], recv_sem.at[0], s.pair()))
        self.waits.append(remote(src, here, send_sem.at[0], recv_sem.at[0], s.pair()))

    def start(self):
        for copy in self.copies:
            copy.start()

    def wait(self):
        for copy in self.waits:
            copy.wait_recv()

    def drain(self):
        for copy in self.copies:
            copy.wait_send()


def member_of(x, y, c):
    return x * 4 + y * 2 + c


def place():
    seq, col = lax.axis_index("seq"), lax.axis_index("grp")
    return seq // 2, seq % 2, col // 2, col % 2


def at_place(z, x, y, c):
    return (z * 2 + x, y * 2 + c)


def gather_sems(count):
    return [
        sems(count), sems(4, count), sems(4, count), sems(2, 4, count), sems(2, 4, count),
        sems(2, 4, count), sems(2, 4, count), sems(4, count), sems(4, count),
    ]


class Gather:
    def __init__(self, ins, outs, semaphores):
        self.ins, self.outs = ins, outs
        (self.loc, self.zs, self.zr, self.ps, self.pr,
         self.qs, self.qr, self.cs, self.cr) = semaphores
        self.place = z, x, y, c = place()
        self.me = member_of(x, y, c)
        self.arrays = range(len(ins))
        self.near = [(1 - x, y), (x, 1 - y)]
        self.started = []
        self.done = 0
        self.local = [
            pltpu.make_async_copy(ins[k], outs[k].at[z, self.me], self.loc.at[k])
            for k in self.arrays
        ]
        self.stages = [self.stage1, self.stage2, self.stage3, self.stage4, self.stage5]

    def go(self, copy):
        copy.start()
        self.started.append(copy)

    def start_layers(self):
        z, x, y, c = self.place
        for copy in self.local:
            copy.start()
        for o in (1, 2, 3):
            for k in self.arrays:
                self.go(remote(self.ins[k], self.outs[k].at[z, self.me], self.zs.at[o, k],
                               self.zr.at[4 - o, k], at_place((z + o) % 4, x, y, c)))

    def push(self, layer, slot, sources):
        z, x, y, c = self.place
        for p, (px, py) in enumerate(self.near):
            for k in self.arrays:
                self.go(remote(sources[k], self.outs[k].at[layer, self.me], self.ps.at[p, slot, k],
                               self.pr.at[p, slot, k], at_place(z, px, py, c)))

    def relay(self, slot):
        z, x, y, c = self.place
        layer = (z + slot) % 4
        for p, (px, py) in enumerate(self.near):
            m = member_of(px, py, c)
            for k in self.arrays:
                part = self.outs[k].at[layer, m]
                remote(part, part, self.ps.at[p, slot, k], self.pr.at[p, slot, k],
                       at_place(z, px, py, c)).wait_recv()
        for k in self.arrays:
            rows = self.ins[k].shape[0] // 2
            for p, (px, py) in enumerate(self.near):
                part = self.outs[k].at[layer, member_of(px, py, c), p * rows : (p + 1) * rows]
                self.go(remote(part, part, self.qs.at[p, slot, k], self.qr.at[p, slot, k],
                               at_place(z, *self.near[1 - p], c)))

    def push_own(self):
        self.push(self.place[0], 0, self.ins)

    def stage1(self):
        z, x, y, c = self.place
        for copy in self.local:
            copy.wait()
        for o in (1, 2, 3):
            layer = (z + o) % 4
            parts = [self.outs[k].at[layer, self.me] for k in self.arrays]
            for k in self.arrays:
                remote(parts[k], parts[k], self.zs.at[o, k], self.zr.at[o, k],
                       at_place(layer, x, y, c)).wait_recv()
            self.push(layer, o, parts)

    def stage2(self):
        self.relay(0)
        self.relay(1)

    def stage3(self):
        z, x, y, c = self.place
        self.relay(2)
        self.across(0, x, y)
        self.relay(3)
        self.across(1, 1 - x, y)
        self.across(2, x, 1 - y)

    def across(self, slot, px, py):
        z, x, y, c = self.place
        m = member_of(px, py, c)
        for k in self.arrays:
            part = self.outs[k].at[:, m]
            self.go(remote(part, part, self.cs.at[slot, k], self.cr.at[slot, k],
                           at_place(z, x, y, 1 - c)))

    def stage4(self):
        z, x, y, c = self.place
        far = member_of(1 - x, 1 - y, c)
        for slot in range(4):
            layer = (z + slot) % 4
            for k in self.arrays:
                rows = self.ins[k].shape[0] // 2
                for p in range(2):
                    part = self.outs[k].at[layer, far, p * rows : (p + 1) * rows]
                    remote(part, part, self.qs.at[p, slot, k], self.qr.at[p, slot, k],
                           at_place(z, *self.near[1 - p], c)).wait_recv()
        self.across(3, 1 - x, 1 - y)

    def stage5(self):
        z, x, y, c = self.place
        for slot, (px, py) in enumerate([(x, y), (1 - x, y), (x, 1 - y), (1 - x, 1 - y)]):
            m = member_of(px, py, 1 - c)
            for k in self.arrays:
                part = self.outs[k].at[:, m]
                remote(part, part, self.cs.at[slot, k], self.cr.at[slot, k],
                       at_place(z, x, y, 1 - c)).wait_recv()

    def advance(self, upto):
        while self.done < upto:
            self.stages[self.done]()
            self.done += 1

    def finish(self):
        self.advance(5)

    def drain(self):
        for copy in self.started:
            copy.wait_send()


def gather_wide_sems():
    return [sems(1), sems(2), sems(2), sems(2), sems(2), sems(4, 4), sems(4, 4), sems(4, 4), sems(4, 4)]


class GatherWide:
    def __init__(self, source, out, semaphores):
        self.source, self.out = source, out
        (self.loc, self.ps, self.pr, self.qs, self.qr, self.zs, self.zr, self.cs, self.cr) = semaphores
        self.place = z, x, y, c = place()
        self.near = [(1 - x, y), (x, 1 - y)]
        self.spots = [(x, y), (1 - x, y), (x, 1 - y), (1 - x, 1 - y)]
        self.started = []
        self.done = 0
        self.stages = [self.stage1, self.stage2, self.stage3, self.stage4, self.stage5]

    def go(self, copy):
        copy.start()
        self.started.append(copy)

    def block(self, layer, p, c):
        return self.out.at[layer, member_of(*p, c)]

    def start(self):
        z, x, y, c = self.place
        self.local = pltpu.make_async_copy(self.source, self.block(z, (x, y), c), self.loc.at[0])
        self.local.start()
        for n, p in enumerate(self.near):
            self.go(remote(self.source, self.block(z, (x, y), c), self.ps.at[n], self.pr.at[n],
                           at_place(z, *p, c)))

    def up(self, slot):
        z, x, y, c = self.place
        part = self.block(z, self.spots[slot], c)
        for o in (1, 2, 3):
            self.go(remote(part, part, self.zs.at[o, slot], self.zr.at[4 - o, slot],
                           at_place((z + o) % 4, x, y, c)))

    def swap(self, o, slot):
        z, x, y, c = self.place
        part = self.block((z + o) % 4, self.spots[slot], c)
        self.go(remote(part, part, self.cs.at[o, slot], self.cr.at[o, slot],
                       at_place(z, x, y, 1 - c)))

    def stage1(self):
        z, x, y, c = self.place
        self.local.wait()
        self.up(0)
        self.swap(0, 0)
        rows = self.source.shape[0] // 2
        for n, p in enumerate(self.near):
            part = self.block(z, p, c)
            remote(part, part, self.ps.at[n], self.pr.at[n], at_place(z, *p, c)).wait_recv()
            part = self.out.at[z, member_of(*p, c), n * rows : (n + 1) * rows]
            self.go(remote(part, part, self.qs.at[n], self.qr.at[n],
                           at_place(z, *self.near[1 - n], c)))
            self.up(1 + n)
            self.swap(0, 1 + n)

    def stage2(self):
        z, x, y, c = self.place
        rows = self.source.shape[0] // 2
        for n in range(2):
            part = self.out.at[z, member_of(*self.spots[3], c), n * rows : (n + 1) * rows]
            remote(part, part, self.qs.at[n], self.qr.at[n],
                   at_place(z, *self.near[1 - n], c)).wait_recv()
        self.up(3)
        self.swap(0, 3)

    def arrive(self, slots):
        z, x, y, c = self.place
        for slot in slots:
            for o in (1, 2, 3):
                layer = (z + o) % 4
                part = self.block(layer, self.spots[slot], c)
                remote(part, part, self.zs.at[o, slot], self.zr.at[o, slot],
                       at_place(layer, x, y, c)).wait_recv()
                self.swap(o, slot)

    def stage3(self):
        self.arrive((0, 1))

    def stage4(self):
        self.arrive((2, 3))

    def stage5(self):
        z, x, y, c = self.place
        for o in range(4):
            for slot in range(4):
                part = self.block((z + o) % 4, self.spots[slot], 1 - c)
                remote(part, part, self.cs.at[o, slot], self.cr.at[o, slot],
                       at_place(z, x, y, 1 - c)).wait_recv()

    def advance(self, upto):
        while self.done < upto:
            self.stages[self.done]()
            self.done += 1

    def drain(self):
        for copy in self.started:
            copy.wait_send()


def reduce_scratch(dims):
    half = [(rows // 2, lanes) for rows, lanes in dims]
    count = len(dims)
    return (
        [pltpu.VMEM((4,) + d, bf16) for d in dims]
        + [pltpu.VMEM((4, 4) + d, bf16) for d in dims]
        + [pltpu.VMEM((4, 4) + d, bf16) for d in half]
        + [pltpu.VMEM((2, 4) + d, bf16) for d in half]
        + [pltpu.VMEM((4,) + d, bf16) for d in dims]
        + [sems(4, count), sems(4, count), sems(4, count)]
        + [sems(3, count) for _ in range(4)]
        + [sems(4, count), sems(4, count)]
    )


def add_to(target, source):
    def step(i, _):
        target[i] = target[i] + source[i]
        return 0

    lax.fori_loop(0, 4, step, 0)


class Reduce:
    def __init__(self, ins, outs, scratch):
        count = len(ins)
        self.ins, self.outs, self.arrays = ins, outs, range(count)
        self.stage, self.across, self.one, self.two, self.deep = [
            scratch[i * count : (i + 1) * count] for i in range(5)
        ]
        (self.loc, self.cs, self.cr, self.xs, self.xr, self.ys, self.yr, self.zs, self.zr) = scratch[
            5 * count :
        ]
        self.place = z, x, y, c = place()
        self.mine, self.px, self.py, self.far = (x, y), (1 - x, y), (x, 1 - y), (1 - x, 1 - y)
        self.other = at_place(z, x, y, 1 - c)
        self.to_x, self.to_y = at_place(z, *self.px, c), at_place(z, *self.py, c)
        self.started = []
        self.done = 0
        self.stages = [self.stage1, self.stage2, self.stage3, self.stage4, self.stage5, self.stage6]

    def slot(self, p):
        return p[0] * 2 + p[1]

    def held(self, k, p):
        if self.stage[k] is None:
            return self.ins[k].at[:, member_of(*p, self.place[3])]
        return self.across[k].at[self.slot(p)]

    def go(self, copy):
        copy.start()
        self.started.append(copy)

    def theirs(self, n, p, k):
        c = self.place[3]
        return remote(self.ins[k].at[:, member_of(*p, 1 - c)], self.across[k].at[self.slot(p)],
                      self.cs.at[n, k], self.cr.at[n, k], self.other)

    def ours(self, n, p, k):
        c = self.place[3]
        return pltpu.make_async_copy(self.ins[k].at[:, member_of(*p, c)],
                                     self.stage[k], self.loc.at[n, k])

    def start(self):
        for n, p in enumerate((self.far, self.px, self.py, self.mine)):
            for k in self.arrays:
                self.go(self.theirs(n, p, k))
                if n == 0 and self.stage[k] is not None:
                    self.ours(n, p, k).start()

    def landed(self, n, p):
        for k in self.arrays:
            self.theirs(n, p, k).wait_recv()
            if self.stage[k] is None:
                add_to(self.held(k, p), self.across[k].at[self.slot(p)])
                continue
            self.ours(n, p, k).wait()
            add_to(self.held(k, p), self.stage[k])
            if n < 3:
                self.ours(n + 1, (self.far, self.px, self.py, self.mine)[n + 1], k).start()

    def part(self, k, p, along_x):
        rows = self.ins[k].shape[2] // 2
        at = 0 if along_x else rows
        return self.held(k, p).at[:, at : at + rows]

    def hop(self, k, p, along_x, i, target):
        source = self.part(k, p, along_x)
        if along_x:
            return remote(source, target, self.xs.at[i, k], self.xr.at[i, k], self.to_x)
        return remote(source, target, self.ys.at[i, k], self.yr.at[i, k], self.to_y)

    def first(self, k, p, along_x):
        i = 0 if p is self.far else 1
        return self.hop(k, p, along_x, i, self.one[k].at[2 * i + (0 if along_x else 1)])

    def second(self, k, along_x):
        if along_x:
            return remote(self.part(k, self.py, True), self.two[k].at[0], self.ys.at[2, k],
                          self.yr.at[2, k], self.to_y)
        return remote(self.part(k, self.px, False), self.two[k].at[1], self.xs.at[2, k],
                      self.xr.at[2, k], self.to_x)

    def stage1(self):
        self.landed(0, self.far)
        for k in self.arrays:
            self.go(self.first(k, self.far, True))
            self.go(self.first(k, self.far, False))

    def stage2(self):
        self.landed(1, self.px)
        for k in self.arrays:
            self.go(self.first(k, self.px, True))
        self.landed(2, self.py)
        for k in self.arrays:
            self.go(self.first(k, self.py, False))

    def stage3(self):
        self.landed(3, self.mine)
        for k in self.arrays:
            for along_x, p in ((True, self.py), (False, self.px)):
                self.first(k, self.far, along_x).wait_recv()
                add_to(self.part(k, p, along_x), self.one[k].at[0 if along_x else 1])
                self.go(self.second(k, along_x))

    def stage4(self):
        for k in self.arrays:
            for along_x, p in ((True, self.px), (False, self.py)):
                self.first(k, p, along_x).wait_recv()
                add_to(self.part(k, self.mine, along_x), self.one[k].at[2 if along_x else 3])

    def last(self, k, o):
        z, x, y, c = self.place
        layer = (z + o) % 4
        return remote(self.held(k, self.mine).at[layer], self.deep[k].at[4 - o],
                      self.zs.at[o, k], self.zr.at[4 - o, k], at_place(layer, x, y, c))

    def stage5(self):
        for k in self.arrays:
            for along_x in (True, False):
                self.second(k, along_x).wait_recv()
                add_to(self.part(k, self.mine, along_x), self.two[k].at[0 if along_x else 1])
            for o in (1, 2, 3):
                self.go(self.last(k, o))

    def stage6(self):
        z, x, y, c = self.place
        for k in self.arrays:
            value = self.held(k, self.mine)[z].astype(f32)
            for o in (1, 2, 3):
                here = self.deep[k].at[o]
                remote(here, here, self.zs.at[o, k], self.zr.at[o, k],
                       at_place((z + o) % 4, x, y, c)).wait_recv()
                value = value + self.deep[k][o].astype(f32)
            self.outs[k][...] = value

    def advance(self, upto):
        while self.done < upto:
            self.stages[self.done]()
            self.done += 1

    def drain(self):
        for copy in self.started:
            copy.wait_send()


class Total:
    def __init__(self, small, out, scratch):
        self.small, self.out = small, out
        self.at_c, self.at_p, self.at_z, self.ss, self.rs = scratch
        self.place = z, x, y, c = place()
        self.plane = ((1 - x, y), (x, 1 - y), (1 - x, 1 - y))
        self.started = []

    def swap(self, buffer, index, n, m, target):
        here = buffer.at[index]
        copy = remote(here, here, self.ss.at[n], self.rs.at[m], target)
        copy.start()
        self.started.append(copy)

    def arrive(self, buffer, index, n, target):
        here = buffer.at[index]
        remote(here, here, self.ss.at[n], self.rs.at[n], target).wait_recv()

    def start(self):
        z, x, y, c = self.place
        self.at_c[c] = self.small[...]
        self.swap(self.at_c, c, 0, 0, at_place(z, x, y, 1 - c))

    def middle(self):
        z, x, y, c = self.place
        self.arrive(self.at_c, 1 - c, 0, at_place(z, x, y, 1 - c))
        self.at_p[x * 2 + y] = self.at_c[0] + self.at_c[1]
        for n, p in enumerate(self.plane):
            self.swap(self.at_p, x * 2 + y, 1 + n, 1 + n, at_place(z, *p, c))

    def late(self):
        z, x, y, c = self.place
        for n, p in enumerate(self.plane):
            self.arrive(self.at_p, p[0] * 2 + p[1], 1 + n, at_place(z, *p, c))
        self.at_z[z] = (self.at_p[0] + self.at_p[1]) + (self.at_p[2] + self.at_p[3])
        for o in (1, 2, 3):
            self.swap(self.at_z, z, 3 + o, 7 - o, at_place((z + o) % 4, x, y, c))

    def finish(self):
        z, x, y, c = self.place
        for o in (1, 2, 3):
            self.arrive(self.at_z, (z + o) % 4, 3 + o, at_place((z + o) % 4, x, y, c))
        self.out[...] = (self.at_z[0] + self.at_z[1]) + (self.at_z[2] + self.at_z[3])
        for copy in self.started:
            copy.wait_send()


def total_scratch(dims):
    return [
        pltpu.VMEM((2,) + dims, f32), pltpu.VMEM((4,) + dims, f32), pltpu.VMEM((4,) + dims, f32),
        sems(7), sems(7),
    ]


def reduce_wide_scratch(dims):
    rows, lanes = dims
    return [
        pltpu.VMEM((4,) + dims, bf16), pltpu.VMEM((4, 4) + dims, bf16),
        pltpu.VMEM((4, 4) + dims, bf16), pltpu.VMEM((4, rows // 2, lanes), bf16),
        pltpu.VMEM((2, rows // 2, lanes), bf16),
        sems(4), sems(4), sems(4), sems(4, 4), sems(4, 4), sems(4), sems(4), sems(2), sems(2),
    ]


class ReduceWide:
    def __init__(self, source, out, scratch):
        self.source, self.out = source, out
        (self.stage, self.own, self.deep, self.one, self.two, self.loc, self.cs, self.cr, self.zs,
         self.zr, self.ps, self.pr, self.qs, self.qr) = scratch
        self.place = z, x, y, c = place()
        self.spots = [(x, y), (1 - x, y), (x, 1 - y), (1 - x, 1 - y)]
        self.other = at_place(z, x, y, 1 - c)
        self.to_x, self.to_y = at_place(z, 1 - x, y, c), at_place(z, x, 1 - y, c)
        self.rows = source.shape[2] // 2
        self.started = []
        self.done = 0
        self.stages = [self.stage1, self.stage2, self.stage3, self.stage4, self.stage5, self.stage6]

    def go(self, copy):
        copy.start()
        self.started.append(copy)

    def theirs(self, n):
        c = self.place[3]
        return remote(self.source.at[:, member_of(*self.spots[n], 1 - c)], self.own.at[n],
                      self.cs.at[n], self.cr.at[n], self.other)

    def ours(self, n):
        c = self.place[3]
        return pltpu.make_async_copy(self.source.at[:, member_of(*self.spots[n], c)],
                                     self.stage, self.loc.at[n])

    def start(self):
        for n in range(4):
            self.go(self.theirs(n))
        self.ours(0).start()

    def landed(self, n):
        z, x, y, c = self.place
        self.ours(n).wait()
        self.theirs(n).wait_recv()
        add_to(self.own.at[n], self.stage)
        if n < 3:
            self.ours(n + 1).start()
        for o in (1, 2, 3):
            layer = (z + o) % 4
            self.go(remote(self.own.at[n, layer], self.deep.at[n, 4 - o], self.zs.at[o, n],
                           self.zr.at[4 - o, n], at_place(layer, x, y, c)))

    def stage1(self):
        self.landed(0)
        self.landed(1)

    def stage2(self):
        self.landed(2)
        self.landed(3)

    def gathered(self, n):
        z, x, y, c = self.place
        total = self.own[n, z].astype(f32)
        for o in (1, 2, 3):
            here = self.deep.at[n, o]
            remote(here, here, self.zs.at[o, n], self.zr.at[o, n],
                   at_place((z + o) % 4, x, y, c)).wait_recv()
            total = total + self.deep[n, o].astype(f32)
        self.own[n, z] = total.astype(bf16)

    def part(self, n, along_x):
        at = 0 if along_x else self.rows
        return self.own.at[n, self.place[0], at : at + self.rows]

    def first(self, i):
        n, along_x = ((3, True), (3, False), (1, True), (2, False))[i]
        return remote(self.part(n, along_x), self.one.at[i], self.ps.at[i], self.pr.at[i],
                      self.to_x if along_x else self.to_y)

    def second(self, along_x):
        if along_x:
            return remote(self.part(2, True), self.two.at[0], self.qs.at[0], self.qr.at[0], self.to_y)
        return remote(self.part(1, False), self.two.at[1], self.qs.at[1], self.qr.at[1], self.to_x)

    def add(self, n, along_x, source):
        at = 0 if along_x else self.rows
        z = self.place[0]
        rows = slice(at, at + self.rows)
        self.own[n, z, rows] = (
            self.own[n, z, rows].astype(f32) + source[...].astype(f32)
        ).astype(bf16)

    def stage3(self):
        for n in (0, 1, 2, 3):
            self.gathered(n)
        for i in range(4):
            self.go(self.first(i))

    def stage4(self):
        for i, (n, along_x) in enumerate(((2, True), (1, False))):
            self.first(i).wait_recv()
            self.add(n, along_x, self.one.at[i])
            self.go(self.second(along_x))

    def stage5(self):
        for i, along_x in ((2, True), (3, False)):
            self.first(i).wait_recv()
            self.add(0, along_x, self.one.at[i])

    def stage6(self):
        z = self.place[0]
        for i, along_x in ((0, True), (1, False)):
            self.second(along_x).wait_recv()
            at = 0 if along_x else self.rows
            rows = slice(at, at + self.rows)
            self.out[rows] = self.own[0, z, rows].astype(f32) + self.two[i].astype(f32)

    def advance(self, upto):
        while self.done < upto:
            self.stages[self.done]()
            self.done += 1

    def drain(self):
        for copy in self.started:
            copy.wait_send()


def norm_parts(values):
    average = jnp.mean(values, axis=-1, keepdims=True)
    centred = values - average
    variance = jnp.mean(centred * centred, axis=-1, keepdims=True)
    inverse = lax.rsqrt(variance + epsilon)
    return centred * inverse, inverse


def norm_backward(hat, inverse, gain, grad):
    scaled = grad * gain
    first = jnp.mean(scaled, axis=-1, keepdims=True)
    second = jnp.mean(scaled * hat, axis=-1, keepdims=True)
    return (scaled - first - hat * second) * inverse


def compact(j, rows, packed, places):
    for place, size in places:
        packed[pl.ds(pl.multiple_of(place + size * j, size), size)] = rows[:size]


def widen(pieces):
    total = pieces[-1]
    for piece in reversed(pieces[:-1]):
        blank = jnp.zeros((piece.shape[0], piece.shape[1] - total.shape[1]), f32)
        total = piece + jnp.concatenate([total, blank], axis=1)
    return total


def join_quad(quad, read):
    wide = jnp.concatenate(
        [swap_chunks(read(4 * quad + i), 4 * quad + i) for i in range(4)], axis=0
    )
    return swap_blocks(wide.T, quad)


def join_quads(read):
    pairs = []
    for half in range(2):
        pairs.append(
            jnp.concatenate([join_quad(quad, read) for quad in (2 * half, 2 * half + 1)], axis=1)
        )
    return jnp.concatenate(pairs, axis=1)


def unit_forward(query, key, out):
    lane = lax.broadcasted_iota(jnp.int32, (256, LANES), 1)
    count = len(query)
    scores = [matmul(query[i](), key, NT) for i in range(count)]
    for i in range(count):
        top = jnp.max(scores[i], axis=1, keepdims=True) * scale2
        prob = jnp.exp2(scores[i] * scale2 - top).astype(bf16)
        value = jnp.where(lane == FLAG + 8, top, matmul(prob, key))
        out[i](value.T[HD : HD + 64])


def forward_kernel(grp, slides, gather, *refs):
    refs = list(refs)
    take = lambda n: [refs.pop(0) for _ in range(n)]
    tokens, cot_in, valid, coordinates, ends, frequency = take(6)
    vectors, in_bias = take(6), take(1)[0]
    query_bias, value_bias = take(2)
    shards = take(6) if gather else take(0)
    given = take(0) if gather else take(4)
    kept = take(7)
    out, grad_middle, grad_merged, small = take(4)
    late_grads = take(3)
    kept += take(1) if gather else take(0)
    send, osend, orecv, acc, qc, kvc, tok_sem, ss, rs, os_, or_, ds, dr = take(13)
    wo, wi, wt = take(3)
    dense_scratch = take(10)
    raw, lines_ref, save_sem = take(3)
    base, msg, q_ref, kv_ref, kv8, kv16, stat = take(7)
    gathered = take(1) if gather else []
    keep_sem = take(1)[0]
    savings = []

    def save(source, target):
        copy = pltpu.make_async_copy(source, target, keep_sem.at[len(savings)])
        copy.start()
        savings.append(copy)

    weight = gathered[0] if gather else given[0]
    cot = dense_scratch[0]
    spot = Spot(grp)
    joined = spot.greet()

    def load(source):
        copies = []
        for c in range(6):
            part = source.at[:, LANES * c : LANES * c + LANES]
            copies.append(pltpu.make_async_copy(part, raw.at[c], tok_sem.at[c]))
            copies[-1].start()
        return copies

    def ordered(copies, target):
        for copy in copies:
            copy.wait()
        for b in range(16):
            rows = [raw[c, pl.ds(order[b], BLOCK, stride=16), :] for c in range(6)]
            target[BLOCK * b : BLOCK * b + BLOCK] = jnp.concatenate(rows, axis=1)

    loads = load(tokens)
    vectors = [item[...].reshape(1, 768) for item in vectors]
    if gather:
        (joint_shard,) = take(1)
        pieces = []
        for inner in range(4):
            pieces += [item[:, HD * inner : HD * inner + HD] for item in shards[:3]]
        joint_shard[...] = jnp.concatenate(pieces, axis=1)
        first = Gather([joint_shard], gathered[:1], take(9))
        rest = Gather([shards[3], shards[4].at[:64]], [wo, wi.at[:, :, :64]], take(9))
        last = Gather([shards[5]], [wt], take(9))
        wide_part = GatherWide(shards[4].at[64:], wi.at[:, :, 64:], take(9))
        joined()
        first.start_layers()
        first.push_own()
        wide_part.start()
        rest.push_own()
        last.push_own()
    else:
        loads_late = [
            pltpu.make_async_copy(source, target, save_sem.at[n])
            for n, (source, target) in enumerate(zip(given[1:], (wo, wi, wt)))
        ]
        for copy in loads_late:
            copy.start()
    place_lane = lax.broadcasted_iota(jnp.int32, (1, 512), 1)
    b = place_lane // BLOCK
    b = (b % 2) * 8 + (b // 2 % 2) * 4 + (b // 4 % 2) * 2 + b // 8
    position = spot.linear * 512 + place_lane % BLOCK * 16 + b
    along = jnp.concatenate(
        [coordinates[...], valid[...].reshape(1, 512), jnp.zeros((LANES - 3, 512), jnp.int32)], axis=0
    )
    lines_ref[...] = along.astype(f32).T
    spots = jnp.concatenate(
        [lines_ref[pl.ds(order[b], BLOCK, stride=16), :] for b in range(16)], axis=0
    )
    keep = spots.T[2:3]
    lines = [jnp.where(keep == 1.0, 0.0, -BIG)]
    before = 0
    for n in range(slides):
        after = before + ends[n]
        inside = (position >= before) & (position < after)
        lines.append(jnp.where(inside, 0.0, -BIG))
        before = after
    lines += [jnp.ones((1, 512), f32), jnp.zeros((14 - slides, 512), f32)]
    flags_all = jnp.concatenate(lines, axis=0)
    gain, shift = vectors[:2]
    lane = lax.broadcasted_iota(jnp.int32, (512, 384), 1)
    angle = jnp.where(lane < 192, spots[:, 0:1], spots[:, 1:2]) * frequency[...]
    sine, cosine = jnp.sin(angle), jnp.cos(angle)
    table = jnp.concatenate(
        [
            jnp.concatenate([sine[:, :192], cosine[:, :192]], axis=1),
            jnp.concatenate([sine[:, 192:], cosine[:, 192:]], axis=1),
        ],
        axis=1,
    )
    ordered(loads, base)
    base[...] = base[...] + table
    save(base, kept[0])
    loads = load(cot_in)
    hat, _ = norm_parts(base[...])
    normed = (hat * gain + shift).astype(bf16)
    if gather:
        first.advance(1)
        rest.start_layers()
        last.start_layers()
        first.advance(3)
        wide_part.advance(1)
        first.finish()
        wide_part.advance(2)
    else:
        joined()
    qb, vb = query_bias[...].reshape(1, 768), value_bias[...].reshape(1, 768)
    plane = [Exchange(spot, send.at[i], msg.at[i], ss.at[i], rs.at[i]) for i in range(2)]
    for quad in range(4):
        pieces = []
        for inner in range(4):
            at = HD * (4 * quad + inner)
            pieces += [qb[:, at : at + HD], jnp.zeros((1, HD), f32), vb[:, at : at + HD]]
        part = matmul(normed, pick(weight, quad)) + jnp.concatenate(pieces, axis=1)
        wide = swap_blocks(part.astype(bf16), quad).T
        flags = flags_all
        flags = jnp.concatenate(
            [flags[:, BLOCK * (b ^ block_swap(quad)) :][:, :BLOCK] for b in range(16)], axis=1
        ).astype(bf16)
        for inner in (0, 2, 1, 3):
            head = 4 * quad + inner
            owner, i = head // 2, head % 2
            own = swap_chunks(wide[144 * inner : 144 * inner + 144], head)
            send[i, owner, :96] = own[48:]
            send[i, owner, 96:112] = swap_chunks(flags, head)
            send[i, owner, 112:] = own[:48]
            if i == 0:
                plane[0].send(owner)
    x, y, c = spot.member // 4, spot.member // 2 % 2, spot.member % 2
    pairs = [
        ((1 - x if a else x) * 2 + (1 - y if b else y)) for a, b in ((0, 0), (0, 1), (1, 0), (1, 1))
    ]
    for pair in pairs:
        plane[1].send(pair * 2 + c)
        plane[1].send(pair * 2 + 1 - c)
    if gather:
        save(gathered[0], kept[7])
    row = lax.broadcasted_iota(jnp.int32, (16, 512), 0)
    deeps = []
    results = [Exchange(spot, osend.at[i], orecv.at[i], os_.at[i], or_.at[i]) for i in range(2)]
    if gather:
        rest.advance(1)
        last.advance(1)
    for i in range(2):
        q, kv = q_ref.at[i], kv_ref.at[i]
        def unit(source, q_from, keys, k_from, out_from, count):
            def reader(n):
                return lambda: source[pl.ds(q_from + 256 * n, 256)]

            def writer(n):
                def save(value):
                    acc[:, pl.ds(out_from + 256 * n, 256)] = value

                return save

            unit_forward(
                [reader(n) for n in range(count)], keys[pl.ds(k_from, 1024)],
                [writer(n) for n in range(count)],
            )

        for n, pair in enumerate(pairs):
            for core in range(2):
                j = pair * 2 + core
                plane[i].wait(j)
                block = msg[i, j]
                key_part = jnp.concatenate([block[:112], jnp.zeros((16, 512), bf16)], axis=0).T
                flags = block[96:112].astype(f32)
                chosen = jnp.where(
                    row == 0, 1.0, jnp.where((row <= slides) & (flags == 0.0), 1.0, 0.0)
                )
                query_part = jnp.concatenate(
                    [block[112:], jnp.zeros((HD, 512), bf16), chosen.astype(bf16),
                     jnp.zeros((16, 512), bf16)],
                    axis=0,
                ).T
                kv[pl.ds(pl.multiple_of(512 * j, 512), 512)] = key_part
                q[pl.ds(pl.multiple_of(512 * j, 512), 512)] = query_part
                compact(j, query_part, qc, ((0, 256), (2048, 128), (3072, 64), (3584, 32)))
                compact(j, key_part, kvc, ((0, 256), (2048, 128)))
                kv8[spot.half, i, pl.ds(pl.multiple_of(64 * j, 64), 64)] = key_part[:64]
                kv16[spot.layer, i, pl.ds(pl.multiple_of(32 * j, 32), 32)] = key_part[:32]
            if n == 3:
                own8, own16 = kv8.at[spot.half, i], kv16.at[spot.layer, i]
                deep = Deep(
                    spot, (own8, own8, kv8.at[1 - spot.half, i]),
                    lambda o, other: (own16, own16, kv16.at[other, i]), ds.at[i], dr.at[i],
                )
                deep.start()
                for source, target in zip((msg, q_ref, kv_ref), kept[1:4]):
                    save(source.at[i], target.at[i])
                deeps.append(deep)
            at = pl.multiple_of(pair * 1024, 1024)
            unit(q, at, kv, at, at, 4)

        if gather:
            rest.advance(1 + 2 * i)

        def late(u, _):
            at = pl.multiple_of(u * 1024, 1024)
            unit(qc, at, kvc, at, pl.multiple_of(at + 4096, 1024), 4)
            return 0

        lax.fori_loop(0, 3, late, 0)
        deep.wait()
        for n in range(2):
            kvc[3072 + 512 * n : 3584 + 512 * n] = kv8[n, i]
        for n in range(4):
            kvc[4096 + 256 * n : 4352 + 256 * n] = kv16[n, i]
        unit(qc, 3072, kvc, 3072, 7168, 2)
        unit(qc, 3584, kvc, 4096, 7680, 1)
        place = lax.broadcasted_iota(jnp.int32, (1, 512), 1)
        uses = jnp.where(place < 32, 5.0, jnp.where(place < 64, 4.0, jnp.where(
            place < 128, 3.0, jnp.where(place < 256, 2.0, 1.0))))
        for j in range(GROUP):
            key = msg[i, j, :HD].astype(f32)
            value = msg[i, j, HD : 2 * HD].astype(f32)
            query = msg[i, j, 112:].astype(f32)
            dropped = msg[i, j, FLAG : FLAG + 1].astype(f32) != 0.0
            own = jnp.where(dropped, column_sum(query * key) * scale2 + jnp.log2(uses), -BIG)
            pieces = [
                acc[:, q_at[r] + (512 >> r) * j : q_at[r] + (512 >> r) * (j + 1)] for r in range(5)
            ]
            top = own
            tops = [piece[HD + 8 : HD + 9] for piece in pieces]
            for item in tops:
                spread = item
                if spread.shape[1] < 512:
                    blank = jnp.full((1, 512 - spread.shape[1]), -BIG, f32)
                    spread = jnp.concatenate([spread, blank], axis=1)
                top = jnp.maximum(top, spread)
            scaled = [
                piece[: HD + 8] * jnp.exp2(item - top[:, : item.shape[1]])
                for piece, item in zip(pieces, tops)
            ]
            mix = widen(scaled)
            weight_own = jnp.exp2(own - top)
            total = mix[HD + 1 + slides : HD + 2 + slides] + weight_own
            result = (mix[:HD] + weight_own * value) / total
            stat[i, j, :HD] = result
            stat[i, j, HD : HD + 8] = jnp.broadcast_to(top + jnp.log2(total), (8, 512))
            osend[i, j] = result.astype(bf16)
            results[i].send(j)
        save(stat.at[i], kept[6].at[i])
        if gather:
            rest.advance(2 + 2 * i)
    if gather:
        wide_part.advance(4)
        last.advance(2)
    for i in range(2):
        for j in range(GROUP):
            results[i].wait(j)
    save(kv8, kept[4])
    save(kv16, kept[5])
    ordered(loads, cot)
    merged = dense_scratch[1]

    def ready(step):
        if not gather:
            for copy in loads_late if step == 0 else ():
                copy.wait()
        elif step == 0:
            rest.finish()
            last.advance(3)
        elif step == 1:
            wide_part.advance(5)
        else:
            last.finish()
            for item in (first, rest, wide_part, last):
                item.drain()

    merged[...] = join_quads(lambda h: orecv[h % 2, h // 2])
    dense_part(
        merged, base, cot, wo, wi, wt, vectors, in_bias, out, grad_middle, grad_merged, small,
        late_grads, save_sem, ready, *dense_scratch[2:],
    )
    for copy in savings:
        copy.wait()
    for item in plane + deeps + results:
        item.drain()


def dense_part(
    merged, base, cot, wo, wi, wt, vectors, in_bias, out, grad_middle, grad_merged, small,
    late_grads, save_sem, ready, hat, low, low_t, cot_low, cot_t, grad_low, acts, slopes,
):
    out_bias, gain, shift, last_bias = vectors[2:]
    ready(0)
    pairs = []
    for g in range(0, 4, 2):
        pair = [pick(wo, g + i) for i in range(2)]
        pairs.append(jnp.concatenate(pair, axis=1))
    full = jnp.concatenate(pairs, axis=1)
    middle = base[...] + matmul(merged[...], full) + out_bias
    out[...] = middle + last_bias
    normal, inverse = norm_parts(middle)
    hat[...] = normal
    low[...] = (normal * gain + shift).astype(bf16)
    low_t[...] = low[...].T
    cot_low[...] = cot[...].astype(bf16)
    cot_t[...] = cot_low[...].T
    small[0:1] = column_sum(cot_low[...].astype(f32))
    grad_middle[...] = jnp.zeros((512, 768), f32)

    ready(1)

    def early(g, _):
        inner = matmul(low[...], pick(wi, g)) + in_bias[
            pl.ds(pl.multiple_of(768 * g, 768), 768)
        ].reshape(1, 768)
        phi = 0.5 * (1.0 + lax.erf(inner * 0.7071067811865476))
        acts[g] = (inner * phi).astype(bf16)
        slopes[g] = (phi + inner * jnp.exp(-0.5 * inner * inner) * 0.3989422804014327).astype(bf16)
        return 0

    lax.fori_loop(0, 4, early, 0)
    ready(2)

    def late(g, _):
        for x in range(2):
            lanes = slice(384 * x, 384 * x + 384)
            part = wt[g, 4 * x : 4 * x + 4].reshape(768, 384)
            now = acts[g, :, lanes]
            out[...] += matmul(now, part, NT)
            back = matmul(cot_low[...], part)
            wt[g, 4 * x : 4 * x + 4] = (
                matmul(cot_t[...], now).astype(bf16).reshape(4, 192, 384)
            )
            grad_low[:, lanes] = (back * slopes[g, :, lanes].astype(f32)).astype(bf16)
        small[pl.ds(4 + g, 1)] = column_sum(grad_low[...].astype(f32))
        grad_middle[...] += matmul(grad_low[...], pick(wi, g), NT)
        put(wi, g, matmul(low_t[...], grad_low[...]).astype(bf16))
        return 0

    lax.fori_loop(0, 4, late, 0)
    saves = [
        pltpu.make_async_copy(source, target, save_sem.at[n])
        for n, (source, target) in enumerate(zip((wo, wi, wt), late_grads))
    ]
    saves[1].start()
    saves[2].start()
    grad = grad_middle[...]
    small[1:2] = column_sum(grad * hat[...])
    small[2:3] = column_sum(grad)
    grad = cot[...] + norm_backward(hat[...], inverse, gain, grad)
    grad_middle[...] = grad
    attended = grad.astype(bf16)
    small[3:4] = column_sum(attended.astype(f32))
    grad_merged[...] = matmul(attended, full, NT).astype(bf16)
    grads = matmul(merged[...].T, attended).astype(bf16)
    for g in range(4):
        put(wo, g, grads[:, 192 * g : 192 * g + 192])
    saves[0].start()
    for copy in saves:
        copy.wait()


def attention_forward(grp, slides, gather, inputs, weights):
    out_shape = [
        shape((512, 768), f32),
        shape((2, GROUP, MSG, 512), bf16),
        shape((2, 4096, LANES), bf16),
        shape((2, 4096, LANES), bf16),
        shape((2, 2, 512, LANES), bf16),
        shape((4, 2, 256, LANES), bf16),
        shape((2, GROUP, 56, 512), f32),
        shape((512, 768), f32),
        shape((512, 768), f32),
        shape((512, 768), bf16),
        shape((8, 768), f32),
    ]
    blocks = [(4, GROUP, 96, 192), (4, GROUP, 96, 768), (4, GROUP, 192, 384)]
    out_specs = [anywhere()] * 7 + [vmem()] * 4 + [anywhere()] * 3
    local = [pltpu.VMEM(item.shape, item.dtype) for item in out_shape[:7]]
    out_shape += [shape(dims, bf16) for dims in blocks]
    in_specs = [anywhere()] * 2 + [vmem()] * 2 + [pl.BlockSpec(memory_space=pltpu.SMEM)]
    in_specs += [vmem()] * 10
    extra = []
    if gather:
        in_specs += [vmem()] * 3 + [anywhere()] * 3
        out_shape += [shape((4, GROUP, 96, 576), bf16)]
        out_specs += [anywhere()]
        local += [pltpu.VMEM((4, GROUP, 96, 576), bf16)]
        extra = [pltpu.VMEM((96, 576), bf16)]
        extra += gather_sems(1) + gather_sems(2) + gather_sems(1) + gather_wide_sems()
    else:
        in_specs += [vmem()] + [anywhere()] * 3
    rows = (512, 768)
    return pl.pallas_call(
        functools.partial(forward_kernel, grp, slides, gather),
        name="forward_and_feed",
        in_specs=in_specs,
        out_specs=out_specs,
        out_shape=out_shape,
        scratch_shapes=[
            pltpu.VMEM((2, GROUP, MSG, 512), bf16),
            pltpu.VMEM((2, GROUP, HD, 512), bf16),
            pltpu.VMEM((2, GROUP, HD, 512), bf16),
            pltpu.VMEM((64, q_all), f32),
            pltpu.VMEM((q_all - 4096, LANES), bf16),
            pltpu.VMEM((k_all - 4096, LANES), bf16),
            sems(6),
            sems(2, GROUP), sems(2, GROUP), sems(2, GROUP), sems(2, GROUP), sems(2, 4), sems(2, 4),
        ]
        + [pltpu.VMEM(dims, bf16) for dims in blocks]
        + [
            pltpu.VMEM(rows, f32), pltpu.VMEM(rows, bf16), pltpu.VMEM(rows, f32),
            pltpu.VMEM(rows, bf16), pltpu.VMEM((768, 512), bf16),
            pltpu.VMEM(rows, bf16), pltpu.VMEM((768, 512), bf16), pltpu.VMEM(rows, bf16),
            pltpu.VMEM((4,) + rows, bf16), pltpu.VMEM((4,) + rows, bf16),
            pltpu.VMEM((6, 512, LANES), f32), pltpu.VMEM((512, LANES), f32), sems(3),
        ]
        + local
        + [sems(12)]
        + extra,
        compiler_params=params(1),
    )(*inputs, *weights)


def backward_kernel(grp, reduce, *refs):
    refs = list(refs)
    take = lambda n: [refs.pop(0) for _ in range(n)]
    gm, gain_ref, shift_ref, small = take(4)
    saved = take(6)
    base_in, middle_in, weight_in = take(3)
    parts = take(3) if reduce else take(0)
    token_grad, joint_out, pack = take(3)
    reduced = take(3) if reduce else take(0)
    (gsend, grecv, rsend, rrecv, got8, got16, send8, send16, rows_ref,
     gs, gr, ss, rs, ds, dr, load_sem) = take(16)
    local = take(13)
    (grads,) = take(1)
    spot = Spot(grp)
    joined = spot.greet()
    shares = [Exchange(spot, gsend.at[i], grecv.at[i], gs.at[i], gr.at[i]) for i in range(2)]
    backs = [Exchange(spot, rsend.at[i], rrecv.at[i], ss.at[i], rs.at[i]) for i in range(2)]
    deeps = []
    if reduce:
        ins = [parts[0], parts[1].at[:, :, :64], parts[2]]
        outs = [reduced[0], reduced[1].at[:64], reduced[2]]
        sums = Reduce(ins, outs, take(len(reduce_scratch([(0, 0)] * 3))))
        wide_sum = ReduceWide(parts[1].at[:, :, 64:], reduced[1].at[64:], take(14))
        last_scratch = [take(len(reduce_scratch([(32, 576)])) - 1) for _ in range(3)]
        total_sum = take(5)
    else:
        sums = wide_sum = None

    attend_backward(
        spot, joined, gm, saved, shares, backs, deeps, sums, wide_sum, gsend, grecv, rsend,
        got8, got16, send8, send16, ds, dr, load_sem, *local,
    )
    rows_f32 = local[11]
    late_loads = [pltpu.make_async_copy(weight_in, grads, load_sem.at[0])]
    for n, source in enumerate((base_in, middle_in)):
        for chunk in range(6):
            at = 3072 * n + 512 * chunk
            late_loads.append(
                pltpu.make_async_copy(
                    source.at[:, LANES * chunk : LANES * chunk + LANES],
                    rows_f32.at[at : at + 512],
                    load_sem.at[1 + 6 * n + chunk],
                )
            )
    for copy in late_loads:
        copy.start()

    def loaded(n):
        at = 3072 * n
        return jnp.concatenate(
            [rows_f32[at + 512 * chunk : at + 512 * chunk + 512] for chunk in range(6)], axis=1
        )

    for copy in late_loads:
        copy.wait()
    gain, shift = gain_ref[...].reshape(1, 768), shift_ref[...].reshape(1, 768)
    hat, inverse = norm_parts(loaded(0))
    low_t = (hat * gain + shift).astype(bf16).T
    for i in range(2):
        for j in range(GROUP):
            backs[i].wait(j)
    if reduce:
        wide_sum.advance(4)
    lines = [[], []]
    grad = jnp.zeros((512, 768), f32)
    for quad in range(4):

        def read(head):
            block = rrecv[head % 2, head // 2]
            return jnp.concatenate([block[2 * HD :], block[: 2 * HD]], axis=0)

        now = join_quad(quad, read)
        grad = grad + matmul(now, pick(grads, quad), NT)
        put(grads, quad, matmul(low_t, now).astype(bf16))
        total = column_sum(now.astype(f32))
        for inner in range(4):
            lines[0].append(total[:, 144 * inner : 144 * inner + HD])
            lines[1].append(total[:, 144 * inner + 96 : 144 * inner + 144])
    if reduce:
        joint = []
        for n in range(3):
            rows = slice(32 * n, 32 * n + 32)
            joint.append(
                Reduce([grads.at[:, :, rows]], [joint_out.at[rows]], [None] + last_scratch[n])
            )
            joint[n].start()
        wide_sum.advance(5)

    def flow(step):
        for n, item in enumerate(joint):
            item.advance(min(max(step - n, 0), 6))

    rows_ref[0:1] = column_sum(grad * hat)
    rows_ref[1:2] = column_sum(grad)
    rows_ref[2:3] = jnp.concatenate(lines[0], axis=1)
    rows_ref[3:4] = jnp.concatenate(lines[1], axis=1)
    rows_ref[4:5] = small[3:4]
    rows_ref[5:6] = small[1:2]
    rows_ref[6:7] = small[2:3]
    rows_ref[7:8] = small[0:1]
    rows_ref[8:12] = small[4:8]
    rows_ref[12:16] = jnp.zeros((4, 768), f32)
    token_grad[...] = loaded(1) + norm_backward(hat, inverse, gain, grad)
    if reduce:
        rest = Total(rows_ref, pack, total_sum)
        rest.start()
        flow(1)
        flow(2)
        rest.middle()
        flow(3)
        flow(4)
        rest.late()
        for step in range(5, 8):
            flow(step)
        sums.advance(6)
        wide_sum.advance(6)
        flow(8)
        rest.finish()
        for item in joint:
            item.drain()
    else:
        pack[...] = rows_ref[...]
        save = pltpu.make_async_copy(grads, joint_out, load_sem.at[3])
        save.start()
        save.wait()
    if reduce:
        sums.drain()
        wide_sum.drain()
    for item in shares + backs + deeps:
        item.drain()


def attend_backward(
    spot, joined, gm, saved, shares, backs, deeps, sums, wide_sum, gsend, grecv, rsend, got8, got16,
    send8, send16, ds, dr, load_sem, q_ref, kv_ref, kv8, kv16, msg, stat,
    qc, kvc, dor, kt, ld, dkv, dqt,
):
    reduce = sums is not None
    loads = [
        pltpu.make_async_copy(source, target, load_sem.at[n])
        for n, (source, target) in enumerate(zip(saved, (q_ref, kv_ref, kv8, kv16, msg, stat)))
    ]
    for copy in loads:
        copy.start()
    for quad in range(4):
        wide = swap_blocks(gm[:, 192 * quad : 192 * quad + 192], quad).T
        for inner in (0, 2, 1, 3):
            head = 4 * quad + inner
            i = head % 2
            gsend[i, head // 2] = swap_chunks(wide[HD * inner : HD * inner + HD], head)
            if quad == 0 and inner == 0:
                joined()
            if i == 0:
                shares[0].send(head // 2)
    for j in range(GROUP):
        shares[1].send(j)
    if reduce:
        wide_sum.start()
        sums.start()
    for copy in loads:
        copy.wait()
    for i in range(2):
        q, kv = q_ref.at[i], kv_ref.at[i]
        for n in range(2):
            kvc[3072 + 512 * n : 3584 + 512 * n] = kv8[n, i]
        for n in range(4):
            kvc[4096 + 256 * n : 4352 + 256 * n] = kv16[n, i]
        for n in range(2):
            kt[7 + n] = kvc[3072 + 1024 * n : 4096 + 1024 * n].T[:HD]
        rows = []
        for j in range(GROUP):
            compact(j, q[512 * j : 512 * j + 512], qc, ((0, 256), (2048, 128), (3072, 64), (3584, 32)))
            compact(j, kv[512 * j : 512 * j + 512], kvc, ((0, 256), (2048, 128)))
            key = msg[i, j, :HD]
            kt[j // 2, :, 512 * (j % 2) : 512 * (j % 2) + 512] = key
            kt[4 + j // 4, :, 256 * (j % 4) : 256 * (j % 4) + 256] = key[:, :256]
            kt[6, :, 128 * j : 128 * j + 128] = key[:, :128]
        for j in range(GROUP):
            shares[i].wait(j)
            grad = grecv[i, j]
            delta = column_sum(grad.astype(f32) * stat[i, j, :HD])
            both = jnp.concatenate(
                [stat[i, j, HD : HD + 1], delta, jnp.zeros((6, 512), f32)], axis=0
            )
            rows.append(both)
            ld[:, 512 * j : 512 * j + 512] = both
            ld[:, 4096 + 256 * j : 4352 + 256 * j] = both[:, :256]
            ld[:, 6144 + 128 * j : 6272 + 128 * j] = both[:, :128]
            tall = jnp.concatenate(
                [jnp.zeros((HD, 512), bf16), grad, jnp.zeros((32, 512), bf16)], axis=0
            ).T
            for r, at in enumerate(q_at):
                size = 512 >> r
                dor[at + size * j : at + size * j + size] = tall[:size]
        ld[:, 7168:7680] = jnp.concatenate([both[:, :64] for both in rows], axis=1)
        ld[:, 7680:7936] = jnp.concatenate([both[:, :32] for both in rows], axis=1)

        def unit(source, q_from, keys, k_from, at, seg, count):
            width = 256 * count
            query = source[pl.ds(q_from, width)]
            grad = dor[pl.ds(at, width)]
            total = ld[0:1, pl.ds(at, width)]
            delta = ld[1:2, pl.ds(at, width)]
            sides = jnp.concatenate([grad, query], axis=0)
            size = 256
            dq = jnp.zeros((HD, width), f32)
            for c in range(1024 // size):
                key = keys[pl.ds(k_from + size * c, size)]
                prob = jnp.exp2(matmul(key, query, NT) * scale2 - total)
                slope = (prob * (matmul(key, grad, NT) - delta)).astype(bf16)
                both = jnp.concatenate([prob.astype(bf16), slope], axis=1)
                dkv[pl.ds(seg * 1024 + size * c, size)] = matmul(both, sides)
                dq = dq + matmul(kt[seg, :, size * c : size * c + size], slope)
            dqt[:, pl.ds(at, width)] = dq

        unit(qc, 3072, kvc, 3072, 7168, 7, 2)
        unit(qc, 3584, kvc, 4096, 7680, 8, 1)
        for n in range(2):
            send8[n, i] = dkv[7168 + 512 * n : 7680 + 512 * n].astype(bf16)
        for n in range(4):
            send16[n, i] = dkv[8192 + 256 * n : 8448 + 256 * n].astype(bf16)
        deep = Deep(
            spot, (send8.at[1 - spot.half, i], got8.at[i], got8.at[i]),
            lambda o, other: (send16.at[other, i], got16.at[4 - o, i], got16.at[o, i]),
            ds.at[i], dr.at[i],
        )
        deep.start()
        deeps.append(deep)
        if reduce:
            if i == 0:
                sums.advance(1)
                wide_sum.advance(1)

        def late(u, _):
            at = pl.multiple_of(u * 1024, 1024)
            unit(qc, at, kvc, at, pl.multiple_of(at + 4096, 1024), u + 4, 4)
            return 0

        lax.fori_loop(0, 3, late, 0)
        if reduce:
            sums.advance(2 + 2 * i)
            wide_sum.advance(2)
        deep.wait()
        spot_lane = lax.broadcasted_iota(jnp.int32, (1, 512), 1)
        uses = jnp.where(spot_lane < 32, 5.0, jnp.where(spot_lane < 64, 4.0, jnp.where(
            spot_lane < 128, 3.0, jnp.where(spot_lane < 256, 2.0, 1.0))))
        for j in range(GROUP):
            if j % 2 == 0:
                unit(q, 512 * j, kv, 512 * j, 512 * j, j // 2, 4)
            tall = dkv[512 * j : 512 * j + 512]
            eight = send8[spot.half, i, 64 * j : 64 * j + 64].astype(f32) + got8[
                i, 64 * j : 64 * j + 64
            ].astype(f32)
            sixteen = send16[spot.layer, i, 32 * j : 32 * j + 32].astype(f32)
            for o in range(1, 4):
                sixteen = sixteen + got16[o, i, 32 * j : 32 * j + 32].astype(f32)
            second = dkv[4096 + 256 * j : 4352 + 256 * j]
            third = dkv[6144 + 128 * j : 6272 + 128 * j]
            fourth = third[:64] + eight
            fourth = jnp.concatenate([fourth[:32] + sixteen, fourth[32:]], axis=0)
            third = jnp.concatenate([fourth, third[64:]], axis=0)
            second = jnp.concatenate([second[:128] + third, second[128:]], axis=0)
            wide = jnp.concatenate([tall[:256] + second, tall[256:]], axis=0).T
            key = msg[i, j, :HD].astype(f32)
            value = msg[i, j, HD : 2 * HD].astype(f32)
            query = msg[i, j, 112:].astype(f32)
            grad = grecv[i, j].astype(f32)
            total = ld[0:1, 512 * j : 512 * j + 512]
            delta = ld[1:2, 512 * j : 512 * j + 512]
            dropped = msg[i, j, FLAG : FLAG + 1].astype(f32) != 0.0
            dots = column_sum(query * key) * scale2 - total
            prob = jnp.where(dropped, uses * jnp.exp2(jnp.where(dropped, dots, 0.0)), 0.0)
            slope = prob * (column_sum(grad * value) - delta)
            dq = widen([dqt[:, at + (512 >> r) * j : at + (512 >> r) * (j + 1)]
                        for r, at in enumerate(q_at)])
            rsend[i, j, :HD] = ((wide[:HD] + slope * query) * scale).astype(bf16)
            rsend[i, j, HD : 2 * HD] = (wide[HD : 2 * HD] + prob * grad).astype(bf16)
            rsend[i, j, 2 * HD :] = ((dq + slope * key) * scale).astype(bf16)
            backs[i].send(j)
        if reduce:
            sums.advance(3 + 2 * i)
            wide_sum.advance(2 + i)


def attention_backward(grp, reduce, inputs, parts):
    out_shape = [
        shape((512, 768), f32),
        shape((96, 576), f32) if reduce else shape((4, GROUP, 96, 576), bf16),
        shape((16, 768), f32),
    ]
    out_specs = [vmem(), vmem() if reduce else anywhere(), vmem()]
    extra = []
    if reduce:
        dims = [part.shape[2:] for part in parts]
        out_shape += [shape(d, f32) for d in dims]
        out_specs += [vmem()] * 3
        extra = (
            reduce_scratch([dims[0], (64, 768), dims[2]]) + reduce_wide_scratch((32, 768))
            + 3 * reduce_scratch([(32, 576)])[1:] + total_scratch((16, 768))
        )
    return pl.pallas_call(
        functools.partial(backward_kernel, grp, reduce),
        name="attention_backward",
        in_specs=[vmem()] * 4 + [anywhere()] * (9 + len(parts)),
        out_specs=out_specs,
        out_shape=out_shape,
        scratch_shapes=[
            pltpu.VMEM((2, GROUP, HD, 512), bf16),
            pltpu.VMEM((2, GROUP, HD, 512), bf16),
            pltpu.VMEM((2, GROUP, 3 * HD, 512), bf16),
            pltpu.VMEM((2, GROUP, 3 * HD, 512), bf16),
            pltpu.VMEM((2, 512, LANES), bf16),
            pltpu.VMEM((4, 2, 256, LANES), bf16),
            pltpu.VMEM((2, 2, 512, LANES), bf16),
            pltpu.VMEM((4, 2, 256, LANES), bf16),
            pltpu.VMEM((16, 768), f32),
            sems(2, GROUP), sems(2, GROUP), sems(2, GROUP), sems(2, GROUP), sems(2, 4), sems(2, 4),
            sems(13),
            pltpu.VMEM((2, 4096, LANES), bf16), pltpu.VMEM((2, 4096, LANES), bf16),
            pltpu.VMEM((2, 2, 512, LANES), bf16), pltpu.VMEM((4, 2, 256, LANES), bf16),
            pltpu.VMEM((2, GROUP, MSG, 512), bf16), pltpu.VMEM((2, GROUP, 56, 512), f32),
            pltpu.VMEM((q_all - 4096, LANES), bf16), pltpu.VMEM((k_all - 4096, LANES), bf16),
            pltpu.VMEM((q_all, LANES), bf16), pltpu.VMEM((9, HD, 1024), bf16),
            pltpu.VMEM((8, q_all), f32), pltpu.VMEM((k_all, LANES), f32),
            pltpu.VMEM((HD, q_all), f32),
            pltpu.VMEM((4, GROUP, 96, 576), bf16),
        ] + extra,
        compiler_params=params(2),
    )(*inputs, *parts)


def finish_kernel(out_in, token_in, joint, b_in, c_in, d_in, pack, *refs):
    out, token, query, key, value, b_out, c_out, d_out = refs[:8]
    vectors = refs[8:]
    for source, target in ((out_in, out), (token_in, token)):
        for b in range(16):
            target[pl.ds(order[b], BLOCK, stride=16), :] = source[BLOCK * b : BLOCK * b + BLOCK]

    @pl.when(pl.program_id(0) == 0)
    def _():
        for n, target in enumerate((query, key, value)):
            target[...] = jnp.concatenate(
                [joint[:, 144 * i + HD * n : 144 * i + HD * n + HD] for i in range(4)], axis=1
            )
        b_out[...] = b_in[...]
        c_out[...] = c_in[...]
        d_out[...] = d_in[...]
        for n in (0, 1, 2, 3, 4, 5, 6):
            vectors[n][...] = pack[n]
        vectors[7][...] = jnp.concatenate([pack[8 + n] for n in range(4)], axis=0)
        vectors[8][...] = pack[7]


def finish(out, token_grad, joint, b_sum, c_sum, d_sum, pack):
    shard, hidden = b_sum.shape[0], d_sum.shape[1]
    sizes = [768] * 7 + [3072, 768]
    wide = pl.BlockSpec((512, LANES), lambda n: (0, n))
    whole = lambda *dims: pl.BlockSpec(dims, lambda n: (0,) * len(dims))
    small = [(shard, 192)] * 4 + [(shard, 768), (192, hidden)] + [(size,) for size in sizes]
    return pl.pallas_call(
        finish_kernel,
        name="finish",
        grid=(6,),
        in_specs=[wide] * 2 + [whole(*item.shape) for item in (joint, b_sum, c_sum, d_sum, pack)],
        out_specs=[wide] * 2 + [whole(*dims) for dims in small],
        out_shape=[shape((512, 768), f32)] * 2 + [shape(dims, f32) for dims in small],
        compiler_params=params(),
    )(out, token_grad, joint, b_sum, c_sum, d_sum, pack)


def all_weights(parts, seq, grp):
    gathered = []
    for n, part in enumerate(parts):
        whole = lax.all_gather(lax.all_gather(part, "grp"), "seq")
        lead = whole.shape[0] // 8
        whole = whole.reshape((8, lead) + whole.shape[1:])
        if n == 3:
            whole = whole.transpose(0, 2, 3, 1, 4)
            whole = whole.reshape(4, GROUP, part.shape[0], lead * part.shape[1])
        else:
            whole = whole.transpose(0, 2, 1, 3, 4)
            whole = whole.reshape(4, GROUP, lead * part.shape[0], part.shape[1])
        gathered.append(whole)
    return gathered


def sum_gradients(parts, small, seq, grp):
    lead = seq // 8
    sums = []
    for n, part in enumerate(parts):
        height, lanes = part.shape[2:]
        whole = part.reshape(8, grp, height, lanes)
        if n == 3:
            whole = whole.reshape(8, grp, height, lead, lanes // lead).transpose(0, 3, 1, 2, 4)
        else:
            whole = whole.reshape(8, grp, lead, height // lead, lanes).transpose(0, 2, 1, 3, 4)
        whole = whole.reshape((seq, grp) + whole.shape[3:]).astype(f32)
        whole = lax.psum_scatter(whole, "seq", scatter_dimension=0)
        sums.append(lax.psum_scatter(whole, "grp", scatter_dimension=0))
    return sums + [lax.psum(small, ("seq", "grp"))]


def body(
    tokens,
    coordinates,
    lengths,
    valid,
    first_gain,
    first_shift,
    query_weight,
    query_bias,
    key_weight,
    value_weight,
    value_bias,
    output_weight,
    output_bias,
    second_gain,
    second_shift,
    inner_weight,
    inner_bias,
    outer_weight,
    outer_bias,
    cotangent,
):
    rows, width = tokens.shape
    grp = lax.axis_size("grp")
    seq = lax.axis_size("seq")
    near = (seq, grp) == (8, 4)
    slides = lengths.shape[0]
    shard = query_weight.shape[0]
    frequency = np.exp(np.arange(192) * (-math.log(10000.0) / 192)).astype(np.float32)
    inputs = [
        tokens, cotangent, valid, coordinates.T, lengths,
        np.concatenate([frequency, frequency]).reshape(1, 384),
        first_gain, first_shift, output_bias, second_gain, second_shift, outer_bias, inner_bias,
        query_bias, value_bias,
    ]
    if near:
        weights = [
            query_weight, key_weight, value_weight, output_weight, inner_weight, outer_weight.T,
        ]
    else:
        heads = [w.reshape(shard, 4, 1, HD) for w in (query_weight, key_weight, value_weight)]
        parts = [
            jnp.concatenate(heads, axis=2).reshape(shard, 576),
            output_weight,
            inner_weight,
            outer_weight.T,
        ]
        weights = all_weights(parts, seq, grp)
    results = attention_forward(grp, slides, near, inputs, weights)
    base, msg, q_rows, kv_rows, kv8, kv16, stat, out, grad_middle, grad_merged, small = results[:11]
    late = results[11:14]
    joint_weight = results[14] if near else weights[0]
    saved = [
        grad_merged, first_gain, first_shift, small, q_rows, kv_rows, kv8, kv16, msg, stat, base, grad_middle,
        joint_weight,
    ]
    results = attention_backward(grp, near, saved, late if near else [])
    token_grad, joint_sum, pack = results[:3]
    if near:
        sums = results[3:]
    else:
        joint_sum, *sums, pack = sum_gradients([joint_sum] + list(late), pack, seq, grp)
    results = finish(out, token_grad, joint_sum, *sums, pack)
    output, token_grad = results[:2]
    sum_query, sum_key, sum_value, sum_output, sum_inner, sum_outer = results[2:8]
    sum_outer = sum_outer.T
    small = results[8:]
    return (
        output,
        token_grad,
        small[0],
        small[1],
        sum_query,
        small[2],
        sum_key,
        sum_value,
        small[3],
        sum_output,
        small[4],
        small[5],
        small[6],
        sum_inner,
        small[7],
        sum_outer,
        small[8],
    )


def solution(mesh):
    placed = (
        P(("seq", "grp"), None),
        P(("seq", "grp"), None),
        P(),
        P(("seq", "grp")),
        P(),
        P(),
        P("seq", "grp"),
        P(),
        P("seq", "grp"),
        P("seq", "grp"),
        P(),
        P("seq", "grp"),
        P(),
        P(),
        P(),
        P("seq", "grp"),
        P(),
        P("seq", "grp"),
        P(),
        P(("seq", "grp"), None),
    )
    return jax.shard_map(
        body,
        mesh=mesh,
        in_specs=placed,
        out_specs=(
            P(("seq", "grp"), None),
            P(("seq", "grp"), None),
            P(),
            P(),
            P("seq", "grp"),
            P(),
            P("seq", "grp"),
            P("seq", "grp"),
            P(),
            P("seq", "grp"),
            P(),
            P(),
            P(),
            P("seq", "grp"),
            P(),
            P("seq", "grp"),
            P(),
        ),
        check_vma=False,
    )
```
